256 devices in a mesh: seq: 16 (over y_lo, z), tensor: 16 (over y_hi, x, core).
Axes of the slice: x: 4, y: 4 (y_hi: 2, y_lo: 2; y = y_hi * 2 + y_lo), z: 8, core: 2. Of those that a mesh axis runs over, the one named last changes fastest.
Arguments:
- teacher_hidden: bfloat16 [2048, 16384], P('seq', 'tensor'), may hold values from -400 to 400
- teacher_gain: float32 [16384], P('tensor'), may hold values from 0.1 to 1.9
- projector: bfloat16 [16384, 8192], P('tensor', 'seq'), may hold values from -0.0625 to 0.0625
- student_hidden: bfloat16 [2048, 8192], P('seq', 'tensor'), may hold values from -20 to 20
- student_gain: float32 [8192], P('tensor'), may hold values from 0.1 to 1.9
- query_weight: bfloat16 [8192, 4096], P(None, 'tensor'), may hold values from -0.6 to 0.6
- kv_weight: bfloat16 [2, 8192, 512], P(None, None, 'tensor'), may hold values from -0.6 to 0.6
- out_weight: bfloat16 [4096, 8192], P('tensor'), may hold values from -0.125 to 0.125
- doc_ids: int32 [2048], P('seq'), may hold values from 0 to 7, never falling along the last dimension, each value on 1 to 1024 neighbouring positions
Outputs:
- student_out: bfloat16 [2048, 8192], P('seq', 'tensor')
- loss_rows: float32 [2048], P('seq')
- grad_attn: bfloat16 [2048, 4096], P('seq', 'tensor')
The draws below stay inside these ranges and needn't reach their ends.
Inputs may be any that keep to these rules, and one draw needn't show every extreme that they name: `doc_ids`: each document's positions are consecutive and ids never fall; a document holds at most 1024 positions.
All inputs are finite; a program needn't handle non-finite values.
Results may differ from the reference program's by a relative error of at most 0.03.
The reference program's roundings to bfloat16 on the way count: a program that leaves them out, or rounds other values in their place, can miss the bound.
Values may be sent and summed in bfloat16 or wider, within the bound.
A program may use at most 128 MiB of HBM per device.

```python
import math
import jax
import jax.numpy as jnp
import numpy as np
from jax import lax

DT = 16384
DS = 8192
HEAD_DIM = 128
HEADS = 32
KV_HEADS = 4
TOKENS = 2048
DOCS = 8
DOC_MOST = 1024


def row_col_scales(key, rows, cols):
    row_key, col_key = jax.random.split(key, 2)
    row_scale = 10.0 ** jax.random.uniform(row_key, (rows, 1), dtype=jnp.float32)
    ramp = 0.5 * jnp.arange(cols, dtype=jnp.float32)[None, :] / cols
    col_scale = 10.0 ** (ramp + 0.5 * jax.random.uniform(col_key, (1, cols), dtype=jnp.float32))
    return row_scale * col_scale


def draw_teacher_hidden(key, part):
    key = jax.random.fold_in(key, 11)
    scale_key, base_key = jax.random.split(key, 2)
    scales = row_col_scales(scale_key, TOKENS, DT)
    base = jax.random.truncated_normal(base_key, -4.0, 4.0, (TOKENS, DT))
    return jnp.clip(base * scales, -400.0, 400.0).astype(jnp.bfloat16)


def draw_student_hidden(key, part):
    key = jax.random.fold_in(key, 23)
    scale_key, base_key = jax.random.split(key, 2)
    scales = 0.05 * row_col_scales(scale_key, TOKENS, DS)
    base = jax.random.truncated_normal(base_key, -4.0, 4.0, (TOKENS, DS))
    return jnp.clip(base * scales, -20.0, 20.0).astype(jnp.bfloat16)


def draw_query_weight(key, part):
    key = jax.random.fold_in(key, 37)
    base = jax.random.truncated_normal(key, -4.0, 4.0, (DS, HEADS * HEAD_DIM)) * DS ** (-0.5)
    return jnp.clip(base, -0.59, 0.59).astype(jnp.bfloat16)


def draw_kv_weight(key, part):
    key = jax.random.fold_in(key, 41)
    base = jax.random.truncated_normal(key, -4.0, 4.0, (2, DS, KV_HEADS * HEAD_DIM)) * DS ** (-0.5)
    return jnp.clip(base, -0.59, 0.59).astype(jnp.bfloat16)


def with_spikes(values, stream_key, source, target, blocks, factor):
    owner, partner = [(jnp.arange(values.shape[dim]) // (values.shape[dim] // blocks)).reshape([-1 if axis == dim else 1 for axis in range(values.ndim)]) for dim in (source, target)]
    chosen = jax.random.permutation(stream_key, blocks)[partner]
    strong = (owner == chosen) | (owner == (partner + blocks // 2) % blocks)
    return jnp.where(strong, factor * values, values)


def block_scale(stream_key, extent, pieces, smallest, top_value):
    level = 1.0
    for axis_at, blocks in pieces:
        steps = jax.random.uniform(jax.random.fold_in(jax.random.fold_in(stream_key, 6), axis_at), (blocks,), jnp.float32, smallest / len(pieces), top_value / len(pieces))
        level = level * jnp.repeat(jnp.exp(steps), extent[axis_at] // blocks).reshape((-1,) + (1,) * (len(extent) - 1 - axis_at))
    return level


def profile(number_of, total, reach, skew):
    portions = [(1 << 20) // math.isqrt(grade ** skew) + 1 for grade in range(2, number_of + 1)]
    surplus, given = total - reach - (number_of - 1), [1] * (number_of - 1)
    while surplus > 0:
        free = [i for i in range(number_of - 1) if given[i] < reach]
        pool, budget = sum([portions[i] for i in free]), surplus
        for i in free:
            addition = min(reach - given[i], max(1, budget * portions[i] // pool), surplus)
            given[i] = given[i] + addition
            surplus = surplus - addition
    return np.array([reach] + given)


def ragged(own_key, count, total, reach, skew):
    if count == 2:
        one = jax.random.randint(own_key, (), max(1, total - reach), min(reach, total - 1) + 1)
        return jnp.stack([one, total - one])
    sizes = jnp.asarray(profile(count, total, reach, skew), jnp.int32)
    couples = (count - 1) // 2
    source_of, taker = sizes[1:1 + 2 * couples:2], sizes[2:2 + 2 * couples:2]
    room = jnp.minimum(source_of - 1, reach - taker)
    moved = jax.random.randint(jax.random.fold_in(own_key, 1), (couples,), 0, 1 << 20) % (room + 1)
    sizes = sizes.at[1:1 + 2 * couples:2].set(source_of - moved).at[2:2 + 2 * couples:2].set(taker + moved)
    return sizes[jax.random.permutation(jax.random.fold_in(own_key, 2), count)]


def noise_with(key, extent, deviation, most, pieces, heavy, kind=jnp.bfloat16):
    entries = deviation * jax.random.normal(key, extent, jnp.float32)
    if pieces:
        entries = entries * block_scale(key, extent, pieces, -0.22, 0.18)
    return jnp.clip(with_spikes(entries, jax.random.fold_in(key, 3), *heavy), -most, most).astype(kind)


def setup_inputs(seed: int = 0) -> dict:
    arg_keys = jax.random.split(jax.random.key(seed), 10)
    teacher_hidden = draw_teacher_hidden(jax.random.fold_in(arg_keys[9], 71), 0)
    teacher_gain = jnp.clip(1.0 + 0.18 * jax.random.normal(arg_keys[1], (DT,), jnp.float32), 0.1, 1.9)
    projector = noise_with(arg_keys[2], (DT, DS), DT ** -0.5, 0.0625, ((0, 16), (1, 16)), (0, 1, 16, 2.0))
    student_hidden = draw_student_hidden(jax.random.fold_in(arg_keys[9], 71), 0)
    student_gain = jnp.clip(1.0 + 0.18 * jax.random.normal(arg_keys[4], (DS,), jnp.float32), 0.1, 1.9)
    query_weight = draw_query_weight(jax.random.fold_in(arg_keys[9], 71), 0)
    kv_weight = draw_kv_weight(jax.random.fold_in(arg_keys[9], 71), 0)
    out_weight = noise_with(arg_keys[7], (HEADS * HEAD_DIM, DS), (HEADS * HEAD_DIM) ** -0.5, 0.125, ((0, 16),), (0, 1, 16, 2.0))
    doc_ids = jnp.searchsorted(jnp.cumsum(ragged(arg_keys[8], DOCS, TOKENS, DOC_MOST, 2)), jnp.arange(TOKENS), side="right").astype(jnp.int32)
    return {"teacher_hidden": teacher_hidden, "teacher_gain": teacher_gain, "projector": projector, "student_hidden": student_hidden, "student_gain": student_gain, "query_weight": query_weight, "kv_weight": kv_weight, "out_weight": out_weight, "doc_ids": doc_ids}


def rotate(values, positions, head_size):
    half = head_size // 2
    freq = jnp.exp(-jnp.log(500000.0) * (2.0 * jnp.arange(half, dtype=jnp.float32) / head_size))
    angle = positions.astype(jnp.float32)[:, None] * freq[None, :]
    cosine = jnp.cos(angle)[:, None, :]
    sine = jnp.sin(angle)[:, None, :]
    first = values[..., :half]
    second = values[..., half:]
    return jnp.concatenate([first * cosine - second * sine, second * cosine + first * sine], axis=-1)

def reference(teacher_hidden, teacher_gain, projector, student_hidden, student_gain, query_weight, kv_weight, out_weight, doc_ids):
    teacher_f = teacher_hidden.astype(jnp.float32)
    teacher_scale = lax.rsqrt(lax.optimization_barrier(jnp.sum(teacher_f * teacher_f, axis=1)) / DT + 1e-05)
    teacher_scaled = (teacher_f * teacher_gain).astype(jnp.bfloat16)
    target = jnp.dot(teacher_scaled, projector, preferred_element_type=jnp.float32) * teacher_scale[:, None]
    student_f = student_hidden.astype(jnp.float32)
    student_scale = lax.rsqrt(lax.optimization_barrier(jnp.sum(student_f * student_f, axis=1)) / DS + 1e-05)
    student_norm = (student_f * student_scale[:, None] * student_gain).astype(jnp.bfloat16)
    query_raw = jnp.dot(student_norm, query_weight, preferred_element_type=jnp.float32)
    key_raw = lax.optimization_barrier(jnp.dot(student_norm, kv_weight[0], preferred_element_type=jnp.float32).astype(jnp.bfloat16))
    value = jnp.dot(student_norm, kv_weight[1], preferred_element_type=jnp.float32).astype(jnp.bfloat16)
    key_raw = jnp.transpose(key_raw.reshape(TOKENS, HEAD_DIM, KV_HEADS), (0, 2, 1))
    value = jnp.transpose(value.reshape(TOKENS, HEAD_DIM, KV_HEADS), (0, 2, 1))
    positions = jnp.arange(TOKENS, dtype=jnp.int32)
    query = (rotate(query_raw.reshape(TOKENS, HEADS, HEAD_DIM), positions, HEAD_DIM) * HEAD_DIM ** (-0.5)).astype(jnp.bfloat16)
    key = rotate(key_raw.astype(jnp.float32), positions, HEAD_DIM).astype(jnp.bfloat16)
    allowed = (positions[None, :] <= positions[:, None]) & (doc_ids[None, :] == doc_ids[:, None])
    group = HEADS // KV_HEADS

    def one_head(head):
        query_head = lax.dynamic_index_in_dim(query, head, 1, False)
        kv_index = head // group
        key_head = lax.dynamic_index_in_dim(key, kv_index, 1, False)
        value_head = lax.dynamic_index_in_dim(value, kv_index, 1, False)
        scores = jnp.einsum('qd,kd->qk', query_head.astype(jnp.float32), key_head.astype(jnp.float32))
        scores = jnp.where(allowed, scores, -1e+30)
        top = lax.optimization_barrier(jnp.max(scores, axis=1, keepdims=True))
        probs = jnp.where(allowed, jnp.exp(scores - top), 0.0)
        total = lax.optimization_barrier(jnp.sum(probs, axis=1, keepdims=True))
        return jnp.dot(probs.astype(jnp.bfloat16), value_head, preferred_element_type=jnp.float32) / total
    heads_out = lax.map(one_head, jnp.arange(HEADS, dtype=jnp.int32))
    attn = jnp.transpose(heads_out, (1, 0, 2)).reshape(TOKENS, HEADS * HEAD_DIM).astype(jnp.bfloat16)
    mixed = student_f + jnp.dot(attn, out_weight, preferred_element_type=jnp.float32)
    difference = mixed - target
    loss_rows = lax.optimization_barrier(jnp.sum(difference * difference, axis=1)) / DS
    grad_attn = jnp.dot(difference.astype(jnp.bfloat16), out_weight.T, preferred_element_type=jnp.float32).astype(jnp.bfloat16)
    return (mixed.astype(jnp.bfloat16), loss_rows, grad_attn)
```

```python
import jax
import jax.numpy as jnp
from jax import lax
from jax.experimental import pallas as pl
from jax.experimental.pallas import tpu as pltpu
from jax.sharding import PartitionSpec as P

DT = 16384
DS = 8192
HEAD_DIM = 128
HEADS = 32
KV_HEADS = 4
ROWS = 128
COLS = 512
BACK = 8
F32 = jnp.float32
BF16 = jnp.bfloat16
MESH = pl.DeviceIdType.MESH
NT = (((1,), (1,)), ((), ()))


def nt_dot(a, b):
    return lax.dot_general(a, b, NT, preferred_element_type=F32)


def body(
    th_h, tgain, pj_h, sh_h, sgain, wq_h, wkv_h, wo_h, docs, cos_t, sin_t,
    out_s, out_l, out_g,
    th_v, tg, pj, wq, wkv, wo,
    hb, hn, sq, sg_s, sg_r,
    kvx_s, kvx_r, kv_own, kv_r, docs_r, q_v, attn_v,
    t_own, t_sib_s, t_sib_r, t_x2, t_ra, t_rb, t_xp, t_xm, t_fm, t_fp, t_ys, t_yr, t_fin,
    o_sib_s, o_sib_r, o_x2, o_ra, o_rb, o_xp, o_xm, o_fm, o_fp, o_ys, o_yr, o_fin,
    t3_s, t3_r, db, g_acc, l_s, l_r,
    load_sem, z_ss, z_rs, p_ss, p_rs,
    ag_ss, ag_rs, dg_ss, dg_rs, sm_ss, sm_rs, kx_ss, kx_rs, kv_ss, kv_rs, kf_ss, kf_rs, dc_ss, dc_rs,
    t_ss, t_rs, o_ss, o_rs, t3_ss, t3_rs, l_ss, l_rs,
):
    s = lax.axis_index("seq")
    t = lax.axis_index("tensor")
    yl, z = s // 8, s % 8
    yh, x, c = t // 8, (t // 2) % 4, t % 2

    def tid(y_, x_, c_):
        return y_ * 8 + x_ * 2 + c_

    xp_, xm_ = (x + 1) % 4, (x + 3) % 4
    xf_ = (x + 2) % 4
    yo_ = 1 - yh
    sib = (s, tid(yh, x, 1 - c))
    dev_xp = (s, tid(yh, xp_, c))
    dev_xm = (s, tid(yh, xm_, c))
    dev_yo = (s, tid(yo_, x, c))
    dev_zp = (yl * 8 + (z + 1) % 8, t)
    dev_zm = (yl * 8 + (z + 7) % 8, t)
    dev_yl = ((1 - yl) * 8 + z, t)
    home = x * 2 + c
    dev_t3 = (yl * 8 + home, yh * 8 + z)
    stays = z == home

    started = []

    def copy(src, dst, ss, rs, dev):
        return pltpu.make_async_remote_copy(
            src_ref=src, dst_ref=dst, send_sem=ss, recv_sem=rs, device_id=dev, device_id_type=MESH
        )

    def send(src, dst, ss, rs, dev):
        one = copy(src, dst, ss, rs, dev)
        one.start()
        started.append(one)

    def arrive(dst, ss, rs):
        copy(dst, dst, ss, rs, sib).wait_recv()

    def load(src, dst, k):
        one = pltpu.make_async_copy(src, dst, load_sem.at[k])
        one.start()
        return one

    l_th = load(th_h, th_v, 0)
    l_sh = load(sh_h, hb.at[t], 1)
    l_wkv = load(wkv_h, wkv, 2)
    l_wq = load(wq_h, wq, 3)
    l_pj = load(pj_h, pj.at[yl], 4)
    l_wo = load(wo_h, wo, 5)

    docs_r[...] = jnp.full(docs_r.shape, -1, jnp.int32)
    docs_r[0] = docs[...]
    kv_r[1] = jnp.zeros((BACK + 1, ROWS, HEAD_DIM), BF16)

    barrier = pltpu.get_barrier_semaphore()

    def greet(k, carry):
        pl.semaphore_signal(barrier, inc=1, device_id=(s, (t + k) % 16), device_id_type=MESH)
        pl.semaphore_signal(barrier, inc=1, device_id=((s + k) % 16, t), device_id_type=MESH)
        return carry

    lax.fori_loop(1, 16, greet, 0)

    @pl.when(jnp.logical_not(stays))
    def _():
        pl.semaphore_signal(barrier, inc=1, device_id=dev_t3, device_id_type=MESH)

    pl.semaphore_wait(barrier, jnp.where(stays, 30, 31))

    class Gather:
        def __init__(self, buf, ss, rs):
            self.buf, self.ss, self.rs = buf, ss, rs
            self.near = [tid(yh, xm_, c), tid(yh, xp_, c)]
            self.opp = tid(yo_, x, c)
            self.onear = [tid(yo_, xm_, c), tid(yo_, xp_, c)]
            self.far = [tid(yh, xf_, c), tid(yo_, xf_, c)]
            self.order = [t] + self.near + [self.opp] + self.onear + self.far

        def whole(self, src, slot, k, dev):
            send(src, self.buf.at[slot], self.ss.at[k], self.rs.at[k], dev)

        def half(self, slot, h, k, dev):
            part = self.buf.at[slot, pl.ds(h * 64, 64)]
            send(part, part, self.ss.at[k], self.rs.at[k], dev)

        def got(self, slot, k):
            arrive(self.buf.at[slot], self.ss.at[k], self.rs.at[k])

        def got_half(self, slot, h, k):
            arrive(self.buf.at[slot, pl.ds(h * 64, 64)], self.ss.at[k], self.rs.at[k])

        def to_sib(self, i):
            slot = self.order[i]
            self.whole(self.buf.at[slot], slot, 16 + i, sib)

        def begin(self, src):
            self.whole(src, t, 0, dev_yo)
            self.whole(src, t, 1, dev_xp)
            self.whole(src, t, 2, dev_xm)
            self.whole(src, t, 16, sib)

        def near_step(self):
            self.got(self.near[0], 1)
            self.half(self.near[0], 0, 3, dev_xp)
            self.to_sib(1)
            self.got(self.near[1], 2)
            self.half(self.near[1], 1, 4, dev_xm)
            self.to_sib(2)

        def opp_step(self):
            self.got(self.opp, 0)
            self.whole(self.buf.at[self.opp], self.opp, 5, dev_xp)
            self.whole(self.buf.at[self.opp], self.opp, 6, dev_xm)
            self.to_sib(3)

        def onear_step(self):
            self.got(self.onear[0], 5)
            self.half(self.onear[0], 0, 7, dev_xp)
            self.to_sib(4)
            self.got(self.onear[1], 6)
            self.half(self.onear[1], 1, 8, dev_xm)
            self.to_sib(5)

        def far_step(self):
            self.got_half(self.far[0], 0, 3)
            self.got_half(self.far[0], 1, 4)
            self.to_sib(6)

        def ofar_step(self):
            self.got_half(self.far[1], 0, 7)
            self.got_half(self.far[1], 1, 8)
            self.to_sib(7)

        def theirs(self, i):
            slot = self.order[i] + 1 - 2 * c
            self.got(slot, 16 + i)
            return slot

    ag = Gather(hb, ag_ss, ag_rs)
    ag.begin(sh_h)

    l_th.wait()
    part = jnp.zeros((ROWS, 128), F32)
    z_slot = (z % 2) * 4 + z // 2
    for i in range(8):
        cols = slice(i * 128, (i + 1) * 128)
        f = th_v[:, cols].astype(F32)
        part = part + f * f
        tg[z_slot, :, cols] = (f * tgain[:, cols]).astype(BF16)

    def ring_slot(d):
        zz = (z + d) % 8
        return (zz % 2) * 4 + zz // 2

    def z_send(d, k, dev, h=None):
        slot = ring_slot(d)
        ref = tg.at[slot] if h is None else tg.at[slot, pl.ds(h * 64, 64)]
        send(ref, ref, z_ss.at[k], z_rs.at[k], dev)

    def z_got(d, k, h=None):
        slot = ring_slot(d)
        ref = tg.at[slot] if h is None else tg.at[slot, pl.ds(h * 64, 64)]
        arrive(ref, z_ss.at[k], z_rs.at[k])

    z_send(0, 0, dev_zp)
    z_send(0, 4, dev_zm)

    sg_s[:, 0:COLS] = sgain[...]
    sg_s[:, COLS:COLS + 128] = jnp.sum(part.T, axis=0, keepdims=True)
    sg_r[t] = sg_s[...]

    def small(k):
        return copy(sg_s, sg_r.at[t], sm_ss.at[k], sm_rs.at[k], (s, (t + k) % 16))

    def small_go(k, carry):
        small(k).start()
        return carry

    def small_got(k, carry):
        arrive(sg_r.at[(t + 16 - k) % 16], sm_ss.at[k], sm_rs.at[k])
        return carry

    def small_end(k, carry):
        small(k).wait_send()
        return carry

    lax.fori_loop(1, 16, small_go, 0)

    def docs_copy(k):
        return copy(docs, docs_r.at[k], dc_ss.at[k], dc_rs.at[k], ((s + k) % 16, t))

    def docs_go(k, carry):
        @pl.when(s + k < 16)
        def _():
            docs_copy(k).start()
        return carry

    lax.fori_loop(1, BACK + 1, docs_go, 0)

    sq[...] = jnp.zeros(sq.shape, F32)

    def add_squares(slot):
        total = sq[...]
        for i in range(4):
            f = hb[slot, :, i * 128:(i + 1) * 128].astype(F32)
            total = total + f * f
        sq[...] = total

    ag.near_step()
    ag.opp_step()
    send(pj_h, pj.at[yl], p_ss, p_rs, dev_yl)
    l_sh.wait()
    add_squares(t)
    add_squares(ag.near[0])
    add_squares(ag.near[1])
    add_squares(ag.opp)
    ag.onear_step()
    z_got(7, 0)
    z_send(7, 1, dev_zp)
    z_got(1, 4)
    z_send(1, 5, dev_zm)
    add_squares(ag.onear[0])
    add_squares(ag.onear[1])
    ag.far_step()
    ag.ofar_step()
    add_squares(ag.far[0])
    add_squares(ag.far[1])
    for i in range(8):
        add_squares(ag.theirs(i))
    lax.fori_loop(1, 16, small_got, 0)

    scale = lax.rsqrt(jnp.sum(sq[...], axis=1, keepdims=True) / DS + 1e-05)
    l_wkv.wait()

    def norm_kv(slot, acc):
        f = hb[slot].astype(F32)
        n = (f * scale * sg_r[slot][:, 0:COLS]).astype(BF16)
        hn[slot] = n
        w = wkv[:, :, pl.ds(pl.multiple_of(slot * COLS, COLS), COLS)].reshape(64, COLS)
        return acc + nt_dot(n, w)

    kv_acc = lax.fori_loop(0, 16, norm_kv, jnp.zeros((ROWS, 64), F32))

    row = lax.broadcasted_iota(jnp.int32, (64, 64), 0)
    col = lax.broadcasted_iota(jnp.int32, (64, 64), 1)
    take = ((row >> 3) & 1) * 32 + (row & 7) * 4 + (row >> 4)
    pick = jnp.where(col == take, 1.0, 0.0).astype(BF16)
    kvx_s[...] = nt_dot(pick, kv_acc.astype(BF16)).astype(BF16).reshape(4, 16, 128)
    kvx_r[t] = kvx_s[t // 4]

    def kvx(k):
        to = (t + k) % 16
        return copy(kvx_s.at[to // 4], kvx_r.at[t], kx_ss.at[k], kx_rs.at[k], (s, to))

    def kvx_go(k, carry):
        kvx(k).start()
        return carry

    def kvx_got(k, carry):
        arrive(kvx_r.at[(t + 16 - k) % 16], kx_ss.at[k], kx_rs.at[k])
        return carry

    def kvx_end(k, carry):
        kvx(k).wait_send()
        return carry

    lax.fori_loop(1, 16, kvx_go, 0)

    z_got(6, 1)
    z_send(6, 2, dev_zp)
    z_got(2, 5)
    z_send(2, 6, dev_zm)

    l_wq.wait()

    def q_step(slot, acc):
        w = wq[pl.ds(pl.multiple_of(slot * COLS, COLS), COLS), :]
        return acc + jnp.dot(hn[slot], w, preferred_element_type=F32)

    q_acc = lax.fori_loop(0, 16, q_step, jnp.zeros((ROWS, 256), F32))
    cos2 = jnp.concatenate([cos_t[...], cos_t[...]], axis=0).T
    sin2 = jnp.concatenate([-sin_t[...], sin_t[...]], axis=0).T
    for h in range(2):
        qh = q_acc[:, h * 128:(h + 1) * 128]
        turned = qh * cos2 + pltpu.roll(qh, 64, 1) * sin2
        q_v[h] = (turned * HEAD_DIM ** (-0.5)).astype(BF16)

    lax.fori_loop(1, 16, kvx_got, 0)
    both = kvx_r[...].astype(F32).reshape(16, 2, 8, ROWS)
    k_raw = both[:, 0].reshape(HEAD_DIM, ROWS)
    v_raw = both[:, 1].reshape(HEAD_DIM, ROWS)
    first, second = k_raw[0:64], k_raw[64:128]
    k_rot = jnp.concatenate(
        [first * cos_t[...] - second * sin_t[...], second * cos_t[...] + first * sin_t[...]], axis=0
    )
    kv_own[0] = k_rot.astype(BF16)
    kv_own[1] = v_raw.T.astype(BF16)
    kv_r[0, 0] = kv_own[0]
    kv_r[1, 0] = kv_own[1]

    def kv_copy(k):
        return copy(kv_own.at[c], kv_r.at[c, k], kv_ss.at[k], kv_rs.at[k], ((s + k) % 16, t))

    def kv_fwd(k):
        return copy(kv_r.at[c, k], kv_r.at[c, k], kf_ss.at[k], kf_rs.at[k], sib)

    def kv_go(k, carry):
        @pl.when(s + k < 16)
        def _():
            kv_copy(k).start()
        return carry

    def kv_mid(k, carry):
        @pl.when(s >= k)
        def _():
            arrive(kv_r.at[c, k], kv_ss.at[k], kv_rs.at[k])
            kv_fwd(k).start()
        return carry

    def kv_got(k, carry):
        @pl.when(s >= k)
        def _():
            arrive(kv_r.at[1 - c, k], kf_ss.at[k], kf_rs.at[k])
            arrive(docs_r.at[k], dc_ss.at[k], dc_rs.at[k])
        return carry

    def kv_end(k, carry):
        @pl.when(s >= k)
        def _():
            kv_fwd(k).wait_send()

        @pl.when(s + k < 16)
        def _():
            kv_copy(k).wait_send()
            docs_copy(k).wait_send()
        return carry

    lax.fori_loop(1, BACK + 1, kv_go, 0)

    class Reduce:
        def __init__(self, own, sib_s, sib_r, x2, ra, rb, xp, xm, fm, fp, ys, yr, fin, ss, rs):
            self.own, self.sib_s, self.sib_r = own, sib_s, sib_r
            self.x2, self.ra, self.rb, self.xp, self.xm, self.fm, self.fp = x2, ra, rb, xp, xm, fm, fp
            self.ys, self.yr, self.fin, self.ss, self.rs = ys, yr, fin, ss, rs
            self.y_order = (yo_, yh)
            self.x_order = (xf_, xp_, xm_, x)

        def go(self, src, dst, k, dev):
            send(src, dst, self.ss.at[k], self.rs.at[k], dev)

        def got(self, dst, k):
            arrive(dst, self.ss.at[k], self.rs.at[k])

        def to_sib(self, k, i):
            slot = self.y_order[i] * 4 + self.x_order[k]
            self.go(self.sib_s.at[slot], self.sib_r.at[slot], k * 2 + i, sib)

        def pair(self, k, i):
            slot = self.y_order[i] * 4 + self.x_order[k]
            value = self.own(self.y_order[i], self.x_order[k])
            self.got(self.sib_r.at[slot], k * 2 + i)
            return value + self.sib_r[slot].astype(F32)

        def far_step(self):
            for i in range(2):
                self.x2[i] = self.pair(0, i).astype(BF16)
                self.go(self.x2.at[i, pl.ds(0, 64)], self.ra.at[i], 8 + i, dev_xp)
                self.go(self.x2.at[i, pl.ds(64, 64)], self.rb.at[i], 10 + i, dev_xm)

        def near_step(self):
            for i in range(2):
                value = self.pair(1, i)
                self.got(self.ra.at[i], 8 + i)
                self.xp[i, 0:64] = (value[0:64] + self.ra[i].astype(F32)).astype(BF16)
                self.xp[i, 64:128] = value[64:128].astype(BF16)
                self.go(self.xp.at[i], self.fm.at[i], 12 + i, dev_xp)
                value = self.pair(2, i)
                self.got(self.rb.at[i], 10 + i)
                self.xm[i, 0:64] = value[0:64].astype(BF16)
                self.xm[i, 64:128] = (value[64:128] + self.rb[i].astype(F32)).astype(BF16)
                self.go(self.xm.at[i], self.fp.at[i], 14 + i, dev_xm)

        def join(self, i):
            value = self.pair(3, i)
            self.got(self.fm.at[i], 12 + i)
            self.got(self.fp.at[i], 14 + i)
            return value + self.fm[i].astype(F32) + self.fp[i].astype(F32)

        def join_step(self):
            self.ys[...] = self.join(0).astype(BF16)
            self.go(self.ys, self.yr, 16, dev_yo)
            self.fin[...] = self.join(1)

        def last(self):
            self.got(self.yr, 16)
            return self.fin[...] + self.yr[...].astype(F32)

    rt = Reduce(
        lambda y_, x_: t_own[y_ * 4 + x_],
        t_sib_s, t_sib_r, t_x2, t_ra, t_rb, t_xp, t_xm, t_fm, t_fp, t_ys, t_yr, t_fin, t_ss, t_rs,
    )

    z_got(5, 2)
    z_send(5, 3, dev_zp, 0)
    z_got(3, 6)
    z_send(3, 7, dev_zm, 1)
    z_got(4, 3, 0)
    z_got(4, 7, 1)
    l_pj.wait()
    arrive(pj.at[1 - yl], p_ss, p_rs)

    def products(core, y_):
        rows = tg[pl.ds(core * 4, 4)].reshape(4 * ROWS, 1024)
        return jnp.dot(rows, pj[y_], preferred_element_type=F32).reshape(4, ROWS, COLS)

    for y_ in range(2):
        t_sib_s[y_ * 4:(y_ + 1) * 4] = products(1 - c, y_).astype(BF16)
    for k in range(4):
        for i in range(2):
            rt.to_sib(k, i)
    for y_ in range(2):
        t_own[y_ * 4:(y_ + 1) * 4] = products(c, y_)
    rt.far_step()

    lax.fori_loop(1, BACK + 1, kv_mid, 0)
    rt.near_step()
    lax.fori_loop(1, BACK + 1, kv_got, 0)
    keys = jnp.concatenate([kv_r[0, j] for j in range(BACK + 1)], axis=1)
    values = kv_r[1].reshape((BACK + 1) * ROWS, HEAD_DIM)
    key_doc = jnp.concatenate([docs_r[j] for j in range(BACK + 1)], axis=1)
    row_doc = jnp.broadcast_to(docs[...].astype(F32), (ROWS, ROWS)).T[:, 0:1].astype(jnp.int32)
    wide = (ROWS, (BACK + 1) * ROWS)
    row_at = lax.broadcasted_iota(jnp.int32, wide, 0)
    key_at = lax.broadcasted_iota(jnp.int32, wide, 1)
    allowed = (key_doc == row_doc) & ((key_at >= ROWS) | (key_at <= row_at))
    for h in range(2):
        scores = jnp.dot(q_v[h], keys, preferred_element_type=F32)
        scores = jnp.where(allowed, scores, -1e30)
        probs = jnp.exp(scores - jnp.max(scores, axis=1, keepdims=True))
        total = jnp.sum(probs, axis=1, keepdims=True)
        acc = jnp.dot(probs.astype(BF16), values, preferred_element_type=F32)
        attn_v[:, h * 128:(h + 1) * 128] = (acc / total).astype(BF16)

    l_wo.wait()

    def out_block(y_, x_, core):
        at = pl.multiple_of(tid(y_, x_, core) * COLS, COLS)
        return jnp.dot(attn_v[...], wo[:, pl.ds(at, COLS)], preferred_element_type=F32)

    ro = Reduce(
        lambda y_, x_: out_block(y_, x_, c),
        o_sib_s, o_sib_r, o_x2, o_ra, o_rb, o_xp, o_xm, o_fm, o_fp, o_ys, o_yr, o_fin, o_ss, o_rs,
    )
    for k in range(4):
        for i in range(2):
            slot = ro.y_order[i] * 4 + ro.x_order[k]
            o_sib_s[slot] = out_block(ro.y_order[i], ro.x_order[k], 1 - c).astype(BF16)
            ro.to_sib(k, i)
    ro.far_step()
    rt.join_step()
    ro.near_step()
    t3_s[...] = rt.last().astype(BF16)

    def t3():
        return copy(t3_s, t3_r, t3_ss, t3_rs, dev_t3)

    @pl.when(stays)
    def _():
        t3_r[...] = t3_s[...]

    @pl.when(jnp.logical_not(stays))
    def _():
        t3().start()

    ro.join_step()

    sums = sg_r[0][:, COLS:COLS + 128]
    for i in range(1, 16):
        sums = sums + sg_r[i][:, COLS:COLS + 128]
    t_scale = jnp.broadcast_to(lax.rsqrt(sums / DT + 1e-05), (ROWS, 128)).T

    @pl.when(jnp.logical_not(stays))
    def _():
        arrive(t3_r, t3_ss, t3_rs)

    mixed = hb[t].astype(F32) + ro.last()
    out_s[...] = mixed.astype(BF16)
    target = t3_r[...].astype(F32) * jnp.concatenate([t_scale] * 4, axis=1)
    difference = mixed - target
    db[t] = difference.astype(BF16)
    dg = Gather(db, dg_ss, dg_rs)
    dg.begin(db.at[t])

    squares = difference * difference
    lanes = squares[:, 0:128] + squares[:, 128:256] + squares[:, 256:384] + squares[:, 384:512]
    l_s[...] = jnp.sum(lanes.T, axis=0, keepdims=True)
    l_r[t] = l_s[...]

    def loss(k):
        return copy(l_s, l_r.at[t], l_ss.at[k], l_rs.at[k], (s, (t + k) % 16))

    def loss_go(k, carry):
        loss(k).start()
        return carry

    def loss_got(k, carry):
        arrive(l_r.at[(t + 16 - k) % 16], l_ss.at[k], l_rs.at[k])
        return carry

    def loss_end(k, carry):
        loss(k).wait_send()
        return carry

    lax.fori_loop(1, 16, loss_go, 0)

    g_acc[...] = jnp.zeros(g_acc.shape, F32)

    def add_grad(slot):
        at = pl.multiple_of(slot * COLS, COLS)
        g_acc[...] += nt_dot(db[slot], wo[:, pl.ds(at, COLS)])

    add_grad(t)
    dg.near_step()
    dg.opp_step()
    add_grad(dg.near[0])
    add_grad(dg.near[1])
    add_grad(dg.opp)
    dg.onear_step()
    add_grad(dg.onear[0])
    add_grad(dg.onear[1])
    add_grad(dg.theirs(0))
    add_grad(dg.theirs(1))
    add_grad(dg.theirs(2))
    add_grad(dg.theirs(3))
    dg.far_step()
    add_grad(dg.far[0])
    dg.ofar_step()
    add_grad(dg.far[1])
    for i in range(4, 8):
        add_grad(dg.theirs(i))
    out_g[...] = g_acc[...].astype(BF16)

    lax.fori_loop(1, 16, loss_got, 0)
    loss_sum = l_r[0]
    for i in range(1, 16):
        loss_sum = loss_sum + l_r[i]
    out_l[...] = loss_sum / DS

    for one in started:
        one.wait_send()
    lax.fori_loop(1, 16, small_end, 0)
    lax.fori_loop(1, 16, kvx_end, 0)
    lax.fori_loop(1, BACK + 1, kv_end, 0)
    lax.fori_loop(1, 16, loss_end, 0)

    @pl.when(jnp.logical_not(stays))
    def _():
        t3().wait_send()


def reduce_buffers():
    block = (ROWS, COLS)
    return [
        pltpu.VMEM((8,) + block, BF16),
        pltpu.VMEM((8,) + block, BF16),
        pltpu.VMEM((2,) + block, BF16),
        pltpu.VMEM((2, 64, COLS), BF16),
        pltpu.VMEM((2, 64, COLS), BF16),
        pltpu.VMEM((2,) + block, BF16),
        pltpu.VMEM((2,) + block, BF16),
        pltpu.VMEM((2,) + block, BF16),
        pltpu.VMEM((2,) + block, BF16),
        pltpu.VMEM(block, BF16),
        pltpu.VMEM(block, BF16),
        pltpu.VMEM(block, F32),
    ]


def on_device(
    teacher_hidden, teacher_gain, projector, student_hidden, student_gain,
    query_weight, kv_weight, out_weight, doc_ids,
):
    block = (ROWS, COLS)
    positions = lax.axis_index("seq") * ROWS + jnp.arange(ROWS, dtype=jnp.int32)
    half = HEAD_DIM // 2
    freq = jnp.exp(-jnp.log(500000.0) * (2.0 * jnp.arange(half, dtype=F32) / HEAD_DIM))
    angle = freq[:, None] * positions.astype(F32)[None, :]
    hbm = pl.BlockSpec(memory_space=pl.ANY)
    vmem = pl.BlockSpec(memory_space=pltpu.VMEM)
    dma = pltpu.SemaphoreType.DMA
    out_s, out_l, out_g = pl.pallas_call(
        body,
        out_shape=(
            jax.ShapeDtypeStruct(block, BF16),
            jax.ShapeDtypeStruct((1, ROWS), F32),
            jax.ShapeDtypeStruct((ROWS, 256), BF16),
        ),
        in_specs=[hbm, vmem, hbm, hbm, vmem, hbm, hbm, hbm, vmem, vmem, vmem],
        out_specs=(vmem, vmem, vmem),
        scratch_shapes=[
            pltpu.VMEM((ROWS, 1024), BF16),
            pltpu.VMEM((8, ROWS, 1024), BF16),
            pltpu.VMEM((2, 1024, COLS), BF16),
            pltpu.VMEM((DS, 256), BF16),
            pltpu.VMEM((2, 32, DS), BF16),
            pltpu.VMEM((256, DS), BF16),
            pltpu.VMEM((16,) + block, BF16),
            pltpu.VMEM((16,) + block, BF16),
            pltpu.VMEM((ROWS, 128), F32),
            pltpu.VMEM((1, 640), F32),
            pltpu.VMEM((16, 1, 640), F32),
            pltpu.VMEM((4, 16, ROWS), BF16),
            pltpu.VMEM((16, 16, ROWS), BF16),
            pltpu.VMEM((2, ROWS, HEAD_DIM), BF16),
            pltpu.VMEM((2, BACK + 1, ROWS, HEAD_DIM), BF16),
            pltpu.VMEM((BACK + 1, 1, ROWS), jnp.int32),
            pltpu.VMEM((2, ROWS, HEAD_DIM), BF16),
            pltpu.VMEM((ROWS, 256), BF16),
            pltpu.VMEM((8,) + block, F32),
            *reduce_buffers(),
            *reduce_buffers(),
            pltpu.VMEM(block, BF16),
            pltpu.VMEM(block, BF16),
            pltpu.VMEM((16,) + block, BF16),
            pltpu.VMEM((ROWS, 256), F32),
            pltpu.VMEM((1, ROWS), F32),
            pltpu.VMEM((16, 1, ROWS), F32),
            dma((6,)),
            dma((8,)), dma((8,)), dma, dma,
            dma((24,)), dma((24,)), dma((24,)), dma((24,)),
            dma((16,)), dma((16,)), dma((16,)), dma((16,)),
            dma((9,)), dma((9,)), dma((9,)), dma((9,)), dma((9,)), dma((9,)),
            dma((17,)), dma((17,)), dma((17,)), dma((17,)),
            dma, dma,
            dma((16,)), dma((16,)),
        ],
        compiler_params=pltpu.CompilerParams(
            collective_id=0, has_side_effects=True, vmem_limit_bytes=56 * 1024 * 1024
        ),
    )(
        teacher_hidden, teacher_gain.reshape(1, -1), projector, student_hidden,
        student_gain.reshape(1, -1), query_weight, jnp.transpose(kv_weight, (0, 2, 1)), out_weight,
        doc_ids.reshape(1, -1), jnp.cos(angle), jnp.sin(angle),
    )
    return out_s, out_l.reshape(ROWS), out_g


def solution(mesh):
    in_specs = (
        P("seq", "tensor"),
        P("tensor"),
        P("tensor", "seq"),
        P("seq", "tensor"),
        P("tensor"),
        P(None, "tensor"),
        P(None, None, "tensor"),
        P("tensor", None),
        P("seq"),
    )
    out_specs = (P("seq", "tensor"), P("seq"), P("seq", "tensor"))
    return jax.shard_map(
        on_device, mesh=mesh, in_specs=in_specs, out_specs=out_specs, check_vma=False
    )
```

```python
import math

import jax
import jax.numpy as jnp
from jax import lax
from jax.experimental import pallas as pl
from jax.experimental.pallas import tpu as pltpu
from jax.sharding import PartitionSpec as P

DT = 16384
DS = 8192
HEAD_DIM = 128
HEADS = 32
KV_HEADS = 4
ROWS = 128
COLS = 512
BACK = 8
F32 = jnp.float32
BF16 = jnp.bfloat16
MESH = pl.DeviceIdType.MESH
NT = (((1,), (1,)), ((), ()))


def nt_dot(a, b):
    return lax.dot_general(a, b, NT, preferred_element_type=F32)


def body(
    th_h, tgain, pj_h, sh_h, sgain, wq_h, wkv_h, wo_h, docs,
    out_s, out_l, out_g,
    th_v, tg, pj, wq, wkv, wo, cos_t, sin_t, out_v,
    hb, hn, sg_s, sg_r, scale_v, q_acc, kv_acc,
    kvx_s, kvx_r, kv_own, kv_r, docs_r, q_v, attn_v,
    t_own, o_own, t_sib_s, t_sib_r, t_x2, t_ra, t_rb, t_xp, t_xm, t_fm, t_fp, t_ys, t_yr, t_fin,
    o_sib_s, o_sib_r, o_x2, o_ra, o_rb, o_xp, o_xm, o_fm, o_fp, o_ys, o_yr, o_fin,
    t3_s, t3_r, ts_v, db, g_acc, l_s, l_r,
    load_sem, z_ss, z_rs, p_ss, p_rs,
    ag_ss, ag_rs, dg_ss, dg_rs, sm_ss, sm_rs, kx_ss, kx_rs, kv_ss, kv_rs, kf_ss, kf_rs, dc_ss, dc_rs,
    t_ss, t_rs, o_ss, o_rs, t3_ss, t3_rs, l_ss, l_rs,
):
    s = lax.axis_index("seq")
    t = lax.axis_index("tensor")
    yl, z = s // 8, s % 8
    yh, x, c = t // 8, (t // 2) % 4, t % 2

    def tid(y_, x_, c_):
        return y_ * 8 + x_ * 2 + c_

    xp_, xm_ = (x + 1) % 4, (x + 3) % 4
    xf_ = (x + 2) % 4
    yo_ = 1 - yh
    sib = (s, tid(yh, x, 1 - c))
    dev_xp = (s, tid(yh, xp_, c))
    dev_xm = (s, tid(yh, xm_, c))
    dev_yo = (s, tid(yo_, x, c))
    dev_zp = (yl * 8 + (z + 1) % 8, t)
    dev_zm = (yl * 8 + (z + 7) % 8, t)
    dev_yl = ((1 - yl) * 8 + z, t)
    home = x * 2 + c
    dev_t3 = (yl * 8 + home, yh * 8 + z)
    stays = z == home

    started = []

    def copy(src, dst, ss, rs, dev):
        return pltpu.make_async_remote_copy(
            src_ref=src, dst_ref=dst, send_sem=ss, recv_sem=rs, device_id=dev, device_id_type=MESH
        )

    def send(src, dst, ss, rs, dev):
        one = copy(src, dst, ss, rs, dev)
        one.start()
        started.append(one)

    def arrive(dst, ss, rs):
        copy(dst, dst, ss, rs, sib).wait_recv()

    def load(src, dst, k):
        one = pltpu.make_async_copy(src, dst, load_sem.at[k])
        one.start()
        return one

    l_th = load(th_h, th_v, 0)
    l_sh = load(sh_h, hb.at[t], 1)
    l_wkv = load(wkv_h, wkv, 2)
    l_wq = load(wq_h, wq, 3)
    l_pj = load(pj_h, pj.at[yl], 4)
    l_wo = load(wo_h, wo, 5)

    docs_r[...] = jnp.full(docs_r.shape, -1, jnp.int32)
    docs_r[0] = docs[...]
    kv_r[1] = jnp.zeros((BACK + 1, ROWS, HEAD_DIM), BF16)

    barrier = pltpu.get_barrier_semaphore()

    def greet(k, carry):
        pl.semaphore_signal(barrier, inc=1, device_id=(s, (t + k) % 16), device_id_type=MESH)
        pl.semaphore_signal(barrier, inc=1, device_id=((s + k) % 16, t), device_id_type=MESH)
        return carry

    lax.fori_loop(1, 16, greet, 0)

    @pl.when(jnp.logical_not(stays))
    def _():
        pl.semaphore_signal(barrier, inc=1, device_id=dev_t3, device_id_type=MESH)

    class Gather:
        def __init__(self, buf, ss, rs):
            self.buf, self.ss, self.rs = buf, ss, rs
            self.near = [tid(yh, xm_, c), tid(yh, xp_, c)]
            self.opp = tid(yo_, x, c)
            self.onear = [tid(yo_, xm_, c), tid(yo_, xp_, c)]
            self.far = [tid(yh, xf_, c), tid(yo_, xf_, c)]
            self.order = [t] + self.near + [self.opp] + self.onear + self.far

        def part(self, slot, h):
            return self.buf.at[slot, pl.ds(h * 64, 64)]

        def half(self, slot, h, k, dev, src=None):
            part = self.part(slot, h)
            send(part if src is None else src, part, self.ss.at[k], self.rs.at[k], dev)

        def got_half(self, slot, h, k):
            arrive(self.part(slot, h), self.ss.at[k], self.rs.at[k])

        def to_sib(self, i):
            slot = self.order[i]
            send(self.buf.at[slot], self.buf.at[slot], self.ss.at[16 + i], self.rs.at[16 + i], sib)

        def begin(self, h, src=None):
            self.half(t, h, 0 + h, dev_yo, src)
            self.half(t, h, 2 + h, dev_xp, src)
            self.half(t, h, 4 + h, dev_xm, src)

        def near_relay(self):
            self.got_half(self.near[0], 0, 2)
            self.half(self.near[0], 0, 6, dev_xp)
            self.got_half(self.near[1], 1, 5)
            self.half(self.near[1], 1, 7, dev_xm)

        def near_rest(self):
            self.got_half(self.near[0], 1, 3)
            self.to_sib(1)
            self.got_half(self.near[1], 0, 4)
            self.to_sib(2)

        def opp_half(self, h):
            self.got_half(self.opp, h, 0 + h)
            self.half(self.opp, h, 8 + h, dev_xp)
            self.half(self.opp, h, 10 + h, dev_xm)
            if h == 1:
                self.to_sib(3)

        def onear_a(self):
            self.got_half(self.onear[0], 0, 8)
            self.half(self.onear[0], 0, 12, dev_xp)

        def onear_b(self):
            self.got_half(self.onear[1], 1, 11)
            self.half(self.onear[1], 1, 13, dev_xm)

        def onear_rest(self):
            self.got_half(self.onear[0], 1, 9)
            self.to_sib(4)
            self.got_half(self.onear[1], 0, 10)
            self.to_sib(5)

        def far_step(self):
            self.got_half(self.far[0], 0, 6)
            self.got_half(self.far[0], 1, 7)
            self.to_sib(6)

        def ofar_step(self):
            self.got_half(self.far[1], 0, 12)
            self.got_half(self.far[1], 1, 13)
            self.to_sib(7)

        def theirs(self, i):
            slot = self.order[i] + 1 - 2 * c
            arrive(self.buf.at[slot], self.ss.at[16 + i], self.rs.at[16 + i])
            return slot

    z_slot = (z % 2) * 4 + z // 2
    l_th.wait()
    part = jnp.zeros((ROWS, 128), F32)
    for i in range(8):
        cols = slice(i * 128, (i + 1) * 128)
        f = th_v[:, cols].astype(F32)
        part = part + f * f
        tg[z_slot, :, cols] = (f * tgain[:, cols]).astype(BF16)
    sg_s[:, COLS:COLS + 128] = jnp.sum(part.T, axis=0, keepdims=True)
    l_sh.wait()
    part = jnp.zeros((ROWS, 128), F32)
    for i in range(4):
        f = hb[t, :, i * 128:(i + 1) * 128].astype(F32)
        part = part + f * f
    sg_s[:, COLS + 128:COLS + 256] = jnp.sum(part.T, axis=0, keepdims=True)
    sg_s[:, 0:COLS] = sgain[...]
    sg_r[t] = sg_s[...]

    pl.semaphore_wait(barrier, jnp.where(stays, 30, 31))

    ag = Gather(hb, ag_ss, ag_rs)
    ag.begin(0)
    ag.begin(1)
    ag.to_sib(0)

    def ring_slot(d):
        zz = (z + d) % 8
        return (zz % 2) * 4 + zz // 2

    def z_ref(d, h):
        return tg.at[ring_slot(d), pl.ds(h * 64, 64)]

    def z_send(k):
        up, down = z_ref(-(k // 2) + 8, k % 2), z_ref(k // 2, 1 - k % 2)
        send(up, up, z_ss.at[k], z_rs.at[k], dev_zp)
        send(down, down, z_ss.at[8 + k], z_rs.at[8 + k], dev_zm)

    def z_got(k):
        up, down = z_ref(-(k // 2) + 7, k % 2), z_ref(k // 2 + 1, 1 - k % 2)
        arrive(up, z_ss.at[k], z_rs.at[k])
        arrive(down, z_ss.at[8 + k], z_rs.at[8 + k])

    def z_step(k):
        z_got(k)
        if k + 2 < 7:
            z_send(k + 2)

    z_send(0)
    z_send(1)

    def small(k):
        return copy(sg_s, sg_r.at[t], sm_ss.at[k], sm_rs.at[k], (s, (t + k) % 16))

    def small_go(k, carry):
        small(k).start()
        return carry

    def small_got(k, carry):
        arrive(sg_r.at[(t + 16 - k) % 16], sm_ss.at[k], sm_rs.at[k])
        return carry

    def small_end(k, carry):
        small(k).wait_send()
        return carry

    lax.fori_loop(1, 16, small_go, 0)

    def docs_copy(k):
        return copy(docs, docs_r.at[k], dc_ss.at[k], dc_rs.at[k], ((s + k) % 16, t))

    def docs_go(k, carry):
        @pl.when(s + k < 16)
        def _():
            docs_copy(k).start()
        return carry

    lax.fori_loop(1, BACK + 1, docs_go, 0)

    entry = lax.broadcasted_iota(jnp.int32, (64, ROWS), 0).astype(F32)
    position = (s * ROWS + lax.broadcasted_iota(jnp.int32, (64, ROWS), 1)).astype(F32)
    angle = position * jnp.exp(-math.log(500000.0) * (2.0 * entry / HEAD_DIM))
    cos_t[...] = jnp.cos(angle)
    sin_t[...] = jnp.sin(angle)
    q_acc[...] = jnp.zeros(q_acc.shape, F32)
    kv_acc[...] = jnp.zeros(kv_acc.shape, F32)

    def process(slot):
        for i in range(4):
            cols = slice(i * 128, (i + 1) * 128)
            f = hb[slot, :, cols].astype(F32)
            hn[slot, :, cols] = (f * scale_v[...] * sg_r[slot][:, cols]).astype(BF16)
        at = pl.multiple_of(slot * COLS, COLS)
        kv_acc[...] += nt_dot(hn[slot], wkv[:, :, pl.ds(at, COLS)].reshape(64, COLS))
        q_acc[...] += jnp.dot(hn[slot], wq[pl.ds(at, COLS), :], preferred_element_type=F32)

    ag.near_relay()
    ag.near_rest()
    z_step(0)
    ag.opp_half(0)
    send(pj_h, pj.at[yl], p_ss, p_rs, dev_yl)
    lax.fori_loop(1, 16, small_got, 0)
    sums = sg_r[0][:, COLS:COLS + 256]
    for i in range(1, 16):
        sums = sums + sg_r[i][:, COLS:COLS + 256]
    ts_v[...] = jnp.broadcast_to(lax.rsqrt(sums[:, 0:128] / DT + 1e-05), (ROWS, 128)).T
    scale_v[...] = jnp.broadcast_to(lax.rsqrt(sums[:, 128:256] / DS + 1e-05), (ROWS, 128)).T
    l_wkv.wait()
    l_wq.wait()
    process(t)
    z_step(1)
    ag.opp_half(1)
    ag.onear_a()
    process(ag.near[0])
    process(ag.near[1])
    process(ag.theirs(0))
    ag.onear_b()
    z_step(2)
    ag.onear_rest()
    process(ag.theirs(1))
    process(ag.theirs(2))
    ag.far_step()
    process(ag.opp)
    process(ag.theirs(3))
    ag.ofar_step()
    process(ag.onear[0])
    process(ag.onear[1])
    z_step(3)
    process(ag.far[0])
    process(ag.theirs(4))
    process(ag.theirs(5))
    process(ag.theirs(6))
    process(ag.far[1])
    process(ag.theirs(7))

    row = lax.broadcasted_iota(jnp.int32, (64, 64), 0)
    col = lax.broadcasted_iota(jnp.int32, (64, 64), 1)
    take = ((row >> 3) & 1) * 32 + (row & 7) * 4 + (row >> 4)
    pick = jnp.where(col == take, 1.0, 0.0).astype(BF16)
    kvx_s[...] = nt_dot(pick, kv_acc[...].astype(BF16)).astype(BF16).reshape(4, 16, 128)
    kvx_r[t] = kvx_s[t // 4]

    def kvx(k):
        to = (t + k) % 16
        return copy(kvx_s.at[to // 4], kvx_r.at[t], kx_ss.at[k], kx_rs.at[k], (s, to))

    def kvx_go(k, carry):
        kvx(k).start()
        return carry

    def kvx_got(k, carry):
        arrive(kvx_r.at[(t + 16 - k) % 16], kx_ss.at[k], kx_rs.at[k])
        return carry

    def kvx_end(k, carry):
        kvx(k).wait_send()
        return carry

    lax.fori_loop(1, 16, kvx_go, 0)
    z_step(4)

    cos2 = jnp.concatenate([cos_t[...], cos_t[...]], axis=0).T
    sin2 = jnp.concatenate([-sin_t[...], sin_t[...]], axis=0).T
    for h in range(2):
        qh = q_acc[:, h * 128:(h + 1) * 128]
        turned = qh * cos2 + pltpu.roll(qh, 64, 1) * sin2
        q_v[h] = (turned * HEAD_DIM ** (-0.5)).astype(BF16)

    lax.fori_loop(1, 16, kvx_got, 0)
    both = kvx_r[...].astype(F32).reshape(16, 2, 8, ROWS)
    k_raw = both[:, 0].reshape(HEAD_DIM, ROWS)
    v_raw = both[:, 1].reshape(HEAD_DIM, ROWS)
    first, second = k_raw[0:64], k_raw[64:128]
    k_rot = jnp.concatenate(
        [first * cos_t[...] - second * sin_t[...], second * cos_t[...] + first * sin_t[...]], axis=0
    )
    kv_own[0] = k_rot.astype(BF16)
    kv_own[1] = v_raw.T.astype(BF16)
    kv_r[0, 0] = kv_own[0]
    kv_r[1, 0] = kv_own[1]

    def kv_copy(k):
        return copy(kv_own.at[c], kv_r.at[c, k], kv_ss.at[k], kv_rs.at[k], ((s + k) % 16, t))

    def kv_fwd(k):
        return copy(kv_r.at[c, k], kv_r.at[c, k], kf_ss.at[k], kf_rs.at[k], sib)

    def kv_go(k, carry):
        @pl.when(s + k < 16)
        def _():
            kv_copy(k).start()
        return carry

    def kv_mid(k, carry):
        @pl.when(s >= k)
        def _():
            arrive(kv_r.at[c, k], kv_ss.at[k], kv_rs.at[k])
            kv_fwd(k).start()
        return carry

    def kv_got(k, carry):
        @pl.when(s >= k)
        def _():
            arrive(kv_r.at[1 - c, k], kf_ss.at[k], kf_rs.at[k])
            arrive(docs_r.at[k], dc_ss.at[k], dc_rs.at[k])
        return carry

    def kv_end(k, carry):
        @pl.when(s >= k)
        def _():
            kv_fwd(k).wait_send()

        @pl.when(s + k < 16)
        def _():
            kv_copy(k).wait_send()
            docs_copy(k).wait_send()
        return carry

    lax.fori_loop(1, BACK + 1, kv_go, 0)

    class Reduce:
        def __init__(self, own, sib_s, sib_r, x2, ra, rb, xp, xm, fm, fp, ys, yr, fin, ss, rs):
            self.own, self.sib_s, self.sib_r = own, sib_s, sib_r
            self.x2, self.ra, self.rb, self.xp, self.xm, self.fm, self.fp = x2, ra, rb, xp, xm, fm, fp
            self.ys, self.yr, self.fin, self.ss, self.rs = ys, yr, fin, ss, rs
            self.y_order = (yo_, yh)
            self.x_order = (xf_, xp_, xm_, x)

        def go(self, src, dst, k, dev):
            send(src, dst, self.ss.at[k], self.rs.at[k], dev)

        def got(self, dst, k):
            arrive(dst, self.ss.at[k], self.rs.at[k])

        def slot(self, k, i):
            return self.y_order[i] * 4 + self.x_order[k]

        def to_sib(self, k, i):
            slot = self.slot(k, i)
            self.go(self.sib_s.at[slot], self.sib_r.at[slot], k * 2 + i, sib)

        def sib_got(self, k, i):
            self.got(self.sib_r.at[self.slot(k, i)], k * 2 + i)

        def pair(self, k, i, h):
            slot, rows = self.slot(k, i), slice(h * 64, h * 64 + 64)
            return self.own[slot, rows] + self.sib_r[slot, rows].astype(F32)

        def far(self, i):
            self.sib_got(0, i)
            self.x2[i, 0:64] = self.pair(0, i, 0).astype(BF16)
            self.go(self.x2.at[i, pl.ds(0, 64)], self.ra.at[i], 8 + i, dev_xp)
            self.x2[i, 64:128] = self.pair(0, i, 1).astype(BF16)
            self.go(self.x2.at[i, pl.ds(64, 64)], self.rb.at[i], 10 + i, dev_xm)

        def near(self, i):
            self.sib_got(1, i)
            self.xp[i, 64:128] = self.pair(1, i, 1).astype(BF16)
            self.go(self.xp.at[i, pl.ds(64, 64)], self.fm.at[i, pl.ds(64, 64)], 12 + i, dev_xp)
            self.sib_got(2, i)
            self.xm[i, 0:64] = self.pair(2, i, 0).astype(BF16)
            self.go(self.xm.at[i, pl.ds(0, 64)], self.fp.at[i, pl.ds(0, 64)], 14 + i, dev_xm)

        def relay(self, i):
            self.got(self.ra.at[i], 8 + i)
            self.xp[i, 0:64] = (self.pair(1, i, 0) + self.ra[i].astype(F32)).astype(BF16)
            self.go(self.xp.at[i, pl.ds(0, 64)], self.fm.at[i, pl.ds(0, 64)], 16 + i, dev_xp)
            self.got(self.rb.at[i], 10 + i)
            self.xm[i, 64:128] = (self.pair(2, i, 1) + self.rb[i].astype(F32)).astype(BF16)
            self.go(self.xm.at[i, pl.ds(64, 64)], self.fp.at[i, pl.ds(64, 64)], 18 + i, dev_xm)

        def join(self, i, h):
            rows, at = slice(h * 64, h * 64 + 64), pl.ds(h * 64, 64)
            if h == 0:
                self.sib_got(3, i)
            self.got(self.fm.at[i, at], (16, 12)[h] + i)
            self.got(self.fp.at[i, at], (14, 18)[h] + i)
            return self.pair(3, i, h) + self.fm[i, rows].astype(F32) + self.fp[i, rows].astype(F32)

        def join_other(self):
            for h in range(2):
                rows, at = slice(h * 64, h * 64 + 64), pl.ds(h * 64, 64)
                self.ys[rows] = self.join(0, h).astype(BF16)
                self.go(self.ys.at[at], self.yr.at[at], 20 + h, dev_yo)

        def join_mine(self):
            for h in range(2):
                self.fin[h * 64:h * 64 + 64] = self.join(1, h)

        def last(self, h):
            rows = slice(h * 64, h * 64 + 64)
            self.got(self.yr.at[pl.ds(h * 64, 64)], 20 + h)
            return self.fin[rows] + self.yr[rows].astype(F32)

    rt = Reduce(t_own, t_sib_s, t_sib_r, t_x2, t_ra, t_rb, t_xp, t_xm, t_fm, t_fp, t_ys, t_yr, t_fin, t_ss, t_rs)

    z_step(5)
    z_step(6)
    l_pj.wait()
    arrive(pj.at[1 - yl], p_ss, p_rs)

    def products(core, y_):
        rows = tg[pl.ds(core * 4, 4)].reshape(4 * ROWS, 1024)
        return jnp.dot(rows, pj[y_], preferred_element_type=F32).reshape(4, ROWS, COLS)

    for y_ in range(2):
        t_sib_s[y_ * 4:(y_ + 1) * 4] = products(1 - c, y_).astype(BF16)
    for k in range(4):
        for i in range(2):
            rt.to_sib(k, i)
    lax.fori_loop(1, BACK + 1, kv_mid, 0)
    for y_ in range(2):
        t_own[y_ * 4:(y_ + 1) * 4] = products(c, y_)
    rt.far(0)
    rt.far(1)
    rt.near(0)
    rt.near(1)

    lax.fori_loop(1, BACK + 1, kv_got, 0)
    keys = jnp.concatenate([kv_r[0, j] for j in range(BACK + 1)], axis=1)
    values = kv_r[1].reshape((BACK + 1) * ROWS, HEAD_DIM)
    key_doc = jnp.concatenate([docs_r[j] for j in range(BACK + 1)], axis=1)
    row_doc = jnp.broadcast_to(docs[...].astype(F32), (ROWS, ROWS)).T[:, 0:1].astype(jnp.int32)
    wide = (ROWS, (BACK + 1) * ROWS)
    row_at = lax.broadcasted_iota(jnp.int32, wide, 0)
    key_at = lax.broadcasted_iota(jnp.int32, wide, 1)
    allowed = (key_doc == row_doc) & ((key_at >= ROWS) | (key_at <= row_at))
    for h in range(2):
        scores = jnp.dot(q_v[h], keys, preferred_element_type=F32)
        scores = jnp.where(allowed, scores, -1e30)
        probs = jnp.exp(scores - jnp.max(scores, axis=1, keepdims=True))
        total = jnp.sum(probs, axis=1, keepdims=True)
        acc = jnp.dot(probs.astype(BF16), values, preferred_element_type=F32)
        attn_v[:, h * 128:(h + 1) * 128] = (acc / total).astype(BF16)

    rt.relay(0)
    rt.relay(1)
    l_wo.wait()

    ro = Reduce(o_own, o_sib_s, o_sib_r, o_x2, o_ra, o_rb, o_xp, o_xm, o_fm, o_fp, o_ys, o_yr, o_fin, o_ss, o_rs)

    def out_block(k, i, core):
        at = pl.multiple_of(tid(ro.y_order[i], ro.x_order[k], core) * COLS, COLS)
        return jnp.dot(attn_v[...], wo[:, pl.ds(at, COLS)], preferred_element_type=F32)

    def out_theirs(k, i):
        o_sib_s[ro.slot(k, i)] = out_block(k, i, 1 - c).astype(BF16)
        ro.to_sib(k, i)

    def out_mine(k, i):
        o_own[ro.slot(k, i)] = out_block(k, i, c)

    for k in range(3):
        for i in range(2):
            out_theirs(k, i)
    for i in range(2):
        out_mine(0, i)
        ro.far(i)
    for i in range(2):
        out_theirs(3, i)
        out_mine(1, i)
        out_mine(2, i)
        ro.near(i)
    rt.join_other()
    out_mine(3, 0)
    out_mine(3, 1)
    ro.relay(0)
    ro.relay(1)
    rt.join_mine()
    ro.join_other()
    for h in range(2):
        t3_s[h * 64:h * 64 + 64] = rt.last(h).astype(BF16)

    def t3():
        return copy(t3_s, t3_r, t3_ss, t3_rs, dev_t3)

    @pl.when(stays)
    def _():
        t3_r[...] = t3_s[...]

    @pl.when(jnp.logical_not(stays))
    def _():
        t3().start()

    ro.join_mine()

    @pl.when(jnp.logical_not(stays))
    def _():
        arrive(t3_r, t3_ss, t3_rs)

    dg = Gather(db, dg_ss, dg_rs)
    for h in range(2):
        rows = slice(h * 64, h * 64 + 64)
        mixed = hb[t, rows].astype(F32) + ro.last(h)
        out_v[rows] = mixed.astype(BF16)
        target = t3_r[rows].astype(F32) * jnp.concatenate([ts_v[rows]] * 4, axis=1)
        difference = mixed - target
        db[t, rows] = difference.astype(BF16)
        dg.begin(h)
        squares = difference * difference
        g_acc[rows, 0:128] = (
            squares[:, 0:128] + squares[:, 128:256] + squares[:, 256:384] + squares[:, 384:512]
        )
    dg.to_sib(0)
    l_out = load(out_v, out_s, 6)
    l_s[...] = jnp.sum(g_acc[:, 0:128].T, axis=0, keepdims=True)
    l_r[t] = l_s[...]

    def loss(k):
        return copy(l_s, l_r.at[t], l_ss.at[k], l_rs.at[k], (s, (t + k) % 16))

    def loss_go(k, carry):
        loss(k).start()
        return carry

    def loss_got(k, carry):
        arrive(l_r.at[(t + 16 - k) % 16], l_ss.at[k], l_rs.at[k])
        return carry

    def loss_end(k, carry):
        loss(k).wait_send()
        return carry

    lax.fori_loop(1, 16, loss_go, 0)

    g_acc[...] = jnp.zeros(g_acc.shape, F32)

    def add_grad(slot):
        at = pl.multiple_of(slot * COLS, COLS)
        g_acc[...] += nt_dot(db[slot], wo[:, pl.ds(at, COLS)])

    add_grad(t)
    dg.near_relay()
    dg.near_rest()
    dg.opp_half(0)
    add_grad(dg.theirs(0))
    add_grad(dg.near[0])
    add_grad(dg.near[1])
    dg.opp_half(1)
    dg.onear_a()
    add_grad(dg.theirs(1))
    add_grad(dg.theirs(2))
    add_grad(dg.opp)
    dg.onear_b()
    dg.onear_rest()
    dg.far_step()
    add_grad(dg.theirs(3))
    add_grad(dg.onear[0])
    add_grad(dg.onear[1])
    dg.ofar_step()
    add_grad(dg.far[0])
    add_grad(dg.theirs(4))
    add_grad(dg.theirs(5))
    add_grad(dg.theirs(6))
    add_grad(dg.far[1])
    lax.fori_loop(1, 16, loss_got, 0)
    loss_sum = l_r[0]
    for i in range(1, 16):
        loss_sum = loss_sum + l_r[i]
    out_l[...] = loss_sum / DS
    add_grad(dg.theirs(7))
    out_g[...] = g_acc[...].astype(BF16)

    l_out.wait()
    for one in started:
        one.wait_send()
    lax.fori_loop(1, 16, small_end, 0)
    lax.fori_loop(1, 16, kvx_end, 0)
    lax.fori_loop(1, BACK + 1, kv_end, 0)
    lax.fori_loop(1, 16, loss_end, 0)

    @pl.when(jnp.logical_not(stays))
    def _():
        t3().wait_send()


def place(a, b, c, out_a, out_b, out_c, sem):
    copies = [
        pltpu.make_async_copy(src, dst, sem.at[k])
        for k, (src, dst) in enumerate(((a, out_a), (b, out_b), (c, out_c)))
    ]
    for one in copies:
        one.start()
    for one in copies:
        one.wait()


def reduce_buffers():
    block = (ROWS, COLS)
    return [
        pltpu.VMEM((8,) + block, BF16),
        pltpu.VMEM((8,) + block, BF16),
        pltpu.VMEM((2,) + block, BF16),
        pltpu.VMEM((2, 64, COLS), BF16),
        pltpu.VMEM((2, 64, COLS), BF16),
        pltpu.VMEM((2,) + block, BF16),
        pltpu.VMEM((2,) + block, BF16),
        pltpu.VMEM((2,) + block, BF16),
        pltpu.VMEM((2,) + block, BF16),
        pltpu.VMEM(block, BF16),
        pltpu.VMEM(block, BF16),
        pltpu.VMEM(block, F32),
    ]


def on_device(
    teacher_hidden, teacher_gain, projector, student_hidden, student_gain,
    query_weight, kv_weight, out_weight, doc_ids,
):
    block = (ROWS, COLS)
    hbm = pl.BlockSpec(memory_space=pl.ANY)
    vmem = pl.BlockSpec(memory_space=pltpu.VMEM)
    dma = pltpu.SemaphoreType.DMA
    out_s, out_l, out_g = pl.pallas_call(
        body,
        out_shape=(
            jax.ShapeDtypeStruct(block, BF16),
            jax.ShapeDtypeStruct((1, ROWS), F32),
            jax.ShapeDtypeStruct((ROWS, 256), BF16),
        ),
        in_specs=[hbm, vmem, hbm, hbm, vmem, hbm, hbm, hbm, vmem],
        out_specs=(hbm, vmem, vmem),
        scratch_shapes=[
            pltpu.VMEM((ROWS, 1024), BF16),
            pltpu.VMEM((8, ROWS, 1024), BF16),
            pltpu.VMEM((2, 1024, COLS), BF16),
            pltpu.VMEM((DS, 256), BF16),
            pltpu.VMEM((2, 32, DS), BF16),
            pltpu.VMEM((256, DS), BF16),
            pltpu.VMEM((64, ROWS), F32),
            pltpu.VMEM((64, ROWS), F32),
            pltpu.VMEM(block, BF16),
            pltpu.VMEM((16,) + block, BF16),
            pltpu.VMEM((16,) + block, BF16),
            pltpu.VMEM((1, 768), F32),
            pltpu.VMEM((16, 1, 768), F32),
            pltpu.VMEM((ROWS, 128), F32),
            pltpu.VMEM((ROWS, 256), F32),
            pltpu.VMEM((ROWS, 64), F32),
            pltpu.VMEM((4, 16, ROWS), BF16),
            pltpu.VMEM((16, 16, ROWS), BF16),
            pltpu.VMEM((2, ROWS, HEAD_DIM), BF16),
            pltpu.VMEM((2, BACK + 1, ROWS, HEAD_DIM), BF16),
            pltpu.VMEM((BACK + 1, 1, ROWS), jnp.int32),
            pltpu.VMEM((2, ROWS, HEAD_DIM), BF16),
            pltpu.VMEM((ROWS, 256), BF16),
            pltpu.VMEM((8,) + block, F32),
            pltpu.VMEM((8,) + block, F32),
            *reduce_buffers(),
            *reduce_buffers(),
            pltpu.VMEM(block, BF16),
            pltpu.VMEM(block, BF16),
            pltpu.VMEM((ROWS, 128), F32),
            pltpu.VMEM((16,) + block, BF16),
            pltpu.VMEM((ROWS, 256), F32),
            pltpu.VMEM((1, ROWS), F32),
            pltpu.VMEM((16, 1, ROWS), F32),
            dma((7,)),
            dma((16,)), dma((16,)), dma, dma,
            dma((24,)), dma((24,)), dma((24,)), dma((24,)),
            dma((16,)), dma((16,)), dma((16,)), dma((16,)),
            dma((9,)), dma((9,)), dma((9,)), dma((9,)), dma((9,)), dma((9,)),
            dma((24,)), dma((24,)), dma((24,)), dma((24,)),
            dma, dma,
            dma((16,)), dma((16,)),
        ],
        compiler_params=pltpu.CompilerParams(
            collective_id=0, has_side_effects=True, vmem_limit_bytes=56 * 1024 * 1024
        ),
    )(
        teacher_hidden, teacher_gain.reshape(1, -1), projector, student_hidden,
        student_gain.reshape(1, -1), query_weight, jnp.transpose(kv_weight, (0, 2, 1)), out_weight,
        doc_ids.reshape(1, -1),
    )
    out_s, out_l, out_g = pl.pallas_call(
        place,
        out_shape=(
            jax.ShapeDtypeStruct(block, BF16),
            jax.ShapeDtypeStruct((1, ROWS), F32),
            jax.ShapeDtypeStruct((ROWS, 256), BF16),
        ),
        in_specs=[hbm, hbm, hbm],
        out_specs=(hbm, hbm, hbm),
        scratch_shapes=[dma((3,))],
    )(out_s, out_l, out_g)
    return out_s, out_l.reshape(ROWS), out_g


def solution(mesh):
    in_specs = (
        P("seq", "tensor"),
        P("tensor"),
        P("tensor", "seq"),
        P("seq", "tensor"),
        P("tensor"),
        P(None, "tensor"),
        P(None, None, "tensor"),
        P("tensor", None),
        P("seq"),
    )
    out_specs = (P("seq", "tensor"), P("seq"), P("seq", "tensor"))
    return jax.shard_map(
        on_device, mesh=mesh, in_specs=in_specs, out_specs=out_specs, check_vma=False
    )
```

```python
import math

import jax
import jax.numpy as jnp
from jax import lax
from jax.experimental import pallas as pl
from jax.experimental.pallas import tpu as pltpu
from jax.sharding import PartitionSpec as P

DT = 16384
DS = 8192
HEAD_DIM = 128
HEADS = 32
KV_HEADS = 4
ROWS = 128
COLS = 512
BACK = 8
F32 = jnp.float32
BF16 = jnp.bfloat16
MESH = pl.DeviceIdType.MESH
NT = (((1,), (1,)), ((), ()))


def nt_dot(a, b):
    return lax.dot_general(a, b, NT, preferred_element_type=F32)


def body(
    th_h, tgain_h, pj_h, sh_h, sgain_h, wq_h, wkv_h, wo_h, docs_h,
    out_s, out_l, out_g,
    tgain, sgain, docs, th_v, tg, pj, wq, wkv, wo, cos_t, sin_t,
    hb, hn, sg_s, sg_r, scale_v, q_acc, kv_acc,
    kvx_s, kvx_r, kv_own, kv_r, docs_r, q_v, attn_v,
    t_own, o_own, t_sib_s, t_sib_r, t_x2, t_ra, t_rb, t_xp, t_xm, t_fm, t_fp, t_ys, t_yr, t_fin,
    o_sib_s, o_sib_r, o_x2, o_ra, o_rb, o_xp, o_xm, o_fm, o_fp, o_ys, o_yr, o_fin,
    t3_s, t3_r, ts_v, db, g_acc, l_s, l_r,
    load_sem, z_ss, z_rs, p_ss, p_rs,
    ag_ss, ag_rs, dg_ss, dg_rs, sm_ss, sm_rs, kx_ss, kx_rs, kv_ss, kv_rs, kf_ss, kf_rs, dc_ss, dc_rs,
    t_ss, t_rs, o_ss, o_rs, t3_ss, t3_rs, l_ss, l_rs,
):
    s = lax.axis_index("seq")
    t = lax.axis_index("tensor")
    yl, z = s // 8, s % 8
    yh, x, c = t // 8, (t // 2) % 4, t % 2

    def tid(y_, x_, c_):
        return y_ * 8 + x_ * 2 + c_

    xp_, xm_ = (x + 1) % 4, (x + 3) % 4
    xf_ = (x + 2) % 4
    yo_ = 1 - yh
    sib = (s, tid(yh, x, 1 - c))
    dev_xp = (s, tid(yh, xp_, c))
    dev_xm = (s, tid(yh, xm_, c))
    dev_yo = (s, tid(yo_, x, c))
    dev_zp = (yl * 8 + (z + 1) % 8, t)
    dev_zm = (yl * 8 + (z + 7) % 8, t)
    dev_yl = ((1 - yl) * 8 + z, t)
    home = x * 2 + c
    dev_t3 = (yl * 8 + home, yh * 8 + z)
    stays = z == home

    started = []

    def copy(src, dst, ss, rs, dev):
        return pltpu.make_async_remote_copy(
            src_ref=src, dst_ref=dst, send_sem=ss, recv_sem=rs, device_id=dev, device_id_type=MESH
        )

    def send(src, dst, ss, rs, dev):
        one = copy(src, dst, ss, rs, dev)
        one.start()
        started.append(one)

    def arrive(dst, ss, rs):
        copy(dst, dst, ss, rs, sib).wait_recv()

    def load(src, dst, k):
        one = pltpu.make_async_copy(src, dst, load_sem.at[k])
        one.start()
        return one

    l_th = load(th_h, th_v, 0)
    l_sh = load(sh_h, hb.at[t], 1)
    l_small = [load(tgain_h, tgain, 7), load(sgain_h, sgain, 8), load(docs_h, docs, 9)]
    l_wkv = load(wkv_h, wkv, 2)
    l_wq = load(wq_h, wq, 3)
    l_pj = load(pj_h, pj.at[yl], 4)
    l_wo = load(wo_h, wo, 5)

    docs_r[...] = jnp.full(docs_r.shape, -1, jnp.int32)
    kv_r[1] = jnp.zeros((BACK + 1, ROWS, HEAD_DIM), BF16)

    barrier = pltpu.get_barrier_semaphore()

    def greet(k, carry):
        pl.semaphore_signal(barrier, inc=1, device_id=(s, (t + k) % 16), device_id_type=MESH)
        pl.semaphore_signal(barrier, inc=1, device_id=((s + k) % 16, t), device_id_type=MESH)
        return carry

    lax.fori_loop(1, 16, greet, 0)

    @pl.when(jnp.logical_not(stays))
    def _():
        pl.semaphore_signal(barrier, inc=1, device_id=dev_t3, device_id_type=MESH)

    class Gather:
        def __init__(self, buf, ss, rs):
            self.buf, self.ss, self.rs = buf, ss, rs
            self.near = [tid(yh, xm_, c), tid(yh, xp_, c)]
            self.opp = tid(yo_, x, c)
            self.onear = [tid(yo_, xm_, c), tid(yo_, xp_, c)]
            self.far = [tid(yh, xf_, c), tid(yo_, xf_, c)]
            self.order = [t] + self.near + [self.opp] + self.onear + self.far

        def part(self, slot, h):
            return self.buf.at[slot, pl.ds(h * 64, 64)]

        def half(self, slot, h, k, dev, src=None):
            part = self.part(slot, h)
            send(part if src is None else src, part, self.ss.at[k], self.rs.at[k], dev)

        def got_half(self, slot, h, k):
            arrive(self.part(slot, h), self.ss.at[k], self.rs.at[k])

        def to_sib(self, i):
            slot = self.order[i]
            send(self.buf.at[slot], self.buf.at[slot], self.ss.at[16 + i], self.rs.at[16 + i], sib)

        def begin(self, h, src=None):
            self.half(t, h, 0 + h, dev_yo, src)
            self.half(t, h, 2 + h, dev_xp, src)
            self.half(t, h, 4 + h, dev_xm, src)

        def near_relay(self):
            self.got_half(self.near[0], 0, 2)
            self.half(self.near[0], 0, 6, dev_xp)
            self.got_half(self.near[1], 1, 5)
            self.half(self.near[1], 1, 7, dev_xm)

        def near_rest(self):
            self.got_half(self.near[0], 1, 3)
            self.to_sib(1)
            self.got_half(self.near[1], 0, 4)
            self.to_sib(2)

        def opp_half(self, h):
            self.got_half(self.opp, h, 0 + h)
            self.half(self.opp, h, 8 + h, dev_xp)
            self.half(self.opp, h, 10 + h, dev_xm)
            if h == 1:
                self.to_sib(3)

        def onear_a(self):
            self.got_half(self.onear[0], 0, 8)
            self.half(self.onear[0], 0, 12, dev_xp)

        def onear_b(self):
            self.got_half(self.onear[1], 1, 11)
            self.half(self.onear[1], 1, 13, dev_xm)

        def onear_rest(self):
            self.got_half(self.onear[0], 1, 9)
            self.to_sib(4)
            self.got_half(self.onear[1], 0, 10)
            self.to_sib(5)

        def far_step(self):
            self.got_half(self.far[0], 0, 6)
            self.got_half(self.far[0], 1, 7)
            self.to_sib(6)

        def ofar_step(self):
            self.got_half(self.far[1], 0, 12)
            self.got_half(self.far[1], 1, 13)
            self.to_sib(7)

        def theirs(self, i):
            slot = self.order[i] + 1 - 2 * c
            arrive(self.buf.at[slot], self.ss.at[16 + i], self.rs.at[16 + i])
            return slot

    z_slot = (z % 2) * 4 + z // 2
    l_th.wait()
    for one in l_small:
        one.wait()
    docs_r[0] = docs[...]
    part = jnp.zeros((ROWS, 128), F32)
    for i in range(8):
        cols = slice(i * 128, (i + 1) * 128)
        f = th_v[:, cols].astype(F32)
        part = part + f * f
        tg[z_slot, :, cols] = (f * tgain[:, cols]).astype(BF16)
    sg_s[:, COLS:COLS + 128] = jnp.sum(part.T, axis=0, keepdims=True)
    l_sh.wait()
    part = jnp.zeros((ROWS, 128), F32)
    for i in range(4):
        f = hb[t, :, i * 128:(i + 1) * 128].astype(F32)
        part = part + f * f
    sg_s[:, COLS + 128:COLS + 256] = jnp.sum(part.T, axis=0, keepdims=True)
    sg_s[:, 0:COLS] = sgain[...]
    sg_r[t] = sg_s[...]

    pl.semaphore_wait(barrier, jnp.where(stays, 30, 31))

    ag = Gather(hb, ag_ss, ag_rs)
    ag.begin(0)
    ag.begin(1)
    ag.to_sib(0)

    def ring_slot(d):
        zz = (z + d) % 8
        return (zz % 2) * 4 + zz // 2

    def z_ref(d, h):
        return tg.at[ring_slot(d), pl.ds(h * 64, 64)]

    def z_send(k):
        up, down = z_ref(-(k // 2) + 8, k % 2), z_ref(k // 2, 1 - k % 2)
        send(up, up, z_ss.at[k], z_rs.at[k], dev_zp)
        send(down, down, z_ss.at[8 + k], z_rs.at[8 + k], dev_zm)

    def z_got(k):
        up, down = z_ref(-(k // 2) + 7, k % 2), z_ref(k // 2 + 1, 1 - k % 2)
        arrive(up, z_ss.at[k], z_rs.at[k])
        arrive(down, z_ss.at[8 + k], z_rs.at[8 + k])

    def z_step(k):
        z_got(k)
        if k + 2 < 7:
            z_send(k + 2)

    def pj_send(k):
        rows = pl.ds(k * 256, 256)
        send(pj_h.at[rows], pj.at[yl, rows], p_ss.at[k], p_rs.at[k], dev_yl)

    z_send(0)
    pj_send(0)
    z_send(1)
    pj_send(1)

    def small(k):
        return copy(sg_s, sg_r.at[t], sm_ss.at[k], sm_rs.at[k], (s, (t + k) % 16))

    def small_go(k, carry):
        small(k).start()
        return carry

    def small_got(k, carry):
        arrive(sg_r.at[(t + 16 - k) % 16], sm_ss.at[k], sm_rs.at[k])
        return carry

    def small_end(k, carry):
        small(k).wait_send()
        return carry

    lax.fori_loop(1, 16, small_go, 0)

    def docs_copy(k):
        return copy(docs, docs_r.at[k], dc_ss.at[k], dc_rs.at[k], ((s + k) % 16, t))

    def docs_go(k, carry):
        @pl.when(s + k < 16)
        def _():
            docs_copy(k).start()
        return carry

    lax.fori_loop(1, BACK + 1, docs_go, 0)

    entry = lax.broadcasted_iota(jnp.int32, (64, ROWS), 0).astype(F32)
    position = (s * ROWS + lax.broadcasted_iota(jnp.int32, (64, ROWS), 1)).astype(F32)
    angle = position * jnp.exp(-math.log(500000.0) * (2.0 * entry / HEAD_DIM))
    cos_t[...] = jnp.cos(angle)
    sin_t[...] = jnp.sin(angle)
    q_acc[...] = jnp.zeros(q_acc.shape, F32)
    kv_acc[...] = jnp.zeros(kv_acc.shape, F32)

    def process(slot):
        for i in range(4):
            cols = slice(i * 128, (i + 1) * 128)
            f = hb[slot, :, cols].astype(F32)
            hn[slot, :, cols] = (f * scale_v[...] * sg_r[slot][:, cols]).astype(BF16)
        at = pl.multiple_of(slot * COLS, COLS)
        kv_acc[...] += nt_dot(hn[slot], wkv[:, :, pl.ds(at, COLS)].reshape(64, COLS))
        q_acc[...] += jnp.dot(hn[slot], wq[pl.ds(at, COLS), :], preferred_element_type=F32)

    ag.near_relay()
    ag.near_rest()
    z_step(0)
    ag.opp_half(0)
    pj_send(2)
    lax.fori_loop(1, 16, small_got, 0)
    sums = sg_r[0][:, COLS:COLS + 256]
    for i in range(1, 16):
        sums = sums + sg_r[i][:, COLS:COLS + 256]
    ts_v[...] = jnp.broadcast_to(lax.rsqrt(sums[:, 0:128] / DT + 1e-05), (ROWS, 128)).T
    scale_v[...] = jnp.broadcast_to(lax.rsqrt(sums[:, 128:256] / DS + 1e-05), (ROWS, 128)).T
    l_wkv.wait()
    l_wq.wait()
    process(t)
    z_step(1)
    ag.opp_half(1)
    pj_send(3)
    ag.onear_a()
    process(ag.near[0])
    process(ag.near[1])
    process(ag.theirs(0))
    ag.onear_b()
    z_step(2)
    ag.onear_rest()
    process(ag.theirs(1))
    process(ag.theirs(2))
    ag.far_step()
    process(ag.opp)
    process(ag.theirs(3))
    ag.ofar_step()
    process(ag.onear[0])
    process(ag.onear[1])
    z_step(3)
    process(ag.far[0])
    process(ag.theirs(4))
    process(ag.theirs(5))
    process(ag.theirs(6))
    process(ag.far[1])
    process(ag.theirs(7))

    row = lax.broadcasted_iota(jnp.int32, (64, 64), 0)
    col = lax.broadcasted_iota(jnp.int32, (64, 64), 1)
    take = ((row >> 3) & 1) * 32 + (row & 7) * 4 + (row >> 4)
    pick = jnp.where(col == take, 1.0, 0.0).astype(BF16)
    kvx_s[...] = nt_dot(pick, kv_acc[...].astype(BF16)).astype(BF16).reshape(4, 16, 128)
    kvx_r[t] = kvx_s[t // 4]

    def kvx(k):
        to = (t + k) % 16
        return copy(kvx_s.at[to // 4], kvx_r.at[t], kx_ss.at[k], kx_rs.at[k], (s, to))

    def kvx_go(k, carry):
        kvx(k).start()
        return carry

    def kvx_got(k, carry):
        arrive(kvx_r.at[(t + 16 - k) % 16], kx_ss.at[k], kx_rs.at[k])
        return carry

    def kvx_end(k, carry):
        kvx(k).wait_send()
        return carry

    lax.fori_loop(1, 16, kvx_go, 0)
    z_step(4)

    cos2 = jnp.concatenate([cos_t[...], cos_t[...]], axis=0).T
    sin2 = jnp.concatenate([-sin_t[...], sin_t[...]], axis=0).T
    for h in range(2):
        qh = q_acc[:, h * 128:(h + 1) * 128]
        turned = qh * cos2 + pltpu.roll(qh, 64, 1) * sin2
        q_v[h] = (turned * HEAD_DIM ** (-0.5)).astype(BF16)

    lax.fori_loop(1, 16, kvx_got, 0)
    both = kvx_r[...].astype(F32).reshape(16, 2, 8, ROWS)
    k_raw = both[:, 0].reshape(HEAD_DIM, ROWS)
    v_raw = both[:, 1].reshape(HEAD_DIM, ROWS)
    first, second = k_raw[0:64], k_raw[64:128]
    k_rot = jnp.concatenate(
        [first * cos_t[...] - second * sin_t[...], second * cos_t[...] + first * sin_t[...]], axis=0
    )
    kv_own[0] = k_rot.astype(BF16)
    kv_own[1] = v_raw.T.astype(BF16)
    kv_r[0, 0] = kv_own[0]
    kv_r[1, 0] = kv_own[1]

    def kv_copy(k):
        return copy(kv_own.at[c], kv_r.at[c, k], kv_ss.at[k], kv_rs.at[k], ((s + k) % 16, t))

    def kv_fwd(k):
        return copy(kv_r.at[c, k], kv_r.at[c, k], kf_ss.at[k], kf_rs.at[k], sib)

    def kv_go(k, carry):
        @pl.when(s + k < 16)
        def _():
            kv_copy(k).start()
        return carry

    def kv_mid(k, carry):
        @pl.when(s >= k)
        def _():
            arrive(kv_r.at[c, k], kv_ss.at[k], kv_rs.at[k])
            kv_fwd(k).start()
        return carry

    def kv_got(k, carry):
        @pl.when(s >= k)
        def _():
            arrive(kv_r.at[1 - c, k], kf_ss.at[k], kf_rs.at[k])
            arrive(docs_r.at[k], dc_ss.at[k], dc_rs.at[k])
        return carry

    def kv_end(k, carry):
        @pl.when(s >= k)
        def _():
            kv_fwd(k).wait_send()

        @pl.when(s + k < 16)
        def _():
            kv_copy(k).wait_send()
            docs_copy(k).wait_send()
        return carry

    lax.fori_loop(1, BACK + 1, kv_go, 0)

    class Reduce:
        def __init__(self, y_order, own, sib_s, sib_r, x2, ra, rb, xp, xm, fm, fp, ys, yr, fin, ss, rs):
            self.own, self.sib_s, self.sib_r = own, sib_s, sib_r
            self.x2, self.ra, self.rb, self.xp, self.xm, self.fm, self.fp = x2, ra, rb, xp, xm, fm, fp
            self.ys, self.yr, self.fin, self.ss, self.rs = ys, yr, fin, ss, rs
            self.y_order = y_order
            self.x_order = (xf_, xp_, xm_, x)

        def go(self, src, dst, k, dev):
            send(src, dst, self.ss.at[k], self.rs.at[k], dev)

        def got(self, dst, k):
            arrive(dst, self.ss.at[k], self.rs.at[k])

        def slot(self, k, i):
            return self.y_order[i] * 4 + self.x_order[k]

        def to_sib(self, k, i):
            slot = self.slot(k, i)
            self.go(self.sib_s.at[slot], self.sib_r.at[slot], k * 2 + i, sib)

        def sib_got(self, k, i):
            self.got(self.sib_r.at[self.slot(k, i)], k * 2 + i)

        def pair(self, k, i, h):
            slot, rows = self.slot(k, i), slice(h * 64, h * 64 + 64)
            return self.own[slot, rows] + self.sib_r[slot, rows].astype(F32)

        def far(self, i):
            self.sib_got(0, i)
            self.x2[i, 0:64] = self.pair(0, i, 0).astype(BF16)
            self.go(self.x2.at[i, pl.ds(0, 64)], self.ra.at[i], 8 + i, dev_xp)
            self.x2[i, 64:128] = self.pair(0, i, 1).astype(BF16)
            self.go(self.x2.at[i, pl.ds(64, 64)], self.rb.at[i], 10 + i, dev_xm)

        def near(self, i):
            self.sib_got(1, i)
            self.xp[i, 64:128] = self.pair(1, i, 1).astype(BF16)
            self.go(self.xp.at[i, pl.ds(64, 64)], self.fm.at[i, pl.ds(64, 64)], 12 + i, dev_xp)
            self.sib_got(2, i)
            self.xm[i, 0:64] = self.pair(2, i, 0).astype(BF16)
            self.go(self.xm.at[i, pl.ds(0, 64)], self.fp.at[i, pl.ds(0, 64)], 14 + i, dev_xm)

        def relay(self, i):
            self.got(self.ra.at[i], 8 + i)
            self.xp[i, 0:64] = (self.pair(1, i, 0) + self.ra[i].astype(F32)).astype(BF16)
            self.go(self.xp.at[i, pl.ds(0, 64)], self.fm.at[i, pl.ds(0, 64)], 16 + i, dev_xp)
            self.got(self.rb.at[i], 10 + i)
            self.xm[i, 64:128] = (self.pair(2, i, 1) + self.rb[i].astype(F32)).astype(BF16)
            self.go(self.xm.at[i, pl.ds(64, 64)], self.fp.at[i, pl.ds(64, 64)], 18 + i, dev_xm)

        def join(self, i, h):
            rows, at = slice(h * 64, h * 64 + 64), pl.ds(h * 64, 64)
            if h == 0:
                self.sib_got(3, i)
            self.got(self.fm.at[i, at], (16, 12)[h] + i)
            self.got(self.fp.at[i, at], (14, 18)[h] + i)
            return self.pair(3, i, h) + self.fm[i, rows].astype(F32) + self.fp[i, rows].astype(F32)

        def join_one(self, i):
            mine = self.y_order[i] == yh
            for h in range(2):
                rows = slice(h * 64, h * 64 + 64)
                value = self.join(i, h)

                @pl.when(mine)
                def _():
                    self.fin[rows] = value

                @pl.when(jnp.logical_not(mine))
                def _():
                    self.ys[rows] = value.astype(BF16)
                    self.to_opp(h).start()

        def to_opp(self, h):
            at = pl.ds(h * 64, 64)
            return copy(self.ys.at[at], self.yr.at[at], self.ss.at[20 + h], self.rs.at[20 + h], dev_yo)

        def join_other(self):
            for h in range(2):
                self.ys[h * 64:h * 64 + 64] = self.join(0, h).astype(BF16)
                self.to_opp(h).start()

        def join_mine(self):
            for h in range(2):
                self.fin[h * 64:h * 64 + 64] = self.join(1, h)

        def end(self):
            for h in range(2):
                self.to_opp(h).wait_send()

        def last(self, h):
            rows = slice(h * 64, h * 64 + 64)
            self.got(self.yr.at[pl.ds(h * 64, 64)], 20 + h)
            return self.fin[rows] + self.yr[rows].astype(F32)

    rt = Reduce((yl, 1 - yl), t_own, t_sib_s, t_sib_r, t_x2, t_ra, t_rb, t_xp, t_xm, t_fm, t_fp, t_ys, t_yr, t_fin, t_ss, t_rs)

    z_step(5)
    z_step(6)

    def products(core, y_):
        rows = tg[pl.ds(core * 4, 4)].reshape(4 * ROWS, 1024)
        return jnp.dot(rows, pj[y_], preferred_element_type=F32).reshape(4, ROWS, COLS)

    def t_wave(i):
        y_ = rt.y_order[i]
        t_sib_s[pl.ds(y_ * 4, 4)] = products(1 - c, y_).astype(BF16)
        for k in range(4):
            rt.to_sib(k, i)
        t_own[pl.ds(y_ * 4, 4)] = products(c, y_)

    l_pj.wait()
    t_wave(0)
    rt.far(0)
    rt.near(0)
    for k in range(4):
        arrive(pj.at[1 - yl, pl.ds(k * 256, 256)], p_ss.at[k], p_rs.at[k])
    t_wave(1)
    rt.relay(0)
    lax.fori_loop(1, BACK + 1, kv_mid, 0)
    rt.far(1)
    rt.near(1)

    lax.fori_loop(1, BACK + 1, kv_got, 0)
    keys = jnp.concatenate([kv_r[0, j] for j in range(BACK + 1)], axis=1)
    values = kv_r[1].reshape((BACK + 1) * ROWS, HEAD_DIM)
    key_doc = jnp.concatenate([docs_r[j] for j in range(BACK + 1)], axis=1)
    row_doc = jnp.broadcast_to(docs[...].astype(F32), (ROWS, ROWS)).T[:, 0:1].astype(jnp.int32)
    wide = (ROWS, (BACK + 1) * ROWS)
    row_at = lax.broadcasted_iota(jnp.int32, wide, 0)
    key_at = lax.broadcasted_iota(jnp.int32, wide, 1)
    allowed = (key_doc == row_doc) & ((key_at >= ROWS) | (key_at <= row_at))
    for h in range(2):
        scores = jnp.dot(q_v[h], keys, preferred_element_type=F32)
        scores = jnp.where(allowed, scores, -1e30)
        probs = jnp.exp(scores - jnp.max(scores, axis=1, keepdims=True))
        total = jnp.sum(probs, axis=1, keepdims=True)
        acc = jnp.dot(probs.astype(BF16), values, preferred_element_type=F32)
        attn_v[:, h * 128:(h + 1) * 128] = (acc / total).astype(BF16)
        if h == 0:
            rt.relay(1)

    rt.join_one(0)
    l_wo.wait()

    ro = Reduce((yo_, yh), o_own, o_sib_s, o_sib_r, o_x2, o_ra, o_rb, o_xp, o_xm, o_fm, o_fp, o_ys, o_yr, o_fin, o_ss, o_rs)

    def out_block(k, i, core):
        at = pl.multiple_of(tid(ro.y_order[i], ro.x_order[k], core) * COLS, COLS)
        return jnp.dot(attn_v[...], wo[:, pl.ds(at, COLS)], preferred_element_type=F32)

    def out_theirs(k, i):
        o_sib_s[ro.slot(k, i)] = out_block(k, i, 1 - c).astype(BF16)
        ro.to_sib(k, i)

    def out_mine(k, i):
        o_own[ro.slot(k, i)] = out_block(k, i, c)

    for k in range(3):
        for i in range(2):
            out_theirs(k, i)
    for i in range(2):
        out_mine(0, i)
        ro.far(i)
    rt.join_one(1)
    for i in range(2):
        out_theirs(3, i)
        out_mine(1, i)
        out_mine(2, i)
        ro.near(i)
    out_mine(3, 0)
    out_mine(3, 1)
    ro.relay(0)
    ro.relay(1)

    def t3(h):
        at = pl.ds(h * 64, 64)
        return copy(t3_s.at[at], t3_r.at[at], t3_ss.at[h], t3_rs.at[h], dev_t3)

    for h in range(2):
        rows = slice(h * 64, h * 64 + 64)
        t3_s[rows] = rt.last(h).astype(BF16)

        @pl.when(stays)
        def _():
            t3_r[rows] = t3_s[rows]

        @pl.when(jnp.logical_not(stays))
        def _():
            t3(h).start()

    ro.join_other()
    ro.join_mine()

    dg = Gather(db, dg_ss, dg_rs)
    for h in range(2):
        rows = slice(h * 64, h * 64 + 64)
        mixed = hb[t, rows].astype(F32) + ro.last(h)
        out_s[rows] = mixed.astype(BF16)

        @pl.when(jnp.logical_not(stays))
        def _():
            arrive(t3_r.at[pl.ds(h * 64, 64)], t3_ss.at[h], t3_rs.at[h])

        target = t3_r[rows].astype(F32) * jnp.concatenate([ts_v[rows]] * 4, axis=1)
        difference = mixed - target
        db[t, rows] = difference.astype(BF16)
        dg.begin(h)
        squares = difference * difference
        g_acc[rows, 0:128] = (
            squares[:, 0:128] + squares[:, 128:256] + squares[:, 256:384] + squares[:, 384:512]
        )
    dg.to_sib(0)
    l_s[...] = jnp.sum(g_acc[:, 0:128].T, axis=0, keepdims=True)
    l_r[t] = l_s[...]

    def loss(k):
        return copy(l_s, l_r.at[t], l_ss.at[k], l_rs.at[k], (s, (t + k) % 16))

    def loss_go(k, carry):
        loss(k).start()
        return carry

    def loss_got(k, carry):
        arrive(l_r.at[(t + 16 - k) % 16], l_ss.at[k], l_rs.at[k])
        return carry

    def loss_end(k, carry):
        loss(k).wait_send()
        return carry

    lax.fori_loop(1, 16, loss_go, 0)

    g_acc[...] = jnp.zeros(g_acc.shape, F32)

    def add_grad(slot):
        at = pl.multiple_of(slot * COLS, COLS)
        g_acc[...] += nt_dot(db[slot], wo[:, pl.ds(at, COLS)])

    add_grad(t)
    dg.near_relay()
    dg.near_rest()
    dg.opp_half(0)
    add_grad(dg.theirs(0))
    add_grad(dg.near[0])
    add_grad(dg.near[1])
    dg.opp_half(1)
    dg.onear_a()
    add_grad(dg.theirs(1))
    add_grad(dg.theirs(2))
    add_grad(dg.opp)
    dg.onear_b()
    dg.onear_rest()
    dg.far_step()
    add_grad(dg.theirs(3))
    add_grad(dg.onear[0])
    add_grad(dg.onear[1])
    dg.ofar_step()
    add_grad(dg.far[0])
    add_grad(dg.theirs(4))
    add_grad(dg.theirs(5))
    add_grad(dg.theirs(6))
    add_grad(dg.far[1])
    lax.fori_loop(1, 16, loss_got, 0)
    loss_sum = l_r[0]
    for i in range(1, 16):
        loss_sum = loss_sum + l_r[i]
    out_l[...] = loss_sum / DS
    add_grad(dg.theirs(7))
    out_g[...] = g_acc[...].astype(BF16)

    for one in started:
        one.wait_send()
    lax.fori_loop(1, 16, small_end, 0)
    lax.fori_loop(1, 16, kvx_end, 0)
    lax.fori_loop(1, BACK + 1, kv_end, 0)
    lax.fori_loop(1, 16, loss_end, 0)

    rt.end()
    ro.end()

    @pl.when(jnp.logical_not(stays))
    def _():
        t3(0).wait_send()
        t3(1).wait_send()


def reduce_buffers():
    block = (ROWS, COLS)
    return [
        pltpu.VMEM((8,) + block, BF16),
        pltpu.VMEM((8,) + block, BF16),
        pltpu.VMEM((2,) + block, BF16),
        pltpu.VMEM((2, 64, COLS), BF16),
        pltpu.VMEM((2, 64, COLS), BF16),
        pltpu.VMEM((2,) + block, BF16),
        pltpu.VMEM((2,) + block, BF16),
        pltpu.VMEM((2,) + block, BF16),
        pltpu.VMEM((2,) + block, BF16),
        pltpu.VMEM(block, BF16),
        pltpu.VMEM(block, BF16),
        pltpu.VMEM(block, F32),
    ]


def on_device(
    teacher_hidden, teacher_gain, projector, student_hidden, student_gain,
    query_weight, kv_weight, out_weight, doc_ids,
):
    block = (ROWS, COLS)
    hbm = pl.BlockSpec(memory_space=pltpu.HBM)
    vmem = pl.BlockSpec(memory_space=pltpu.VMEM)
    dma = pltpu.SemaphoreType.DMA
    out_s, out_l, out_g = pl.pallas_call(
        body,
        out_shape=(
            jax.ShapeDtypeStruct(block, BF16),
            jax.ShapeDtypeStruct((1, ROWS), F32),
            jax.ShapeDtypeStruct((ROWS, 256), BF16),
        ),
        in_specs=[hbm] * 9,
        out_specs=(vmem, vmem, vmem),
        scratch_shapes=[
            pltpu.VMEM((1, 1024), F32),
            pltpu.VMEM((1, COLS), F32),
            pltpu.VMEM((1, ROWS), jnp.int32),
            pltpu.VMEM((ROWS, 1024), BF16),
            pltpu.VMEM((8, ROWS, 1024), BF16),
            pltpu.VMEM((2, 1024, COLS), BF16),
            pltpu.VMEM((DS, 256), BF16),
            pltpu.VMEM((2, 32, DS), BF16),
            pltpu.VMEM((256, DS), BF16),
            pltpu.VMEM((64, ROWS), F32),
            pltpu.VMEM((64, ROWS), F32),
            pltpu.VMEM((16,) + block, BF16),
            pltpu.VMEM((16,) + block, BF16),
            pltpu.VMEM((1, 768), F32),
            pltpu.VMEM((16, 1, 768), F32),
            pltpu.VMEM((ROWS, 128), F32),
            pltpu.VMEM((ROWS, 256), F32),
            pltpu.VMEM((ROWS, 64), F32),
            pltpu.VMEM((4, 16, ROWS), BF16),
            pltpu.VMEM((16, 16, ROWS), BF16),
            pltpu.VMEM((2, ROWS, HEAD_DIM), BF16),
            pltpu.VMEM((2, BACK + 1, ROWS, HEAD_DIM), BF16),
            pltpu.VMEM((BACK + 1, 1, ROWS), jnp.int32),
            pltpu.VMEM((2, ROWS, HEAD_DIM), BF16),
            pltpu.VMEM((ROWS, 256), BF16),
            pltpu.VMEM((8,) + block, F32),
            pltpu.VMEM((8,) + block, F32),
            *reduce_buffers(),
            *reduce_buffers(),
            pltpu.VMEM(block, BF16),
            pltpu.VMEM(block, BF16),
            pltpu.VMEM((ROWS, 128), F32),
            pltpu.VMEM((16,) + block, BF16),
            pltpu.VMEM((ROWS, 256), F32),
            pltpu.VMEM((1, ROWS), F32),
            pltpu.VMEM((16, 1, ROWS), F32),
            dma((10,)),
            dma((16,)), dma((16,)), dma((4,)), dma((4,)),
            dma((24,)), dma((24,)), dma((24,)), dma((24,)),
            dma((16,)), dma((16,)), dma((16,)), dma((16,)),
            dma((9,)), dma((9,)), dma((9,)), dma((9,)), dma((9,)), dma((9,)),
            dma((24,)), dma((24,)), dma((24,)), dma((24,)),
            dma((2,)), dma((2,)),
            dma((16,)), dma((16,)),
        ],
        compiler_params=pltpu.CompilerParams(
            collective_id=0, has_side_effects=True, vmem_limit_bytes=40 * 1024 * 1024
        ),
    )(
        *(
            pltpu.with_memory_space_constraint(one, pltpu.HBM)
            for one in (
                teacher_hidden, teacher_gain.reshape(1, -1), projector, student_hidden,
                student_gain.reshape(1, -1), query_weight, jnp.transpose(kv_weight, (0, 2, 1)),
                out_weight, doc_ids.reshape(1, -1),
            )
        )
    )
    return out_s, out_l.reshape(ROWS), out_g


def solution(mesh):
    in_specs = (
        P("seq", "tensor"),
        P("tensor"),
        P("tensor", "seq"),
        P("seq", "tensor"),
        P("tensor"),
        P(None, "tensor"),
        P(None, None, "tensor"),
        P("tensor", None),
        P("seq"),
    )
    out_specs = (P("seq", "tensor"), P("seq"), P("seq", "tensor"))
    return jax.shard_map(
        on_device, mesh=mesh, in_specs=in_specs, out_specs=out_specs, check_vma=False
    )
```

```python
import math

import jax
import jax.numpy as jnp
from jax import lax
from jax.experimental import pallas as pl
from jax.experimental.pallas import tpu as pltpu
from jax.sharding import PartitionSpec as P

DT = 16384
DS = 8192
HEAD_DIM = 128
HEADS = 32
KV_HEADS = 4
ROWS = 128
COLS = 512
BACK = 8
F32 = jnp.float32
BF16 = jnp.bfloat16
MESH = pl.DeviceIdType.MESH
NT = (((1,), (1,)), ((), ()))


def nt_dot(a, b):
    return lax.dot_general(a, b, NT, preferred_element_type=F32)


def body(
    th_h, tgain_h, pj_h, sh_h, sgain_h, wq_h, wkv_h, wo_h, docs_h,
    out_s, out_l, out_g,
    tgain, sgain, docs, th_v, tg, pj, wq, wkv, wo, cos_t, sin_t,
    hb, hn, sg_s, sg_r, scale_v, q_acc, kv_acc,
    kvx_s, kvx_r, kv_own, kv_r, docs_z, docs_o, q_v, attn_v,
    t_own, o_own, t_sib_s, t_sib_r, t_x2, t_ra, t_rb, t_xp, t_xm, t_fm, t_fp, t_ys, t_yr, t_fin,
    o_sib_s, o_sib_r, o_x2, o_ra, o_rb, o_xp, o_xm, o_fm, o_fp, o_ys, o_yr, o_fin,
    t3_s, t3_r, ts_v, db, g_acc, l_s, l_r,
    load_sem, z_ss, z_rs, p_ss, p_rs,
    ag_ss, ag_rs, dg_ss, dg_rs, sm_ss, sm_rs, kx_ss, kx_rs, kv_ss, kv_rs, kf_ss, kf_rs, dc_ss, dc_rs,
    t_ss, t_rs, o_ss, o_rs, t3_ss, t3_rs, l_ss, l_rs,
):
    s = lax.axis_index("seq")
    t = lax.axis_index("tensor")
    yl, z = s // 8, s % 8
    yh, x, c = t // 8, (t // 2) % 4, t % 2

    def tid(y_, x_, c_):
        return y_ * 8 + x_ * 2 + c_

    xp_, xm_ = (x + 1) % 4, (x + 3) % 4
    xf_ = (x + 2) % 4
    yo_ = 1 - yh
    sib = (s, tid(yh, x, 1 - c))
    dev_xp = (s, tid(yh, xp_, c))
    dev_xm = (s, tid(yh, xm_, c))
    dev_yo = (s, tid(yo_, x, c))
    dev_zp = (yl * 8 + (z + 1) % 8, t)
    dev_zm = (yl * 8 + (z + 7) % 8, t)
    dev_yl = ((1 - yl) * 8 + z, t)
    home = x * 2 + c
    dev_t3 = (yl * 8 + home, yh * 8 + z)
    stays = z == home

    started = []

    def copy(src, dst, ss, rs, dev):
        return pltpu.make_async_remote_copy(
            src_ref=src, dst_ref=dst, send_sem=ss, recv_sem=rs, device_id=dev, device_id_type=MESH
        )

    def send(src, dst, ss, rs, dev):
        one = copy(src, dst, ss, rs, dev)
        one.start()
        started.append(one)

    def arrive(dst, ss, rs):
        copy(dst, dst, ss, rs, sib).wait_recv()

    def load(src, dst, k):
        one = pltpu.make_async_copy(src, dst, load_sem.at[k])
        one.start()
        return one

    l_th = load(th_h, th_v, 0)
    l_sh = load(sh_h, hb.at[t], 1)
    l_small = [load(tgain_h, tgain, 7), load(sgain_h, sgain, 8), load(docs_h, docs, 9)]
    l_wkv = load(wkv_h, wkv, 2)
    l_wq = load(wq_h, wq, 3)
    l_pj = load(pj_h, pj.at[yl], 4)
    l_wo = load(wo_h, wo, 5)

    kv_r[1] = jnp.zeros((BACK + 1, ROWS, HEAD_DIM), BF16)

    barrier = pltpu.get_barrier_semaphore()
    for dev in (sib, dev_xp, dev_xm, dev_yo, dev_zp, dev_zm, dev_yl):
        pl.semaphore_signal(barrier, inc=1, device_id=dev, device_id_type=MESH)

    class Gather:
        def __init__(self, buf, ss, rs):
            self.buf, self.ss, self.rs = buf, ss, rs
            self.near = [tid(yh, xm_, c), tid(yh, xp_, c)]
            self.opp = tid(yo_, x, c)
            self.onear = [tid(yo_, xm_, c), tid(yo_, xp_, c)]
            self.far = [tid(yh, xf_, c), tid(yo_, xf_, c)]
            self.order = [t] + self.near + [self.opp] + self.onear + self.far

        def part(self, slot, h):
            return self.buf.at[slot, pl.ds(h * 64, 64)]

        def half(self, slot, h, k, dev, src=None):
            part = self.part(slot, h)
            send(part if src is None else src, part, self.ss.at[k], self.rs.at[k], dev)

        def got_half(self, slot, h, k):
            arrive(self.part(slot, h), self.ss.at[k], self.rs.at[k])

        def to_sib(self, i):
            slot = self.order[i]
            send(self.buf.at[slot], self.buf.at[slot], self.ss.at[16 + i], self.rs.at[16 + i], sib)

        def begin(self, h, src=None):
            self.half(t, h, 0 + h, dev_yo, src)
            self.half(t, h, 2 + h, dev_xp, src)
            self.half(t, h, 4 + h, dev_xm, src)

        def near_relay(self):
            self.got_half(self.near[0], 0, 2)
            self.half(self.near[0], 0, 6, dev_xp)
            self.got_half(self.near[1], 1, 5)
            self.half(self.near[1], 1, 7, dev_xm)

        def near_rest(self):
            self.got_half(self.near[0], 1, 3)
            self.to_sib(1)
            self.got_half(self.near[1], 0, 4)
            self.to_sib(2)

        def opp_half(self, h):
            self.got_half(self.opp, h, 0 + h)
            self.half(self.opp, h, 8 + h, dev_xp)
            self.half(self.opp, h, 10 + h, dev_xm)
            if h == 1:
                self.to_sib(3)

        def onear_a(self):
            self.got_half(self.onear[0], 0, 8)
            self.half(self.onear[0], 0, 12, dev_xp)

        def onear_b(self):
            self.got_half(self.onear[1], 1, 11)
            self.half(self.onear[1], 1, 13, dev_xm)

        def onear_rest(self):
            self.got_half(self.onear[0], 1, 9)
            self.to_sib(4)
            self.got_half(self.onear[1], 0, 10)
            self.to_sib(5)

        def far_step(self):
            self.got_half(self.far[0], 0, 6)
            self.got_half(self.far[0], 1, 7)
            self.to_sib(6)

        def ofar_step(self):
            self.got_half(self.far[1], 0, 12)
            self.got_half(self.far[1], 1, 13)
            self.to_sib(7)

        def theirs(self, i):
            slot = self.order[i] + 1 - 2 * c
            arrive(self.buf.at[slot], self.ss.at[16 + i], self.rs.at[16 + i])
            return slot

    z_slot = (z % 2) * 4 + z // 2
    l_th.wait()
    for one in l_small:
        one.wait()
    docs_z[z] = docs[...]
    part = jnp.zeros((ROWS, 128), F32)
    for i in range(8):
        cols = slice(i * 128, (i + 1) * 128)
        f = th_v[:, cols].astype(F32)
        part = part + f * f
        tg[z_slot, :, cols] = (f * tgain[:, cols]).astype(BF16)
    sg_s[:, COLS:COLS + 128] = jnp.sum(part.T, axis=0, keepdims=True)
    l_sh.wait()
    part = jnp.zeros((ROWS, 128), F32)
    for i in range(4):
        f = hb[t, :, i * 128:(i + 1) * 128].astype(F32)
        part = part + f * f
    sg_s[:, COLS + 128:COLS + 256] = jnp.sum(part.T, axis=0, keepdims=True)
    sg_s[:, 0:COLS] = sgain[...]
    sg_r[t] = sg_s[...]

    pl.semaphore_wait(barrier, 7)

    ag = Gather(hb, ag_ss, ag_rs)

    def ring_slot(d):
        zz = (z + d) % 8
        return (zz % 2) * 4 + zz // 2

    def z_ref(d, h):
        return tg.at[ring_slot(d), pl.ds(h * 64, 64)]

    def z_send(k):
        up, down = z_ref(-(k // 2) + 8, k % 2), z_ref(k // 2, 1 - k % 2)
        send(up, up, z_ss.at[k], z_rs.at[k], dev_zp)
        send(down, down, z_ss.at[8 + k], z_rs.at[8 + k], dev_zm)

    def z_got(k):
        up, down = z_ref(-(k // 2) + 7, k % 2), z_ref(k // 2 + 1, 1 - k % 2)
        arrive(up, z_ss.at[k], z_rs.at[k])
        arrive(down, z_ss.at[8 + k], z_rs.at[8 + k])

    def z_step(k):
        z_got(k)
        if k + 2 < 7:
            z_send(k + 2)

    def pj_send(k):
        rows = pl.ds(k * 256, 256)
        send(pj_h.at[rows], pj.at[yl, rows], p_ss.at[k], p_rs.at[k], dev_yl)


    def small_send(i, k, dev):
        slot = ag.order[i]
        send(sg_r.at[slot], sg_r.at[slot], sm_ss.at[k], sm_rs.at[k], dev)

    def small_got(i, k):
        arrive(sg_r.at[ag.order[i]], sm_ss.at[k], sm_rs.at[k])

    def small_sib(i):
        small_send(i, 8 + i, sib)

    def small_theirs(i):
        arrive(sg_r.at[ag.order[i] + 1 - 2 * c], sm_ss.at[8 + i], sm_rs.at[8 + i])

    def docs_send(d, k, dev):
        ref = docs_z.at[(z + d) % 8]
        send(ref, ref, dc_ss.at[k], dc_rs.at[k], dev)

    def docs_step(k):
        arrive(docs_z.at[(z + 7 - k) % 8], dc_ss.at[k], dc_rs.at[k])
        if k < 3:
            arrive(docs_z.at[(z + 1 + k) % 8], dc_ss.at[4 + k], dc_rs.at[4 + k])
            docs_send(7 - k, k + 1, dev_zp)
            if k < 2:
                docs_send(1 + k, k + 5, dev_zm)
        else:
            send(docs_z, docs_o, dc_ss.at[8], dc_rs.at[8], dev_yl)

    small_send(0, 0, dev_yo)
    small_send(0, 1, dev_xp)
    small_send(0, 2, dev_xm)
    small_sib(0)
    ag.begin(0)
    ag.begin(1)
    ag.to_sib(0)
    docs_send(0, 0, dev_zp)
    docs_send(0, 4, dev_zm)
    z_send(0)
    pj_send(0)
    z_send(1)
    pj_send(1)

    entry = lax.broadcasted_iota(jnp.int32, (64, ROWS), 0).astype(F32)
    position = (s * ROWS + lax.broadcasted_iota(jnp.int32, (64, ROWS), 1)).astype(F32)
    angle = position * jnp.exp(-math.log(500000.0) * (2.0 * entry / HEAD_DIM))
    cos_t[...] = jnp.cos(angle)
    sin_t[...] = jnp.sin(angle)
    q_acc[...] = jnp.zeros(q_acc.shape, F32)
    kv_acc[...] = jnp.zeros(kv_acc.shape, F32)

    def process(slot):
        for i in range(4):
            cols = slice(i * 128, (i + 1) * 128)
            f = hb[slot, :, cols].astype(F32)
            hn[slot, :, cols] = (f * scale_v[...] * sg_r[slot][:, cols]).astype(BF16)
        at = pl.multiple_of(slot * COLS, COLS)
        kv_acc[...] += nt_dot(hn[slot], wkv[:, :, pl.ds(at, COLS)].reshape(64, COLS))
        q_acc[...] += jnp.dot(hn[slot], wq[pl.ds(at, COLS), :], preferred_element_type=F32)

    small_got(1, 1)
    small_send(1, 3, dev_xp)
    small_sib(1)
    small_got(2, 2)
    small_sib(2)
    small_got(3, 0)
    small_send(3, 4, dev_xp)
    small_send(3, 5, dev_xm)
    small_sib(3)
    docs_step(0)
    ag.near_relay()
    small_got(6, 3)
    small_sib(6)
    docs_step(1)
    ag.near_rest()
    small_got(4, 4)
    small_send(4, 6, dev_xp)
    small_sib(4)
    small_got(5, 5)
    small_sib(5)
    ag.opp_half(0)
    z_step(0)
    pj_send(2)
    docs_step(2)
    small_got(7, 6)
    small_sib(7)
    for i in range(8):
        small_theirs(i)
    docs_step(3)
    sums = sg_r[0][:, COLS:COLS + 256]
    for i in range(1, 16):
        sums = sums + sg_r[i][:, COLS:COLS + 256]
    ts_v[...] = jnp.broadcast_to(lax.rsqrt(sums[:, 0:128] / DT + 1e-05), (ROWS, 128)).T
    scale_v[...] = jnp.broadcast_to(lax.rsqrt(sums[:, 128:256] / DS + 1e-05), (ROWS, 128)).T
    l_wkv.wait()
    l_wq.wait()
    process(t)
    z_step(1)
    ag.opp_half(1)
    pj_send(3)
    ag.onear_a()
    process(ag.near[0])
    process(ag.near[1])
    process(ag.theirs(0))
    ag.onear_b()
    z_step(2)
    ag.onear_rest()
    process(ag.theirs(1))
    process(ag.theirs(2))
    ag.far_step()
    process(ag.opp)
    process(ag.theirs(3))
    ag.ofar_step()
    process(ag.onear[0])
    process(ag.onear[1])
    z_step(3)
    process(ag.far[0])
    process(ag.theirs(4))
    process(ag.theirs(5))
    process(ag.theirs(6))
    process(ag.far[1])
    process(ag.theirs(7))

    row = lax.broadcasted_iota(jnp.int32, (64, 64), 0)
    col = lax.broadcasted_iota(jnp.int32, (64, 64), 1)
    take = ((row >> 3) & 1) * 32 + (row & 7) * 4 + (row >> 4)
    pick = jnp.where(col == take, 1.0, 0.0).astype(BF16)
    kvx_s[...] = nt_dot(pick, kv_acc[...].astype(BF16)).astype(BF16).reshape(4, 16, 128)
    kvx_r[t] = kvx_s[t // 4]

    def kvx(k):
        to = (t + k) % 16
        return copy(kvx_s.at[to // 4], kvx_r.at[t], kx_ss.at[k], kx_rs.at[k], (s, to))

    def kvx_go(k, carry):
        kvx(k).start()
        return carry

    def kvx_got(k, carry):
        arrive(kvx_r.at[(t + 16 - k) % 16], kx_ss.at[k], kx_rs.at[k])
        return carry

    def kvx_end(k, carry):
        kvx(k).wait_send()
        return carry

    lax.fori_loop(1, 16, kvx_go, 0)
    z_step(4)

    cos2 = jnp.concatenate([cos_t[...], cos_t[...]], axis=0).T
    sin2 = jnp.concatenate([-sin_t[...], sin_t[...]], axis=0).T
    for h in range(2):
        qh = q_acc[:, h * 128:(h + 1) * 128]
        turned = qh * cos2 + pltpu.roll(qh, 64, 1) * sin2
        q_v[h] = (turned * HEAD_DIM ** (-0.5)).astype(BF16)

    lax.fori_loop(1, 16, kvx_got, 0)
    both = kvx_r[...].astype(F32).reshape(16, 2, 8, ROWS)
    k_raw = both[:, 0].reshape(HEAD_DIM, ROWS)
    v_raw = both[:, 1].reshape(HEAD_DIM, ROWS)
    first, second = k_raw[0:64], k_raw[64:128]
    k_rot = jnp.concatenate(
        [first * cos_t[...] - second * sin_t[...], second * cos_t[...] + first * sin_t[...]], axis=0
    )
    kv_own[0] = k_rot.astype(BF16)
    kv_own[1] = v_raw.T.astype(BF16)
    kv_r[0, 0] = kv_own[0]
    kv_r[1, 0] = kv_own[1]

    def kv_copy(k):
        return copy(kv_own.at[c], kv_r.at[c, k], kv_ss.at[k], kv_rs.at[k], ((s + k) % 16, t))

    def kv_fwd(k):
        return copy(kv_r.at[c, k], kv_r.at[c, k], kf_ss.at[k], kf_rs.at[k], sib)

    def kv_go(k, carry):
        @pl.when(s + k < 16)
        def _():
            kv_copy(k).start()
        return carry

    def kv_mid(k, carry):
        @pl.when(s >= k)
        def _():
            arrive(kv_r.at[c, k], kv_ss.at[k], kv_rs.at[k])
            kv_fwd(k).start()
        return carry

    def kv_got(k, carry):
        @pl.when(s >= k)
        def _():
            arrive(kv_r.at[1 - c, k], kf_ss.at[k], kf_rs.at[k])
        return carry

    def kv_end(k, carry):
        @pl.when(s >= k)
        def _():
            kv_fwd(k).wait_send()

        @pl.when(s + k < 16)
        def _():
            kv_copy(k).wait_send()
        return carry

    arrive(docs_o, dc_ss.at[8], dc_rs.at[8])
    lax.fori_loop(1, BACK + 1, kv_go, 0)

    class Reduce:
        def __init__(self, y_order, own, sib_s, sib_r, x2, ra, rb, xp, xm, fm, fp, ys, yr, fin, ss, rs):
            self.own, self.sib_s, self.sib_r = own, sib_s, sib_r
            self.x2, self.ra, self.rb, self.xp, self.xm, self.fm, self.fp = x2, ra, rb, xp, xm, fm, fp
            self.ys, self.yr, self.fin, self.ss, self.rs = ys, yr, fin, ss, rs
            self.y_order = y_order
            self.x_order = (xf_, xp_, xm_, x)

        def go(self, src, dst, k, dev):
            send(src, dst, self.ss.at[k], self.rs.at[k], dev)

        def got(self, dst, k):
            arrive(dst, self.ss.at[k], self.rs.at[k])

        def slot(self, k, i):
            return self.y_order[i] * 4 + self.x_order[k]

        def to_sib(self, k, i):
            slot = self.slot(k, i)
            self.go(self.sib_s.at[slot], self.sib_r.at[slot], k * 2 + i, sib)

        def sib_got(self, k, i):
            self.got(self.sib_r.at[self.slot(k, i)], k * 2 + i)

        def pair(self, k, i, h):
            slot, rows = self.slot(k, i), slice(h * 64, h * 64 + 64)
            return self.own[slot, rows] + self.sib_r[slot, rows].astype(F32)

        def far(self, i):
            self.sib_got(0, i)
            self.x2[i, 0:64] = self.pair(0, i, 0).astype(BF16)
            self.go(self.x2.at[i, pl.ds(0, 64)], self.ra.at[i], 8 + i, dev_xp)
            self.x2[i, 64:128] = self.pair(0, i, 1).astype(BF16)
            self.go(self.x2.at[i, pl.ds(64, 64)], self.rb.at[i], 10 + i, dev_xm)

        def near(self, i):
            self.sib_got(1, i)
            self.xp[i, 64:128] = self.pair(1, i, 1).astype(BF16)
            self.go(self.xp.at[i, pl.ds(64, 64)], self.fm.at[i, pl.ds(64, 64)], 12 + i, dev_xp)
            self.sib_got(2, i)
            self.xm[i, 0:64] = self.pair(2, i, 0).astype(BF16)
            self.go(self.xm.at[i, pl.ds(0, 64)], self.fp.at[i, pl.ds(0, 64)], 14 + i, dev_xm)

        def relay(self, i):
            self.got(self.ra.at[i], 8 + i)
            self.xp[i, 0:64] = (self.pair(1, i, 0) + self.ra[i].astype(F32)).astype(BF16)
            self.go(self.xp.at[i, pl.ds(0, 64)], self.fm.at[i, pl.ds(0, 64)], 16 + i, dev_xp)
            self.got(self.rb.at[i], 10 + i)
            self.xm[i, 64:128] = (self.pair(2, i, 1) + self.rb[i].astype(F32)).astype(BF16)
            self.go(self.xm.at[i, pl.ds(64, 64)], self.fp.at[i, pl.ds(64, 64)], 18 + i, dev_xm)

        def join(self, i, h):
            rows, at = slice(h * 64, h * 64 + 64), pl.ds(h * 64, 64)
            if h == 0:
                self.sib_got(3, i)
            self.got(self.fm.at[i, at], (16, 12)[h] + i)
            self.got(self.fp.at[i, at], (14, 18)[h] + i)
            return self.pair(3, i, h) + self.fm[i, rows].astype(F32) + self.fp[i, rows].astype(F32)

        def join_one(self, i):
            mine = self.y_order[i] == yh
            for h in range(2):
                rows = slice(h * 64, h * 64 + 64)
                value = self.join(i, h)

                @pl.when(mine)
                def _():
                    self.fin[rows] = value

                @pl.when(jnp.logical_not(mine))
                def _():
                    self.ys[rows] = value.astype(BF16)
                    self.to_opp(h).start()

        def to_opp(self, h):
            at = pl.ds(h * 64, 64)
            return copy(self.ys.at[at], self.yr.at[at], self.ss.at[20 + h], self.rs.at[20 + h], dev_yo)

        def join_other(self):
            for h in range(2):
                self.ys[h * 64:h * 64 + 64] = self.join(0, h).astype(BF16)
                self.to_opp(h).start()

        def join_mine(self):
            for h in range(2):
                self.fin[h * 64:h * 64 + 64] = self.join(1, h)

        def end(self):
            for h in range(2):
                self.to_opp(h).wait_send()

        def last(self, h):
            rows = slice(h * 64, h * 64 + 64)
            self.got(self.yr.at[pl.ds(h * 64, 64)], 20 + h)
            return self.fin[rows] + self.yr[rows].astype(F32)

    rt = Reduce((yl, 1 - yl), t_own, t_sib_s, t_sib_r, t_x2, t_ra, t_rb, t_xp, t_xm, t_fm, t_fp, t_ys, t_yr, t_fin, t_ss, t_rs)

    z_step(5)
    z_step(6)

    def products(core, y_):
        rows = tg[pl.ds(core * 4, 4)].reshape(4 * ROWS, 1024)
        return jnp.dot(rows, pj[y_], preferred_element_type=F32).reshape(4, ROWS, COLS)

    def t_wave(i):
        y_ = rt.y_order[i]
        t_sib_s[pl.ds(y_ * 4, 4)] = products(1 - c, y_).astype(BF16)
        for k in range(4):
            rt.to_sib(k, i)
        t_own[pl.ds(y_ * 4, 4)] = products(c, y_)

    l_pj.wait()
    t_wave(0)
    rt.far(0)
    rt.near(0)
    for k in range(4):
        arrive(pj.at[1 - yl, pl.ds(k * 256, 256)], p_ss.at[k], p_rs.at[k])
    t_wave(1)
    rt.relay(0)
    lax.fori_loop(1, BACK + 1, kv_mid, 0)
    rt.far(1)
    rt.near(1)

    lax.fori_loop(1, BACK + 1, kv_got, 0)
    keys = jnp.concatenate([kv_r[0, j] for j in range(BACK + 1)], axis=1)
    values = kv_r[1].reshape((BACK + 1) * ROWS, HEAD_DIM)

    def docs_back(j):
        at = (z + 8 - j) % 8
        return jnp.where(z >= j, docs_z[at], jnp.where(yl == 1, docs_o[at], -1))

    key_doc = jnp.concatenate([docs_back(j) for j in range(BACK + 1)], axis=1)
    row_doc = jnp.broadcast_to(docs[...].astype(F32), (ROWS, ROWS)).T[:, 0:1].astype(jnp.int32)
    wide = (ROWS, (BACK + 1) * ROWS)
    row_at = lax.broadcasted_iota(jnp.int32, wide, 0)
    key_at = lax.broadcasted_iota(jnp.int32, wide, 1)
    allowed = (key_doc == row_doc) & ((key_at >= ROWS) | (key_at <= row_at))
    for h in range(2):
        scores = jnp.dot(q_v[h], keys, preferred_element_type=F32)
        scores = jnp.where(allowed, scores, -1e30)
        probs = jnp.exp(scores - jnp.max(scores, axis=1, keepdims=True))
        total = jnp.sum(probs, axis=1, keepdims=True)
        acc = jnp.dot(probs.astype(BF16), values, preferred_element_type=F32)
        attn_v[:, h * 128:(h + 1) * 128] = (acc / total).astype(BF16)
        if h == 0:
            rt.relay(1)

    rt.join_one(0)
    l_wo.wait()

    ro = Reduce((yo_, yh), o_own, o_sib_s, o_sib_r, o_x2, o_ra, o_rb, o_xp, o_xm, o_fm, o_fp, o_ys, o_yr, o_fin, o_ss, o_rs)

    def out_block(k, i, core):
        at = pl.multiple_of(tid(ro.y_order[i], ro.x_order[k], core) * COLS, COLS)
        return jnp.dot(attn_v[...], wo[:, pl.ds(at, COLS)], preferred_element_type=F32)

    def out_theirs(k, i):
        o_sib_s[ro.slot(k, i)] = out_block(k, i, 1 - c).astype(BF16)
        ro.to_sib(k, i)

    def out_mine(k, i):
        o_own[ro.slot(k, i)] = out_block(k, i, c)

    for k in range(3):
        for i in range(2):
            out_theirs(k, i)
    out_mine(0, 0)
    ro.far(0)
    out_mine(1, 0)
    out_mine(2, 0)
    ro.near(0)
    rt.join_one(1)
    out_mine(0, 1)
    ro.relay(0)
    ro.far(1)
    out_mine(1, 1)
    out_mine(2, 1)
    ro.near(1)
    out_theirs(3, 0)
    out_theirs(3, 1)
    out_mine(3, 0)
    out_mine(3, 1)
    ro.relay(1)

    def t3(h):
        at = pl.ds(h * 64, 64)
        return copy(t3_s.at[at], t3_r.at[at], t3_ss.at[h], t3_rs.at[h], dev_t3)

    ro.join_other()
    for h in range(2):
        rows = slice(h * 64, h * 64 + 64)
        t3_s[rows] = rt.last(h).astype(BF16)

        @pl.when(stays)
        def _():
            t3_r[rows] = t3_s[rows]

        @pl.when(jnp.logical_not(stays))
        def _():
            t3(h).start()

    ro.join_mine()

    dg = Gather(db, dg_ss, dg_rs)
    for h in range(2):
        rows = slice(h * 64, h * 64 + 64)
        mixed = hb[t, rows].astype(F32) + ro.last(h)
        out_s[rows] = mixed.astype(BF16)

        @pl.when(jnp.logical_not(stays))
        def _():
            arrive(t3_r.at[pl.ds(h * 64, 64)], t3_ss.at[h], t3_rs.at[h])

        target = t3_r[rows].astype(F32) * jnp.concatenate([ts_v[rows]] * 4, axis=1)
        difference = mixed - target
        db[t, rows] = difference.astype(BF16)
        dg.begin(h)
        squares = difference * difference
        g_acc[rows, 0:128] = (
            squares[:, 0:128] + squares[:, 128:256] + squares[:, 256:384] + squares[:, 384:512]
        )
    dg.to_sib(0)
    l_s[...] = jnp.sum(g_acc[:, 0:128].T, axis=0, keepdims=True)
    l_r[t] = l_s[...]

    def loss(k):
        return copy(l_s, l_r.at[t], l_ss.at[k], l_rs.at[k], (s, (t + k) % 16))

    def loss_go(k, carry):
        loss(k).start()
        return carry

    def loss_got(k, carry):
        arrive(l_r.at[(t + 16 - k) % 16], l_ss.at[k], l_rs.at[k])
        return carry

    def loss_end(k, carry):
        loss(k).wait_send()
        return carry

    lax.fori_loop(1, 16, loss_go, 0)

    g_acc[...] = jnp.zeros(g_acc.shape, F32)

    def add_grad(slot):
        at = pl.multiple_of(slot * COLS, COLS)
        g_acc[...] += nt_dot(db[slot], wo[:, pl.ds(at, COLS)])

    add_grad(t)
    dg.near_relay()
    dg.near_rest()
    dg.opp_half(0)
    add_grad(dg.theirs(0))
    add_grad(dg.near[0])
    add_grad(dg.near[1])
    dg.opp_half(1)
    dg.onear_a()
    add_grad(dg.theirs(1))
    add_grad(dg.theirs(2))
    add_grad(dg.opp)
    dg.onear_b()
    dg.onear_rest()
    dg.far_step()
    add_grad(dg.theirs(3))
    add_grad(dg.onear[0])
    add_grad(dg.onear[1])
    dg.ofar_step()
    add_grad(dg.far[0])
    add_grad(dg.theirs(4))
    add_grad(dg.theirs(5))
    add_grad(dg.theirs(6))
    add_grad(dg.far[1])
    lax.fori_loop(1, 16, loss_got, 0)
    loss_sum = l_r[0]
    for i in range(1, 16):
        loss_sum = loss_sum + l_r[i]
    out_l[...] = loss_sum / DS
    add_grad(dg.theirs(7))
    out_g[...] = g_acc[...].astype(BF16)

    for one in started:
        one.wait_send()
    lax.fori_loop(1, 16, kvx_end, 0)
    lax.fori_loop(1, BACK + 1, kv_end, 0)
    lax.fori_loop(1, 16, loss_end, 0)

    rt.end()
    ro.end()

    @pl.when(jnp.logical_not(stays))
    def _():
        t3(0).wait_send()
        t3(1).wait_send()


def reduce_buffers():
    block = (ROWS, COLS)
    return [
        pltpu.VMEM((8,) + block, BF16),
        pltpu.VMEM((8,) + block, BF16),
        pltpu.VMEM((2,) + block, BF16),
        pltpu.VMEM((2, 64, COLS), BF16),
        pltpu.VMEM((2, 64, COLS), BF16),
        pltpu.VMEM((2,) + block, BF16),
        pltpu.VMEM((2,) + block, BF16),
        pltpu.VMEM((2,) + block, BF16),
        pltpu.VMEM((2,) + block, BF16),
        pltpu.VMEM(block, BF16),
        pltpu.VMEM(block, BF16),
        pltpu.VMEM(block, F32),
    ]


def on_device(
    teacher_hidden, teacher_gain, projector, student_hidden, student_gain,
    query_weight, kv_weight, out_weight, doc_ids,
):
    block = (ROWS, COLS)
    hbm = pl.BlockSpec(memory_space=pltpu.HBM)
    vmem = pl.BlockSpec(memory_space=pltpu.VMEM)
    dma = pltpu.SemaphoreType.DMA
    out_s, out_l, out_g = pl.pallas_call(
        body,
        out_shape=(
            jax.ShapeDtypeStruct(block, BF16),
            jax.ShapeDtypeStruct((1, ROWS), F32),
            jax.ShapeDtypeStruct((ROWS, 256), BF16),
        ),
        in_specs=[hbm] * 9,
        out_specs=(vmem, vmem, vmem),
        scratch_shapes=[
            pltpu.VMEM((1, 1024), F32),
            pltpu.VMEM((1, COLS), F32),
            pltpu.VMEM((1, ROWS), jnp.int32),
            pltpu.VMEM((ROWS, 1024), BF16),
            pltpu.VMEM((8, ROWS, 1024), BF16),
            pltpu.VMEM((2, 1024, COLS), BF16),
            pltpu.VMEM((DS, 256), BF16),
            pltpu.VMEM((2, 32, DS), BF16),
            pltpu.VMEM((256, DS), BF16),
            pltpu.VMEM((64, ROWS), F32),
            pltpu.VMEM((64, ROWS), F32),
            pltpu.VMEM((16,) + block, BF16),
            pltpu.VMEM((16,) + block, BF16),
            pltpu.VMEM((1, 768), F32),
            pltpu.VMEM((16, 1, 768), F32),
            pltpu.VMEM((ROWS, 128), F32),
            pltpu.VMEM((ROWS, 256), F32),
            pltpu.VMEM((ROWS, 64), F32),
            pltpu.VMEM((4, 16, ROWS), BF16),
            pltpu.VMEM((16, 16, ROWS), BF16),
            pltpu.VMEM((2, ROWS, HEAD_DIM), BF16),
            pltpu.VMEM((2, BACK + 1, ROWS, HEAD_DIM), BF16),
            pltpu.VMEM((8, 1, ROWS), jnp.int32),
            pltpu.VMEM((8, 1, ROWS), jnp.int32),
            pltpu.VMEM((2, ROWS, HEAD_DIM), BF16),
            pltpu.VMEM((ROWS, 256), BF16),
            pltpu.VMEM((8,) + block, F32),
            pltpu.VMEM((8,) + block, F32),
            *reduce_buffers(),
            *reduce_buffers(),
            pltpu.VMEM(block, BF16),
            pltpu.VMEM(block, BF16),
            pltpu.VMEM((ROWS, 128), F32),
            pltpu.VMEM((16,) + block, BF16),
            pltpu.VMEM((ROWS, 256), F32),
            pltpu.VMEM((1, ROWS), F32),
            pltpu.VMEM((16, 1, ROWS), F32),
            dma((10,)),
            dma((16,)), dma((16,)), dma((4,)), dma((4,)),
            dma((24,)), dma((24,)), dma((24,)), dma((24,)),
            dma((16,)), dma((16,)), dma((16,)), dma((16,)),
            dma((9,)), dma((9,)), dma((9,)), dma((9,)), dma((9,)), dma((9,)),
            dma((24,)), dma((24,)), dma((24,)), dma((24,)),
            dma((2,)), dma((2,)),
            dma((16,)), dma((16,)),
        ],
        compiler_params=pltpu.CompilerParams(
            collective_id=0, has_side_effects=True, vmem_limit_bytes=40 * 1024 * 1024
        ),
    )(
        *(
            pltpu.with_memory_space_constraint(one, pltpu.HBM)
            for one in (
                teacher_hidden, teacher_gain.reshape(1, -1), projector, student_hidden,
                student_gain.reshape(1, -1), query_weight, jnp.transpose(kv_weight, (0, 2, 1)),
                out_weight, doc_ids.reshape(1, -1),
            )
        )
    )
    return out_s, out_l.reshape(ROWS), out_g


def solution(mesh):
    in_specs = (
        P("seq", "tensor"),
        P("tensor"),
        P("tensor", "seq"),
        P("seq", "tensor"),
        P("tensor"),
        P(None, "tensor"),
        P(None, None, "tensor"),
        P("tensor", None),
        P("seq"),
    )
    out_specs = (P("seq", "tensor"), P("seq"), P("seq", "tensor"))
    return jax.shard_map(
        on_device, mesh=mesh, in_specs=in_specs, out_specs=out_specs, check_vma=False
    )
```

```python
import math

import jax
import jax.numpy as jnp
from jax import lax
from jax.experimental import pallas as pl
from jax.experimental.pallas import tpu as pltpu
from jax.sharding import PartitionSpec as P

DT = 16384
DS = 8192
HEAD_DIM = 128
HEADS = 32
KV_HEADS = 4
ROWS = 128
COLS = 512
BACK = 8
F32 = jnp.float32
BF16 = jnp.bfloat16
MESH = pl.DeviceIdType.MESH
NT = (((1,), (1,)), ((), ()))


def nt_dot(a, b):
    return lax.dot_general(a, b, NT, preferred_element_type=F32)


def body(
    th_h, tgain_h, pj_h, sh_h, sgain_h, wq_h, wkv_h, wo_h, docs_h,
    out_s, out_l, out_g,
    tgain, sgain, docs, th_v, tg, pj, wq, wkv, wo, cos_t, sin_t,
    hb, hn, sg_s, sg_r, scale_v, q_acc, kv_acc,
    kvx_s, kvx_r, kv_own, kv_r, docs_z, docs_o, q_v, attn_v,
    t_own, o_own, t_sib_s, t_sib_r, t_x2, t_ra, t_rb, t_xp, t_xm, t_fm, t_fp, t_ys, t_yr, t_fin,
    o_sib_s, o_sib_r, o_x2, o_ra, o_rb, o_xp, o_xm, o_fm, o_fp, o_ys, o_yr, o_fin,
    t3_s, t3_r, ts_v, db, g_acc, l_s, l_r,
    load_sem, z_ss, z_rs, p_ss, p_rs,
    ag_ss, ag_rs, dg_ss, dg_rs, sm_ss, sm_rs, kx_ss, kx_rs, kv_ss, kv_rs, kf_ss, kf_rs, dc_ss, dc_rs,
    t_ss, t_rs, o_ss, o_rs, t3_ss, t3_rs, l_ss, l_rs,
):
    s = lax.axis_index("seq")
    t = lax.axis_index("tensor")
    yl, z = s // 8, s % 8
    yh, x, c = t // 8, (t // 2) % 4, t % 2

    def tid(y_, x_, c_):
        return y_ * 8 + x_ * 2 + c_

    xp_, xm_ = (x + 1) % 4, (x + 3) % 4
    xf_ = (x + 2) % 4
    yo_ = 1 - yh
    sib = (s, tid(yh, x, 1 - c))
    dev_xp = (s, tid(yh, xp_, c))
    dev_xm = (s, tid(yh, xm_, c))
    dev_yo = (s, tid(yo_, x, c))
    dev_zp = (yl * 8 + (z + 1) % 8, t)
    dev_zm = (yl * 8 + (z + 7) % 8, t)
    dev_yl = ((1 - yl) * 8 + z, t)
    home = x * 2 + c
    dev_t3 = (yl * 8 + home, yh * 8 + z)
    stays = z == home

    started = []

    def copy(src, dst, ss, rs, dev):
        return pltpu.make_async_remote_copy(
            src_ref=src, dst_ref=dst, send_sem=ss, recv_sem=rs, device_id=dev, device_id_type=MESH
        )

    def send(src, dst, ss, rs, dev):
        one = copy(src, dst, ss, rs, dev)
        one.start()
        started.append(one)

    def arrive(dst, ss, rs):
        copy(dst, dst, ss, rs, sib).wait_recv()

    def load(src, dst, k):
        one = pltpu.make_async_copy(src, dst, load_sem.at[k])
        one.start()
        return one

    l_th = load(th_h, th_v, 0)
    l_sh = load(sh_h, hb.at[t], 1)
    l_small = [load(tgain_h, tgain, 7), load(sgain_h, sgain, 8), load(docs_h, docs, 9)]
    l_wkv = load(wkv_h, wkv, 2)
    l_wq = load(wq_h, wq, 3)
    l_pj = load(pj_h, pj.at[yl], 4)
    l_wo = load(wo_h, wo, 5)

    kv_r[1] = jnp.zeros((BACK + 1, ROWS, HEAD_DIM), BF16)

    barrier = pltpu.get_barrier_semaphore()
    for dev in (sib, dev_xp, dev_xm, dev_yo, dev_zp, dev_zm, dev_yl):
        pl.semaphore_signal(barrier, inc=1, device_id=dev, device_id_type=MESH)

    class Gather:
        def __init__(self, buf, ss, rs):
            self.buf, self.ss, self.rs = buf, ss, rs
            self.near = [tid(yh, xm_, c), tid(yh, xp_, c)]
            self.opp = tid(yo_, x, c)
            self.onear = [tid(yo_, xm_, c), tid(yo_, xp_, c)]
            self.far = [tid(yh, xf_, c), tid(yo_, xf_, c)]
            self.order = [t] + self.near + [self.opp] + self.onear + self.far

        def part(self, slot, h):
            return self.buf.at[slot, pl.ds(h * 64, 64)]

        def half(self, slot, h, k, dev, src=None):
            part = self.part(slot, h)
            send(part if src is None else src, part, self.ss.at[k], self.rs.at[k], dev)

        def got_half(self, slot, h, k):
            arrive(self.part(slot, h), self.ss.at[k], self.rs.at[k])

        def to_sib(self, i):
            slot = self.order[i]
            send(self.buf.at[slot], self.buf.at[slot], self.ss.at[16 + i], self.rs.at[16 + i], sib)

        def begin(self, h, src=None):
            self.half(t, h, 0 + h, dev_yo, src)
            self.half(t, h, 2 + h, dev_xp, src)
            self.half(t, h, 4 + h, dev_xm, src)

        def near_relay(self):
            self.got_half(self.near[0], 0, 2)
            self.half(self.near[0], 0, 6, dev_xp)
            self.got_half(self.near[1], 1, 5)
            self.half(self.near[1], 1, 7, dev_xm)

        def near_rest(self):
            self.got_half(self.near[0], 1, 3)
            self.to_sib(1)
            self.got_half(self.near[1], 0, 4)
            self.to_sib(2)

        def opp_half(self, h):
            self.got_half(self.opp, h, 0 + h)
            self.half(self.opp, h, 8 + h, dev_xp)
            self.half(self.opp, h, 10 + h, dev_xm)
            if h == 1:
                self.to_sib(3)

        def onear_a(self):
            self.got_half(self.onear[0], 0, 8)
            self.half(self.onear[0], 0, 12, dev_xp)

        def onear_b(self):
            self.got_half(self.onear[1], 1, 11)
            self.half(self.onear[1], 1, 13, dev_xm)

        def onear_rest(self):
            self.got_half(self.onear[0], 1, 9)
            self.to_sib(4)
            self.got_half(self.onear[1], 0, 10)
            self.to_sib(5)

        def far_step(self):
            self.got_half(self.far[0], 0, 6)
            self.got_half(self.far[0], 1, 7)
            self.to_sib(6)

        def ofar_step(self):
            self.got_half(self.far[1], 0, 12)
            self.got_half(self.far[1], 1, 13)
            self.to_sib(7)

        def theirs(self, i):
            slot = self.order[i] + 1 - 2 * c
            arrive(self.buf.at[slot], self.ss.at[16 + i], self.rs.at[16 + i])
            return slot

    z_slot = (z % 2) * 4 + z // 2
    l_th.wait()
    for one in l_small:
        one.wait()
    docs_z[z] = docs[...]
    part = jnp.zeros((ROWS, 128), F32)
    for i in range(8):
        cols = slice(i * 128, (i + 1) * 128)
        f = th_v[:, cols].astype(F32)
        part = part + f * f
        tg[z_slot, :, cols] = (f * tgain[:, cols]).astype(BF16)
    sg_s[:, COLS:COLS + 128] = jnp.sum(part.T, axis=0, keepdims=True)
    l_sh.wait()
    part = jnp.zeros((ROWS, 128), F32)
    for i in range(4):
        f = hb[t, :, i * 128:(i + 1) * 128].astype(F32)
        part = part + f * f
    sg_s[:, COLS + 128:COLS + 256] = jnp.sum(part.T, axis=0, keepdims=True)
    sg_s[:, 0:COLS] = sgain[...]
    sg_r[t] = sg_s[...]

    pl.semaphore_wait(barrier, 7)

    ag = Gather(hb, ag_ss, ag_rs)

    def ring_slot(d):
        zz = (z + d) % 8
        return (zz % 2) * 4 + zz // 2

    def z_ref(d, h):
        return tg.at[ring_slot(d), pl.ds(h * 64, 64)]

    def z_send(k):
        up, down = z_ref(-(k // 2) + 8, k % 2), z_ref(k // 2, 1 - k % 2)
        send(up, up, z_ss.at[k], z_rs.at[k], dev_zp)
        send(down, down, z_ss.at[8 + k], z_rs.at[8 + k], dev_zm)

    def z_got(k):
        up, down = z_ref(-(k // 2) + 7, k % 2), z_ref(k // 2 + 1, 1 - k % 2)
        arrive(up, z_ss.at[k], z_rs.at[k])
        arrive(down, z_ss.at[8 + k], z_rs.at[8 + k])

    def z_step(k):
        z_got(k)
        if k + 2 < 7:
            z_send(k + 2)

    def pj_send(k):
        rows = pl.ds(k * 256, 256)
        send(pj_h.at[rows], pj.at[yl, rows], p_ss.at[k], p_rs.at[k], dev_yl)


    def small_send(i, k, dev):
        slot = ag.order[i]
        send(sg_r.at[slot], sg_r.at[slot], sm_ss.at[k], sm_rs.at[k], dev)

    def small_got(i, k):
        arrive(sg_r.at[ag.order[i]], sm_ss.at[k], sm_rs.at[k])

    def small_sib(i):
        small_send(i, 8 + i, sib)

    def small_theirs(i):
        arrive(sg_r.at[ag.order[i] + 1 - 2 * c], sm_ss.at[8 + i], sm_rs.at[8 + i])

    def docs_send(d, k, dev):
        ref = docs_z.at[(z + d) % 8]
        send(ref, ref, dc_ss.at[k], dc_rs.at[k], dev)

    def docs_step(k):
        arrive(docs_z.at[(z + 7 - k) % 8], dc_ss.at[k], dc_rs.at[k])
        if k < 3:
            arrive(docs_z.at[(z + 1 + k) % 8], dc_ss.at[4 + k], dc_rs.at[4 + k])
            docs_send(7 - k, k + 1, dev_zp)
            if k < 2:
                docs_send(1 + k, k + 5, dev_zm)
        else:
            send(docs_z, docs_o, dc_ss.at[8], dc_rs.at[8], dev_yl)

    small_send(0, 0, dev_yo)
    small_send(0, 1, dev_xp)
    small_send(0, 2, dev_xm)
    small_sib(0)
    ag.begin(0)
    ag.begin(1)
    ag.to_sib(0)
    docs_send(0, 0, dev_zp)
    docs_send(0, 4, dev_zm)
    z_send(0)
    pj_send(0)
    z_send(1)
    pj_send(1)

    entry = lax.broadcasted_iota(jnp.int32, (64, ROWS), 0).astype(F32)
    position = (s * ROWS + lax.broadcasted_iota(jnp.int32, (64, ROWS), 1)).astype(F32)
    angle = position * jnp.exp(-math.log(500000.0) * (2.0 * entry / HEAD_DIM))
    cos_t[...] = jnp.cos(angle)
    sin_t[...] = jnp.sin(angle)
    q_acc[...] = jnp.zeros(q_acc.shape, F32)
    kv_acc[...] = jnp.zeros(kv_acc.shape, F32)

    def process(slot):
        for i in range(4):
            cols = slice(i * 128, (i + 1) * 128)
            f = hb[slot, :, cols].astype(F32)
            hn[slot, :, cols] = (f * scale_v[...] * sg_r[slot][:, cols]).astype(BF16)
        at = pl.multiple_of(slot * COLS, COLS)
        kv_acc[...] += nt_dot(hn[slot], wkv[:, :, pl.ds(at, COLS)].reshape(64, COLS))
        q_acc[...] += jnp.dot(hn[slot], wq[pl.ds(at, COLS), :], preferred_element_type=F32)

    small_got(1, 1)
    small_send(1, 3, dev_xp)
    small_sib(1)
    small_got(2, 2)
    small_sib(2)
    small_got(3, 0)
    small_send(3, 4, dev_xp)
    small_send(3, 5, dev_xm)
    small_sib(3)
    docs_step(0)
    ag.near_relay()
    small_got(6, 3)
    small_sib(6)
    docs_step(1)
    ag.near_rest()
    small_got(4, 4)
    small_send(4, 6, dev_xp)
    small_sib(4)
    small_got(5, 5)
    small_sib(5)
    ag.opp_half(0)
    z_step(0)
    pj_send(2)
    docs_step(2)
    small_got(7, 6)
    small_sib(7)
    for i in range(8):
        small_theirs(i)
    docs_step(3)
    sums = sg_r[0][:, COLS:COLS + 256]
    for i in range(1, 16):
        sums = sums + sg_r[i][:, COLS:COLS + 256]
    ts_v[...] = jnp.broadcast_to(lax.rsqrt(sums[:, 0:128] / DT + 1e-05), (ROWS, 128)).T
    scale_v[...] = jnp.broadcast_to(lax.rsqrt(sums[:, 128:256] / DS + 1e-05), (ROWS, 128)).T
    l_wkv.wait()
    l_wq.wait()
    process(t)
    z_step(1)
    ag.opp_half(1)
    pj_send(3)
    ag.onear_a()
    process(ag.near[0])
    process(ag.near[1])
    process(ag.theirs(0))
    ag.onear_b()
    z_step(2)
    ag.onear_rest()
    process(ag.theirs(1))
    process(ag.theirs(2))
    ag.far_step()
    process(ag.opp)
    process(ag.theirs(3))
    ag.ofar_step()
    process(ag.onear[0])
    process(ag.onear[1])
    z_step(3)
    process(ag.far[0])
    process(ag.theirs(4))
    process(ag.theirs(5))
    process(ag.theirs(6))
    process(ag.far[1])
    process(ag.theirs(7))

    row = lax.broadcasted_iota(jnp.int32, (64, 64), 0)
    col = lax.broadcasted_iota(jnp.int32, (64, 64), 1)
    take = ((row >> 3) & 1) * 32 + (row & 7) * 4 + (row >> 4)
    pick = jnp.where(col == take, 1.0, 0.0).astype(BF16)
    kvx_s[...] = nt_dot(pick, kv_acc[...].astype(BF16)).astype(BF16).reshape(4, 16, 128)
    kvx_r[t] = kvx_s[t // 4]

    def kvx(k):
        to = (t + k) % 16
        return copy(kvx_s.at[to // 4], kvx_r.at[t], kx_ss.at[k], kx_rs.at[k], (s, to))

    def kvx_go(k, carry):
        kvx(k).start()
        return carry

    def kvx_got(k, carry):
        arrive(kvx_r.at[(t + 16 - k) % 16], kx_ss.at[k], kx_rs.at[k])
        return carry

    def kvx_end(k, carry):
        kvx(k).wait_send()
        return carry

    lax.fori_loop(1, 16, kvx_go, 0)
    z_step(4)

    cos2 = jnp.concatenate([cos_t[...], cos_t[...]], axis=0).T
    sin2 = jnp.concatenate([-sin_t[...], sin_t[...]], axis=0).T
    for h in range(2):
        qh = q_acc[:, h * 128:(h + 1) * 128]
        turned = qh * cos2 + pltpu.roll(qh, 64, 1) * sin2
        q_v[h] = (turned * HEAD_DIM ** (-0.5)).astype(BF16)

    lax.fori_loop(1, 16, kvx_got, 0)
    both = kvx_r[...].astype(F32).reshape(16, 2, 8, ROWS)
    k_raw = both[:, 0].reshape(HEAD_DIM, ROWS)
    v_raw = both[:, 1].reshape(HEAD_DIM, ROWS)
    first, second = k_raw[0:64], k_raw[64:128]
    k_rot = jnp.concatenate(
        [first * cos_t[...] - second * sin_t[...], second * cos_t[...] + first * sin_t[...]], axis=0
    )
    kv_own[0] = k_rot.astype(BF16)
    kv_own[1] = v_raw.T.astype(BF16)
    kv_r[0, 0] = kv_own[0]
    kv_r[1, 0] = kv_own[1]

    def kv_copy(k):
        return copy(kv_own.at[c], kv_r.at[c, k], kv_ss.at[k], kv_rs.at[k], ((s + k) % 16, t))

    def kv_fwd(k):
        return copy(kv_r.at[c, k], kv_r.at[c, k], kf_ss.at[k], kf_rs.at[k], sib)

    def kv_go(k, carry):
        @pl.when(s + k < 16)
        def _():
            kv_copy(k).start()
        return carry

    def kv_mid(k, carry):
        @pl.when(s >= k)
        def _():
            arrive(kv_r.at[c, k], kv_ss.at[k], kv_rs.at[k])
            kv_fwd(k).start()
        return carry

    def kv_got(k, carry):
        @pl.when(s >= k)
        def _():
            arrive(kv_r.at[1 - c, k], kf_ss.at[k], kf_rs.at[k])
        return carry

    def kv_end(k, carry):
        @pl.when(s >= k)
        def _():
            kv_fwd(k).wait_send()

        @pl.when(s + k < 16)
        def _():
            kv_copy(k).wait_send()
        return carry

    arrive(docs_o, dc_ss.at[8], dc_rs.at[8])
    lax.fori_loop(1, BACK + 1, kv_go, 0)

    class Reduce:
        def __init__(self, y_order, own, sib_s, sib_r, x2, ra, rb, xp, xm, fm, fp, ys, yr, fin, ss, rs):
            self.own, self.sib_s, self.sib_r = own, sib_s, sib_r
            self.x2, self.ra, self.rb, self.xp, self.xm, self.fm, self.fp = x2, ra, rb, xp, xm, fm, fp
            self.ys, self.yr, self.fin, self.ss, self.rs = ys, yr, fin, ss, rs
            self.y_order = y_order
            self.x_order = (xf_, xp_, xm_, x)

        def go(self, src, dst, k, dev):
            send(src, dst, self.ss.at[k], self.rs.at[k], dev)

        def got(self, dst, k):
            arrive(dst, self.ss.at[k], self.rs.at[k])

        def slot(self, k, i):
            return self.y_order[i] * 4 + self.x_order[k]

        def to_sib(self, k, i):
            slot = self.slot(k, i)
            self.go(self.sib_s.at[slot], self.sib_r.at[slot], k * 2 + i, sib)

        def sib_got(self, k, i):
            self.got(self.sib_r.at[self.slot(k, i)], k * 2 + i)

        def pair(self, k, i, h):
            slot, rows = self.slot(k, i), slice(h * 64, h * 64 + 64)
            return self.own[slot, rows] + self.sib_r[slot, rows].astype(F32)

        def far(self, i):
            self.sib_got(0, i)
            self.x2[i, 0:64] = self.pair(0, i, 0).astype(BF16)
            self.go(self.x2.at[i, pl.ds(0, 64)], self.ra.at[i], 8 + i, dev_xp)
            self.x2[i, 64:128] = self.pair(0, i, 1).astype(BF16)
            self.go(self.x2.at[i, pl.ds(64, 64)], self.rb.at[i], 10 + i, dev_xm)

        def near(self, i):
            self.sib_got(1, i)
            self.xp[i, 64:128] = self.pair(1, i, 1).astype(BF16)
            self.go(self.xp.at[i, pl.ds(64, 64)], self.fm.at[i, pl.ds(64, 64)], 12 + i, dev_xp)
            self.sib_got(2, i)
            self.xm[i, 0:64] = self.pair(2, i, 0).astype(BF16)
            self.go(self.xm.at[i, pl.ds(0, 64)], self.fp.at[i, pl.ds(0, 64)], 14 + i, dev_xm)

        def relay(self, i):
            self.got(self.ra.at[i], 8 + i)
            self.xp[i, 0:64] = (self.pair(1, i, 0) + self.ra[i].astype(F32)).astype(BF16)
            self.go(self.xp.at[i, pl.ds(0, 64)], self.fm.at[i, pl.ds(0, 64)], 16 + i, dev_xp)
            self.got(self.rb.at[i], 10 + i)
            self.xm[i, 64:128] = (self.pair(2, i, 1) + self.rb[i].astype(F32)).astype(BF16)
            self.go(self.xm.at[i, pl.ds(64, 64)], self.fp.at[i, pl.ds(64, 64)], 18 + i, dev_xm)

        def join(self, i, h):
            rows, at = slice(h * 64, h * 64 + 64), pl.ds(h * 64, 64)
            if h == 0:
                self.sib_got(3, i)
            self.got(self.fm.at[i, at], (16, 12)[h] + i)
            self.got(self.fp.at[i, at], (14, 18)[h] + i)
            return self.pair(3, i, h) + self.fm[i, rows].astype(F32) + self.fp[i, rows].astype(F32)

        def join_one(self, i):
            mine = self.y_order[i] == yh
            for h in range(2):
                rows = slice(h * 64, h * 64 + 64)
                value = self.join(i, h)

                @pl.when(mine)
                def _():
                    self.fin[rows] = value

                @pl.when(jnp.logical_not(mine))
                def _():
                    self.ys[rows] = value.astype(BF16)
                    self.to_opp(h).start()

        def to_opp(self, h):
            at = pl.ds(h * 64, 64)
            return copy(self.ys.at[at], self.yr.at[at], self.ss.at[20 + h], self.rs.at[20 + h], dev_yo)

        def join_other(self):
            for h in range(2):
                self.ys[h * 64:h * 64 + 64] = self.join(0, h).astype(BF16)
                self.to_opp(h).start()

        def join_mine(self):
            for h in range(2):
                self.fin[h * 64:h * 64 + 64] = self.join(1, h)

        def end(self):
            for h in range(2):
                self.to_opp(h).wait_send()

        def last(self, h):
            rows = slice(h * 64, h * 64 + 64)
            self.got(self.yr.at[pl.ds(h * 64, 64)], 20 + h)
            return self.fin[rows] + self.yr[rows].astype(F32)

    rt = Reduce((yl, 1 - yl), t_own, t_sib_s, t_sib_r, t_x2, t_ra, t_rb, t_xp, t_xm, t_fm, t_fp, t_ys, t_yr, t_fin, t_ss, t_rs)

    z_step(5)
    z_step(6)

    def products(core, y_):
        rows = tg[pl.ds(core * 4, 4)].reshape(4 * ROWS, 1024)
        return jnp.dot(rows, pj[y_], preferred_element_type=F32).reshape(4, ROWS, COLS)

    def t_wave(i):
        y_ = rt.y_order[i]
        t_sib_s[pl.ds(y_ * 4, 4)] = products(1 - c, y_).astype(BF16)
        for k in range(4):
            rt.to_sib(k, i)
        t_own[pl.ds(y_ * 4, 4)] = products(c, y_)

    l_pj.wait()
    t_wave(0)
    rt.far(0)
    rt.near(0)
    for k in range(4):
        arrive(pj.at[1 - yl, pl.ds(k * 256, 256)], p_ss.at[k], p_rs.at[k])
    t_wave(1)
    rt.relay(0)
    rt.far(1)
    rt.near(1)
    rt.join_one(0)
    lax.fori_loop(1, BACK + 1, kv_mid, 0)
    rt.relay(1)

    lax.fori_loop(1, BACK + 1, kv_got, 0)
    keys = jnp.concatenate([kv_r[0, j] for j in range(BACK + 1)], axis=1)
    values = kv_r[1].reshape((BACK + 1) * ROWS, HEAD_DIM)

    def docs_back(j):
        at = (z + 8 - j) % 8
        return jnp.where(z >= j, docs_z[at], jnp.where(yl == 1, docs_o[at], -1))

    key_doc = jnp.concatenate([docs_back(j) for j in range(BACK + 1)], axis=1)
    row_doc = jnp.broadcast_to(docs[...].astype(F32), (ROWS, ROWS)).T[:, 0:1].astype(jnp.int32)
    wide = (ROWS, (BACK + 1) * ROWS)
    row_at = lax.broadcasted_iota(jnp.int32, wide, 0)
    key_at = lax.broadcasted_iota(jnp.int32, wide, 1)
    allowed = (key_doc == row_doc) & ((key_at >= ROWS) | (key_at <= row_at))
    for h in range(2):
        scores = jnp.dot(q_v[h], keys, preferred_element_type=F32)
        scores = jnp.where(allowed, scores, -1e30)
        probs = jnp.exp(scores - jnp.max(scores, axis=1, keepdims=True))
        total = jnp.sum(probs, axis=1, keepdims=True)
        acc = jnp.dot(probs.astype(BF16), values, preferred_element_type=F32)
        attn_v[:, h * 128:(h + 1) * 128] = (acc / total).astype(BF16)

    rt.join_one(1)
    l_wo.wait()

    ro = Reduce((yo_, yh), o_own, o_sib_s, o_sib_r, o_x2, o_ra, o_rb, o_xp, o_xm, o_fm, o_fp, o_ys, o_yr, o_fin, o_ss, o_rs)

    def out_block(k, i, core):
        at = pl.multiple_of(tid(ro.y_order[i], ro.x_order[k], core) * COLS, COLS)
        return jnp.dot(attn_v[...], wo[:, pl.ds(at, COLS)], preferred_element_type=F32)

    def out_theirs(k, i):
        o_sib_s[ro.slot(k, i)] = out_block(k, i, 1 - c).astype(BF16)
        ro.to_sib(k, i)

    def out_mine(k, i):
        o_own[ro.slot(k, i)] = out_block(k, i, c)

    for k in range(3):
        for i in range(2):
            out_theirs(k, i)
    out_mine(0, 0)
    ro.far(0)
    out_mine(1, 0)
    out_mine(2, 0)
    ro.near(0)
    out_mine(0, 1)
    ro.relay(0)
    ro.far(1)
    out_mine(1, 1)
    out_mine(2, 1)
    ro.near(1)
    out_theirs(3, 0)
    out_theirs(3, 1)
    out_mine(3, 0)
    out_mine(3, 1)
    ro.relay(1)

    def t3(h):
        at = pl.ds(h * 64, 64)
        return copy(t3_s.at[at], t3_r.at[at], t3_ss.at[h], t3_rs.at[h], dev_t3)

    for h in range(2):
        rows = slice(h * 64, h * 64 + 64)
        t3_s[rows] = rt.last(h).astype(BF16)

        @pl.when(stays)
        def _():
            t3_r[rows] = t3_s[rows]

        @pl.when(jnp.logical_not(stays))
        def _():
            t3(h).start()

    ro.join_other()
    ro.join_mine()

    dg = Gather(db, dg_ss, dg_rs)
    for h in range(2):
        rows = slice(h * 64, h * 64 + 64)
        mixed = hb[t, rows].astype(F32) + ro.last(h)
        out_s[rows] = mixed.astype(BF16)

        @pl.when(jnp.logical_not(stays))
        def _():
            arrive(t3_r.at[pl.ds(h * 64, 64)], t3_ss.at[h], t3_rs.at[h])

        target = t3_r[rows].astype(F32) * jnp.concatenate([ts_v[rows]] * 4, axis=1)
        difference = mixed - target
        db[t, rows] = difference.astype(BF16)
        dg.begin(h)
        squares = difference * difference
        g_acc[rows, 0:128] = (
            squares[:, 0:128] + squares[:, 128:256] + squares[:, 256:384] + squares[:, 384:512]
        )
    dg.to_sib(0)
    l_s[...] = jnp.sum(g_acc[:, 0:128].T, axis=0, keepdims=True)
    l_r[t] = l_s[...]

    def loss(k):
        return copy(l_s, l_r.at[t], l_ss.at[k], l_rs.at[k], (s, (t + k) % 16))

    def loss_go(k, carry):
        loss(k).start()
        return carry

    def loss_got(k, carry):
        arrive(l_r.at[(t + 16 - k) % 16], l_ss.at[k], l_rs.at[k])
        return carry

    def loss_end(k, carry):
        loss(k).wait_send()
        return carry

    lax.fori_loop(1, 16, loss_go, 0)

    g_acc[...] = jnp.zeros(g_acc.shape, F32)

    def add_grad(slot):
        at = pl.multiple_of(slot * COLS, COLS)
        g_acc[...] += nt_dot(db[slot], wo[:, pl.ds(at, COLS)])

    add_grad(t)
    dg.near_relay()
    dg.near_rest()
    dg.opp_half(0)
    add_grad(dg.theirs(0))
    add_grad(dg.near[0])
    add_grad(dg.near[1])
    dg.opp_half(1)
    dg.onear_a()
    add_grad(dg.theirs(1))
    add_grad(dg.theirs(2))
    add_grad(dg.opp)
    dg.onear_b()
    dg.onear_rest()
    dg.far_step()
    add_grad(dg.theirs(3))
    add_grad(dg.onear[0])
    add_grad(dg.onear[1])
    dg.ofar_step()
    add_grad(dg.far[0])
    add_grad(dg.theirs(4))
    add_grad(dg.theirs(5))
    add_grad(dg.theirs(6))
    add_grad(dg.far[1])
    lax.fori_loop(1, 16, loss_got, 0)
    loss_sum = l_r[0]
    for i in range(1, 16):
        loss_sum = loss_sum + l_r[i]
    out_l[...] = loss_sum / DS
    add_grad(dg.theirs(7))
    out_g[...] = g_acc[...].astype(BF16)

    for one in started:
        one.wait_send()
    lax.fori_loop(1, 16, kvx_end, 0)
    lax.fori_loop(1, BACK + 1, kv_end, 0)
    lax.fori_loop(1, 16, loss_end, 0)

    rt.end()
    ro.end()

    @pl.when(jnp.logical_not(stays))
    def _():
        t3(0).wait_send()
        t3(1).wait_send()


def reduce_buffers():
    block = (ROWS, COLS)
    return [
        pltpu.VMEM((8,) + block, BF16),
        pltpu.VMEM((8,) + block, BF16),
        pltpu.VMEM((2,) + block, BF16),
        pltpu.VMEM((2, 64, COLS), BF16),
        pltpu.VMEM((2, 64, COLS), BF16),
        pltpu.VMEM((2,) + block, BF16),
        pltpu.VMEM((2,) + block, BF16),
        pltpu.VMEM((2,) + block, BF16),
        pltpu.VMEM((2,) + block, BF16),
        pltpu.VMEM(block, BF16),
        pltpu.VMEM(block, BF16),
        pltpu.VMEM(block, F32),
    ]


def on_device(
    teacher_hidden, teacher_gain, projector, student_hidden, student_gain,
    query_weight, kv_weight, out_weight, doc_ids,
):
    block = (ROWS, COLS)
    hbm = pl.BlockSpec(memory_space=pltpu.HBM)
    vmem = pl.BlockSpec(memory_space=pltpu.VMEM)
    dma = pltpu.SemaphoreType.DMA
    out_s, out_l, out_g = pl.pallas_call(
        body,
        out_shape=(
            jax.ShapeDtypeStruct(block, BF16),
            jax.ShapeDtypeStruct((1, ROWS), F32),
            jax.ShapeDtypeStruct((ROWS, 256), BF16),
        ),
        in_specs=[hbm] * 9,
        out_specs=(vmem, vmem, vmem),
        scratch_shapes=[
            pltpu.VMEM((1, 1024), F32),
            pltpu.VMEM((1, COLS), F32),
            pltpu.VMEM((1, ROWS), jnp.int32),
            pltpu.VMEM((ROWS, 1024), BF16),
            pltpu.VMEM((8, ROWS, 1024), BF16),
            pltpu.VMEM((2, 1024, COLS), BF16),
            pltpu.VMEM((DS, 256), BF16),
            pltpu.VMEM((2, 32, DS), BF16),
            pltpu.VMEM((256, DS), BF16),
            pltpu.VMEM((64, ROWS), F32),
            pltpu.VMEM((64, ROWS), F32),
            pltpu.VMEM((16,) + block, BF16),
            pltpu.VMEM((16,) + block, BF16),
            pltpu.VMEM((1, 768), F32),
            pltpu.VMEM((16, 1, 768), F32),
            pltpu.VMEM((ROWS, 128), F32),
            pltpu.VMEM((ROWS, 256), F32),
            pltpu.VMEM((ROWS, 64), F32),
            pltpu.VMEM((4, 16, ROWS), BF16),
            pltpu.VMEM((16, 16, ROWS), BF16),
            pltpu.VMEM((2, ROWS, HEAD_DIM), BF16),
            pltpu.VMEM((2, BACK + 1, ROWS, HEAD_DIM), BF16),
            pltpu.VMEM((8, 1, ROWS), jnp.int32),
            pltpu.VMEM((8, 1, ROWS), jnp.int32),
            pltpu.VMEM((2, ROWS, HEAD_DIM), BF16),
            pltpu.VMEM((ROWS, 256), BF16),
            pltpu.VMEM((8,) + block, F32),
            pltpu.VMEM((8,) + block, F32),
            *reduce_buffers(),
            *reduce_buffers(),
            pltpu.VMEM(block, BF16),
            pltpu.VMEM(block, BF16),
            pltpu.VMEM((ROWS, 128), F32),
            pltpu.VMEM((16,) + block, BF16),
            pltpu.VMEM((ROWS, 256), F32),
            pltpu.VMEM((1, ROWS), F32),
            pltpu.VMEM((16, 1, ROWS), F32),
            dma((10,)),
            dma((16,)), dma((16,)), dma((4,)), dma((4,)),
            dma((24,)), dma((24,)), dma((24,)), dma((24,)),
            dma((16,)), dma((16,)), dma((16,)), dma((16,)),
            dma((9,)), dma((9,)), dma((9,)), dma((9,)), dma((9,)), dma((9,)),
            dma((24,)), dma((24,)), dma((24,)), dma((24,)),
            dma((2,)), dma((2,)),
            dma((16,)), dma((16,)),
        ],
        compiler_params=pltpu.CompilerParams(
            collective_id=0, has_side_effects=True, vmem_limit_bytes=40 * 1024 * 1024
        ),
    )(
        *(
            pltpu.with_memory_space_constraint(one, pltpu.HBM)
            for one in (
                teacher_hidden, teacher_gain.reshape(1, -1), projector, student_hidden,
                student_gain.reshape(1, -1), query_weight, jnp.transpose(kv_weight, (0, 2, 1)),
                out_weight, doc_ids.reshape(1, -1),
            )
        )
    )
    return out_s, out_l.reshape(ROWS), out_g


def solution(mesh):
    in_specs = (
        P("seq", "tensor"),
        P("tensor"),
        P("tensor", "seq"),
        P("seq", "tensor"),
        P("tensor"),
        P(None, "tensor"),
        P(None, None, "tensor"),
        P("tensor", None),
        P("seq"),
    )
    out_specs = (P("seq", "tensor"), P("seq"), P("seq", "tensor"))
    return jax.shard_map(
        on_device, mesh=mesh, in_specs=in_specs, out_specs=out_specs, check_vma=False
    )
```

```python
import math

import jax
import jax.numpy as jnp
from jax import lax
from jax.experimental import pallas as pl
from jax.experimental.pallas import tpu as pltpu
from jax.sharding import PartitionSpec as P

DT = 16384
DS = 8192
HEAD_DIM = 128
HEADS = 32
KV_HEADS = 4
ROWS = 128
COLS = 512
BACK = 8
F32 = jnp.float32
BF16 = jnp.bfloat16
MESH = pl.DeviceIdType.MESH
NT = (((1,), (1,)), ((), ()))


def nt_dot(a, b):
    return lax.dot_general(a, b, NT, preferred_element_type=F32)


def body(
    th_h, tgain_h, pj_h, sh_h, sgain_h, wq_h, wkv_h, wo_h, docs_h,
    out_s, out_l, out_g,
    tgain, sgain, docs, th_v, tg, pj, wq, wkv, wo, cos_t, sin_t,
    hb, sg_s, sg_r, sum_s, sum_r, scale_v, q_acc, q_in, kv_acc, kv_in,
    kvx_s, kvx_r, kv_own, kv_r, docs_z, docs_o, q_v, attn_v,
    t_own, o_own, o_x2, t_sib_s, t_sib_r, t_x2, t_ra, t_rb, t_xp, t_xm, t_fm, t_fp, t_ys, t_yr, t_fin,
    o_ra, o_rb, o_xp, o_xm, o_fm, o_fp, o_ys, o_yr, o_fin,
    t3_s, t3_r, ts_v, db, g_acc, g_in, l_v, l_s, l_r,
    load_sem, w_load, w_ss, w_rs, x_ss, x_rs, z_ss, z_rs, p_ss, p_rs,
    ag_ss, ag_rs, dg_ss, dg_rs, sm_ss, sm_rs, kx_ss, kx_rs, kv_ss, kv_rs, kf_ss, kf_rs, dc_ss, dc_rs,
    t_ss, t_rs, o_ss, o_rs, t3_ss, t3_rs, l_ss, l_rs,
):
    s = lax.axis_index("seq")
    t = lax.axis_index("tensor")
    yl, z = s // 8, s % 8
    yh, x, c = t // 8, (t // 2) % 4, t % 2

    def tid(y_, x_, c_):
        return y_ * 8 + x_ * 2 + c_

    xp_, xm_ = (x + 1) % 4, (x + 3) % 4
    xf_ = (x + 2) % 4
    yo_ = 1 - yh
    sib = (s, tid(yh, x, 1 - c))
    dev_xp = (s, tid(yh, xp_, c))
    dev_xm = (s, tid(yh, xm_, c))
    dev_yo = (s, tid(yo_, x, c))
    dev_zp = (yl * 8 + (z + 1) % 8, t)
    dev_zm = (yl * 8 + (z + 7) % 8, t)
    dev_yl = ((1 - yl) * 8 + z, t)
    home = x * 2 + c
    dev_t3 = (yl * 8 + home, yh * 8 + z)
    stays = z == home

    started = []

    def copy(src, dst, ss, rs, dev):
        return pltpu.make_async_remote_copy(
            src_ref=src, dst_ref=dst, send_sem=ss, recv_sem=rs, device_id=dev, device_id_type=MESH
        )

    def send(src, dst, ss, rs, dev):
        one = copy(src, dst, ss, rs, dev)
        one.start()
        started.append(one)

    def arrive(dst, ss, rs):
        copy(dst, dst, ss, rs, sib).wait_recv()

    def load(src, dst, k):
        one = pltpu.make_async_copy(src, dst, load_sem.at[k])
        one.start()
        return one

    l_th = load(th_h, th_v, 0)
    mine = yh * 4 + x
    l_sh = load(sh_h, hb.at[mine], 1)
    l_small = [load(tgain_h, tgain, 7), load(sgain_h, sgain, 8), load(docs_h, docs, 9)]
    l_wkv = load(wkv_h, wkv.at[c], 2)
    l_wq = load(wq_h.at[:, c], wq.at[:, c], 3)
    l_pj = load(pj_h, pj.at[yl], 4)

    def wo_part(j, core):
        return wo_h.at[:, pl.ds(pl.multiple_of((j * 2 + core) * COLS, COLS), COLS)]

    def wo_load(j):
        return pltpu.make_async_copy(wo_part(j, c), wo.at[j, c], w_load.at[j])

    def wo_send(j):
        return copy(wo_part(j, 1 - c), wo.at[j, c], w_ss.at[j], w_rs.at[j], sib)

    def wo_go(j, carry):
        wo_load(j).start()
        wo_send(j).start()
        return carry

    def wo_got(j, carry):
        wo_load(j).wait()
        arrive(wo.at[j, 1 - c], w_ss.at[j], w_rs.at[j])
        return carry

    def wo_end(j, carry):
        wo_send(j).wait_send()
        return carry

    kv_r[1] = jnp.zeros((BACK + 1, ROWS, HEAD_DIM), BF16)

    barrier = pltpu.get_barrier_semaphore()
    for dev in (sib, dev_xp, dev_xm, dev_yo, dev_zp, dev_zm, dev_yl):
        pl.semaphore_signal(barrier, inc=1, device_id=dev, device_id_type=MESH)

    class Gather:
        def __init__(self, buf, ss, rs):
            self.buf, self.ss, self.rs = buf, ss, rs
            self.near = [yh * 4 + xm_, yh * 4 + xp_]
            self.opp = yo_ * 4 + x
            self.onear = [yo_ * 4 + xm_, yo_ * 4 + xp_]
            self.far = [yh * 4 + xf_, yo_ * 4 + xf_]
            self.order = [mine] + self.near + [self.opp] + self.onear + self.far

        def part(self, slot, h):
            return self.buf.at[slot, pl.ds(h * 64, 64)]

        def half(self, slot, h, k, dev):
            part = self.part(slot, h)
            send(part, part, self.ss.at[k], self.rs.at[k], dev)

        def got_half(self, slot, h, k):
            arrive(self.part(slot, h), self.ss.at[k], self.rs.at[k])

        def begin(self, h):
            self.half(mine, h, 0 + h, dev_yo)
            self.half(mine, h, 2 + h, dev_xp)
            self.half(mine, h, 4 + h, dev_xm)

        def near_relay(self):
            self.got_half(self.near[0], 0, 2)
            self.half(self.near[0], 0, 6, dev_xp)
            self.got_half(self.near[1], 1, 5)
            self.half(self.near[1], 1, 7, dev_xm)

        def near_rest(self):
            self.got_half(self.near[0], 1, 3)
            self.got_half(self.near[1], 0, 4)

        def opp_half(self, h):
            self.got_half(self.opp, h, 0 + h)
            self.half(self.opp, h, 8 + h, dev_xp)
            self.half(self.opp, h, 10 + h, dev_xm)

        def onear_a(self):
            self.got_half(self.onear[0], 0, 8)
            self.half(self.onear[0], 0, 12, dev_xp)

        def onear_b(self):
            self.got_half(self.onear[1], 1, 11)
            self.half(self.onear[1], 1, 13, dev_xm)

        def onear_rest(self):
            self.got_half(self.onear[0], 1, 9)
            self.got_half(self.onear[1], 0, 10)

        def far_step(self):
            self.got_half(self.far[0], 0, 6)
            self.got_half(self.far[0], 1, 7)

        def ofar_step(self):
            self.got_half(self.far[1], 0, 12)
            self.got_half(self.far[1], 1, 13)

    z_slot = (z % 2) * 4 + z // 2
    l_th.wait()
    for one in l_small:
        one.wait()
    docs_z[z] = docs[...]
    part = jnp.zeros((ROWS, 128), F32)
    for i in range(8):
        cols = slice(i * 128, (i + 1) * 128)
        f = th_v[:, cols].astype(F32)
        part = part + f * f
        tg[z_slot, :, cols] = (f * tgain[:, cols]).astype(BF16)
    sg_s[:, COLS:COLS + 128] = jnp.sum(part.T, axis=0, keepdims=True)
    l_sh.wait()
    part = jnp.zeros((ROWS, 128), F32)
    for i in range(4):
        f = hb[mine, :, i * 128:(i + 1) * 128].astype(F32)
        part = part + f * f
    sg_s[:, COLS + 128:COLS + 256] = jnp.sum(part.T, axis=0, keepdims=True)
    sg_s[:, 0:COLS] = sgain[...]
    sg_r[mine] = sg_s[...]

    pl.semaphore_wait(barrier, 7)

    ag = Gather(hb, ag_ss, ag_rs)

    def ring_slot(d):
        zz = (z + d) % 8
        return (zz % 2) * 4 + zz // 2

    def z_ref(d, h):
        return tg.at[ring_slot(d), pl.ds(h * 64, 64)]

    def z_send(k):
        up, down = z_ref(-(k // 2) + 8, k % 2), z_ref(k // 2, 1 - k % 2)
        send(up, up, z_ss.at[k], z_rs.at[k], dev_zp)
        send(down, down, z_ss.at[8 + k], z_rs.at[8 + k], dev_zm)

    def z_got(k):
        up, down = z_ref(-(k // 2) + 7, k % 2), z_ref(k // 2 + 1, 1 - k % 2)
        arrive(up, z_ss.at[k], z_rs.at[k])
        arrive(down, z_ss.at[8 + k], z_rs.at[8 + k])

    def z_step(k):
        z_got(k)
        if k + 2 < 7:
            z_send(k + 2)

    def pj_send(k):
        rows = pl.ds(k * 256, 256)
        send(pj_h.at[rows], pj.at[yl, rows], p_ss.at[k], p_rs.at[k], dev_yl)


    def small_send(i, k, dev):
        slot = ag.order[i]
        send(sg_r.at[slot], sg_r.at[slot], sm_ss.at[k], sm_rs.at[k], dev)

    def small_got(i, k):
        arrive(sg_r.at[ag.order[i]], sm_ss.at[k], sm_rs.at[k])

    def docs_send(d, k, dev):
        ref = docs_z.at[(z + d) % 8]
        send(ref, ref, dc_ss.at[k], dc_rs.at[k], dev)

    def docs_step(k):
        arrive(docs_z.at[(z + 7 - k) % 8], dc_ss.at[k], dc_rs.at[k])
        if k < 3:
            arrive(docs_z.at[(z + 1 + k) % 8], dc_ss.at[4 + k], dc_rs.at[4 + k])
            docs_send(7 - k, k + 1, dev_zp)
            if k < 2:
                docs_send(1 + k, k + 5, dev_zm)
        else:
            send(docs_z, docs_o, dc_ss.at[8], dc_rs.at[8], dev_yl)

    small_send(0, 0, dev_yo)
    small_send(0, 1, dev_xp)
    small_send(0, 2, dev_xm)
    ag.begin(0)
    ag.begin(1)
    send(wkv_h, wkv.at[c], x_ss.at[0], x_rs.at[0], sib)
    send(wq_h.at[:, 1 - c], wq.at[:, c], x_ss.at[1], x_rs.at[1], sib)
    docs_send(0, 0, dev_zp)
    docs_send(0, 4, dev_zm)
    z_send(0)
    pj_send(0)
    z_send(1)
    pj_send(1)

    entry = lax.broadcasted_iota(jnp.int32, (64, ROWS), 0).astype(F32)
    position = (s * ROWS + lax.broadcasted_iota(jnp.int32, (64, ROWS), 1)).astype(F32)
    angle = position * jnp.exp(-math.log(500000.0) * (2.0 * entry / HEAD_DIM))
    cos_t[...] = jnp.cos(angle)
    sin_t[...] = jnp.sin(angle)

    def process(slots, first=False):
        blocks = []
        for slot in slots:
            parts = []
            for i in range(4):
                cols = slice(i * 128, (i + 1) * 128)
                f = hb[slot, :, cols].astype(F32)
                parts.append((f * scale_v[...] * sg_r[slot][:, cols]).astype(BF16))
            blocks.append(jnp.concatenate(parts, axis=1))
        n = jnp.concatenate(blocks, axis=1)
        w = []
        for slot in slots:
            at = pl.multiple_of((slot * 2 + c) * COLS, COLS)
            w.append(wkv[:, :, :, pl.ds(at, COLS)].reshape(128, COLS))
        kv = nt_dot(jnp.concatenate(w, axis=1), n)
        for core in range(2):
            w = jnp.concatenate([wq[slot, core] for slot in slots], axis=0)
            q = jnp.dot(n, w, preferred_element_type=F32)
            k = kv[core * 64:core * 64 + 64]
            q_acc[core] = q if first else q_acc[core] + q
            kv_acc[core] = k if first else kv_acc[core] + k

    small_got(1, 1)
    small_send(1, 3, dev_xp)
    small_got(2, 2)
    small_got(3, 0)
    small_send(3, 4, dev_xp)
    small_send(3, 5, dev_xm)
    docs_step(0)
    ag.near_relay()
    small_got(6, 3)
    docs_step(1)
    small_got(4, 4)
    small_send(4, 6, dev_xp)
    small_got(5, 5)
    ag.near_rest()
    ag.opp_half(0)
    z_step(0)
    pj_send(2)
    small_got(7, 6)
    sums = sg_r[0][:, COLS:COLS + 256]
    for i in range(1, 8):
        sums = sums + sg_r[i][:, COLS:COLS + 256]
    sum_s[...] = sums
    send(sum_s, sum_r, x_ss.at[2], x_rs.at[2], sib)
    docs_step(2)
    ag.opp_half(1)
    pj_send(3)
    arrive(sum_r, x_ss.at[2], x_rs.at[2])
    sums = sum_s[...] + sum_r[...]
    ts_v[...] = jnp.broadcast_to(lax.rsqrt(sums[:, 0:128] / DT + 1e-05), (ROWS, 128)).T
    scale_v[...] = jnp.broadcast_to(lax.rsqrt(sums[:, 128:256] / DS + 1e-05), (ROWS, 128)).T
    docs_step(3)
    z_step(1)
    ag.onear_a()
    l_wkv.wait()
    l_wq.wait()
    arrive(wkv.at[1 - c], x_ss.at[0], x_rs.at[0])
    arrive(wq.at[:, 1 - c], x_ss.at[1], x_rs.at[1])
    process([mine] + ag.near, True)
    ag.onear_b()
    z_step(2)
    ag.far_step()
    process([ag.opp, ag.far[0]])
    ag.onear_rest()
    process(ag.onear)
    z_step(3)
    ag.ofar_step()
    process([ag.far[1]])
    send(kv_acc.at[1 - c], kv_in, x_ss.at[3], x_rs.at[3], sib)
    send(q_acc.at[1 - c], q_in, x_ss.at[4], x_rs.at[4], sib)
    lax.fori_loop(0, 8, wo_go, 0)
    arrive(kv_in, x_ss.at[3], x_rs.at[3])

    row = lax.broadcasted_iota(jnp.int32, (64, 64), 0)
    col = lax.broadcasted_iota(jnp.int32, (64, 64), 1)
    take = ((row >> 3) & 1) * 32 + (row & 7) * 4 + (row >> 4)
    pick = jnp.where(col == take, 1.0, 0.0).astype(BF16)
    kv_mine = (kv_acc[c] + kv_in[...]).astype(BF16)
    kvx_s[...] = jnp.dot(pick, kv_mine, preferred_element_type=F32).astype(BF16).reshape(4, 16, 128)
    kvx_r[t] = kvx_s[t // 4]

    def kvx(k):
        to = (t + k) % 16
        return copy(kvx_s.at[to // 4], kvx_r.at[t], kx_ss.at[k], kx_rs.at[k], (s, to))

    def kvx_go(k, carry):
        kvx(k).start()
        return carry

    def kvx_got(k, carry):
        arrive(kvx_r.at[(t + 16 - k) % 16], kx_ss.at[k], kx_rs.at[k])
        return carry

    def kvx_end(k, carry):
        kvx(k).wait_send()
        return carry

    lax.fori_loop(1, 16, kvx_go, 0)
    z_step(4)

    cos2 = jnp.concatenate([cos_t[...], cos_t[...]], axis=0).T
    sin2 = jnp.concatenate([-sin_t[...], sin_t[...]], axis=0).T
    arrive(q_in, x_ss.at[4], x_rs.at[4])
    q_mine = q_acc[c] + q_in[...]
    for h in range(2):
        qh = q_mine[:, h * 128:(h + 1) * 128]
        turned = qh * cos2 + pltpu.roll(qh, 64, 1) * sin2
        q_v[h] = (turned * HEAD_DIM ** (-0.5)).astype(BF16)

    lax.fori_loop(1, 16, kvx_got, 0)
    both = kvx_r[...].astype(F32).reshape(16, 2, 8, ROWS)
    k_raw = both[:, 0].reshape(HEAD_DIM, ROWS)
    v_raw = both[:, 1].reshape(HEAD_DIM, ROWS)
    first, second = k_raw[0:64], k_raw[64:128]
    k_rot = jnp.concatenate(
        [first * cos_t[...] - second * sin_t[...], second * cos_t[...] + first * sin_t[...]], axis=0
    )
    kv_own[0] = k_rot.astype(BF16)
    kv_own[1] = v_raw.T.astype(BF16)
    kv_r[0, 0] = kv_own[0]
    kv_r[1, 0] = kv_own[1]

    def kv_copy(k):
        return copy(kv_own.at[c], kv_r.at[c, k], kv_ss.at[k], kv_rs.at[k], ((s + k) % 16, t))

    def kv_fwd(k):
        return copy(kv_r.at[c, k], kv_r.at[c, k], kf_ss.at[k], kf_rs.at[k], sib)

    def kv_go(k, carry):
        @pl.when(s + k < 16)
        def _():
            kv_copy(k).start()
        return carry

    def kv_mid(k, carry):
        @pl.when(s >= k)
        def _():
            arrive(kv_r.at[c, k], kv_ss.at[k], kv_rs.at[k])
            kv_fwd(k).start()
        return carry

    def kv_got(k, carry):
        @pl.when(s >= k)
        def _():
            arrive(kv_r.at[1 - c, k], kf_ss.at[k], kf_rs.at[k])
        return carry

    def kv_end(k, carry):
        @pl.when(s >= k)
        def _():
            kv_fwd(k).wait_send()

        @pl.when(s + k < 16)
        def _():
            kv_copy(k).wait_send()
        return carry

    arrive(docs_o, dc_ss.at[8], dc_rs.at[8])
    lax.fori_loop(1, BACK + 1, kv_go, 0)

    class Reduce:
        def __init__(self, y_order, own, sib_s, sib_r, x2, ra, rb, xp, xm, fm, fp, ys, yr, fin, ss, rs):
            self.own, self.sib_s, self.sib_r = own, sib_s, sib_r
            self.x2, self.ra, self.rb, self.xp, self.xm, self.fm, self.fp = x2, ra, rb, xp, xm, fm, fp
            self.ys, self.yr, self.fin, self.ss, self.rs = ys, yr, fin, ss, rs
            self.y_order = y_order
            self.x_order = (xf_, xp_, xm_, x)

        def go(self, src, dst, k, dev):
            send(src, dst, self.ss.at[k], self.rs.at[k], dev)

        def got(self, dst, k):
            arrive(dst, self.ss.at[k], self.rs.at[k])

        def slot(self, k, i):
            return self.y_order[i] * 4 + self.x_order[k]

        def to_sib(self, k, i):
            slot = self.slot(k, i)
            self.go(self.sib_s.at[slot], self.sib_r.at[slot], k * 2 + i, sib)

        def sib_got(self, k, i):
            if self.sib_r is not None:
                self.got(self.sib_r.at[self.slot(k, i)], k * 2 + i)

        def pair(self, k, i, h):
            slot, rows = self.slot(k, i), slice(h * 64, h * 64 + 64)
            value = self.own[slot, rows]
            return value if self.sib_r is None else value + self.sib_r[slot, rows].astype(F32)

        def far(self, i):
            self.sib_got(0, i)
            self.x2[i, 0:64] = self.pair(0, i, 0).astype(BF16)
            self.go(self.x2.at[i, pl.ds(0, 64)], self.ra.at[i], 8 + i, dev_xp)
            self.x2[i, 64:128] = self.pair(0, i, 1).astype(BF16)
            self.go(self.x2.at[i, pl.ds(64, 64)], self.rb.at[i], 10 + i, dev_xm)

        def near(self, i):
            self.sib_got(1, i)
            self.xp[i, 64:128] = self.pair(1, i, 1).astype(BF16)
            self.go(self.xp.at[i, pl.ds(64, 64)], self.fm.at[i, pl.ds(64, 64)], 12 + i, dev_xp)
            self.sib_got(2, i)
            self.xm[i, 0:64] = self.pair(2, i, 0).astype(BF16)
            self.go(self.xm.at[i, pl.ds(0, 64)], self.fp.at[i, pl.ds(0, 64)], 14 + i, dev_xm)

        def relay(self, i):
            self.got(self.ra.at[i], 8 + i)
            self.xp[i, 0:64] = (self.pair(1, i, 0) + self.ra[i].astype(F32)).astype(BF16)
            self.go(self.xp.at[i, pl.ds(0, 64)], self.fm.at[i, pl.ds(0, 64)], 16 + i, dev_xp)
            self.got(self.rb.at[i], 10 + i)
            self.xm[i, 64:128] = (self.pair(2, i, 1) + self.rb[i].astype(F32)).astype(BF16)
            self.go(self.xm.at[i, pl.ds(64, 64)], self.fp.at[i, pl.ds(64, 64)], 18 + i, dev_xm)

        def join(self, i, h):
            rows, at = slice(h * 64, h * 64 + 64), pl.ds(h * 64, 64)
            if h == 0:
                self.sib_got(3, i)
            self.got(self.fm.at[i, at], (16, 12)[h] + i)
            self.got(self.fp.at[i, at], (14, 18)[h] + i)
            return self.pair(3, i, h) + self.fm[i, rows].astype(F32) + self.fp[i, rows].astype(F32)

        def join_one(self, i):
            mine = self.y_order[i] == yh
            for h in range(2):
                rows = slice(h * 64, h * 64 + 64)
                value = self.join(i, h)

                @pl.when(mine)
                def _():
                    self.fin[rows] = value

                @pl.when(jnp.logical_not(mine))
                def _():
                    self.ys[rows] = value.astype(BF16)
                    self.to_opp(h).start()

        def to_opp(self, h):
            at = pl.ds(h * 64, 64)
            return copy(self.ys.at[at], self.yr.at[at], self.ss.at[20 + h], self.rs.at[20 + h], dev_yo)

        def join_other(self):
            for h in range(2):
                self.ys[h * 64:h * 64 + 64] = self.join(0, h).astype(BF16)
                self.to_opp(h).start()

        def join_mine(self):
            for h in range(2):
                self.fin[h * 64:h * 64 + 64] = self.join(1, h)

        def end(self):
            for h in range(2):
                self.to_opp(h).wait_send()

        def last(self, h):
            rows = slice(h * 64, h * 64 + 64)
            self.got(self.yr.at[pl.ds(h * 64, 64)], 20 + h)
            return self.fin[rows] + self.yr[rows].astype(F32)

    rt = Reduce((yl, 1 - yl), t_own, t_sib_s, t_sib_r, t_x2, t_ra, t_rb, t_xp, t_xm, t_fm, t_fp, t_ys, t_yr, t_fin, t_ss, t_rs)

    z_step(5)
    z_step(6)

    def products(core, y_):
        rows = tg[pl.ds(core * 4, 4)].reshape(4 * ROWS, 1024)
        return jnp.dot(rows, pj[y_], preferred_element_type=F32).reshape(4, ROWS, COLS)

    def t_wave(i):
        y_ = rt.y_order[i]
        t_sib_s[pl.ds(y_ * 4, 4)] = products(1 - c, y_).astype(BF16)
        for k in range(4):
            rt.to_sib(k, i)
        t_own[pl.ds(y_ * 4, 4)] = products(c, y_)

    l_pj.wait()
    t_wave(0)
    rt.far(0)
    rt.near(0)
    for k in range(4):
        arrive(pj.at[1 - yl, pl.ds(k * 256, 256)], p_ss.at[k], p_rs.at[k])
    t_wave(1)
    rt.relay(0)
    lax.fori_loop(1, BACK + 1, kv_mid, 0)
    rt.far(1)
    rt.near(1)

    lax.fori_loop(1, BACK + 1, kv_got, 0)
    keys = jnp.concatenate([kv_r[0, j] for j in range(BACK + 1)], axis=1)
    values = kv_r[1].reshape((BACK + 1) * ROWS, HEAD_DIM)

    def docs_back(j):
        at = (z + 8 - j) % 8
        return jnp.where(z >= j, docs_z[at], jnp.where(yl == 1, docs_o[at], -1))

    key_doc = jnp.concatenate([docs_back(j) for j in range(BACK + 1)], axis=1)
    row_doc = jnp.broadcast_to(docs[...].astype(F32), (ROWS, ROWS)).T[:, 0:1].astype(jnp.int32)
    wide = (ROWS, (BACK + 1) * ROWS)
    row_at = lax.broadcasted_iota(jnp.int32, wide, 0)
    key_at = lax.broadcasted_iota(jnp.int32, wide, 1)
    allowed = (key_doc == row_doc) & ((key_at >= ROWS) | (key_at <= row_at))
    for h in range(2):
        scores = jnp.dot(q_v[h], keys, preferred_element_type=F32)
        scores = jnp.where(allowed, scores, -1e30)
        probs = jnp.exp(scores - jnp.max(scores, axis=1, keepdims=True))
        total = jnp.sum(probs, axis=1, keepdims=True)
        acc = jnp.dot(probs.astype(BF16), values, preferred_element_type=F32)
        attn_v[c * 2 + h] = (acc / total).astype(BF16)
        send(attn_v.at[c * 2 + h], attn_v.at[c * 2 + h], x_ss.at[5 + h], x_rs.at[5 + h], sib)
        if h == 0:
            rt.relay(1)

    rt.join_one(0)
    lax.fori_loop(0, 8, wo_got, 0)

    ro = Reduce((yo_, yh), o_own, None, None, o_x2, o_ra, o_rb, o_xp, o_xm, o_fm, o_fp, o_ys, o_yr, o_fin, o_ss, o_rs)

    for h in range(2):
        arrive(attn_v.at[2 - 2 * c + h], x_ss.at[5 + h], x_rs.at[5 + h])
    attn = jnp.concatenate([attn_v[i] for i in range(4)], axis=1)

    def out_block(k, i):
        slot = ro.slot(k, i)
        o_own[slot] = jnp.dot(attn, wo[slot].reshape(COLS, COLS), preferred_element_type=F32)

    out_block(0, 0)
    ro.far(0)
    out_block(1, 0)
    out_block(2, 0)
    ro.near(0)
    out_block(0, 1)
    ro.relay(0)
    ro.far(1)
    rt.join_one(1)
    out_block(1, 1)
    out_block(2, 1)
    ro.near(1)
    out_block(3, 0)
    out_block(3, 1)
    ro.relay(1)

    def t3(h):
        at = pl.ds(h * 64, 64)
        return copy(t3_s.at[at], t3_r.at[at], t3_ss.at[h], t3_rs.at[h], dev_t3)

    ro.join_other()
    for h in range(2):
        rows = slice(h * 64, h * 64 + 64)
        t3_s[rows] = rt.last(h).astype(BF16)

        @pl.when(stays)
        def _():
            t3_r[rows] = t3_s[rows]

        @pl.when(jnp.logical_not(stays))
        def _():
            t3(h).start()

    ro.join_mine()

    dg = Gather(db, dg_ss, dg_rs)
    for h in range(2):
        rows = slice(h * 64, h * 64 + 64)
        mixed = hb[mine, rows].astype(F32) + ro.last(h)
        out_s[rows] = mixed.astype(BF16)

        @pl.when(jnp.logical_not(stays))
        def _():
            arrive(t3_r.at[pl.ds(h * 64, 64)], t3_ss.at[h], t3_rs.at[h])

        target = t3_r[rows].astype(F32) * jnp.concatenate([ts_v[rows]] * 4, axis=1)
        difference = mixed - target
        db[mine, rows] = difference.astype(BF16)
        dg.begin(h)
        squares = difference * difference
        l_v[rows] = (
            squares[:, 0:128] + squares[:, 128:256] + squares[:, 256:384] + squares[:, 384:512]
        )
    l_s[...] = jnp.sum(l_v[...].T, axis=0, keepdims=True)
    l_r[t] = l_s[...]

    def loss(k):
        return copy(l_s, l_r.at[t], l_ss.at[k], l_rs.at[k], (s, (t + k) % 16))

    def loss_go(k, carry):
        loss(k).start()
        return carry

    def loss_got(k, carry):
        arrive(l_r.at[(t + 16 - k) % 16], l_ss.at[k], l_rs.at[k])
        return carry

    def loss_end(k, carry):
        loss(k).wait_send()
        return carry

    lax.fori_loop(1, 16, loss_go, 0)

    def add_grad(slots, first=False):
        d = jnp.concatenate([db[slot] for slot in slots], axis=1)
        for core in range(2):
            w = jnp.concatenate([wo[slot, core] for slot in slots], axis=1)
            g = nt_dot(d, w)
            g_acc[core] = g if first else g_acc[core] + g

    dg.near_relay()
    dg.opp_half(0)
    dg.near_rest()
    add_grad([mine] + dg.near, True)
    dg.opp_half(1)
    dg.onear_a()
    dg.far_step()
    add_grad([dg.opp, dg.far[0]])
    dg.onear_b()
    dg.onear_rest()
    add_grad(dg.onear)
    lax.fori_loop(1, 16, loss_got, 0)
    loss_sum = l_r[0]
    for i in range(1, 16):
        loss_sum = loss_sum + l_r[i]
    out_l[...] = loss_sum / DS
    dg.ofar_step()
    add_grad([dg.far[1]])
    send(g_acc.at[1 - c], g_in, x_ss.at[7], x_rs.at[7], sib)
    arrive(g_in, x_ss.at[7], x_rs.at[7])
    out_g[...] = (g_acc[c] + g_in[...]).astype(BF16)

    for one in started:
        one.wait_send()
    lax.fori_loop(0, 8, wo_end, 0)
    lax.fori_loop(1, 16, kvx_end, 0)
    lax.fori_loop(1, BACK + 1, kv_end, 0)
    lax.fori_loop(1, 16, loss_end, 0)

    rt.end()
    ro.end()

    @pl.when(jnp.logical_not(stays))
    def _():
        t3(0).wait_send()
        t3(1).wait_send()


def reduce_buffers():
    block = (ROWS, COLS)
    return [
        pltpu.VMEM((2, 64, COLS), BF16),
        pltpu.VMEM((2, 64, COLS), BF16),
        pltpu.VMEM((2,) + block, BF16),
        pltpu.VMEM((2,) + block, BF16),
        pltpu.VMEM((2,) + block, BF16),
        pltpu.VMEM((2,) + block, BF16),
        pltpu.VMEM(block, BF16),
        pltpu.VMEM(block, BF16),
        pltpu.VMEM(block, F32),
    ]


def on_device(
    teacher_hidden, teacher_gain, projector, student_hidden, student_gain,
    query_weight, kv_weight, out_weight, doc_ids,
):
    block = (ROWS, COLS)
    hbm = pl.BlockSpec(memory_space=pltpu.HBM)
    vmem = pl.BlockSpec(memory_space=pltpu.VMEM)
    dma = pltpu.SemaphoreType.DMA
    out_s, out_l, out_g = pl.pallas_call(
        body,
        out_shape=(
            jax.ShapeDtypeStruct(block, BF16),
            jax.ShapeDtypeStruct((1, ROWS), F32),
            jax.ShapeDtypeStruct((ROWS, 256), BF16),
        ),
        in_specs=[hbm] * 9,
        out_specs=(vmem, vmem, vmem),
        scratch_shapes=[
            pltpu.VMEM((1, 1024), F32),
            pltpu.VMEM((1, COLS), F32),
            pltpu.VMEM((1, ROWS), jnp.int32),
            pltpu.VMEM((ROWS, 1024), BF16),
            pltpu.VMEM((8, ROWS, 1024), BF16),
            pltpu.VMEM((2, 1024, COLS), BF16),
            pltpu.VMEM((8, 2, COLS, 256), BF16),
            pltpu.VMEM((2, 2, 32, DS), BF16),
            pltpu.VMEM((8, 2, 256, COLS), BF16),
            pltpu.VMEM((64, ROWS), F32),
            pltpu.VMEM((64, ROWS), F32),
            pltpu.VMEM((8,) + block, BF16),
            pltpu.VMEM((1, 768), F32),
            pltpu.VMEM((8, 1, 768), F32),
            pltpu.VMEM((1, 256), F32),
            pltpu.VMEM((1, 256), F32),
            pltpu.VMEM((ROWS, 128), F32),
            pltpu.VMEM((2, ROWS, 256), F32),
            pltpu.VMEM((ROWS, 256), F32),
            pltpu.VMEM((2, 64, ROWS), F32),
            pltpu.VMEM((64, ROWS), F32),
            pltpu.VMEM((4, 16, ROWS), BF16),
            pltpu.VMEM((16, 16, ROWS), BF16),
            pltpu.VMEM((2, ROWS, HEAD_DIM), BF16),
            pltpu.VMEM((2, BACK + 1, ROWS, HEAD_DIM), BF16),
            pltpu.VMEM((8, 1, ROWS), jnp.int32),
            pltpu.VMEM((8, 1, ROWS), jnp.int32),
            pltpu.VMEM((2, ROWS, HEAD_DIM), BF16),
            pltpu.VMEM((4, ROWS, HEAD_DIM), BF16),
            pltpu.VMEM((8,) + block, F32),
            pltpu.VMEM((8,) + block, F32),
            pltpu.VMEM((2,) + block, BF16),
            pltpu.VMEM((8,) + block, BF16),
            pltpu.VMEM((8,) + block, BF16),
            pltpu.VMEM((2,) + block, BF16),
            *reduce_buffers(),
            *reduce_buffers(),
            pltpu.VMEM(block, BF16),
            pltpu.VMEM(block, BF16),
            pltpu.VMEM((ROWS, 128), F32),
            pltpu.VMEM((8,) + block, BF16),
            pltpu.VMEM((2, ROWS, 256), F32),
            pltpu.VMEM((ROWS, 256), F32),
            pltpu.VMEM((ROWS, 128), F32),
            pltpu.VMEM((1, ROWS), F32),
            pltpu.VMEM((16, 1, ROWS), F32),
            dma((10,)),
            dma((8,)), dma((8,)), dma((8,)), dma((8,)), dma((8,)),
            dma((16,)), dma((16,)), dma((4,)), dma((4,)),
            dma((24,)), dma((24,)), dma((24,)), dma((24,)),
            dma((16,)), dma((16,)), dma((16,)), dma((16,)),
            dma((9,)), dma((9,)), dma((9,)), dma((9,)), dma((9,)), dma((9,)),
            dma((24,)), dma((24,)), dma((24,)), dma((24,)),
            dma((2,)), dma((2,)),
            dma((16,)), dma((16,)),
        ],
        compiler_params=pltpu.CompilerParams(
            collective_id=0, has_side_effects=True, vmem_limit_bytes=40 * 1024 * 1024
        ),
    )(
        *(
            pltpu.with_memory_space_constraint(one, pltpu.HBM)
            for one in (
                teacher_hidden, teacher_gain.reshape(1, -1), projector, student_hidden,
                student_gain.reshape(1, -1), query_weight.reshape(8, 2, COLS, 256), jnp.transpose(kv_weight, (0, 2, 1)),
                out_weight, doc_ids.reshape(1, -1),
            )
        )
    )
    return out_s, out_l.reshape(ROWS), out_g


def solution(mesh):
    in_specs = (
        P("seq", "tensor"),
        P("tensor"),
        P("tensor", "seq"),
        P("seq", "tensor"),
        P("tensor"),
        P(None, "tensor"),
        P(None, None, "tensor"),
        P("tensor", None),
        P("seq"),
    )
    out_specs = (P("seq", "tensor"), P("seq"), P("seq", "tensor"))
    return jax.shard_map(
        on_device, mesh=mesh, in_specs=in_specs, out_specs=out_specs, check_vma=False
    )
```

```python
import math

import jax
import jax.numpy as jnp
from jax import lax
from jax.experimental import pallas as pl
from jax.experimental.pallas import tpu as pltpu
from jax.sharding import PartitionSpec as P

DT = 16384
DS = 8192
HEAD_DIM = 128
HEADS = 32
KV_HEADS = 4
ROWS = 128
COLS = 512
BACK = 8
F32 = jnp.float32
BF16 = jnp.bfloat16
MESH = pl.DeviceIdType.MESH
NT = (((1,), (1,)), ((), ()))


def nt_dot(a, b):
    return lax.dot_general(a, b, NT, preferred_element_type=F32)


def body(
    th_h, tgain_h, pj_h, sh_h, sgain_h, wq_h, wkv_h, wo_h, docs_h,
    out_s, out_l, out_g,
    tgain, sgain, docs, th_v, tg, pj, wq, wkv, wo, cos_t, sin_t,
    hb, sg_s, sg_r, sum_s, sum_r, scale_v, q_acc, q_in, kv_acc, kv_in,
    kvx_s, kvx_r, kv_own, kv_r, docs_z, docs_o, q_v, attn_v,
    t_own, t_part, o_own, o_x2, t_sib_s, t_sib_r, t_x2, t_ra, t_rb, t_xp, t_xm, t_fm, t_fp, t_ys, t_yr, t_fin,
    o_ra, o_rb, o_xp, o_xm, o_fm, o_fp, o_ys, o_yr, o_fin,
    t3_s, t3_r, ts_v, db, g_acc, g_in, l_v, l_s, l_r,
    load_sem, w_load, w_ss, w_rs, x_ss, x_rs, z_ss, z_rs, p_ss, p_rs,
    ag_ss, ag_rs, dg_ss, dg_rs, sm_ss, sm_rs, kx_ss, kx_rs, kv_ss, kv_rs, kf_ss, kf_rs, dc_ss, dc_rs,
    t_ss, t_rs, o_ss, o_rs, t3_ss, t3_rs, l_ss, l_rs,
):
    s = lax.axis_index("seq")
    t = lax.axis_index("tensor")
    yl, z = s // 8, s % 8
    yh, x, c = t // 8, (t // 2) % 4, t % 2

    def tid(y_, x_, c_):
        return y_ * 8 + x_ * 2 + c_

    xp_, xm_ = (x + 1) % 4, (x + 3) % 4
    xf_ = (x + 2) % 4
    yo_ = 1 - yh
    sib = (s, tid(yh, x, 1 - c))
    dev_xp = (s, tid(yh, xp_, c))
    dev_xm = (s, tid(yh, xm_, c))
    dev_yo = (s, tid(yo_, x, c))
    dev_zp = (yl * 8 + (z + 1) % 8, t)
    dev_zm = (yl * 8 + (z + 7) % 8, t)
    dev_yl = ((1 - yl) * 8 + z, t)
    turn = jnp.where(c == 0, x, jnp.where(x == 0, 4, 8 - x))
    dev_t3 = (yl * 8 + (z + turn) % 8, yh * 8 + z)
    stays = (z == 0) & (x == 0) & (c == 0)

    started = []

    def copy(src, dst, ss, rs, dev):
        return pltpu.make_async_remote_copy(
            src_ref=src, dst_ref=dst, send_sem=ss, recv_sem=rs, device_id=dev, device_id_type=MESH
        )

    def send(src, dst, ss, rs, dev):
        one = copy(src, dst, ss, rs, dev)
        one.start()
        started.append(one)

    def arrive(dst, ss, rs):
        copy(dst, dst, ss, rs, sib).wait_recv()

    def load(src, dst, k):
        one = pltpu.make_async_copy(src, dst, load_sem.at[k])
        one.start()
        return one

    l_th = load(th_h, th_v, 0)
    mine = yh * 4 + x
    l_sh = load(sh_h, hb.at[mine], 1)
    l_small = [load(tgain_h, tgain, 7), load(sgain_h, sgain, 8), load(docs_h, docs, 9)]
    l_wkv = load(wkv_h, wkv.at[c], 2)
    l_wq = load(wq_h.at[:, c], wq.at[:, c], 3)
    l_pj = load(pj_h, pj.at[yl], 4)

    def wo_part(j, core):
        return wo_h.at[:, pl.ds(pl.multiple_of((j * 2 + core) * COLS, COLS), COLS)]

    def wo_load(j):
        return pltpu.make_async_copy(wo_part(j, c), wo.at[j, c], w_load.at[j])

    def wo_send(j):
        return copy(wo_part(j, 1 - c), wo.at[j, c], w_ss.at[j], w_rs.at[j], sib)

    def wo_go(j, carry):
        wo_load(j).start()
        wo_send(j).start()
        return carry

    def wo_got(j, carry):
        wo_load(j).wait()
        arrive(wo.at[j, 1 - c], w_ss.at[j], w_rs.at[j])
        return carry

    def wo_end(j, carry):
        wo_send(j).wait_send()
        return carry

    kv_r[1] = jnp.zeros((BACK + 1, ROWS, HEAD_DIM), BF16)

    barrier = pltpu.get_barrier_semaphore()
    for dev in (sib, dev_xp, dev_xm, dev_yo, dev_zp, dev_zm, dev_yl):
        pl.semaphore_signal(barrier, inc=1, device_id=dev, device_id_type=MESH)

    class Gather:
        def __init__(self, buf, ss, rs):
            self.buf, self.ss, self.rs = buf, ss, rs
            self.near = [yh * 4 + xm_, yh * 4 + xp_]
            self.opp = yo_ * 4 + x
            self.onear = [yo_ * 4 + xm_, yo_ * 4 + xp_]
            self.far = [yh * 4 + xf_, yo_ * 4 + xf_]
            self.order = [mine] + self.near + [self.opp] + self.onear + self.far

        def part(self, slot, h):
            return self.buf.at[slot, pl.ds(h * 64, 64)]

        def half(self, slot, h, k, dev):
            part = self.part(slot, h)
            send(part, part, self.ss.at[k], self.rs.at[k], dev)

        def got_half(self, slot, h, k):
            arrive(self.part(slot, h), self.ss.at[k], self.rs.at[k])

        def begin(self, h):
            self.half(mine, h, 0 + h, dev_yo)
            self.half(mine, h, 2 + h, dev_xp)
            self.half(mine, h, 4 + h, dev_xm)

        def near_relay(self):
            self.got_half(self.near[0], 0, 2)
            self.half(self.near[0], 0, 6, dev_xp)
            self.got_half(self.near[1], 1, 5)
            self.half(self.near[1], 1, 7, dev_xm)

        def near_rest(self):
            self.got_half(self.near[0], 1, 3)
            self.got_half(self.near[1], 0, 4)

        def opp_half(self, h):
            self.got_half(self.opp, h, 0 + h)
            self.half(self.opp, h, 8 + h, dev_xp)
            self.half(self.opp, h, 10 + h, dev_xm)

        def onear_a(self):
            self.got_half(self.onear[0], 0, 8)
            self.half(self.onear[0], 0, 12, dev_xp)

        def onear_b(self):
            self.got_half(self.onear[1], 1, 11)
            self.half(self.onear[1], 1, 13, dev_xm)

        def onear_rest(self):
            self.got_half(self.onear[0], 1, 9)
            self.got_half(self.onear[1], 0, 10)

        def far_step(self):
            self.got_half(self.far[0], 0, 6)
            self.got_half(self.far[0], 1, 7)

        def ofar_step(self):
            self.got_half(self.far[1], 0, 12)
            self.got_half(self.far[1], 1, 13)

    z_slot = 0
    l_th.wait()
    for one in l_small:
        one.wait()
    docs_z[z] = docs[...]
    part = jnp.zeros((ROWS, 128), F32)
    for i in range(8):
        cols = slice(i * 128, (i + 1) * 128)
        f = th_v[:, cols].astype(F32)
        part = part + f * f
        tg[z_slot, :, cols] = (f * tgain[:, cols]).astype(BF16)
    sg_s[:, COLS:COLS + 128] = jnp.sum(part.T, axis=0, keepdims=True)
    l_sh.wait()
    part = jnp.zeros((ROWS, 128), F32)
    for i in range(4):
        f = hb[mine, :, i * 128:(i + 1) * 128].astype(F32)
        part = part + f * f
    sg_s[:, COLS + 128:COLS + 256] = jnp.sum(part.T, axis=0, keepdims=True)
    sg_s[:, 0:COLS] = sgain[...]
    sg_r[mine] = sg_s[...]

    pl.semaphore_wait(barrier, 7)

    ag = Gather(hb, ag_ss, ag_rs)

    def ring_slot(d):
        return (0, 1, 2, 3, 4, 7, 6, 5)[d % 8]

    def z_ref(d, h):
        return tg.at[ring_slot(d), pl.ds(h * 64, 64)]

    def z_send(k):
        d = k // 2
        send(z_ref(8 - d, k % 2), z_ref(7 - d, k % 2), z_ss.at[k], z_rs.at[k], dev_zp)
        send(z_ref(d, 1 - k % 2), z_ref(d + 1, 1 - k % 2), z_ss.at[8 + k], z_rs.at[8 + k], dev_zm)

    def z_got(k):
        up, down = z_ref(-(k // 2) + 7, k % 2), z_ref(k // 2 + 1, 1 - k % 2)
        arrive(up, z_ss.at[k], z_rs.at[k])
        arrive(down, z_ss.at[8 + k], z_rs.at[8 + k])

    def z_step(k):
        z_got(k)
        if k + 2 < 7:
            z_send(k + 2)

    def pj_send(k):
        rows = pl.ds(k * 256, 256)
        send(pj_h.at[rows], pj.at[yl, rows], p_ss.at[k], p_rs.at[k], dev_yl)


    def small_send(i, k, dev):
        slot = ag.order[i]
        send(sg_r.at[slot], sg_r.at[slot], sm_ss.at[k], sm_rs.at[k], dev)

    def small_got(i, k):
        arrive(sg_r.at[ag.order[i]], sm_ss.at[k], sm_rs.at[k])

    def docs_send(d, k, dev):
        ref = docs_z.at[(z + d) % 8]
        send(ref, ref, dc_ss.at[k], dc_rs.at[k], dev)

    def docs_step(k):
        arrive(docs_z.at[(z + 7 - k) % 8], dc_ss.at[k], dc_rs.at[k])
        if k < 3:
            arrive(docs_z.at[(z + 1 + k) % 8], dc_ss.at[4 + k], dc_rs.at[4 + k])
            docs_send(7 - k, k + 1, dev_zp)
            if k < 2:
                docs_send(1 + k, k + 5, dev_zm)
        else:
            send(docs_z, docs_o, dc_ss.at[8], dc_rs.at[8], dev_yl)

    small_send(0, 0, dev_yo)
    small_send(0, 1, dev_xp)
    small_send(0, 2, dev_xm)
    ag.begin(0)
    ag.begin(1)
    send(wkv_h, wkv.at[c], x_ss.at[0], x_rs.at[0], sib)
    send(wq_h.at[:, 1 - c], wq.at[:, c], x_ss.at[1], x_rs.at[1], sib)
    docs_send(0, 0, dev_zp)
    docs_send(0, 4, dev_zm)
    z_send(0)
    pj_send(0)
    z_send(1)
    pj_send(1)
    pj_send(2)

    entry = lax.broadcasted_iota(jnp.int32, (64, ROWS), 0).astype(F32)
    position = (s * ROWS + lax.broadcasted_iota(jnp.int32, (64, ROWS), 1)).astype(F32)
    angle = position * jnp.exp(-math.log(500000.0) * (2.0 * entry / HEAD_DIM))
    cos_t[...] = jnp.cos(angle)
    sin_t[...] = jnp.sin(angle)

    def process(slots, first=False):
        blocks = []
        for slot in slots:
            parts = []
            for i in range(4):
                cols = slice(i * 128, (i + 1) * 128)
                f = hb[slot, :, cols].astype(F32)
                parts.append((f * scale_v[...] * sg_r[slot][:, cols]).astype(BF16))
            blocks.append(jnp.concatenate(parts, axis=1))
        n = jnp.concatenate(blocks, axis=1)
        w = []
        for slot in slots:
            at = pl.multiple_of((slot * 2 + c) * COLS, COLS)
            w.append(wkv[:, :, :, pl.ds(at, COLS)].reshape(128, COLS))
        kv = nt_dot(jnp.concatenate(w, axis=1), n)
        for core in range(2):
            w = jnp.concatenate([wq[slot, core] for slot in slots], axis=0)
            q = jnp.dot(n, w, preferred_element_type=F32)
            k = kv[core * 64:core * 64 + 64]
            q_acc[core] = q if first else q_acc[core] + q
            kv_acc[core] = k if first else kv_acc[core] + k

    small_got(1, 1)
    small_send(1, 3, dev_xp)
    small_got(2, 2)
    small_got(3, 0)
    small_send(3, 4, dev_xp)
    small_send(3, 5, dev_xm)
    docs_step(0)
    ag.near_relay()
    small_got(6, 3)
    docs_step(1)
    small_got(4, 4)
    small_send(4, 6, dev_xp)
    small_got(5, 5)
    ag.near_rest()
    ag.opp_half(0)
    z_step(0)
    pj_send(3)
    small_got(7, 6)
    sums = sg_r[0][:, COLS:COLS + 256]
    for i in range(1, 8):
        sums = sums + sg_r[i][:, COLS:COLS + 256]
    sum_s[...] = sums
    send(sum_s, sum_r, x_ss.at[2], x_rs.at[2], sib)
    docs_step(2)
    ag.opp_half(1)
    arrive(sum_r, x_ss.at[2], x_rs.at[2])
    sums = sum_s[...] + sum_r[...]
    ts_v[...] = jnp.broadcast_to(lax.rsqrt(sums[:, 0:128] / DT + 1e-05), (ROWS, 128)).T
    scale_v[...] = jnp.broadcast_to(lax.rsqrt(sums[:, 128:256] / DS + 1e-05), (ROWS, 128)).T
    docs_step(3)
    z_step(1)
    ag.onear_a()
    l_wkv.wait()
    l_wq.wait()
    arrive(wkv.at[1 - c], x_ss.at[0], x_rs.at[0])
    arrive(wq.at[:, 1 - c], x_ss.at[1], x_rs.at[1])
    process([mine] + ag.near, True)
    ag.onear_b()
    z_step(2)
    ag.far_step()
    process([ag.opp, ag.far[0]])
    ag.onear_rest()
    process(ag.onear)
    z_step(3)
    ag.ofar_step()
    process([ag.far[1]])
    send(kv_acc.at[1 - c], kv_in, x_ss.at[3], x_rs.at[3], sib)
    send(q_acc.at[1 - c], q_in, x_ss.at[4], x_rs.at[4], sib)
    lax.fori_loop(0, 8, wo_go, 0)
    arrive(kv_in, x_ss.at[3], x_rs.at[3])

    row = lax.broadcasted_iota(jnp.int32, (64, 64), 0)
    col = lax.broadcasted_iota(jnp.int32, (64, 64), 1)
    take = ((row >> 3) & 1) * 32 + (row & 7) * 4 + (row >> 4)
    pick = jnp.where(col == take, 1.0, 0.0).astype(BF16)
    kv_mine = (kv_acc[c] + kv_in[...]).astype(BF16)
    kvx_s[...] = jnp.dot(pick, kv_mine, preferred_element_type=F32).astype(BF16).reshape(4, 16, 128)
    kvx_r[t] = kvx_s[t // 4]

    def kvx(k):
        to = (t + k) % 16
        return copy(kvx_s.at[to // 4], kvx_r.at[t], kx_ss.at[k], kx_rs.at[k], (s, to))

    def kvx_go(k, carry):
        kvx(k).start()
        return carry

    def kvx_got(k, carry):
        arrive(kvx_r.at[(t + 16 - k) % 16], kx_ss.at[k], kx_rs.at[k])
        return carry

    def kvx_end(k, carry):
        kvx(k).wait_send()
        return carry

    lax.fori_loop(1, 16, kvx_go, 0)
    z_step(4)

    cos2 = jnp.concatenate([cos_t[...], cos_t[...]], axis=0).T
    sin2 = jnp.concatenate([-sin_t[...], sin_t[...]], axis=0).T
    arrive(q_in, x_ss.at[4], x_rs.at[4])
    q_mine = q_acc[c] + q_in[...]
    for h in range(2):
        qh = q_mine[:, h * 128:(h + 1) * 128]
        turned = qh * cos2 + pltpu.roll(qh, 64, 1) * sin2
        q_v[h] = (turned * HEAD_DIM ** (-0.5)).astype(BF16)

    lax.fori_loop(1, 16, kvx_got, 0)
    both = kvx_r[...].astype(F32).reshape(16, 2, 8, ROWS)
    k_raw = both[:, 0].reshape(HEAD_DIM, ROWS)
    v_raw = both[:, 1].reshape(HEAD_DIM, ROWS)
    first, second = k_raw[0:64], k_raw[64:128]
    k_rot = jnp.concatenate(
        [first * cos_t[...] - second * sin_t[...], second * cos_t[...] + first * sin_t[...]], axis=0
    )
    kv_own[0] = k_rot.astype(BF16)
    kv_own[1] = v_raw.T.astype(BF16)
    kv_r[0, 0] = kv_own[0]
    kv_r[1, 0] = kv_own[1]

    def kv_copy(k):
        return copy(kv_own.at[c], kv_r.at[c, k], kv_ss.at[k], kv_rs.at[k], ((s + k) % 16, t))

    def kv_fwd(k):
        return copy(kv_r.at[c, k], kv_r.at[c, k], kf_ss.at[k], kf_rs.at[k], sib)

    def kv_go(k, carry):
        @pl.when(s + k < 16)
        def _():
            kv_copy(k).start()
        return carry

    def kv_mid(k, carry):
        @pl.when(s >= k)
        def _():
            arrive(kv_r.at[c, k], kv_ss.at[k], kv_rs.at[k])
            kv_fwd(k).start()
        return carry

    def kv_got(k, carry):
        @pl.when(s >= k)
        def _():
            arrive(kv_r.at[1 - c, k], kf_ss.at[k], kf_rs.at[k])
        return carry

    def kv_end(k, carry):
        @pl.when(s >= k)
        def _():
            kv_fwd(k).wait_send()

        @pl.when(s + k < 16)
        def _():
            kv_copy(k).wait_send()
        return carry

    arrive(docs_o, dc_ss.at[8], dc_rs.at[8])
    lax.fori_loop(1, BACK + 1, kv_go, 0)

    class Reduce:
        def __init__(self, y_order, own, sib_s, sib_r, x2, ra, rb, xp, xm, fm, fp, ys, yr, fin, ss, rs):
            self.own, self.sib_s, self.sib_r = own, sib_s, sib_r
            self.x2, self.ra, self.rb, self.xp, self.xm, self.fm, self.fp = x2, ra, rb, xp, xm, fm, fp
            self.ys, self.yr, self.fin, self.ss, self.rs = ys, yr, fin, ss, rs
            self.y_order = y_order
            self.x_order = (xf_, xp_, xm_, x)

        def go(self, src, dst, k, dev):
            send(src, dst, self.ss.at[k], self.rs.at[k], dev)

        def got(self, dst, k):
            arrive(dst, self.ss.at[k], self.rs.at[k])

        def slot(self, k, i):
            return self.y_order[i] * 4 + self.x_order[k]

        def to_sib(self, k, i):
            slot = self.slot(k, i)
            self.go(self.sib_s.at[slot], self.sib_r.at[slot], k * 2 + i, sib)

        def sib_got(self, k, i):
            if self.sib_r is not None:
                self.got(self.sib_r.at[self.slot(k, i)], k * 2 + i)

        def pair(self, k, i, h):
            slot, rows = self.slot(k, i), slice(h * 64, h * 64 + 64)
            value = self.own[slot, rows]
            return value if self.sib_r is None else value + self.sib_r[slot, rows].astype(F32)

        def far(self, i):
            self.sib_got(0, i)
            self.x2[i, 0:64] = self.pair(0, i, 0).astype(BF16)
            self.go(self.x2.at[i, pl.ds(0, 64)], self.ra.at[i], 8 + i, dev_xp)
            self.x2[i, 64:128] = self.pair(0, i, 1).astype(BF16)
            self.go(self.x2.at[i, pl.ds(64, 64)], self.rb.at[i], 10 + i, dev_xm)

        def near(self, i):
            self.sib_got(1, i)
            self.xp[i, 64:128] = self.pair(1, i, 1).astype(BF16)
            self.go(self.xp.at[i, pl.ds(64, 64)], self.fm.at[i, pl.ds(64, 64)], 12 + i, dev_xp)
            self.sib_got(2, i)
            self.xm[i, 0:64] = self.pair(2, i, 0).astype(BF16)
            self.go(self.xm.at[i, pl.ds(0, 64)], self.fp.at[i, pl.ds(0, 64)], 14 + i, dev_xm)

        def relay(self, i):
            self.got(self.ra.at[i], 8 + i)
            self.xp[i, 0:64] = (self.pair(1, i, 0) + self.ra[i].astype(F32)).astype(BF16)
            self.go(self.xp.at[i, pl.ds(0, 64)], self.fm.at[i, pl.ds(0, 64)], 16 + i, dev_xp)
            self.got(self.rb.at[i], 10 + i)
            self.xm[i, 64:128] = (self.pair(2, i, 1) + self.rb[i].astype(F32)).astype(BF16)
            self.go(self.xm.at[i, pl.ds(64, 64)], self.fp.at[i, pl.ds(64, 64)], 18 + i, dev_xm)

        def join(self, i, h):
            rows, at = slice(h * 64, h * 64 + 64), pl.ds(h * 64, 64)
            if h == 0:
                self.sib_got(3, i)
            self.got(self.fm.at[i, at], (16, 12)[h] + i)
            self.got(self.fp.at[i, at], (14, 18)[h] + i)
            return self.pair(3, i, h) + self.fm[i, rows].astype(F32) + self.fp[i, rows].astype(F32)

        def join_one(self, i):
            mine = self.y_order[i] == yh
            for h in range(2):
                rows = slice(h * 64, h * 64 + 64)
                value = self.join(i, h)

                @pl.when(mine)
                def _():
                    self.fin[rows] = value

                @pl.when(jnp.logical_not(mine))
                def _():
                    self.ys[rows] = value.astype(BF16)
                    self.to_opp(h).start()

        def to_opp(self, h):
            at = pl.ds(h * 64, 64)
            return copy(self.ys.at[at], self.yr.at[at], self.ss.at[20 + h], self.rs.at[20 + h], dev_yo)

        def join_other(self):
            for h in range(2):
                self.ys[h * 64:h * 64 + 64] = self.join(0, h).astype(BF16)
                self.to_opp(h).start()

        def join_mine(self):
            for h in range(2):
                self.fin[h * 64:h * 64 + 64] = self.join(1, h)

        def end(self):
            for h in range(2):
                self.to_opp(h).wait_send()

        def last(self, h):
            rows = slice(h * 64, h * 64 + 64)
            self.got(self.yr.at[pl.ds(h * 64, 64)], 20 + h)
            return self.fin[rows] + self.yr[rows].astype(F32)

    rt = Reduce((yl, 1 - yl), t_own, t_sib_s, t_sib_r, t_x2, t_ra, t_rb, t_xp, t_xm, t_fm, t_fp, t_ys, t_yr, t_fin, t_ss, t_rs)

    z_step(5)
    z_step(6)

    def products(core, y_, k, width):
        rows = tg[pl.ds(core * 4, 4), :, k * width:(k + 1) * width].reshape(4 * ROWS, width)
        return jnp.dot(rows, pj[y_, k * width:(k + 1) * width], preferred_element_type=F32).reshape(4, ROWS, COLS)

    l_pj.wait()
    first = pl.ds(yl * 4, 4)
    t_sib_s[first] = products(1 - c, yl, 0, 1024).astype(BF16)
    for k in range(4):
        rt.to_sib(k, 0)
    t_own[first] = products(c, yl, 0, 1024)
    rt.far(0)
    rt.near(0)

    other = pl.ds((1 - yl) * 4, 4)
    for k in range(4):
        arrive(pj.at[1 - yl, pl.ds(k * 256, 256)], p_ss.at[k], p_rs.at[k])
        theirs = products(1 - c, 1 - yl, k, 256)
        if k == 0:
            t_part[...] = theirs
        elif k < 3:
            t_part[...] += theirs
        else:
            t_sib_s[other] = (t_part[...] + theirs).astype(BF16)
            for j in range(4):
                rt.to_sib(j, 1)
        if k == 0:
            t_own[other] = products(c, 1 - yl, k, 256)
        else:
            t_own[other] += products(c, 1 - yl, k, 256)
        if k == 1:
            rt.relay(0)
    rt.far(1)
    rt.near(1)
    rt.join_one(0)
    lax.fori_loop(1, BACK + 1, kv_mid, 0)
    rt.relay(1)

    lax.fori_loop(1, BACK + 1, kv_got, 0)
    keys = jnp.concatenate([kv_r[0, j] for j in range(BACK + 1)], axis=1)
    values = kv_r[1].reshape((BACK + 1) * ROWS, HEAD_DIM)

    def docs_back(j):
        at = (z + 8 - j) % 8
        return jnp.where(z >= j, docs_z[at], jnp.where(yl == 1, docs_o[at], -1))

    key_doc = jnp.concatenate([docs_back(j) for j in range(BACK + 1)], axis=1)
    row_doc = jnp.broadcast_to(docs[...].astype(F32), (ROWS, ROWS)).T[:, 0:1].astype(jnp.int32)
    wide = (ROWS, (BACK + 1) * ROWS)
    row_at = lax.broadcasted_iota(jnp.int32, wide, 0)
    key_at = lax.broadcasted_iota(jnp.int32, wide, 1)
    allowed = (key_doc == row_doc) & ((key_at >= ROWS) | (key_at <= row_at))
    for h in range(2):
        scores = jnp.dot(q_v[h], keys, preferred_element_type=F32)
        scores = jnp.where(allowed, scores, -1e30)
        probs = jnp.exp(scores - jnp.max(scores, axis=1, keepdims=True))
        total = jnp.sum(probs, axis=1, keepdims=True)
        acc = jnp.dot(probs.astype(BF16), values, preferred_element_type=F32)
        attn_v[c * 2 + h] = (acc / total).astype(BF16)
        send(attn_v.at[c * 2 + h], attn_v.at[c * 2 + h], x_ss.at[5 + h], x_rs.at[5 + h], sib)
    lax.fori_loop(0, 8, wo_got, 0)

    ro = Reduce((yo_, yh), o_own, None, None, o_x2, o_ra, o_rb, o_xp, o_xm, o_fm, o_fp, o_ys, o_yr, o_fin, o_ss, o_rs)

    for h in range(2):
        arrive(attn_v.at[2 - 2 * c + h], x_ss.at[5 + h], x_rs.at[5 + h])
    attn = jnp.concatenate([attn_v[i] for i in range(4)], axis=1)

    def out_block(k, i):
        slot = ro.slot(k, i)
        o_own[slot] = jnp.dot(attn, wo[slot].reshape(COLS, COLS), preferred_element_type=F32)

    out_block(0, 0)
    ro.far(0)
    out_block(1, 0)
    out_block(2, 0)
    ro.near(0)
    rt.join_one(1)
    out_block(0, 1)
    ro.relay(0)
    ro.far(1)
    out_block(1, 1)
    out_block(2, 1)
    ro.near(1)
    out_block(3, 0)
    out_block(3, 1)
    ro.relay(1)

    def t3(h):
        at = pl.ds(h * 64, 64)
        return copy(t3_s.at[at], t3_r.at[at], t3_ss.at[h], t3_rs.at[h], dev_t3)

    for h in range(2):
        rows = slice(h * 64, h * 64 + 64)
        t3_s[rows] = rt.last(h).astype(BF16)

        @pl.when(stays)
        def _():
            t3_r[rows] = t3_s[rows]

        @pl.when(jnp.logical_not(stays))
        def _():
            t3(h).start()

    ro.join_other()
    ro.join_mine()

    dg = Gather(db, dg_ss, dg_rs)
    for h in range(2):
        rows = slice(h * 64, h * 64 + 64)
        mixed = hb[mine, rows].astype(F32) + ro.last(h)
        out_s[rows] = mixed.astype(BF16)

        @pl.when(jnp.logical_not(stays))
        def _():
            arrive(t3_r.at[pl.ds(h * 64, 64)], t3_ss.at[h], t3_rs.at[h])

        target = t3_r[rows].astype(F32) * jnp.concatenate([ts_v[rows]] * 4, axis=1)
        difference = mixed - target
        db[mine, rows] = difference.astype(BF16)
        dg.begin(h)
        squares = difference * difference
        l_v[rows] = (
            squares[:, 0:128] + squares[:, 128:256] + squares[:, 256:384] + squares[:, 384:512]
        )
    l_s[...] = jnp.sum(l_v[...].T, axis=0, keepdims=True)
    l_r[t] = l_s[...]

    def loss(k):
        return copy(l_s, l_r.at[t], l_ss.at[k], l_rs.at[k], (s, (t + k) % 16))

    def loss_go(k, carry):
        loss(k).start()
        return carry

    def loss_got(k, carry):
        arrive(l_r.at[(t + 16 - k) % 16], l_ss.at[k], l_rs.at[k])
        return carry

    def loss_end(k, carry):
        loss(k).wait_send()
        return carry

    lax.fori_loop(1, 16, loss_go, 0)

    def add_grad(slots, first=False):
        d = jnp.concatenate([db[slot] for slot in slots], axis=1)
        for core in range(2):
            w = jnp.concatenate([wo[slot, core] for slot in slots], axis=1)
            g = nt_dot(d, w)
            g_acc[core] = g if first else g_acc[core] + g

    dg.near_relay()
    dg.opp_half(0)
    dg.near_rest()
    add_grad([mine] + dg.near, True)
    dg.opp_half(1)
    dg.onear_a()
    dg.far_step()
    add_grad([dg.opp, dg.far[0]])
    dg.onear_b()
    dg.onear_rest()
    add_grad(dg.onear)
    lax.fori_loop(1, 16, loss_got, 0)
    loss_sum = l_r[0]
    for i in range(1, 16):
        loss_sum = loss_sum + l_r[i]
    out_l[...] = loss_sum / DS
    dg.ofar_step()
    add_grad([dg.far[1]])
    send(g_acc.at[1 - c], g_in, x_ss.at[7], x_rs.at[7], sib)
    arrive(g_in, x_ss.at[7], x_rs.at[7])
    out_g[...] = (g_acc[c] + g_in[...]).astype(BF16)

    for one in started:
        one.wait_send()
    lax.fori_loop(0, 8, wo_end, 0)
    lax.fori_loop(1, 16, kvx_end, 0)
    lax.fori_loop(1, BACK + 1, kv_end, 0)
    lax.fori_loop(1, 16, loss_end, 0)

    rt.end()
    ro.end()

    @pl.when(jnp.logical_not(stays))
    def _():
        t3(0).wait_send()
        t3(1).wait_send()


def reduce_buffers():
    block = (ROWS, COLS)
    return [
        pltpu.VMEM((2, 64, COLS), BF16),
        pltpu.VMEM((2, 64, COLS), BF16),
        pltpu.VMEM((2,) + block, BF16),
        pltpu.VMEM((2,) + block, BF16),
        pltpu.VMEM((2,) + block, BF16),
        pltpu.VMEM((2,) + block, BF16),
        pltpu.VMEM(block, BF16),
        pltpu.VMEM(block, BF16),
        pltpu.VMEM(block, F32),
    ]


def on_device(
    teacher_hidden, teacher_gain, projector, student_hidden, student_gain,
    query_weight, kv_weight, out_weight, doc_ids,
):
    block = (ROWS, COLS)
    hbm = pl.BlockSpec(memory_space=pltpu.HBM)
    vmem = pl.BlockSpec(memory_space=pltpu.VMEM)
    dma = pltpu.SemaphoreType.DMA
    out_s, out_l, out_g = pl.pallas_call(
        body,
        out_shape=(
            jax.ShapeDtypeStruct(block, BF16),
            jax.ShapeDtypeStruct((1, ROWS), F32),
            jax.ShapeDtypeStruct((ROWS, 256), BF16),
        ),
        in_specs=[hbm] * 9,
        out_specs=(vmem, vmem, vmem),
        scratch_shapes=[
            pltpu.VMEM((1, 1024), F32),
            pltpu.VMEM((1, COLS), F32),
            pltpu.VMEM((1, ROWS), jnp.int32),
            pltpu.VMEM((ROWS, 1024), BF16),
            pltpu.VMEM((8, ROWS, 1024), BF16),
            pltpu.VMEM((2, 1024, COLS), BF16),
            pltpu.VMEM((8, 2, COLS, 256), BF16),
            pltpu.VMEM((2, 2, 32, DS), BF16),
            pltpu.VMEM((8, 2, 256, COLS), BF16),
            pltpu.VMEM((64, ROWS), F32),
            pltpu.VMEM((64, ROWS), F32),
            pltpu.VMEM((8,) + block, BF16),
            pltpu.VMEM((1, 768), F32),
            pltpu.VMEM((8, 1, 768), F32),
            pltpu.VMEM((1, 256), F32),
            pltpu.VMEM((1, 256), F32),
            pltpu.VMEM((ROWS, 128), F32),
            pltpu.VMEM((2, ROWS, 256), F32),
            pltpu.VMEM((ROWS, 256), F32),
            pltpu.VMEM((2, 64, ROWS), F32),
            pltpu.VMEM((64, ROWS), F32),
            pltpu.VMEM((4, 16, ROWS), BF16),
            pltpu.VMEM((16, 16, ROWS), BF16),
            pltpu.VMEM((2, ROWS, HEAD_DIM), BF16),
            pltpu.VMEM((2, BACK + 1, ROWS, HEAD_DIM), BF16),
            pltpu.VMEM((8, 1, ROWS), jnp.int32),
            pltpu.VMEM((8, 1, ROWS), jnp.int32),
            pltpu.VMEM((2, ROWS, HEAD_DIM), BF16),
            pltpu.VMEM((4, ROWS, HEAD_DIM), BF16),
            pltpu.VMEM((8,) + block, F32),
            pltpu.VMEM((4,) + block, F32),
            pltpu.VMEM((8,) + block, F32),
            pltpu.VMEM((2,) + block, BF16),
            pltpu.VMEM((8,) + block, BF16),
            pltpu.VMEM((8,) + block, BF16),
            pltpu.VMEM((2,) + block, BF16),
            *reduce_buffers(),
            *reduce_buffers(),
            pltpu.VMEM(block, BF16),
            pltpu.VMEM(block, BF16),
            pltpu.VMEM((ROWS, 128), F32),
            pltpu.VMEM((8,) + block, BF16),
            pltpu.VMEM((2, ROWS, 256), F32),
            pltpu.VMEM((ROWS, 256), F32),
            pltpu.VMEM((ROWS, 128), F32),
            pltpu.VMEM((1, ROWS), F32),
            pltpu.VMEM((16, 1, ROWS), F32),
            dma((10,)),
            dma((8,)), dma((8,)), dma((8,)), dma((8,)), dma((8,)),
            dma((16,)), dma((16,)), dma((4,)), dma((4,)),
            dma((24,)), dma((24,)), dma((24,)), dma((24,)),
            dma((16,)), dma((16,)), dma((16,)), dma((16,)),
            dma((9,)), dma((9,)), dma((9,)), dma((9,)), dma((9,)), dma((9,)),
            dma((24,)), dma((24,)), dma((24,)), dma((24,)),
            dma((2,)), dma((2,)),
            dma((16,)), dma((16,)),
        ],
        compiler_params=pltpu.CompilerParams(
            collective_id=0, has_side_effects=True, vmem_limit_bytes=40 * 1024 * 1024
        ),
    )(
        *(
            pltpu.with_memory_space_constraint(one, pltpu.HBM)
            for one in (
                teacher_hidden, teacher_gain.reshape(1, -1), projector, student_hidden,
                student_gain.reshape(1, -1), query_weight.reshape(8, 2, COLS, 256), jnp.transpose(kv_weight, (0, 2, 1)),
                out_weight, doc_ids.reshape(1, -1),
            )
        )
    )
    return out_s, out_l.reshape(ROWS), out_g


def solution(mesh):
    in_specs = (
        P("seq", "tensor"),
        P("tensor"),
        P("tensor", "seq"),
        P("seq", "tensor"),
        P("tensor"),
        P(None, "tensor"),
        P(None, None, "tensor"),
        P("tensor", None),
        P("seq"),
    )
    out_specs = (P("seq", "tensor"), P("seq"), P("seq", "tensor"))
    return jax.shard_map(
        on_device, mesh=mesh, in_specs=in_specs, out_specs=out_specs, check_vma=False
    )
```

```python
import math

import jax
import jax.numpy as jnp
from jax import lax
from jax.experimental import pallas as pl
from jax.experimental.pallas import tpu as pltpu
from jax.sharding import PartitionSpec as P

DT = 16384
DS = 8192
HEAD_DIM = 128
HEADS = 32
KV_HEADS = 4
ROWS = 128
COLS = 512
BACK = 8
F32 = jnp.float32
BF16 = jnp.bfloat16
MESH = pl.DeviceIdType.MESH
NT = (((1,), (1,)), ((), ()))


def nt_dot(a, b):
    return lax.dot_general(a, b, NT, preferred_element_type=F32)


def body(
    th_h, tgain_h, pj_h, sh_h, sgain_h, wq_h, wkv_h, wo_h, docs_h,
    out_s, out_l, out_g,
    tgain, sgain, docs, th_v, tg, pj, wq, wkv, wo, cos_t, sin_t,
    hb, sg_s, sg_r, sum_s, sum_r, scale_v, q_acc, q_in, kv_acc, kv_in,
    kvx_s, kvx_r, kv_own, kv_r, docs_z, docs_o, q_v, attn_v, bias,
    t_own, t_part, o_own, o_x2, t_sib_s, t_sib_r, t_x2, t_ra, t_rb, t_xp, t_xm, t_fm, t_fp, t_ys, t_yr, t_fin,
    o_ra, o_rb, o_xp, o_xm, o_fm, o_fp, o_ys, o_yr, o_fin,
    t3_s, t3_r, ts_v, db, g_acc, g_in, l_v, l_s, l_r,
    load_sem, w_load, w_ss, w_rs, x_ss, x_rs, z_ss, z_rs, p_ss, p_rs,
    ag_ss, ag_rs, dg_ss, dg_rs, sm_ss, sm_rs, kx_ss, kx_rs, kv_ss, kv_rs, kf_ss, kf_rs, dc_ss, dc_rs,
    t_ss, t_rs, o_ss, o_rs, t3_ss, t3_rs, l_ss, l_rs,
):
    s = lax.axis_index("seq")
    t = lax.axis_index("tensor")
    yl, z = s // 8, s % 8
    yh, x, c = t // 8, (t // 2) % 4, t % 2

    def tid(y_, x_, c_):
        return y_ * 8 + x_ * 2 + c_

    xp_, xm_ = (x + 1) % 4, (x + 3) % 4
    xf_ = (x + 2) % 4
    yo_ = 1 - yh
    sib = (s, tid(yh, x, 1 - c))
    dev_xp = (s, tid(yh, xp_, c))
    dev_xm = (s, tid(yh, xm_, c))
    dev_yo = (s, tid(yo_, x, c))
    dev_zp = (yl * 8 + (z + 1) % 8, t)
    dev_zm = (yl * 8 + (z + 7) % 8, t)
    dev_yl = ((1 - yl) * 8 + z, t)
    turn = jnp.where(c == 0, x, jnp.where(x == 0, 4, 8 - x))
    dev_t3 = (yl * 8 + (z + turn) % 8, yh * 8 + z)
    stays = (z == 0) & (x == 0) & (c == 0)

    started = []

    def copy(src, dst, ss, rs, dev):
        return pltpu.make_async_remote_copy(
            src_ref=src, dst_ref=dst, send_sem=ss, recv_sem=rs, device_id=dev, device_id_type=MESH
        )

    def send(src, dst, ss, rs, dev):
        one = copy(src, dst, ss, rs, dev)
        one.start()
        started.append(one)

    def flush():
        for one in started:
            one.wait_send()
        started.clear()

    def arrive(dst, ss, rs):
        copy(dst, dst, ss, rs, sib).wait_recv()

    def load(src, dst, k):
        one = pltpu.make_async_copy(src, dst, load_sem.at[k])
        one.start()
        return one

    l_th = load(th_h, th_v, 0)
    mine = yh * 4 + x
    l_sh = load(sh_h, hb.at[mine], 1)
    l_small = [load(tgain_h, tgain, 7), load(sgain_h, sgain, 8), load(docs_h, docs, 9)]
    l_wkv = load(wkv_h, wkv.at[c], 2)
    l_wq = load(wq_h.at[:, c], wq.at[:, c], 3)
    l_pj = load(pj_h, pj.at[yl], 4)

    def wo_part(j, core):
        return wo_h.at[:, pl.ds(pl.multiple_of((j * 2 + core) * COLS, COLS), COLS)]

    def wo_load(j):
        return pltpu.make_async_copy(wo_part(j, c), wo.at[j, c], w_load.at[j])

    def wo_send(j):
        return copy(wo_part(j, 1 - c), wo.at[j, c], w_ss.at[j], w_rs.at[j], sib)

    def wo_go(j, carry):
        wo_load(j).start()
        wo_send(j).start()
        return carry

    def wo_got(j, carry):
        wo_load(j).wait()
        arrive(wo.at[j, 1 - c], w_ss.at[j], w_rs.at[j])
        return carry

    def wo_end(j, carry):
        wo_send(j).wait_send()
        return carry

    kv_r[...] = jnp.zeros(kv_r.shape, BF16)

    barrier = pltpu.get_barrier_semaphore()
    for dev in (sib, dev_xp, dev_xm, dev_yo, dev_zp, dev_zm, dev_yl):
        pl.semaphore_signal(barrier, inc=1, device_id=dev, device_id_type=MESH)

    class Gather:
        def __init__(self, buf, ss, rs):
            self.buf, self.ss, self.rs = buf, ss, rs
            self.near = [yh * 4 + xm_, yh * 4 + xp_]
            self.opp = yo_ * 4 + x
            self.onear = [yo_ * 4 + xm_, yo_ * 4 + xp_]
            self.far = [yh * 4 + xf_, yo_ * 4 + xf_]
            self.order = [mine] + self.near + [self.opp] + self.onear + self.far

        def part(self, slot, h):
            return self.buf.at[slot, pl.ds(h * 64, 64)]

        def half(self, slot, h, k, dev):
            part = self.part(slot, h)
            send(part, part, self.ss.at[k], self.rs.at[k], dev)

        def got_half(self, slot, h, k):
            arrive(self.part(slot, h), self.ss.at[k], self.rs.at[k])

        def begin(self, h):
            self.half(mine, h, 0 + h, dev_yo)
            self.half(mine, h, 2 + h, dev_xp)
            self.half(mine, h, 4 + h, dev_xm)

        def near_relay(self):
            self.got_half(self.near[0], 0, 2)
            self.half(self.near[0], 0, 6, dev_xp)
            self.got_half(self.near[1], 1, 5)
            self.half(self.near[1], 1, 7, dev_xm)

        def near_rest(self):
            self.got_half(self.near[0], 1, 3)
            self.got_half(self.near[1], 0, 4)

        def opp_half(self, h):
            self.got_half(self.opp, h, 0 + h)
            self.half(self.opp, h, 8 + h, dev_xp)
            self.half(self.opp, h, 10 + h, dev_xm)

        def onear_a(self):
            self.got_half(self.onear[0], 0, 8)
            self.half(self.onear[0], 0, 12, dev_xp)

        def onear_b(self):
            self.got_half(self.onear[1], 1, 11)
            self.half(self.onear[1], 1, 13, dev_xm)

        def onear_rest(self):
            self.got_half(self.onear[0], 1, 9)
            self.got_half(self.onear[1], 0, 10)

        def far_step(self):
            self.got_half(self.far[0], 0, 6)
            self.got_half(self.far[0], 1, 7)

        def ofar_step(self):
            self.got_half(self.far[1], 0, 12)
            self.got_half(self.far[1], 1, 13)

    def pj_send(k):
        rows = pl.ds(k * 256, 256)
        send(pj_h.at[rows], pj.at[yl, rows], p_ss.at[k], p_rs.at[k], dev_yl)

    ag = Gather(hb, ag_ss, ag_rs)
    l_sh.wait()
    pl.semaphore_wait(barrier, 7)
    ag.begin(0)
    ag.begin(1)
    pj_send(0)
    pj_send(1)
    send(wkv_h, wkv.at[c], x_ss.at[0], x_rs.at[0], sib)
    send(wq_h.at[:, 1 - c], wq.at[:, c], x_ss.at[1], x_rs.at[1], sib)

    z_slot = 0
    l_th.wait()
    for one in l_small:
        one.wait()
    docs_z[z] = docs[...]
    part = jnp.zeros((ROWS, 128), F32)
    for i in range(8):
        cols = slice(i * 128, (i + 1) * 128)
        f = th_v[:, cols].astype(F32)
        part = part + f * f
        tg[z_slot, :, cols] = (f * tgain[:, cols]).astype(BF16)
    sg_s[:, COLS:COLS + 128] = jnp.sum(part.T, axis=0, keepdims=True)
    part = jnp.zeros((ROWS, 128), F32)
    for i in range(4):
        f = hb[mine, :, i * 128:(i + 1) * 128].astype(F32)
        part = part + f * f
    sg_s[:, COLS + 128:COLS + 256] = jnp.sum(part.T, axis=0, keepdims=True)
    sg_s[:, 0:COLS] = sgain[...]
    sg_r[mine] = sg_s[...]


    def ring_slot(d):
        return (0, 1, 2, 3, 4, 7, 6, 5)[d % 8]

    def z_ref(d, h):
        return tg.at[ring_slot(d), pl.ds(h * 64, 64)]

    def z_send(k):
        d = k // 2
        send(z_ref(8 - d, k % 2), z_ref(7 - d, k % 2), z_ss.at[k], z_rs.at[k], dev_zp)
        send(z_ref(d, 1 - k % 2), z_ref(d + 1, 1 - k % 2), z_ss.at[8 + k], z_rs.at[8 + k], dev_zm)

    def z_got(k):
        up, down = z_ref(-(k // 2) + 7, k % 2), z_ref(k // 2 + 1, 1 - k % 2)
        arrive(up, z_ss.at[k], z_rs.at[k])
        arrive(down, z_ss.at[8 + k], z_rs.at[8 + k])

    def z_step(k):
        z_got(k)
        if k + 2 < 7:
            z_send(k + 2)

    def small_send(i, k, dev):
        slot = ag.order[i]
        send(sg_r.at[slot], sg_r.at[slot], sm_ss.at[k], sm_rs.at[k], dev)

    def small_got(i, k):
        arrive(sg_r.at[ag.order[i]], sm_ss.at[k], sm_rs.at[k])

    def docs_send(d, k, dev):
        ref = docs_z.at[(z + d) % 8]
        send(ref, ref, dc_ss.at[k], dc_rs.at[k], dev)

    def docs_step(k):
        arrive(docs_z.at[(z + 7 - k) % 8], dc_ss.at[k], dc_rs.at[k])
        if k < 3:
            arrive(docs_z.at[(z + 1 + k) % 8], dc_ss.at[4 + k], dc_rs.at[4 + k])
            docs_send(7 - k, k + 1, dev_zp)
            if k < 2:
                docs_send(1 + k, k + 5, dev_zm)
        else:
            send(docs_z, docs_o, dc_ss.at[8], dc_rs.at[8], dev_yl)

    small_send(0, 0, dev_yo)
    small_send(0, 1, dev_xp)
    small_send(0, 2, dev_xm)
    docs_send(0, 0, dev_zp)
    docs_send(0, 4, dev_zm)
    z_send(0)
    z_send(1)
    pj_send(2)

    entry = lax.broadcasted_iota(jnp.int32, (64, ROWS), 0).astype(F32)
    position = (s * ROWS + lax.broadcasted_iota(jnp.int32, (64, ROWS), 1)).astype(F32)
    angle = position * jnp.exp(-math.log(500000.0) * (2.0 * entry / HEAD_DIM))
    cos_t[...] = jnp.cos(angle)
    sin_t[...] = jnp.sin(angle)

    def process(slots, first=False):
        blocks = []
        for slot in slots:
            parts = []
            for i in range(4):
                cols = slice(i * 128, (i + 1) * 128)
                f = hb[slot, :, cols].astype(F32)
                parts.append((f * scale_v[...] * sg_r[slot][:, cols]).astype(BF16))
            blocks.append(jnp.concatenate(parts, axis=1))
        n = jnp.concatenate(blocks, axis=1)
        w = []
        for slot in slots:
            at = pl.multiple_of((slot * 2 + c) * COLS, COLS)
            w.append(wkv[:, :, :, pl.ds(at, COLS)].reshape(128, COLS))
        kv = nt_dot(jnp.concatenate(w, axis=1), n)
        for core in range(2):
            w = jnp.concatenate([wq[slot, core] for slot in slots], axis=0)
            q = jnp.dot(n, w, preferred_element_type=F32)
            k = kv[core * 64:core * 64 + 64]
            q_acc[core] = q if first else q_acc[core] + q
            kv_acc[core] = k if first else kv_acc[core] + k

    small_got(1, 1)
    small_send(1, 3, dev_xp)
    small_got(2, 2)
    small_got(3, 0)
    small_send(3, 4, dev_xp)
    small_send(3, 5, dev_xm)
    docs_step(0)
    ag.near_relay()
    small_got(6, 3)
    docs_step(1)
    small_got(4, 4)
    small_send(4, 6, dev_xp)
    small_got(5, 5)
    ag.near_rest()
    ag.opp_half(0)
    z_step(0)
    pj_send(3)
    small_got(7, 6)
    sums = sg_r[0][:, COLS:COLS + 256]
    for i in range(1, 8):
        sums = sums + sg_r[i][:, COLS:COLS + 256]
    sum_s[...] = sums
    send(sum_s, sum_r, x_ss.at[2], x_rs.at[2], sib)
    docs_step(2)
    ag.opp_half(1)
    arrive(sum_r, x_ss.at[2], x_rs.at[2])
    sums = sum_s[...] + sum_r[...]
    ts_v[...] = jnp.broadcast_to(lax.rsqrt(sums[:, 0:128] / DT + 1e-05), (ROWS, 128)).T
    scale_v[...] = jnp.broadcast_to(lax.rsqrt(sums[:, 128:256] / DS + 1e-05), (ROWS, 128)).T
    docs_step(3)
    z_step(1)
    ag.onear_a()
    l_wkv.wait()
    l_wq.wait()
    arrive(wkv.at[1 - c], x_ss.at[0], x_rs.at[0])
    arrive(wq.at[:, 1 - c], x_ss.at[1], x_rs.at[1])
    process([mine] + ag.near, True)
    ag.onear_b()
    z_step(2)
    ag.far_step()
    process([ag.opp, ag.far[0]])
    ag.onear_rest()
    process(ag.onear)
    z_step(3)
    ag.ofar_step()
    process([ag.far[1]])
    send(kv_acc.at[1 - c], kv_in, x_ss.at[3], x_rs.at[3], sib)
    send(q_acc.at[1 - c], q_in, x_ss.at[4], x_rs.at[4], sib)
    lax.fori_loop(0, 8, wo_go, 0)
    arrive(kv_in, x_ss.at[3], x_rs.at[3])

    row = lax.broadcasted_iota(jnp.int32, (64, 64), 0)
    col = lax.broadcasted_iota(jnp.int32, (64, 64), 1)
    take = ((row >> 3) & 1) * 32 + (row & 7) * 4 + (row >> 4)
    pick = jnp.where(col == take, 1.0, 0.0).astype(BF16)
    kv_mine = (kv_acc[c] + kv_in[...]).astype(BF16)
    kvx_s[...] = jnp.dot(pick, kv_mine, preferred_element_type=F32).astype(BF16).reshape(4, 16, 128)
    kvx_r[t] = kvx_s[t // 4]

    def kvx(k):
        to = (t + k) % 16
        return copy(kvx_s.at[to // 4], kvx_r.at[t], kx_ss.at[k], kx_rs.at[k], (s, to))

    def kvx_go(k, carry):
        kvx(k).start()
        return carry

    def kvx_got(k, carry):
        arrive(kvx_r.at[(t + 16 - k) % 16], kx_ss.at[k], kx_rs.at[k])
        return carry

    def kvx_end(k, carry):
        kvx(k).wait_send()
        return carry

    lax.fori_loop(1, 16, kvx_go, 0)
    z_step(4)

    cos2 = jnp.concatenate([cos_t[...], cos_t[...]], axis=0).T
    sin2 = jnp.concatenate([-sin_t[...], sin_t[...]], axis=0).T
    arrive(q_in, x_ss.at[4], x_rs.at[4])
    q_mine = q_acc[c] + q_in[...]
    for h in range(2):
        qh = q_mine[:, h * 128:(h + 1) * 128]
        turned = qh * cos2 + pltpu.roll(qh, 64, 1) * sin2
        q_v[h] = (turned * HEAD_DIM ** (-0.5)).astype(BF16)

    lax.fori_loop(1, 16, kvx_got, 0)
    both = kvx_r[...].astype(F32).reshape(16, 2, 8, ROWS)
    k_raw = both[:, 0].reshape(HEAD_DIM, ROWS)
    v_raw = both[:, 1].reshape(HEAD_DIM, ROWS)
    first, second = k_raw[0:64], k_raw[64:128]
    k_rot = jnp.concatenate(
        [first * cos_t[...] - second * sin_t[...], second * cos_t[...] + first * sin_t[...]], axis=0
    )
    kv_own[0] = k_rot.astype(BF16)
    kv_own[1] = v_raw.T.astype(BF16)
    kv_r[0, 0] = kv_own[0]
    kv_r[1, 0] = kv_own[1]

    def kv_copy(k):
        return copy(kv_own.at[c], kv_r.at[c, k], kv_ss.at[k], kv_rs.at[k], ((s + k) % 16, t))

    def kv_fwd(k):
        return copy(kv_r.at[c, k], kv_r.at[c, k], kf_ss.at[k], kf_rs.at[k], sib)

    def kv_go(k):
        @pl.when(s + k < 16)
        def _():
            kv_copy(k).start()

    def kv_mid(k):
        @pl.when(s >= k)
        def _():
            arrive(kv_r.at[c, k], kv_ss.at[k], kv_rs.at[k])
            kv_fwd(k).start()

    def kv_got(k, carry):
        @pl.when(s >= k)
        def _():
            arrive(kv_r.at[1 - c, k], kf_ss.at[k], kf_rs.at[k])
        return carry

    def kv_end(k, carry):
        @pl.when(s >= k)
        def _():
            kv_fwd(k).wait_send()

        @pl.when(s + k < 16)
        def _():
            kv_copy(k).wait_send()
        return carry

    arrive(docs_o, dc_ss.at[8], dc_rs.at[8])
    for k in (4, 5, 3, 6, 2, 7, 1, 8):
        kv_go(k)

    def docs_back(j):
        at = (z + 8 - j) % 8
        return jnp.where(z >= j, docs_z[at], jnp.where(yl == 1, docs_o[at], -1))

    key_doc = jnp.concatenate([docs_back(j) for j in range(BACK + 1)], axis=1)
    row_doc = jnp.broadcast_to(docs[...].astype(F32), (ROWS, ROWS)).T[:, 0:1].astype(jnp.int32)
    wide = (ROWS, (BACK + 1) * ROWS)
    row_at = lax.broadcasted_iota(jnp.int32, wide, 0)
    key_at = lax.broadcasted_iota(jnp.int32, wide, 1)
    allowed = (key_doc == row_doc) & ((key_at >= ROWS) | (key_at <= row_at))
    bias[...] = jnp.where(allowed, 0.0, -1e30)

    class Reduce:
        def __init__(self, y_order, own, sib_s, sib_r, x2, ra, rb, xp, xm, fm, fp, ys, yr, fin, ss, rs):
            self.own, self.sib_s, self.sib_r = own, sib_s, sib_r
            self.x2, self.ra, self.rb, self.xp, self.xm, self.fm, self.fp = x2, ra, rb, xp, xm, fm, fp
            self.ys, self.yr, self.fin, self.ss, self.rs = ys, yr, fin, ss, rs
            self.y_order = y_order
            self.x_order = (xf_, xp_, xm_, x)

        def go(self, src, dst, k, dev):
            send(src, dst, self.ss.at[k], self.rs.at[k], dev)

        def got(self, dst, k):
            arrive(dst, self.ss.at[k], self.rs.at[k])

        def slot(self, k, i):
            return self.y_order[i] * 4 + self.x_order[k]

        def to_sib(self, k, i):
            slot = self.slot(k, i)
            self.go(self.sib_s.at[slot], self.sib_r.at[slot], k * 2 + i, sib)

        def sib_got(self, k, i):
            if self.sib_r is not None:
                self.got(self.sib_r.at[self.slot(k, i)], k * 2 + i)

        def pair(self, k, i, h):
            slot, rows = self.slot(k, i), slice(h * 64, h * 64 + 64)
            value = self.own[slot, rows]
            return value if self.sib_r is None else value + self.sib_r[slot, rows].astype(F32)

        def far(self, i):
            self.sib_got(0, i)
            self.x2[i, 0:64] = self.pair(0, i, 0).astype(BF16)
            self.go(self.x2.at[i, pl.ds(0, 64)], self.ra.at[i], 8 + i, dev_xp)
            self.x2[i, 64:128] = self.pair(0, i, 1).astype(BF16)
            self.go(self.x2.at[i, pl.ds(64, 64)], self.rb.at[i], 10 + i, dev_xm)

        def near(self, i):
            self.sib_got(1, i)
            self.xp[i, 64:128] = self.pair(1, i, 1).astype(BF16)
            self.go(self.xp.at[i, pl.ds(64, 64)], self.fm.at[i, pl.ds(64, 64)], 12 + i, dev_xp)
            self.sib_got(2, i)
            self.xm[i, 0:64] = self.pair(2, i, 0).astype(BF16)
            self.go(self.xm.at[i, pl.ds(0, 64)], self.fp.at[i, pl.ds(0, 64)], 14 + i, dev_xm)

        def relay(self, i):
            self.got(self.ra.at[i], 8 + i)
            self.xp[i, 0:64] = (self.pair(1, i, 0) + self.ra[i].astype(F32)).astype(BF16)
            self.go(self.xp.at[i, pl.ds(0, 64)], self.fm.at[i, pl.ds(0, 64)], 16 + i, dev_xp)
            self.got(self.rb.at[i], 10 + i)
            self.xm[i, 64:128] = (self.pair(2, i, 1) + self.rb[i].astype(F32)).astype(BF16)
            self.go(self.xm.at[i, pl.ds(64, 64)], self.fp.at[i, pl.ds(64, 64)], 18 + i, dev_xm)

        def join(self, i, h):
            rows, at = slice(h * 64, h * 64 + 64), pl.ds(h * 64, 64)
            if h == 0:
                self.sib_got(3, i)
            self.got(self.fm.at[i, at], (16, 12)[h] + i)
            self.got(self.fp.at[i, at], (14, 18)[h] + i)
            return self.pair(3, i, h) + self.fm[i, rows].astype(F32) + self.fp[i, rows].astype(F32)

        def join_one(self, i):
            mine = self.y_order[i] == yh
            for h in range(2):
                rows = slice(h * 64, h * 64 + 64)
                value = self.join(i, h)

                @pl.when(mine)
                def _():
                    self.fin[rows] = value

                @pl.when(jnp.logical_not(mine))
                def _():
                    self.ys[rows] = value.astype(BF16)
                    self.to_opp(h).start()

        def to_opp(self, h):
            at = pl.ds(h * 64, 64)
            return copy(self.ys.at[at], self.yr.at[at], self.ss.at[20 + h], self.rs.at[20 + h], dev_yo)

        def join_other(self):
            for h in range(2):
                self.ys[h * 64:h * 64 + 64] = self.join(0, h).astype(BF16)
                self.to_opp(h).start()

        def join_mine(self):
            for h in range(2):
                self.fin[h * 64:h * 64 + 64] = self.join(1, h)

        def end(self):
            for h in range(2):
                self.to_opp(h).wait_send()

        def last(self, h):
            rows = slice(h * 64, h * 64 + 64)
            self.got(self.yr.at[pl.ds(h * 64, 64)], 20 + h)
            return self.fin[rows] + self.yr[rows].astype(F32)

    rt = Reduce((yl, 1 - yl), t_own, t_sib_s, t_sib_r, t_x2, t_ra, t_rb, t_xp, t_xm, t_fm, t_fp, t_ys, t_yr, t_fin, t_ss, t_rs)

    z_step(5)
    z_step(6)

    def products(core, y_, k, width):
        rows = tg[pl.ds(core * 4, 4), :, k * width:(k + 1) * width].reshape(4 * ROWS, width)
        return jnp.dot(rows, pj[y_, k * width:(k + 1) * width], preferred_element_type=F32).reshape(4, ROWS, COLS)

    l_pj.wait()
    first = pl.ds(yl * 4, 4)
    t_sib_s[first] = products(1 - c, yl, 0, 1024).astype(BF16)
    for k in range(4):
        rt.to_sib(k, 0)
    t_own[first] = products(c, yl, 0, 1024)
    rt.far(0)
    rt.near(0)

    other = pl.ds((1 - yl) * 4, 4)
    for k in range(4):
        arrive(pj.at[1 - yl, pl.ds(k * 256, 256)], p_ss.at[k], p_rs.at[k])
        theirs = products(1 - c, 1 - yl, k, 256)
        if k == 0:
            t_part[...] = theirs
        elif k < 3:
            t_part[...] += theirs
        else:
            t_sib_s[other] = (t_part[...] + theirs).astype(BF16)
            for j in range(4):
                rt.to_sib(j, 1)
        if k == 0:
            t_own[other] = products(c, 1 - yl, k, 256)
        else:
            t_own[other] += products(c, 1 - yl, k, 256)
        if k == 1:
            rt.relay(0)
    rt.far(1)
    rt.near(1)
    rt.join_one(0)
    for k in (1, 8, 2, 7):
        kv_mid(k)
    rt.relay(1)
    for k in (3, 6, 5, 4):
        kv_mid(k)

    lax.fori_loop(1, BACK + 1, kv_got, 0)
    keys = jnp.concatenate([kv_r[0, j] for j in range(BACK + 1)], axis=1)
    values = kv_r[1].reshape((BACK + 1) * ROWS, HEAD_DIM)
    for h in range(2):
        scores = jnp.dot(q_v[h], keys, preferred_element_type=F32)
        scores = scores + bias[...]
        probs = jnp.exp(scores - jnp.max(scores, axis=1, keepdims=True))
        total = jnp.sum(probs, axis=1, keepdims=True)
        acc = jnp.dot(probs.astype(BF16), values, preferred_element_type=F32)
        attn_v[c * 2 + h] = (acc / total).astype(BF16)
        send(attn_v.at[c * 2 + h], attn_v.at[c * 2 + h], x_ss.at[5 + h], x_rs.at[5 + h], sib)
    lax.fori_loop(0, 8, wo_got, 0)

    ro = Reduce((yo_, yh), o_own, None, None, o_x2, o_ra, o_rb, o_xp, o_xm, o_fm, o_fp, o_ys, o_yr, o_fin, o_ss, o_rs)

    for h in range(2):
        arrive(attn_v.at[2 - 2 * c + h], x_ss.at[5 + h], x_rs.at[5 + h])
    attn = jnp.concatenate([attn_v[i] for i in range(4)], axis=1)

    def out_block(k, i):
        slot = ro.slot(k, i)
        o_own[slot] = jnp.dot(attn, wo[slot].reshape(COLS, COLS), preferred_element_type=F32)

    out_block(0, 0)
    ro.far(0)
    rt.join_one(1)
    out_block(1, 0)
    out_block(2, 0)
    ro.near(0)
    out_block(0, 1)
    ro.relay(0)
    ro.far(1)
    out_block(1, 1)
    out_block(2, 1)
    ro.near(1)
    out_block(3, 0)
    out_block(3, 1)
    ro.relay(1)

    def t3(h):
        at = pl.ds(h * 64, 64)
        return copy(t3_s.at[at], t3_r.at[at], t3_ss.at[h], t3_rs.at[h], dev_t3)

    for h in range(2):
        rows = slice(h * 64, h * 64 + 64)
        t3_s[rows] = rt.last(h).astype(BF16)

        @pl.when(stays)
        def _():
            t3_r[rows] = t3_s[rows]

        @pl.when(jnp.logical_not(stays))
        def _():
            t3(h).start()

    ro.join_other()
    ro.join_mine()

    def before_end():
        flush()
        lax.fori_loop(0, 8, wo_end, 0)
        lax.fori_loop(1, 16, kvx_end, 0)
        lax.fori_loop(1, BACK + 1, kv_end, 0)
        rt.end()
        ro.end()

        @pl.when(jnp.logical_not(stays))
        def _():
            t3(0).wait_send()
            t3(1).wait_send()

    dg = Gather(db, dg_ss, dg_rs)
    for h in range(2):
        rows = slice(h * 64, h * 64 + 64)
        mixed = hb[mine, rows].astype(F32) + ro.last(h)
        out_s[rows] = mixed.astype(BF16)

        @pl.when(jnp.logical_not(stays))
        def _():
            arrive(t3_r.at[pl.ds(h * 64, 64)], t3_ss.at[h], t3_rs.at[h])

        target = t3_r[rows].astype(F32) * jnp.concatenate([ts_v[rows]] * 4, axis=1)
        difference = mixed - target
        db[mine, rows] = difference.astype(BF16)
        dg.begin(h)
        squares = difference * difference
        l_v[rows] = (
            squares[:, 0:128] + squares[:, 128:256] + squares[:, 256:384] + squares[:, 384:512]
        )
    l_s[...] = jnp.sum(l_v[...].T, axis=0, keepdims=True)
    l_r[t] = l_s[...]

    def loss(k):
        return copy(l_s, l_r.at[t], l_ss.at[k], l_rs.at[k], (s, (t + k) % 16))

    def loss_go(k, carry):
        loss(k).start()
        return carry

    def loss_got(k, carry):
        arrive(l_r.at[(t + 16 - k) % 16], l_ss.at[k], l_rs.at[k])
        return carry

    def loss_end(k, carry):
        loss(k).wait_send()
        return carry

    lax.fori_loop(1, 16, loss_go, 0)

    def add_grad(slots, first=False):
        d = jnp.concatenate([db[slot] for slot in slots], axis=1)
        for core in range(2):
            w = jnp.concatenate([wo[slot, core] for slot in slots], axis=1)
            g = nt_dot(d, w)
            g_acc[core] = g if first else g_acc[core] + g

    dg.near_relay()
    dg.opp_half(0)
    dg.near_rest()
    before_end()
    add_grad([mine] + dg.near, True)
    dg.opp_half(1)
    dg.onear_a()
    dg.far_step()
    add_grad([dg.opp, dg.far[0]])
    dg.onear_b()
    dg.onear_rest()
    add_grad(dg.onear)
    lax.fori_loop(1, 16, loss_got, 0)
    loss_sum = l_r[0]
    for i in range(1, 16):
        loss_sum = loss_sum + l_r[i]
    out_l[...] = loss_sum / DS
    dg.ofar_step()
    add_grad([dg.far[1]])
    send(g_acc.at[1 - c], g_in, x_ss.at[7], x_rs.at[7], sib)
    arrive(g_in, x_ss.at[7], x_rs.at[7])
    out_g[...] = (g_acc[c] + g_in[...]).astype(BF16)

    flush()
    lax.fori_loop(1, 16, loss_end, 0)


def reduce_buffers():
    block = (ROWS, COLS)
    return [
        pltpu.VMEM((2, 64, COLS), BF16),
        pltpu.VMEM((2, 64, COLS), BF16),
        pltpu.VMEM((2,) + block, BF16),
        pltpu.VMEM((2,) + block, BF16),
        pltpu.VMEM((2,) + block, BF16),
        pltpu.VMEM((2,) + block, BF16),
        pltpu.VMEM(block, BF16),
        pltpu.VMEM(block, BF16),
        pltpu.VMEM(block, F32),
    ]


def on_device(
    teacher_hidden, teacher_gain, projector, student_hidden, student_gain,
    query_weight, kv_weight, out_weight, doc_ids,
):
    block = (ROWS, COLS)
    hbm = pl.BlockSpec(memory_space=pltpu.HBM)
    vmem = pl.BlockSpec(memory_space=pltpu.VMEM)
    dma = pltpu.SemaphoreType.DMA
    out_s, out_l, out_g = pl.pallas_call(
        body,
        out_shape=(
            jax.ShapeDtypeStruct(block, BF16),
            jax.ShapeDtypeStruct((1, ROWS), F32),
            jax.ShapeDtypeStruct((ROWS, 256), BF16),
        ),
        in_specs=[hbm] * 9,
        out_specs=(vmem, vmem, vmem),
        scratch_shapes=[
            pltpu.VMEM((1, 1024), F32),
            pltpu.VMEM((1, COLS), F32),
            pltpu.VMEM((1, ROWS), jnp.int32),
            pltpu.VMEM((ROWS, 1024), BF16),
            pltpu.VMEM((8, ROWS, 1024), BF16),
            pltpu.VMEM((2, 1024, COLS), BF16),
            pltpu.VMEM((8, 2, COLS, 256), BF16),
            pltpu.VMEM((2, 2, 32, DS), BF16),
            pltpu.VMEM((8, 2, 256, COLS), BF16),
            pltpu.VMEM((64, ROWS), F32),
            pltpu.VMEM((64, ROWS), F32),
            pltpu.VMEM((8,) + block, BF16),
            pltpu.VMEM((1, 768), F32),
            pltpu.VMEM((8, 1, 768), F32),
            pltpu.VMEM((1, 256), F32),
            pltpu.VMEM((1, 256), F32),
            pltpu.VMEM((ROWS, 128), F32),
            pltpu.VMEM((2, ROWS, 256), F32),
            pltpu.VMEM((ROWS, 256), F32),
            pltpu.VMEM((2, 64, ROWS), F32),
            pltpu.VMEM((64, ROWS), F32),
            pltpu.VMEM((4, 16, ROWS), BF16),
            pltpu.VMEM((16, 16, ROWS), BF16),
            pltpu.VMEM((2, ROWS, HEAD_DIM), BF16),
            pltpu.VMEM((2, BACK + 1, ROWS, HEAD_DIM), BF16),
            pltpu.VMEM((8, 1, ROWS), jnp.int32),
            pltpu.VMEM((8, 1, ROWS), jnp.int32),
            pltpu.VMEM((2, ROWS, HEAD_DIM), BF16),
            pltpu.VMEM((4, ROWS, HEAD_DIM), BF16),
            pltpu.VMEM((ROWS, (BACK + 1) * ROWS), F32),
            pltpu.VMEM((8,) + block, F32),
            pltpu.VMEM((4,) + block, F32),
            pltpu.VMEM((8,) + block, F32),
            pltpu.VMEM((2,) + block, BF16),
            pltpu.VMEM((8,) + block, BF16),
            pltpu.VMEM((8,) + block, BF16),
            pltpu.VMEM((2,) + block, BF16),
            *reduce_buffers(),
            *reduce_buffers(),
            pltpu.VMEM(block, BF16),
            pltpu.VMEM(block, BF16),
            pltpu.VMEM((ROWS, 128), F32),
            pltpu.VMEM((8,) + block, BF16),
            pltpu.VMEM((2, ROWS, 256), F32),
            pltpu.VMEM((ROWS, 256), F32),
            pltpu.VMEM((ROWS, 128), F32),
            pltpu.VMEM((1, ROWS), F32),
            pltpu.VMEM((16, 1, ROWS), F32),
            dma((10,)),
            dma((8,)), dma((8,)), dma((8,)), dma((8,)), dma((8,)),
            dma((16,)), dma((16,)), dma((4,)), dma((4,)),
            dma((24,)), dma((24,)), dma((24,)), dma((24,)),
            dma((16,)), dma((16,)), dma((16,)), dma((16,)),
            dma((9,)), dma((9,)), dma((9,)), dma((9,)), dma((9,)), dma((9,)),
            dma((24,)), dma((24,)), dma((24,)), dma((24,)),
            dma((2,)), dma((2,)),
            dma((16,)), dma((16,)),
        ],
        compiler_params=pltpu.CompilerParams(
            collective_id=0, has_side_effects=True, vmem_limit_bytes=40 * 1024 * 1024
        ),
    )(
        *(
            pltpu.with_memory_space_constraint(one, pltpu.HBM)
            for one in (
                teacher_hidden, teacher_gain.reshape(1, -1), projector, student_hidden,
                student_gain.reshape(1, -1), query_weight.reshape(8, 2, COLS, 256), jnp.transpose(kv_weight, (0, 2, 1)),
                out_weight, doc_ids.reshape(1, -1),
            )
        )
    )
    return out_s, out_l.reshape(ROWS), out_g


def solution(mesh):
    in_specs = (
        P("seq", "tensor"),
        P("tensor"),
        P("tensor", "seq"),
        P("seq", "tensor"),
        P("tensor"),
        P(None, "tensor"),
        P(None, None, "tensor"),
        P("tensor", None),
        P("seq"),
    )
    out_specs = (P("seq", "tensor"), P("seq"), P("seq", "tensor"))
    return jax.shard_map(
        on_device, mesh=mesh, in_specs=in_specs, out_specs=out_specs, check_vma=False
    )
```

```python
import math

import jax
import jax.numpy as jnp
from jax import lax
from jax.experimental import pallas as pl
from jax.experimental.pallas import tpu as pltpu
from jax.sharding import PartitionSpec as P

DT = 16384
DS = 8192
HEAD_DIM = 128
HEADS = 32
KV_HEADS = 4
ROWS = 128
COLS = 512
BACK = 8
F32 = jnp.float32
BF16 = jnp.bfloat16
MESH = pl.DeviceIdType.MESH
NT = (((1,), (1,)), ((), ()))


def nt_dot(a, b):
    return lax.dot_general(a, b, NT, preferred_element_type=F32)


def body(
    th_h, tgain_h, pj_h, sh_h, sgain_h, wq_h, wkv_h, wo_h, docs_h,
    out_s, out_l, out_g,
    tgain, sgain, docs, th_v, tg, pj, wq, wkv, wo, cos_t, sin_t,
    hb, sg_s, sg_r, sum_s, sum_r, scale_v, q_acc, q_in, kv_acc, kv_in,
    kvx_s, kvx_r, kv_own, kv_r, docs_z, docs_o, q_v, attn_v, bias,
    t_own, t_part, o_own, o_x2, t_sib_s, t_sib_r, t_x2, t_ra, t_rb, t_xp, t_xm, t_fm, t_fp, t_ys, t_yr, t_fin,
    o_ra, o_rb, o_xp, o_xm, o_fm, o_fp, o_ys, o_yr, o_fin,
    t3_s, t3_r, ts_v, db, g_acc, g_in, l_v, l_s, l_r,
    load_sem, w_load, w_ss, w_rs, v_load, v_ss, v_rs, u_ss, u_rs, x_ss, x_rs, z_ss, z_rs, p_ss, p_rs,
    ag_ss, ag_rs, dg_ss, dg_rs, sm_ss, sm_rs, kx_ss, kx_rs, kv_ss, kv_rs, kf_ss, kf_rs, dc_ss, dc_rs,
    t_ss, t_rs, o_ss, o_rs, t3_ss, t3_rs, l_ss, l_rs,
):
    s = lax.axis_index("seq")
    t = lax.axis_index("tensor")
    yl, z = s // 8, s % 8
    yh, x, c = t // 8, (t // 2) % 4, t % 2

    def tid(y_, x_, c_):
        return y_ * 8 + x_ * 2 + c_

    xp_, xm_ = (x + 1) % 4, (x + 3) % 4
    xf_ = (x + 2) % 4
    yo_ = 1 - yh
    sib = (s, tid(yh, x, 1 - c))
    dev_xp = (s, tid(yh, xp_, c))
    dev_xm = (s, tid(yh, xm_, c))
    dev_yo = (s, tid(yo_, x, c))
    dev_zp = (yl * 8 + (z + 1) % 8, t)
    dev_zm = (yl * 8 + (z + 7) % 8, t)
    dev_yl = ((1 - yl) * 8 + z, t)
    turn = jnp.where(c == 0, x, jnp.where(x == 0, 4, 8 - x))
    dev_t3 = (yl * 8 + (z + turn) % 8, yh * 8 + z)
    stays = (z == 0) & (x == 0) & (c == 0)

    started = []

    def copy(src, dst, ss, rs, dev):
        return pltpu.make_async_remote_copy(
            src_ref=src, dst_ref=dst, send_sem=ss, recv_sem=rs, device_id=dev, device_id_type=MESH
        )

    def send(src, dst, ss, rs, dev):
        one = copy(src, dst, ss, rs, dev)
        one.start()
        started.append(one)

    def flush():
        for one in started:
            one.wait_send()
        started.clear()

    def arrive(dst, ss, rs):
        copy(dst, dst, ss, rs, sib).wait_recv()

    def load(src, dst, k):
        one = pltpu.make_async_copy(src, dst, load_sem.at[k])
        one.start()
        return one

    l_th = load(th_h, th_v, 0)
    mine = yh * 4 + x
    l_sh = load(sh_h, hb.at[mine], 1)
    l_small = [load(tgain_h, tgain, 7), load(sgain_h, sgain, 8), load(docs_h, docs, 9)]

    def wkv_part(j, core):
        return wkv_h.at[:, :, pl.ds(pl.multiple_of((j * 2 + core) * COLS, COLS), COLS)]

    def wkv_load(j):
        return pltpu.make_async_copy(wkv_part(j, c), wkv.at[j, c], v_load.at[j])

    def wkv_go(j, carry):
        wkv_load(j).start()
        return carry

    def wo_part(j, core):
        return wo_h.at[:, pl.ds(pl.multiple_of((j * 2 + core) * COLS, COLS), COLS)]

    def wo_load(j):
        return pltpu.make_async_copy(wo_part(j, c), wo.at[j, c], w_load.at[j])

    def wo_send(j):
        return copy(wo_part(j, 1 - c), wo.at[j, c], w_ss.at[j], w_rs.at[j], sib)

    def wo_fetch(j, carry):
        wo_load(j).start()
        return carry

    def wo_go(j, carry):
        wo_send(j).start()
        return carry

    def wo_got(j, carry):
        wo_load(j).wait()
        arrive(wo.at[j, 1 - c], w_ss.at[j], w_rs.at[j])
        return carry

    def wo_end(j, carry):
        wo_send(j).wait_send()
        return carry

    kv_r[...] = jnp.zeros(kv_r.shape, BF16)

    barrier = pltpu.get_barrier_semaphore()
    for dev in (sib, dev_xp, dev_xm, dev_yo, dev_zp, dev_zm, dev_yl):
        pl.semaphore_signal(barrier, inc=1, device_id=dev, device_id_type=MESH)

    class Gather:
        def __init__(self, buf, ss, rs):
            self.buf, self.ss, self.rs = buf, ss, rs
            self.near = [yh * 4 + xm_, yh * 4 + xp_]
            self.opp = yo_ * 4 + x
            self.onear = [yo_ * 4 + xm_, yo_ * 4 + xp_]
            self.far = [yh * 4 + xf_, yo_ * 4 + xf_]
            self.order = [mine] + self.near + [self.opp] + self.onear + self.far

        def part(self, slot, h):
            return self.buf.at[slot, pl.ds(h * 64, 64)]

        def half(self, slot, h, k, dev):
            part = self.part(slot, h)
            send(part, part, self.ss.at[k], self.rs.at[k], dev)

        def got_half(self, slot, h, k):
            arrive(self.part(slot, h), self.ss.at[k], self.rs.at[k])

        def begin(self, h):
            self.half(mine, h, 0 + h, dev_yo)
            self.half(mine, h, 2 + h, dev_xp)
            self.half(mine, h, 4 + h, dev_xm)

        def near_relay(self):
            self.got_half(self.near[0], 0, 2)
            self.half(self.near[0], 0, 6, dev_xp)
            self.got_half(self.near[1], 1, 5)
            self.half(self.near[1], 1, 7, dev_xm)

        def near_rest(self):
            self.got_half(self.near[0], 1, 3)
            self.got_half(self.near[1], 0, 4)

        def opp_half(self, h):
            self.got_half(self.opp, h, 0 + h)
            self.half(self.opp, h, 8 + h, dev_xp)
            self.half(self.opp, h, 10 + h, dev_xm)

        def onear_a(self):
            self.got_half(self.onear[0], 0, 8)
            self.half(self.onear[0], 0, 12, dev_xp)

        def onear_b(self):
            self.got_half(self.onear[1], 1, 11)
            self.half(self.onear[1], 1, 13, dev_xm)

        def onear_rest(self):
            self.got_half(self.onear[0], 1, 9)
            self.got_half(self.onear[1], 0, 10)

        def far_step(self):
            self.got_half(self.far[0], 0, 6)
            self.got_half(self.far[0], 1, 7)

        def ofar_step(self):
            self.got_half(self.far[1], 0, 12)
            self.got_half(self.far[1], 1, 13)

    def pj_send(k):
        rows = pl.ds(k * 128, 128)
        send(pj_h.at[rows], pj.at[yl, rows], p_ss.at[k], p_rs.at[k], dev_yl)

    def wkv_send(j):
        return copy(wkv_part(j, 1 - c), wkv.at[j, c], v_ss.at[j], v_rs.at[j], sib)

    def wq_send(j):
        return copy(wq_h.at[j, 1 - c], wq.at[j, c], u_ss.at[j], u_rs.at[j], sib)

    def w_go(j, carry):
        wkv_send(j).start()
        wq_send(j).start()
        return carry

    def w_end(j, carry):
        wkv_send(j).wait_send()
        wq_send(j).wait_send()
        return carry

    def w_got(slot):
        wkv_load(slot).wait()
        arrive(wkv.at[slot, 1 - c], v_ss.at[slot], v_rs.at[slot])
        arrive(wq.at[slot, 1 - c], u_ss.at[slot], u_rs.at[slot])

    ag = Gather(hb, ag_ss, ag_rs)
    l_sh.wait()
    pl.semaphore_wait(barrier, 7)
    ag.begin(0)

    z_slot = 0
    l_th.wait()
    for one in l_small:
        one.wait()
    docs_z[z] = docs[...]
    part = jnp.zeros((ROWS, 128), F32)
    for i in range(8):
        cols = slice(i * 128, (i + 1) * 128)
        f = th_v[:, cols].astype(F32)
        part = part + f * f
        tg[z_slot, :, cols] = (f * tgain[:, cols]).astype(BF16)
    sg_s[:, COLS:COLS + 128] = jnp.sum(part.T, axis=0, keepdims=True)
    part = jnp.zeros((ROWS, 128), F32)
    for i in range(4):
        f = hb[mine, :, i * 128:(i + 1) * 128].astype(F32)
        part = part + f * f
    sg_s[:, COLS + 128:COLS + 256] = jnp.sum(part.T, axis=0, keepdims=True)
    sg_s[:, 0:COLS] = sgain[...]
    sg_r[mine] = sg_s[...]

    def ring_slot(d):
        return (0, 1, 2, 3, 4, 7, 6, 5)[d % 8]

    def z_ref(d, h):
        return tg.at[ring_slot(d), pl.ds(h * 64, 64)]

    def z_send(k):
        d = k // 2
        send(z_ref(8 - d, k % 2), z_ref(7 - d, k % 2), z_ss.at[k], z_rs.at[k], dev_zp)
        send(z_ref(d, 1 - k % 2), z_ref(d + 1, 1 - k % 2), z_ss.at[8 + k], z_rs.at[8 + k], dev_zm)

    def z_got(k):
        up, down = z_ref(-(k // 2) + 7, k % 2), z_ref(k // 2 + 1, 1 - k % 2)
        arrive(up, z_ss.at[k], z_rs.at[k])
        arrive(down, z_ss.at[8 + k], z_rs.at[8 + k])

    def z_step(k):
        z_got(k)
        if k + 2 < 7:
            z_send(k + 2)

    def small_send(i, k, dev):
        slot = ag.order[i]
        send(sg_r.at[slot], sg_r.at[slot], sm_ss.at[k], sm_rs.at[k], dev)

    def small_got(i, k):
        arrive(sg_r.at[ag.order[i]], sm_ss.at[k], sm_rs.at[k])

    def docs_send(d, k, dev):
        ref = docs_z.at[(z + d) % 8]
        send(ref, ref, dc_ss.at[k], dc_rs.at[k], dev)

    def docs_step(k):
        arrive(docs_z.at[(z + 7 - k) % 8], dc_ss.at[k], dc_rs.at[k])
        if k < 3:
            arrive(docs_z.at[(z + 1 + k) % 8], dc_ss.at[4 + k], dc_rs.at[4 + k])
            docs_send(7 - k, k + 1, dev_zp)
            if k < 2:
                docs_send(1 + k, k + 5, dev_zm)
        else:
            send(docs_z, docs_o, dc_ss.at[8], dc_rs.at[8], dev_yl)

    small_send(0, 0, dev_yo)
    small_send(0, 1, dev_xp)
    small_send(0, 2, dev_xm)
    ag.begin(1)
    docs_send(0, 0, dev_zp)
    docs_send(0, 4, dev_zm)
    z_send(0)
    pj_send(0)
    lax.fori_loop(0, 8, wkv_go, 0)
    l_wq = load(wq_h.at[:, c], wq.at[:, c], 3)
    lax.fori_loop(0, 8, w_go, 0)
    z_send(1)
    l_pj = load(pj_h, pj.at[yl], 4)

    entry = lax.broadcasted_iota(jnp.int32, (64, ROWS), 0).astype(F32)
    position = (s * ROWS + lax.broadcasted_iota(jnp.int32, (64, ROWS), 1)).astype(F32)
    angle = position * jnp.exp(-math.log(500000.0) * (2.0 * entry / HEAD_DIM))
    cos_t[...] = jnp.cos(angle)
    sin_t[...] = jnp.sin(angle)

    def process(slots, first=False):
        blocks, w = [], []
        for slot in slots:
            parts = []
            for i in range(4):
                cols = slice(i * 128, (i + 1) * 128)
                f = hb[slot, :, cols].astype(F32)
                parts.append((f * scale_v[...] * sg_r[slot][:, cols]).astype(BF16))
            blocks.append(jnp.concatenate(parts, axis=1))
        n = jnp.concatenate(blocks, axis=1)
        for slot in slots:
            w_got(slot)
            w.append(wkv[slot].reshape(128, COLS))
        kv = nt_dot(jnp.concatenate(w, axis=1), n)
        for core in range(2):
            w = jnp.concatenate([wq[slot, core] for slot in slots], axis=0)
            q = jnp.dot(n, w, preferred_element_type=F32)
            k = kv[core * 64:core * 64 + 64]
            q_acc[core] = q if first else q_acc[core] + q
            kv_acc[core] = k if first else kv_acc[core] + k

    small_got(1, 1)
    small_send(1, 3, dev_xp)
    small_got(2, 2)
    small_got(3, 0)
    small_send(3, 4, dev_xp)
    small_send(3, 5, dev_xm)
    docs_step(0)
    ag.near_relay()
    pj_send(1)
    small_got(6, 3)
    docs_step(1)
    small_got(4, 4)
    small_send(4, 6, dev_xp)
    small_got(5, 5)
    ag.near_rest()
    ag.opp_half(0)
    z_step(0)
    pj_send(2)
    small_got(7, 6)
    sums = sg_r[0][:, COLS:COLS + 256]
    for i in range(1, 8):
        sums = sums + sg_r[i][:, COLS:COLS + 256]
    sum_s[...] = sums
    send(sum_s, sum_r, x_ss.at[2], x_rs.at[2], sib)
    docs_step(2)
    ag.opp_half(1)
    pj_send(3)
    arrive(sum_r, x_ss.at[2], x_rs.at[2])
    sums = sum_s[...] + sum_r[...]
    ts_v[...] = jnp.broadcast_to(lax.rsqrt(sums[:, 0:128] / DT + 1e-05), (ROWS, 128)).T
    scale_v[...] = jnp.broadcast_to(lax.rsqrt(sums[:, 128:256] / DS + 1e-05), (ROWS, 128)).T
    docs_step(3)
    z_step(1)
    ag.onear_a()
    pj_send(4)
    l_wq.wait()
    process([mine] + ag.near, True)
    ag.onear_b()
    pj_send(5)
    z_step(2)
    ag.far_step()
    process([ag.opp, ag.far[0]])
    pj_send(6)
    ag.onear_rest()
    process(ag.onear)
    pj_send(7)
    z_step(3)
    ag.ofar_step()
    process([ag.far[1]])
    send(kv_acc.at[1 - c], kv_in, x_ss.at[3], x_rs.at[3], sib)
    send(q_acc.at[1 - c], q_in, x_ss.at[4], x_rs.at[4], sib)
    arrive(kv_in, x_ss.at[3], x_rs.at[3])

    row = lax.broadcasted_iota(jnp.int32, (64, 64), 0)
    col = lax.broadcasted_iota(jnp.int32, (64, 64), 1)
    take = ((row >> 3) & 1) * 32 + (row & 7) * 4 + (row >> 4)
    pick = jnp.where(col == take, 1.0, 0.0).astype(BF16)
    kv_mine = (kv_acc[c] + kv_in[...]).astype(BF16)
    kvx_s[...] = jnp.dot(pick, kv_mine, preferred_element_type=F32).astype(BF16).reshape(4, 16, 128)
    kvx_r[t] = kvx_s[t // 4]

    def kvx(k):
        to = (t + k) % 16
        return copy(kvx_s.at[to // 4], kvx_r.at[t], kx_ss.at[k], kx_rs.at[k], (s, to))

    def kvx_go(k, carry):
        kvx(k).start()
        return carry

    def kvx_got(k, carry):
        arrive(kvx_r.at[(t + 16 - k) % 16], kx_ss.at[k], kx_rs.at[k])
        return carry

    def kvx_end(k, carry):
        kvx(k).wait_send()
        return carry

    lax.fori_loop(1, 16, kvx_go, 0)
    z_step(4)

    cos2 = jnp.concatenate([cos_t[...], cos_t[...]], axis=0).T
    sin2 = jnp.concatenate([-sin_t[...], sin_t[...]], axis=0).T
    arrive(q_in, x_ss.at[4], x_rs.at[4])
    q_mine = q_acc[c] + q_in[...]
    for h in range(2):
        qh = q_mine[:, h * 128:(h + 1) * 128]
        turned = qh * cos2 + pltpu.roll(qh, 64, 1) * sin2
        q_v[h] = (turned * HEAD_DIM ** (-0.5)).astype(BF16)

    lax.fori_loop(1, 16, kvx_got, 0)
    both = kvx_r[...].astype(F32).reshape(16, 2, 8, ROWS)
    k_raw = both[:, 0].reshape(HEAD_DIM, ROWS)
    v_raw = both[:, 1].reshape(HEAD_DIM, ROWS)
    first, second = k_raw[0:64], k_raw[64:128]
    k_rot = jnp.concatenate(
        [first * cos_t[...] - second * sin_t[...], second * cos_t[...] + first * sin_t[...]], axis=0
    )
    kv_own[0] = k_rot.astype(BF16)
    kv_own[1] = v_raw.T.astype(BF16)
    kv_r[0, 0] = kv_own[0]
    kv_r[1, 0] = kv_own[1]

    def kv_copy(k):
        return copy(kv_own.at[c], kv_r.at[c, k], kv_ss.at[k], kv_rs.at[k], ((s + k) % 16, t))

    def kv_fwd(k):
        return copy(kv_r.at[c, k], kv_r.at[c, k], kf_ss.at[k], kf_rs.at[k], sib)

    def kv_go(k):
        @pl.when(s + k < 16)
        def _():
            kv_copy(k).start()

    def kv_mid(k):
        @pl.when(s >= k)
        def _():
            arrive(kv_r.at[c, k], kv_ss.at[k], kv_rs.at[k])
            kv_fwd(k).start()

    def kv_got(k, carry):
        @pl.when(s >= k)
        def _():
            arrive(kv_r.at[1 - c, k], kf_ss.at[k], kf_rs.at[k])
        return carry

    def kv_end(k, carry):
        @pl.when(s >= k)
        def _():
            kv_fwd(k).wait_send()

        @pl.when(s + k < 16)
        def _():
            kv_copy(k).wait_send()
        return carry

    arrive(docs_o, dc_ss.at[8], dc_rs.at[8])
    for k in range(1, BACK + 1):
        kv_go(k)

    def docs_back(j):
        at = (z + 8 - j) % 8
        return jnp.where(z >= j, docs_z[at], jnp.where(yl == 1, docs_o[at], -1))

    key_doc = jnp.concatenate([docs_back(j) for j in range(BACK + 1)], axis=1)
    row_doc = jnp.broadcast_to(docs[...].astype(F32), (ROWS, ROWS)).T[:, 0:1].astype(jnp.int32)
    wide = (ROWS, (BACK + 1) * ROWS)
    row_at = lax.broadcasted_iota(jnp.int32, wide, 0)
    key_at = lax.broadcasted_iota(jnp.int32, wide, 1)
    allowed = (key_doc == row_doc) & ((key_at >= ROWS) | (key_at <= row_at))
    bias[...] = jnp.where(allowed, 0.0, -1e30)

    class Reduce:
        def __init__(self, y_order, own, sib_s, sib_r, x2, ra, rb, xp, xm, fm, fp, ys, yr, fin, ss, rs):
            self.own, self.sib_s, self.sib_r = own, sib_s, sib_r
            self.x2, self.ra, self.rb, self.xp, self.xm, self.fm, self.fp = x2, ra, rb, xp, xm, fm, fp
            self.ys, self.yr, self.fin, self.ss, self.rs = ys, yr, fin, ss, rs
            self.y_order = y_order
            self.x_order = (xf_, xp_, xm_, x)

        def go(self, src, dst, k, dev):
            send(src, dst, self.ss.at[k], self.rs.at[k], dev)

        def got(self, dst, k):
            arrive(dst, self.ss.at[k], self.rs.at[k])

        def slot(self, k, i):
            return self.y_order[i] * 4 + self.x_order[k]

        def to_sib(self, k, i):
            slot = self.slot(k, i)
            self.go(self.sib_s.at[slot], self.sib_r.at[slot], k * 2 + i, sib)

        def sib_got(self, k, i):
            if self.sib_r is not None:
                self.got(self.sib_r.at[self.slot(k, i)], k * 2 + i)

        def pair(self, k, i, h):
            slot, rows = self.slot(k, i), slice(h * 64, h * 64 + 64)
            value = self.own[slot, rows]
            return value if self.sib_r is None else value + self.sib_r[slot, rows].astype(F32)

        def far(self, i):
            self.sib_got(0, i)
            self.x2[i, 0:64] = self.pair(0, i, 0).astype(BF16)
            self.go(self.x2.at[i, pl.ds(0, 64)], self.ra.at[i], 8 + i, dev_xp)
            self.x2[i, 64:128] = self.pair(0, i, 1).astype(BF16)
            self.go(self.x2.at[i, pl.ds(64, 64)], self.rb.at[i], 10 + i, dev_xm)

        def near(self, i):
            self.sib_got(1, i)
            self.xp[i, 64:128] = self.pair(1, i, 1).astype(BF16)
            self.go(self.xp.at[i, pl.ds(64, 64)], self.fm.at[i, pl.ds(64, 64)], 12 + i, dev_xp)
            self.sib_got(2, i)
            self.xm[i, 0:64] = self.pair(2, i, 0).astype(BF16)
            self.go(self.xm.at[i, pl.ds(0, 64)], self.fp.at[i, pl.ds(0, 64)], 14 + i, dev_xm)

        def relay(self, i):
            self.got(self.ra.at[i], 8 + i)
            self.xp[i, 0:64] = (self.pair(1, i, 0) + self.ra[i].astype(F32)).astype(BF16)
            self.go(self.xp.at[i, pl.ds(0, 64)], self.fm.at[i, pl.ds(0, 64)], 16 + i, dev_xp)
            self.got(self.rb.at[i], 10 + i)
            self.xm[i, 64:128] = (self.pair(2, i, 1) + self.rb[i].astype(F32)).astype(BF16)
            self.go(self.xm.at[i, pl.ds(64, 64)], self.fp.at[i, pl.ds(64, 64)], 18 + i, dev_xm)

        def join(self, i, h):
            rows, at = slice(h * 64, h * 64 + 64), pl.ds(h * 64, 64)
            if h == 0:
                self.sib_got(3, i)
            self.got(self.fm.at[i, at], (16, 12)[h] + i)
            self.got(self.fp.at[i, at], (14, 18)[h] + i)
            return self.pair(3, i, h) + self.fm[i, rows].astype(F32) + self.fp[i, rows].astype(F32)

        def join_one(self, i):
            mine = self.y_order[i] == yh
            for h in range(2):
                rows = slice(h * 64, h * 64 + 64)
                value = self.join(i, h)

                @pl.when(mine)
                def _():
                    self.fin[rows] = value

                @pl.when(jnp.logical_not(mine))
                def _():
                    self.ys[rows] = value.astype(BF16)
                    self.to_opp(h).start()

        def to_opp(self, h):
            at = pl.ds(h * 64, 64)
            return copy(self.ys.at[at], self.yr.at[at], self.ss.at[20 + h], self.rs.at[20 + h], dev_yo)

        def join_other(self):
            for h in range(2):
                self.ys[h * 64:h * 64 + 64] = self.join(0, h).astype(BF16)
                self.to_opp(h).start()

        def join_mine(self):
            for h in range(2):
                self.fin[h * 64:h * 64 + 64] = self.join(1, h)

        def end(self):
            for h in range(2):
                self.to_opp(h).wait_send()

        def last(self, h):
            rows = slice(h * 64, h * 64 + 64)
            self.got(self.yr.at[pl.ds(h * 64, 64)], 20 + h)
            return self.fin[rows] + self.yr[rows].astype(F32)

    rt = Reduce((yl, 1 - yl), t_own, t_sib_s, t_sib_r, t_x2, t_ra, t_rb, t_xp, t_xm, t_fm, t_fp, t_ys, t_yr, t_fin, t_ss, t_rs)

    z_step(5)
    z_step(6)

    def products(core, y_, k, width):
        rows = tg[pl.ds(core * 4, 4), :, k * width:(k + 1) * width].reshape(4 * ROWS, width)
        return jnp.dot(rows, pj[y_, k * width:(k + 1) * width], preferred_element_type=F32).reshape(4, ROWS, COLS)

    l_pj.wait()
    first = pl.ds(yl * 4, 4)
    t_sib_s[first] = products(1 - c, yl, 0, 1024).astype(BF16)
    for k in range(4):
        rt.to_sib(k, 0)
    t_own[first] = products(c, yl, 0, 1024)
    rt.far(0)
    rt.near(0)
    lax.fori_loop(0, 8, wo_fetch, 0)
    lax.fori_loop(0, 8, wo_go, 0)

    other = pl.ds((1 - yl) * 4, 4)
    for k in range(4):
        for part in (2 * k, 2 * k + 1):
            arrive(pj.at[1 - yl, pl.ds(part * 128, 128)], p_ss.at[part], p_rs.at[part])
        theirs = products(1 - c, 1 - yl, k, 256)
        if k == 0:
            t_part[...] = theirs
        elif k < 3:
            t_part[...] += theirs
        else:
            t_sib_s[other] = (t_part[...] + theirs).astype(BF16)
            for j in range(4):
                rt.to_sib(j, 1)
        if k == 0:
            t_own[other] = products(c, 1 - yl, k, 256)
        else:
            t_own[other] += products(c, 1 - yl, k, 256)
        if k == 1:
            rt.relay(0)
    rt.far(1)
    rt.near(1)
    rt.join_one(0)
    for k in (1, 2, 3, 4):
        kv_mid(k)
    rt.relay(1)
    for k in (5, 6, 7, 8):
        kv_mid(k)

    lax.fori_loop(1, BACK + 1, kv_got, 0)
    keys = jnp.concatenate([kv_r[0, j] for j in range(BACK + 1)], axis=1)
    values = kv_r[1].reshape((BACK + 1) * ROWS, HEAD_DIM)
    for h in range(2):
        scores = jnp.dot(q_v[h], keys, preferred_element_type=F32)
        scores = scores + bias[...]
        probs = jnp.exp(scores - jnp.max(scores, axis=1, keepdims=True))
        total = jnp.sum(probs, axis=1, keepdims=True)
        acc = jnp.dot(probs.astype(BF16), values, preferred_element_type=F32)
        attn_v[c * 2 + h] = (acc / total).astype(BF16)
        send(attn_v.at[c * 2 + h], attn_v.at[c * 2 + h], x_ss.at[5 + h], x_rs.at[5 + h], sib)
    lax.fori_loop(0, 8, wo_got, 0)

    ro = Reduce((yo_, yh), o_own, None, None, o_x2, o_ra, o_rb, o_xp, o_xm, o_fm, o_fp, o_ys, o_yr, o_fin, o_ss, o_rs)

    for h in range(2):
        arrive(attn_v.at[2 - 2 * c + h], x_ss.at[5 + h], x_rs.at[5 + h])
    attn = jnp.concatenate([attn_v[i] for i in range(4)], axis=1)

    def out_block(k, i):
        slot = ro.slot(k, i)
        o_own[slot] = jnp.dot(attn, wo[slot].reshape(COLS, COLS), preferred_element_type=F32)

    out_block(0, 0)
    ro.far(0)
    rt.join_one(1)
    out_block(1, 0)
    out_block(2, 0)
    ro.near(0)
    out_block(0, 1)
    ro.relay(0)
    ro.far(1)
    out_block(1, 1)
    out_block(2, 1)
    ro.near(1)
    out_block(3, 0)
    out_block(3, 1)
    ro.relay(1)

    def t3(h):
        at = pl.ds(h * 64, 64)
        return copy(t3_s.at[at], t3_r.at[at], t3_ss.at[h], t3_rs.at[h], dev_t3)

    for h in range(2):
        rows = slice(h * 64, h * 64 + 64)
        t3_s[rows] = rt.last(h).astype(BF16)

        @pl.when(stays)
        def _():
            t3_r[rows] = t3_s[rows]

        @pl.when(jnp.logical_not(stays))
        def _():
            t3(h).start()

    ro.join_other()
    ro.join_mine()

    def before_end():
        flush()
        lax.fori_loop(0, 8, w_end, 0)
        lax.fori_loop(0, 8, wo_end, 0)
        lax.fori_loop(1, 16, kvx_end, 0)
        lax.fori_loop(1, BACK + 1, kv_end, 0)
        rt.end()
        ro.end()

        @pl.when(jnp.logical_not(stays))
        def _():
            t3(0).wait_send()
            t3(1).wait_send()

    dg = Gather(db, dg_ss, dg_rs)
    for h in range(2):
        rows = slice(h * 64, h * 64 + 64)
        mixed = hb[mine, rows].astype(F32) + ro.last(h)
        out_s[rows] = mixed.astype(BF16)

        @pl.when(jnp.logical_not(stays))
        def _():
            arrive(t3_r.at[pl.ds(h * 64, 64)], t3_ss.at[h], t3_rs.at[h])

        target = t3_r[rows].astype(F32) * jnp.concatenate([ts_v[rows]] * 4, axis=1)
        difference = mixed - target
        db[mine, rows] = difference.astype(BF16)
        dg.begin(h)
        squares = difference * difference
        l_v[rows] = (
            squares[:, 0:128] + squares[:, 128:256] + squares[:, 256:384] + squares[:, 384:512]
        )
    l_s[...] = jnp.sum(l_v[...].T, axis=0, keepdims=True)
    l_r[t] = l_s[...]

    def loss(k):
        return copy(l_s, l_r.at[t], l_ss.at[k], l_rs.at[k], (s, (t + k) % 16))

    def loss_go(k, carry):
        loss(k).start()
        return carry

    def loss_got(k, carry):
        arrive(l_r.at[(t + 16 - k) % 16], l_ss.at[k], l_rs.at[k])
        return carry

    def loss_end(k, carry):
        loss(k).wait_send()
        return carry

    lax.fori_loop(1, 16, loss_go, 0)

    def add_grad(slots, first=False):
        d = jnp.concatenate([db[slot] for slot in slots], axis=1)
        for core in range(2):
            w = jnp.concatenate([wo[slot, core] for slot in slots], axis=1)
            g = nt_dot(d, w)
            g_acc[core] = g if first else g_acc[core] + g

    dg.near_relay()
    dg.opp_half(0)
    dg.near_rest()
    before_end()
    add_grad([mine] + dg.near, True)
    dg.opp_half(1)
    dg.onear_a()
    dg.far_step()
    add_grad([dg.opp, dg.far[0]])
    dg.onear_b()
    dg.onear_rest()
    add_grad(dg.onear)
    lax.fori_loop(1, 16, loss_got, 0)
    loss_sum = l_r[0]
    for i in range(1, 16):
        loss_sum = loss_sum + l_r[i]
    out_l[...] = loss_sum / DS
    dg.ofar_step()
    add_grad([dg.far[1]])
    send(g_acc.at[1 - c], g_in, x_ss.at[7], x_rs.at[7], sib)
    arrive(g_in, x_ss.at[7], x_rs.at[7])
    out_g[...] = (g_acc[c] + g_in[...]).astype(BF16)

    flush()
    lax.fori_loop(1, 16, loss_end, 0)


def reduce_buffers():
    block = (ROWS, COLS)
    return [
        pltpu.VMEM((2, 64, COLS), BF16),
        pltpu.VMEM((2, 64, COLS), BF16),
        pltpu.VMEM((2,) + block, BF16),
        pltpu.VMEM((2,) + block, BF16),
        pltpu.VMEM((2,) + block, BF16),
        pltpu.VMEM((2,) + block, BF16),
        pltpu.VMEM(block, BF16),
        pltpu.VMEM(block, BF16),
        pltpu.VMEM(block, F32),
    ]


def on_device(
    teacher_hidden, teacher_gain, projector, student_hidden, student_gain,
    query_weight, kv_weight, out_weight, doc_ids,
):
    block = (ROWS, COLS)
    hbm = pl.BlockSpec(memory_space=pltpu.HBM)
    vmem = pl.BlockSpec(memory_space=pltpu.VMEM)
    dma = pltpu.SemaphoreType.DMA
    out_s, out_l, out_g = pl.pallas_call(
        body,
        out_shape=(
            jax.ShapeDtypeStruct(block, BF16),
            jax.ShapeDtypeStruct((1, ROWS), F32),
            jax.ShapeDtypeStruct((ROWS, 256), BF16),
        ),
        in_specs=[hbm] * 9,
        out_specs=(vmem, vmem, vmem),
        scratch_shapes=[
            pltpu.VMEM((1, 1024), F32),
            pltpu.VMEM((1, COLS), F32),
            pltpu.VMEM((1, ROWS), jnp.int32),
            pltpu.VMEM((ROWS, 1024), BF16),
            pltpu.VMEM((8, ROWS, 1024), BF16),
            pltpu.VMEM((2, 1024, COLS), BF16),
            pltpu.VMEM((8, 2, COLS, 256), BF16),
            pltpu.VMEM((8, 2, 2, 32, COLS), BF16),
            pltpu.VMEM((8, 2, 256, COLS), BF16),
            pltpu.VMEM((64, ROWS), F32),
            pltpu.VMEM((64, ROWS), F32),
            pltpu.VMEM((8,) + block, BF16),
            pltpu.VMEM((1, 768), F32),
            pltpu.VMEM((8, 1, 768), F32),
            pltpu.VMEM((1, 256), F32),
            pltpu.VMEM((1, 256), F32),
            pltpu.VMEM((ROWS, 128), F32),
            pltpu.VMEM((2, ROWS, 256), F32),
            pltpu.VMEM((ROWS, 256), F32),
            pltpu.VMEM((2, 64, ROWS), F32),
            pltpu.VMEM((64, ROWS), F32),
            pltpu.VMEM((4, 16, ROWS), BF16),
            pltpu.VMEM((16, 16, ROWS), BF16),
            pltpu.VMEM((2, ROWS, HEAD_DIM), BF16),
            pltpu.VMEM((2, BACK + 1, ROWS, HEAD_DIM), BF16),
            pltpu.VMEM((8, 1, ROWS), jnp.int32),
            pltpu.VMEM((8, 1, ROWS), jnp.int32),
            pltpu.VMEM((2, ROWS, HEAD_DIM), BF16),
            pltpu.VMEM((4, ROWS, HEAD_DIM), BF16),
            pltpu.VMEM((ROWS, (BACK + 1) * ROWS), F32),
            pltpu.VMEM((8,) + block, F32),
            pltpu.VMEM((4,) + block, F32),
            pltpu.VMEM((8,) + block, F32),
            pltpu.VMEM((2,) + block, BF16),
            pltpu.VMEM((8,) + block, BF16),
            pltpu.VMEM((8,) + block, BF16),
            pltpu.VMEM((2,) + block, BF16),
            *reduce_buffers(),
            *reduce_buffers(),
            pltpu.VMEM(block, BF16),
            pltpu.VMEM(block, BF16),
            pltpu.VMEM((ROWS, 128), F32),
            pltpu.VMEM((8,) + block, BF16),
            pltpu.VMEM((2, ROWS, 256), F32),
            pltpu.VMEM((ROWS, 256), F32),
            pltpu.VMEM((ROWS, 128), F32),
            pltpu.VMEM((1, ROWS), F32),
            pltpu.VMEM((16, 1, ROWS), F32),
            dma((10,)),
            *[dma((8,)) for _ in range(10)],
            dma((16,)), dma((16,)), dma((8,)), dma((8,)),
            dma((24,)), dma((24,)), dma((24,)), dma((24,)),
            dma((16,)), dma((16,)), dma((16,)), dma((16,)),
            dma((9,)), dma((9,)), dma((9,)), dma((9,)), dma((9,)), dma((9,)),
            dma((24,)), dma((24,)), dma((24,)), dma((24,)),
            dma((2,)), dma((2,)),
            dma((16,)), dma((16,)),
        ],
        compiler_params=pltpu.CompilerParams(
            collective_id=0, has_side_effects=True, vmem_limit_bytes=40 * 1024 * 1024
        ),
    )(
        *(
            pltpu.with_memory_space_constraint(one, pltpu.HBM)
            for one in (
                teacher_hidden, teacher_gain.reshape(1, -1), projector, student_hidden,
                student_gain.reshape(1, -1), query_weight.reshape(8, 2, COLS, 256), jnp.transpose(kv_weight, (0, 2, 1)),
                out_weight, doc_ids.reshape(1, -1),
            )
        )
    )
    return out_s, out_l.reshape(ROWS), out_g


def solution(mesh):
    in_specs = (
        P("seq", "tensor"),
        P("tensor"),
        P("tensor", "seq"),
        P("seq", "tensor"),
        P("tensor"),
        P(None, "tensor"),
        P(None, None, "tensor"),
        P("tensor", None),
        P("seq"),
    )
    out_specs = (P("seq", "tensor"), P("seq"), P("seq", "tensor"))
    return jax.shard_map(
        on_device, mesh=mesh, in_specs=in_specs, out_specs=out_specs, check_vma=False
    )
```

```python
import math

import jax
import jax.numpy as jnp
from jax import lax
from jax.experimental import pallas as pl
from jax.experimental.pallas import tpu as pltpu
from jax.sharding import PartitionSpec as P

DT = 16384
DS = 8192
HEAD_DIM = 128
HEADS = 32
KV_HEADS = 4
ROWS = 128
COLS = 512
BACK = 8
F32 = jnp.float32
BF16 = jnp.bfloat16
MESH = pl.DeviceIdType.MESH
NT = (((1,), (1,)), ((), ()))


def nt_dot(a, b):
    return lax.dot_general(a, b, NT, preferred_element_type=F32)


def body(
    th_h, tgain_h, pj_h, sh_h, sgain_h, wq_h, wkv_h, wo_h, docs_h,
    out_s, out_l, out_g,
    tgain, sgain, docs, th_v, tg, pj, wq, wkv, wo, cos_t, sin_t,
    hb, sg_s, sg_r, sum_s, sum_r, scale_v, q_acc, q_in, kv_acc, kv_in,
    kvx_s, kvx_r, kv_own, kv_r, docs_z, docs_o, q_v, attn_v, bias,
    t_own, t_part, o_own, o_x2, t_sib_s, t_sib_r, t_x2, t_ra, t_rb, t_xp, t_xm, t_fm, t_fp, t_ys, t_yr, t_fin,
    o_ra, o_rb, o_xp, o_xm, o_fm, o_fp, o_ys, o_yr, o_fin,
    t3_s, t3_r, ts_v, db, g_acc, g_in, l_v, l_s, l_r,
    load_sem, w_load, w_ss, w_rs, v_load, v_ss, v_rs, u_ss, u_rs, x_ss, x_rs, z_ss, z_rs, p_ss, p_rs,
    ag_ss, ag_rs, dg_ss, dg_rs, sm_ss, sm_rs, kx_ss, kx_rs, kv_ss, kv_rs, kf_ss, kf_rs, dc_ss, dc_rs,
    t_ss, t_rs, o_ss, o_rs, t3_ss, t3_rs, l_ss, l_rs,
):
    s = lax.axis_index("seq")
    t = lax.axis_index("tensor")
    yl, z = s // 8, s % 8
    yh, x, c = t // 8, (t // 2) % 4, t % 2

    def tid(y_, x_, c_):
        return y_ * 8 + x_ * 2 + c_

    xp_, xm_ = (x + 1) % 4, (x + 3) % 4
    xf_ = (x + 2) % 4
    yo_ = 1 - yh
    sib = (s, tid(yh, x, 1 - c))
    dev_xp = (s, tid(yh, xp_, c))
    dev_xm = (s, tid(yh, xm_, c))
    dev_yo = (s, tid(yo_, x, c))
    dev_zp = (yl * 8 + (z + 1) % 8, t)
    dev_zm = (yl * 8 + (z + 7) % 8, t)
    dev_yl = ((1 - yl) * 8 + z, t)
    turn = jnp.where(c == 0, x, jnp.where(x == 0, 4, 8 - x))
    dev_t3 = (yl * 8 + (z + turn) % 8, yh * 8 + z)
    stays = (z == 0) & (x == 0) & (c == 0)

    started = []

    def copy(src, dst, ss, rs, dev):
        return pltpu.make_async_remote_copy(
            src_ref=src, dst_ref=dst, send_sem=ss, recv_sem=rs, device_id=dev, device_id_type=MESH
        )

    def send(src, dst, ss, rs, dev):
        one = copy(src, dst, ss, rs, dev)
        one.start()
        started.append(one)

    def flush():
        for one in started:
            one.wait_send()
        started.clear()

    def arrive(dst, ss, rs):
        copy(dst, dst, ss, rs, sib).wait_recv()

    def load(src, dst, k):
        one = pltpu.make_async_copy(src, dst, load_sem.at[k])
        one.start()
        return one

    l_th = load(th_h, th_v, 0)
    mine = yh * 4 + x
    l_sh = load(sh_h, hb.at[mine], 1)
    l_small = [load(tgain_h, tgain, 7), load(sgain_h, sgain, 8), load(docs_h, docs, 9)]

    def wkv_part(j, core):
        return wkv_h.at[:, :, pl.ds(pl.multiple_of((j * 2 + core) * COLS, COLS), COLS)]

    def wkv_load(j):
        return pltpu.make_async_copy(wkv_part(j, c), wkv.at[j, c], v_load.at[j])

    def wkv_go(j, carry):
        wkv_load(j).start()
        return carry

    def wo_part(j, core):
        return wo_h.at[:, pl.ds(pl.multiple_of((j * 2 + core) * COLS, COLS), COLS)]

    def wo_load(j):
        return pltpu.make_async_copy(wo_part(j, c), wo.at[j, c], w_load.at[j])

    def wo_send(j):
        return copy(wo_part(j, 1 - c), wo.at[j, c], w_ss.at[j], w_rs.at[j], sib)

    def wo_fetch(j, carry):
        wo_load(j).start()
        return carry

    def wo_go(j, carry):
        wo_send(j).start()
        return carry

    def wo_got(j, carry):
        wo_load(j).wait()
        arrive(wo.at[j, 1 - c], w_ss.at[j], w_rs.at[j])
        return carry

    def wo_end(j, carry):
        wo_send(j).wait_send()
        return carry

    lax.fori_loop(0, 8, wkv_go, 0)
    l_wq = load(wq_h.at[:, c], wq.at[:, c], 3)

    kv_r[...] = jnp.zeros(kv_r.shape, BF16)

    barrier = pltpu.get_barrier_semaphore()
    for dev in (sib, dev_xp, dev_xm, dev_yo, dev_zp, dev_zm, dev_yl):
        pl.semaphore_signal(barrier, inc=1, device_id=dev, device_id_type=MESH)

    class Gather:
        def __init__(self, buf, ss, rs):
            self.buf, self.ss, self.rs = buf, ss, rs
            self.near = [yh * 4 + xm_, yh * 4 + xp_]
            self.opp = yo_ * 4 + x
            self.onear = [yo_ * 4 + xm_, yo_ * 4 + xp_]
            self.far = [yh * 4 + xf_, yo_ * 4 + xf_]
            self.order = [mine] + self.near + [self.opp] + self.onear + self.far

        def part(self, slot, h):
            return self.buf.at[slot, pl.ds(h * 64, 64)]

        def half(self, slot, h, k, dev):
            part = self.part(slot, h)
            send(part, part, self.ss.at[k], self.rs.at[k], dev)

        def got_half(self, slot, h, k):
            arrive(self.part(slot, h), self.ss.at[k], self.rs.at[k])

        def begin(self, h):
            self.half(mine, h, 0 + h, dev_yo)
            self.half(mine, h, 2 + h, dev_xp)
            self.half(mine, h, 4 + h, dev_xm)

        def near_relay(self):
            self.got_half(self.near[0], 0, 2)
            self.half(self.near[0], 0, 6, dev_xp)
            self.got_half(self.near[1], 1, 5)
            self.half(self.near[1], 1, 7, dev_xm)

        def near_rest(self):
            self.got_half(self.near[0], 1, 3)
            self.got_half(self.near[1], 0, 4)

        def opp_half(self, h):
            self.got_half(self.opp, h, 0 + h)
            self.half(self.opp, h, 8 + h, dev_xp)
            self.half(self.opp, h, 10 + h, dev_xm)

        def onear_a(self):
            self.got_half(self.onear[0], 0, 8)
            self.half(self.onear[0], 0, 12, dev_xp)

        def onear_b(self):
            self.got_half(self.onear[1], 1, 11)
            self.half(self.onear[1], 1, 13, dev_xm)

        def onear_rest(self):
            self.got_half(self.onear[0], 1, 9)
            self.got_half(self.onear[1], 0, 10)

        def far_step(self):
            self.got_half(self.far[0], 0, 6)
            self.got_half(self.far[0], 1, 7)

        def ofar_step(self):
            self.got_half(self.far[1], 0, 12)
            self.got_half(self.far[1], 1, 13)

    def pj_send(k):
        rows = pl.ds(k * 256, 256)
        send(pj_h.at[rows], pj.at[yl, rows], p_ss.at[k], p_rs.at[k], dev_yl)

    def wkv_send(j):
        return copy(wkv_part(j, 1 - c), wkv.at[j, c], v_ss.at[j], v_rs.at[j], sib)

    def wq_send(j):
        return copy(wq_h.at[j, 1 - c], wq.at[j, c], u_ss.at[j], u_rs.at[j], sib)

    def w_go(j, carry):
        wkv_send(j).start()
        wq_send(j).start()
        return carry

    def w_end(j, carry):
        wkv_send(j).wait_send()
        wq_send(j).wait_send()
        return carry

    def w_got(slot):
        wkv_load(slot).wait()
        arrive(wkv.at[slot, 1 - c], v_ss.at[slot], v_rs.at[slot])
        arrive(wq.at[slot, 1 - c], u_ss.at[slot], u_rs.at[slot])

    ag = Gather(hb, ag_ss, ag_rs)
    l_sh.wait()

    z_slot = 0
    l_th.wait()
    for one in l_small:
        one.wait()
    docs_z[z] = docs[...]
    part = jnp.zeros((ROWS, 128), F32)
    for i in range(8):
        cols = slice(i * 128, (i + 1) * 128)
        f = th_v[:, cols].astype(F32)
        part = part + f * f
        tg[z_slot, :, cols] = (f * tgain[:, cols]).astype(BF16)
    sg_s[:, COLS:COLS + 128] = jnp.sum(part.T, axis=0, keepdims=True)
    part = jnp.zeros((ROWS, 128), F32)
    for i in range(4):
        f = hb[mine, :, i * 128:(i + 1) * 128].astype(F32)
        part = part + f * f
    sg_s[:, COLS + 128:COLS + 256] = jnp.sum(part.T, axis=0, keepdims=True)
    sg_s[:, 0:COLS] = sgain[...]
    sg_r[mine] = sg_s[...]

    def ring_slot(d):
        return (0, 1, 2, 3, 4, 7, 6, 5)[d % 8]

    def z_ref(d, h):
        return tg.at[ring_slot(d), pl.ds(h * 64, 64)]

    def z_send(k):
        d = k // 2
        send(z_ref(8 - d, k % 2), z_ref(7 - d, k % 2), z_ss.at[k], z_rs.at[k], dev_zp)
        send(z_ref(d, 1 - k % 2), z_ref(d + 1, 1 - k % 2), z_ss.at[8 + k], z_rs.at[8 + k], dev_zm)

    def z_got(k):
        up, down = z_ref(-(k // 2) + 7, k % 2), z_ref(k // 2 + 1, 1 - k % 2)
        arrive(up, z_ss.at[k], z_rs.at[k])
        arrive(down, z_ss.at[8 + k], z_rs.at[8 + k])

    def z_step(k):
        z_got(k)
        if k + 2 < 7:
            z_send(k + 2)

    def small_send(i, k, dev):
        slot = ag.order[i]
        send(sg_r.at[slot], sg_r.at[slot], sm_ss.at[k], sm_rs.at[k], dev)

    def small_got(i, k):
        arrive(sg_r.at[ag.order[i]], sm_ss.at[k], sm_rs.at[k])

    def docs_send(d, k, dev):
        ref = docs_z.at[(z + d) % 8]
        send(ref, ref, dc_ss.at[k], dc_rs.at[k], dev)

    def docs_step(k):
        arrive(docs_z.at[(z + 7 - k) % 8], dc_ss.at[k], dc_rs.at[k])
        if k < 3:
            arrive(docs_z.at[(z + 1 + k) % 8], dc_ss.at[4 + k], dc_rs.at[4 + k])
            docs_send(7 - k, k + 1, dev_zp)
            if k < 2:
                docs_send(1 + k, k + 5, dev_zm)
        else:
            send(docs_z, docs_o, dc_ss.at[8], dc_rs.at[8], dev_yl)

    pl.semaphore_wait(barrier, 7)
    small_send(0, 0, dev_yo)
    small_send(0, 1, dev_xp)
    small_send(0, 2, dev_xm)
    ag.begin(0)
    ag.begin(1)
    docs_send(0, 0, dev_zp)
    docs_send(0, 4, dev_zm)
    z_send(0)
    pj_send(0)
    lax.fori_loop(0, 8, w_go, 0)
    z_send(1)
    pj_send(1)
    pj_send(2)
    l_pj = load(pj_h, pj.at[yl], 4)

    entry = lax.broadcasted_iota(jnp.int32, (64, ROWS), 0).astype(F32)
    position = (s * ROWS + lax.broadcasted_iota(jnp.int32, (64, ROWS), 1)).astype(F32)
    angle = position * jnp.exp(-math.log(500000.0) * (2.0 * entry / HEAD_DIM))
    cos_t[...] = jnp.cos(angle)
    sin_t[...] = jnp.sin(angle)

    def process(slots, first=False):
        blocks, w = [], []
        for slot in slots:
            parts = []
            for i in range(4):
                cols = slice(i * 128, (i + 1) * 128)
                f = hb[slot, :, cols].astype(F32)
                parts.append((f * scale_v[...] * sg_r[slot][:, cols]).astype(BF16))
            blocks.append(jnp.concatenate(parts, axis=1))
        n = jnp.concatenate(blocks, axis=1)
        for slot in slots:
            w_got(slot)
            w.append(wkv[slot].reshape(128, COLS))
        kv = nt_dot(jnp.concatenate(w, axis=1), n)
        for core in range(2):
            w = jnp.concatenate([wq[slot, core] for slot in slots], axis=0)
            q = jnp.dot(n, w, preferred_element_type=F32)
            k = kv[core * 64:core * 64 + 64]
            q_acc[core] = q if first else q_acc[core] + q
            kv_acc[core] = k if first else kv_acc[core] + k

    small_got(1, 1)
    small_send(1, 3, dev_xp)
    small_got(2, 2)
    small_got(3, 0)
    small_send(3, 4, dev_xp)
    small_send(3, 5, dev_xm)
    docs_step(0)
    ag.near_relay()
    small_got(6, 3)
    docs_step(1)
    small_got(4, 4)
    small_send(4, 6, dev_xp)
    small_got(5, 5)
    ag.near_rest()
    ag.opp_half(0)
    z_step(0)
    pj_send(3)
    small_got(7, 6)
    sums = sg_r[0][:, COLS:COLS + 256]
    for i in range(1, 8):
        sums = sums + sg_r[i][:, COLS:COLS + 256]
    sum_s[...] = sums
    send(sum_s, sum_r, x_ss.at[2], x_rs.at[2], sib)
    docs_step(2)
    ag.opp_half(1)
    arrive(sum_r, x_ss.at[2], x_rs.at[2])
    sums = sum_s[...] + sum_r[...]
    ts_v[...] = jnp.broadcast_to(lax.rsqrt(sums[:, 0:128] / DT + 1e-05), (ROWS, 128)).T
    scale_v[...] = jnp.broadcast_to(lax.rsqrt(sums[:, 128:256] / DS + 1e-05), (ROWS, 128)).T
    docs_step(3)
    z_step(1)
    ag.onear_a()
    l_wq.wait()
    process([mine] + ag.near, True)
    ag.onear_b()
    z_step(2)
    ag.far_step()
    process([ag.opp, ag.far[0]])
    ag.onear_rest()
    process(ag.onear)
    z_step(3)
    ag.ofar_step()
    process([ag.far[1]])
    send(kv_acc.at[1 - c], kv_in, x_ss.at[3], x_rs.at[3], sib)
    send(q_acc.at[1 - c], q_in, x_ss.at[4], x_rs.at[4], sib)
    arrive(kv_in, x_ss.at[3], x_rs.at[3])

    row = lax.broadcasted_iota(jnp.int32, (64, 64), 0)
    col = lax.broadcasted_iota(jnp.int32, (64, 64), 1)
    take = ((row >> 3) & 1) * 32 + (row & 7) * 4 + (row >> 4)
    pick = jnp.where(col == take, 1.0, 0.0).astype(BF16)
    kv_mine = (kv_acc[c] + kv_in[...]).astype(BF16)
    kvx_s[...] = jnp.dot(pick, kv_mine, preferred_element_type=F32).astype(BF16).reshape(4, 16, 128)
    kvx_r[t] = kvx_s[t // 4]

    def kvx(k):
        to = (t + k) % 16
        return copy(kvx_s.at[to // 4], kvx_r.at[t], kx_ss.at[k], kx_rs.at[k], (s, to))

    def kvx_go(k, carry):
        kvx(k).start()
        return carry

    def kvx_got(k, carry):
        arrive(kvx_r.at[(t + 16 - k) % 16], kx_ss.at[k], kx_rs.at[k])
        return carry

    def kvx_end(k, carry):
        kvx(k).wait_send()
        return carry

    lax.fori_loop(1, 16, kvx_go, 0)
    lax.fori_loop(0, 8, wo_fetch, 0)
    lax.fori_loop(0, 8, wo_go, 0)
    z_step(4)

    cos2 = jnp.concatenate([cos_t[...], cos_t[...]], axis=0).T
    sin2 = jnp.concatenate([-sin_t[...], sin_t[...]], axis=0).T
    arrive(q_in, x_ss.at[4], x_rs.at[4])
    q_mine = q_acc[c] + q_in[...]
    for h in range(2):
        qh = q_mine[:, h * 128:(h + 1) * 128]
        turned = qh * cos2 + pltpu.roll(qh, 64, 1) * sin2
        q_v[h] = (turned * HEAD_DIM ** (-0.5)).astype(BF16)

    lax.fori_loop(1, 16, kvx_got, 0)
    both = kvx_r[...].astype(F32).reshape(16, 2, 8, ROWS)
    k_raw = both[:, 0].reshape(HEAD_DIM, ROWS)
    v_raw = both[:, 1].reshape(HEAD_DIM, ROWS)
    first, second = k_raw[0:64], k_raw[64:128]
    k_rot = jnp.concatenate(
        [first * cos_t[...] - second * sin_t[...], second * cos_t[...] + first * sin_t[...]], axis=0
    )
    kv_own[0] = k_rot.astype(BF16)
    kv_own[1] = v_raw.T.astype(BF16)
    kv_r[0, 0] = kv_own[0]
    kv_r[1, 0] = kv_own[1]

    def kv_copy(k):
        return copy(kv_own.at[c], kv_r.at[c, k], kv_ss.at[k], kv_rs.at[k], ((s + k) % 16, t))

    def kv_fwd(k):
        return copy(kv_r.at[c, k], kv_r.at[c, k], kf_ss.at[k], kf_rs.at[k], sib)

    def kv_go(k):
        @pl.when(s + k < 16)
        def _():
            kv_copy(k).start()

    def kv_mid(k):
        @pl.when(s >= k)
        def _():
            arrive(kv_r.at[c, k], kv_ss.at[k], kv_rs.at[k])
            kv_fwd(k).start()

    def kv_got(k, carry):
        @pl.when(s >= k)
        def _():
            arrive(kv_r.at[1 - c, k], kf_ss.at[k], kf_rs.at[k])
        return carry

    def kv_end(k, carry):
        @pl.when(s >= k)
        def _():
            kv_fwd(k).wait_send()

        @pl.when(s + k < 16)
        def _():
            kv_copy(k).wait_send()
        return carry

    arrive(docs_o, dc_ss.at[8], dc_rs.at[8])
    for k in range(1, BACK + 1):
        kv_go(k)

    def docs_back(j):
        at = (z + 8 - j) % 8
        return jnp.where(z >= j, docs_z[at], jnp.where(yl == 1, docs_o[at], -1))

    key_doc = jnp.concatenate([docs_back(j) for j in range(BACK + 1)], axis=1)
    row_doc = jnp.broadcast_to(docs[...].astype(F32), (ROWS, ROWS)).T[:, 0:1].astype(jnp.int32)
    wide = (ROWS, (BACK + 1) * ROWS)
    row_at = lax.broadcasted_iota(jnp.int32, wide, 0)
    key_at = lax.broadcasted_iota(jnp.int32, wide, 1)
    allowed = (key_doc == row_doc) & ((key_at >= ROWS) | (key_at <= row_at))
    bias[...] = jnp.where(allowed, 0.0, -1e30)

    class Reduce:
        def __init__(self, y_order, own, sib_s, sib_r, x2, ra, rb, xp, xm, fm, fp, ys, yr, fin, ss, rs):
            self.own, self.sib_s, self.sib_r = own, sib_s, sib_r
            self.x2, self.ra, self.rb, self.xp, self.xm, self.fm, self.fp = x2, ra, rb, xp, xm, fm, fp
            self.ys, self.yr, self.fin, self.ss, self.rs = ys, yr, fin, ss, rs
            self.y_order = y_order
            self.x_order = (xf_, xp_, xm_, x)

        def go(self, src, dst, k, dev):
            send(src, dst, self.ss.at[k], self.rs.at[k], dev)

        def got(self, dst, k):
            arrive(dst, self.ss.at[k], self.rs.at[k])

        def slot(self, k, i):
            return self.y_order[i] * 4 + self.x_order[k]

        def to_sib(self, k, i):
            slot = self.slot(k, i)
            self.go(self.sib_s.at[slot], self.sib_r.at[slot], k * 2 + i, sib)

        def sib_got(self, k, i):
            if self.sib_r is not None:
                self.got(self.sib_r.at[self.slot(k, i)], k * 2 + i)

        def pair(self, k, i, h):
            slot, rows = self.slot(k, i), slice(h * 64, h * 64 + 64)
            value = self.own[slot, rows]
            return value if self.sib_r is None else value + self.sib_r[slot, rows].astype(F32)

        def far(self, i):
            self.sib_got(0, i)
            self.x2[i, 0:64] = self.pair(0, i, 0).astype(BF16)
            self.go(self.x2.at[i, pl.ds(0, 64)], self.ra.at[i], 8 + i, dev_xp)
            self.x2[i, 64:128] = self.pair(0, i, 1).astype(BF16)
            self.go(self.x2.at[i, pl.ds(64, 64)], self.rb.at[i], 10 + i, dev_xm)

        def near(self, i):
            self.sib_got(1, i)
            self.xp[i, 64:128] = self.pair(1, i, 1).astype(BF16)
            self.go(self.xp.at[i, pl.ds(64, 64)], self.fm.at[i, pl.ds(64, 64)], 12 + i, dev_xp)
            self.sib_got(2, i)
            self.xm[i, 0:64] = self.pair(2, i, 0).astype(BF16)
            self.go(self.xm.at[i, pl.ds(0, 64)], self.fp.at[i, pl.ds(0, 64)], 14 + i, dev_xm)

        def relay(self, i):
            self.got(self.ra.at[i], 8 + i)
            self.xp[i, 0:64] = (self.pair(1, i, 0) + self.ra[i].astype(F32)).astype(BF16)
            self.go(self.xp.at[i, pl.ds(0, 64)], self.fm.at[i, pl.ds(0, 64)], 16 + i, dev_xp)
            self.got(self.rb.at[i], 10 + i)
            self.xm[i, 64:128] = (self.pair(2, i, 1) + self.rb[i].astype(F32)).astype(BF16)
            self.go(self.xm.at[i, pl.ds(64, 64)], self.fp.at[i, pl.ds(64, 64)], 18 + i, dev_xm)

        def join(self, i, h):
            rows, at = slice(h * 64, h * 64 + 64), pl.ds(h * 64, 64)
            if h == 0:
                self.sib_got(3, i)
            self.got(self.fm.at[i, at], (16, 12)[h] + i)
            self.got(self.fp.at[i, at], (14, 18)[h] + i)
            return self.pair(3, i, h) + self.fm[i, rows].astype(F32) + self.fp[i, rows].astype(F32)

        def join_one(self, i):
            mine = self.y_order[i] == yh
            for h in range(2):
                rows = slice(h * 64, h * 64 + 64)
                value = self.join(i, h)

                @pl.when(mine)
                def _():
                    self.fin[rows] = value

                @pl.when(jnp.logical_not(mine))
                def _():
                    self.ys[rows] = value.astype(BF16)
                    self.to_opp(h).start()

        def to_opp(self, h):
            at = pl.ds(h * 64, 64)
            return copy(self.ys.at[at], self.yr.at[at], self.ss.at[20 + h], self.rs.at[20 + h], dev_yo)

        def join_other(self):
            for h in range(2):
                self.ys[h * 64:h * 64 + 64] = self.join(0, h).astype(BF16)
                self.to_opp(h).start()

        def join_mine(self):
            for h in range(2):
                self.fin[h * 64:h * 64 + 64] = self.join(1, h)

        def end(self):
            for h in range(2):
                self.to_opp(h).wait_send()

        def last(self, h):
            rows = slice(h * 64, h * 64 + 64)
            self.got(self.yr.at[pl.ds(h * 64, 64)], 20 + h)
            return self.fin[rows] + self.yr[rows].astype(F32)

    rt = Reduce((yl, 1 - yl), t_own, t_sib_s, t_sib_r, t_x2, t_ra, t_rb, t_xp, t_xm, t_fm, t_fp, t_ys, t_yr, t_fin, t_ss, t_rs)

    z_step(5)
    z_step(6)

    def products(core, y_, k, width):
        rows = tg[pl.ds(core * 4, 4), :, k * width:(k + 1) * width].reshape(4 * ROWS, width)
        return jnp.dot(rows, pj[y_, k * width:(k + 1) * width], preferred_element_type=F32).reshape(4, ROWS, COLS)

    l_pj.wait()
    first = pl.ds(yl * 4, 4)
    t_sib_s[first] = products(1 - c, yl, 0, 1024).astype(BF16)
    for k in range(4):
        rt.to_sib(k, 0)
    t_own[first] = products(c, yl, 0, 1024)
    rt.far(0)
    rt.near(0)

    other = pl.ds((1 - yl) * 4, 4)
    for k in range(4):
        arrive(pj.at[1 - yl, pl.ds(k * 256, 256)], p_ss.at[k], p_rs.at[k])
        theirs = products(1 - c, 1 - yl, k, 256)
        if k == 0:
            t_part[...] = theirs
        elif k < 3:
            t_part[...] += theirs
        else:
            t_sib_s[other] = (t_part[...] + theirs).astype(BF16)
            for j in range(4):
                rt.to_sib(j, 1)
        if k == 0:
            t_own[other] = products(c, 1 - yl, k, 256)
        else:
            t_own[other] += products(c, 1 - yl, k, 256)
        if k == 1:
            rt.relay(0)
    rt.far(1)
    rt.near(1)
    rt.join_one(0)
    for k in range(1, BACK + 1):
        kv_mid(k)
    rt.relay(1)

    lax.fori_loop(1, BACK + 1, kv_got, 0)
    keys = jnp.concatenate([kv_r[0, j] for j in range(BACK + 1)], axis=1)
    values = kv_r[1].reshape((BACK + 1) * ROWS, HEAD_DIM)
    for h in range(2):
        scores = jnp.dot(q_v[h], keys, preferred_element_type=F32)
        scores = scores + bias[...]
        probs = jnp.exp(scores - jnp.max(scores, axis=1, keepdims=True))
        total = jnp.sum(probs, axis=1, keepdims=True)
        acc = jnp.dot(probs.astype(BF16), values, preferred_element_type=F32)
        attn_v[c * 2 + h] = (acc / total).astype(BF16)
        send(attn_v.at[c * 2 + h], attn_v.at[c * 2 + h], x_ss.at[5 + h], x_rs.at[5 + h], sib)
    lax.fori_loop(0, 8, wo_got, 0)

    ro = Reduce((yo_, yh), o_own, None, None, o_x2, o_ra, o_rb, o_xp, o_xm, o_fm, o_fp, o_ys, o_yr, o_fin, o_ss, o_rs)

    for h in range(2):
        arrive(attn_v.at[2 - 2 * c + h], x_ss.at[5 + h], x_rs.at[5 + h])
    attn = jnp.concatenate([attn_v[i] for i in range(4)], axis=1)

    def out_block(k, i):
        slot = ro.slot(k, i)
        o_own[slot] = jnp.dot(attn, wo[slot].reshape(COLS, COLS), preferred_element_type=F32)

    out_block(0, 0)
    ro.far(0)
    out_block(1, 0)
    out_block(2, 0)
    ro.near(0)
    rt.join_one(1)
    out_block(0, 1)
    ro.relay(0)
    ro.far(1)
    out_block(1, 1)
    out_block(2, 1)
    ro.near(1)
    out_block(3, 0)
    out_block(3, 1)
    ro.relay(1)

    def t3(h):
        at = pl.ds(h * 64, 64)
        return copy(t3_s.at[at], t3_r.at[at], t3_ss.at[h], t3_rs.at[h], dev_t3)

    for h in range(2):
        rows = slice(h * 64, h * 64 + 64)
        t3_s[rows] = rt.last(h).astype(BF16)

        @pl.when(stays)
        def _():
            t3_r[rows] = t3_s[rows]

        @pl.when(jnp.logical_not(stays))
        def _():
            t3(h).start()

    ro.join_other()
    ro.join_mine()

    early = list(started)
    started.clear()

    def before_end():
        for one in early:
            one.wait_send()
        lax.fori_loop(0, 8, w_end, 0)
        lax.fori_loop(0, 8, wo_end, 0)
        lax.fori_loop(1, 16, kvx_end, 0)
        lax.fori_loop(1, BACK + 1, kv_end, 0)
        rt.end()
        ro.end()

        @pl.when(jnp.logical_not(stays))
        def _():
            t3(0).wait_send()
            t3(1).wait_send()

    dg = Gather(db, dg_ss, dg_rs)
    for h in range(2):
        rows = slice(h * 64, h * 64 + 64)
        mixed = hb[mine, rows].astype(F32) + ro.last(h)
        out_s[rows] = mixed.astype(BF16)

        @pl.when(jnp.logical_not(stays))
        def _():
            arrive(t3_r.at[pl.ds(h * 64, 64)], t3_ss.at[h], t3_rs.at[h])

        target = t3_r[rows].astype(F32) * jnp.concatenate([ts_v[rows]] * 4, axis=1)
        difference = mixed - target
        db[mine, rows] = difference.astype(BF16)
        dg.begin(h)
        squares = difference * difference
        l_v[rows] = (
            squares[:, 0:128] + squares[:, 128:256] + squares[:, 256:384] + squares[:, 384:512]
        )
    l_s[...] = jnp.sum(l_v[...].T, axis=0, keepdims=True)
    l_r[t] = l_s[...]

    def loss(k):
        return copy(l_s, l_r.at[t], l_ss.at[k], l_rs.at[k], (s, (t + k) % 16))

    def loss_go(k, carry):
        loss(k).start()
        return carry

    def loss_got(k, carry):
        arrive(l_r.at[(t + 16 - k) % 16], l_ss.at[k], l_rs.at[k])
        return carry

    def loss_end(k, carry):
        loss(k).wait_send()
        return carry

    lax.fori_loop(1, 16, loss_go, 0)

    def add_grad(slots, first=False):
        d = jnp.concatenate([db[slot] for slot in slots], axis=1)
        for core in range(2):
            w = jnp.concatenate([wo[slot, core] for slot in slots], axis=1)
            g = nt_dot(d, w)
            g_acc[core] = g if first else g_acc[core] + g

    dg.near_relay()
    dg.opp_half(0)
    dg.near_rest()
    before_end()
    add_grad([mine] + dg.near, True)
    dg.opp_half(1)
    dg.onear_a()
    dg.far_step()
    add_grad([dg.opp, dg.far[0]])
    dg.onear_b()
    dg.onear_rest()
    add_grad(dg.onear)
    lax.fori_loop(1, 16, loss_got, 0)
    loss_sum = l_r[0]
    for i in range(1, 16):
        loss_sum = loss_sum + l_r[i]
    out_l[...] = loss_sum / DS
    dg.ofar_step()
    add_grad([dg.far[1]])
    send(g_acc.at[1 - c], g_in, x_ss.at[7], x_rs.at[7], sib)
    arrive(g_in, x_ss.at[7], x_rs.at[7])
    out_g[...] = (g_acc[c] + g_in[...]).astype(BF16)

    flush()
    lax.fori_loop(1, 16, loss_end, 0)


def reduce_buffers():
    block = (ROWS, COLS)
    return [
        pltpu.VMEM((2, 64, COLS), BF16),
        pltpu.VMEM((2, 64, COLS), BF16),
        pltpu.VMEM((2,) + block, BF16),
        pltpu.VMEM((2,) + block, BF16),
        pltpu.VMEM((2,) + block, BF16),
        pltpu.VMEM((2,) + block, BF16),
        pltpu.VMEM(block, BF16),
        pltpu.VMEM(block, BF16),
        pltpu.VMEM(block, F32),
    ]


def on_device(
    teacher_hidden, teacher_gain, projector, student_hidden, student_gain,
    query_weight, kv_weight, out_weight, doc_ids,
):
    block = (ROWS, COLS)
    hbm = pl.BlockSpec(memory_space=pltpu.HBM)
    vmem = pl.BlockSpec(memory_space=pltpu.VMEM)
    dma = pltpu.SemaphoreType.DMA
    out_s, out_l, out_g = pl.pallas_call(
        body,
        out_shape=(
            jax.ShapeDtypeStruct(block, BF16),
            jax.ShapeDtypeStruct((1, ROWS), F32),
            jax.ShapeDtypeStruct((ROWS, 256), BF16),
        ),
        in_specs=[hbm] * 9,
        out_specs=(vmem, vmem, vmem),
        scratch_shapes=[
            pltpu.VMEM((1, 1024), F32),
            pltpu.VMEM((1, COLS), F32),
            pltpu.VMEM((1, ROWS), jnp.int32),
            pltpu.VMEM((ROWS, 1024), BF16),
            pltpu.VMEM((8, ROWS, 1024), BF16),
            pltpu.VMEM((2, 1024, COLS), BF16),
            pltpu.VMEM((8, 2, COLS, 256), BF16),
            pltpu.VMEM((8, 2, 2, 32, COLS), BF16),
            pltpu.VMEM((8, 2, 256, COLS), BF16),
            pltpu.VMEM((64, ROWS), F32),
            pltpu.VMEM((64, ROWS), F32),
            pltpu.VMEM((8,) + block, BF16),
            pltpu.VMEM((1, 768), F32),
            pltpu.VMEM((8, 1, 768), F32),
            pltpu.VMEM((1, 256), F32),
            pltpu.VMEM((1, 256), F32),
            pltpu.VMEM((ROWS, 128), F32),
            pltpu.VMEM((2, ROWS, 256), F32),
            pltpu.VMEM((ROWS, 256), F32),
            pltpu.VMEM((2, 64, ROWS), F32),
            pltpu.VMEM((64, ROWS), F32),
            pltpu.VMEM((4, 16, ROWS), BF16),
            pltpu.VMEM((16, 16, ROWS), BF16),
            pltpu.VMEM((2, ROWS, HEAD_DIM), BF16),
            pltpu.VMEM((2, BACK + 1, ROWS, HEAD_DIM), BF16),
            pltpu.VMEM((8, 1, ROWS), jnp.int32),
            pltpu.VMEM((8, 1, ROWS), jnp.int32),
            pltpu.VMEM((2, ROWS, HEAD_DIM), BF16),
            pltpu.VMEM((4, ROWS, HEAD_DIM), BF16),
            pltpu.VMEM((ROWS, (BACK + 1) * ROWS), F32),
            pltpu.VMEM((8,) + block, F32),
            pltpu.VMEM((4,) + block, F32),
            pltpu.VMEM((8,) + block, F32),
            pltpu.VMEM((2,) + block, BF16),
            pltpu.VMEM((8,) + block, BF16),
            pltpu.VMEM((8,) + block, BF16),
            pltpu.VMEM((2,) + block, BF16),
            *reduce_buffers(),
            *reduce_buffers(),
            pltpu.VMEM(block, BF16),
            pltpu.VMEM(block, BF16),
            pltpu.VMEM((ROWS, 128), F32),
            pltpu.VMEM((8,) + block, BF16),
            pltpu.VMEM((2, ROWS, 256), F32),
            pltpu.VMEM((ROWS, 256), F32),
            pltpu.VMEM((ROWS, 128), F32),
            pltpu.VMEM((1, ROWS), F32),
            pltpu.VMEM((16, 1, ROWS), F32),
            dma((10,)),
            *[dma((8,)) for _ in range(10)],
            dma((16,)), dma((16,)), dma((8,)), dma((8,)),
            dma((24,)), dma((24,)), dma((24,)), dma((24,)),
            dma((16,)), dma((16,)), dma((16,)), dma((16,)),
            dma((9,)), dma((9,)), dma((9,)), dma((9,)), dma((9,)), dma((9,)),
            dma((24,)), dma((24,)), dma((24,)), dma((24,)),
            dma((2,)), dma((2,)),
            dma((16,)), dma((16,)),
        ],
        compiler_params=pltpu.CompilerParams(
            collective_id=0, has_side_effects=True, vmem_limit_bytes=40 * 1024 * 1024
        ),
    )(
        *(
            pltpu.with_memory_space_constraint(one, pltpu.HBM)
            for one in (
                teacher_hidden, teacher_gain.reshape(1, -1), projector, student_hidden,
                student_gain.reshape(1, -1), query_weight.reshape(8, 2, COLS, 256), jnp.transpose(kv_weight, (0, 2, 1)),
                out_weight, doc_ids.reshape(1, -1),
            )
        )
    )
    return out_s, out_l.reshape(ROWS), out_g


def solution(mesh):
    in_specs = (
        P("seq", "tensor"),
        P("tensor"),
        P("tensor", "seq"),
        P("seq", "tensor"),
        P("tensor"),
        P(None, "tensor"),
        P(None, None, "tensor"),
        P("tensor", None),
        P("seq"),
    )
    out_specs = (P("seq", "tensor"), P("seq"), P("seq", "tensor"))
    return jax.shard_map(
        on_device, mesh=mesh, in_specs=in_specs, out_specs=out_specs, check_vma=False
    )
```

```python
import math

import jax
import jax.numpy as jnp
from jax import lax
from jax.experimental import pallas as pl
from jax.experimental.pallas import tpu as pltpu
from jax.sharding import PartitionSpec as P

DT = 16384
DS = 8192
HEAD_DIM = 128
HEADS = 32
KV_HEADS = 4
ROWS = 128
COLS = 512
BACK = 8
F32 = jnp.float32
BF16 = jnp.bfloat16
MESH = pl.DeviceIdType.MESH
NT = (((1,), (1,)), ((), ()))


def nt_dot(a, b):
    return lax.dot_general(a, b, NT, preferred_element_type=F32)


def body(
    th_h, tgain_h, pj_h, sh_h, sgain_h, wq_h, wkv_h, wo_h, docs_h,
    out_s, out_l, out_g,
    tgain, sgain, docs, th_v, tg, pj, wq, wkv, wo, cos_t, sin_t,
    hb, sg_s, sg_r, sum_s, sum_r, scale_v, q_acc, q_in, kv_acc, kv_in,
    kvx_s, kvx_r, kv_own, kv_r, docs_z, docs_o, q_v, attn_v, bias,
    t_own, t_part, o_own, o_x2, t_sib_s, t_sib_r, t_x2, t_ra, t_rb, t_xp, t_xm, t_fm, t_fp, t_ys, t_yr, t_fin,
    o_ra, o_rb, o_xp, o_xm, o_fm, o_fp, o_ys, o_yr, o_fin,
    t3_s, t3_r, ts_v, db, g_acc, g_in, l_v, l_s, l_r,
    load_sem, w_load, w_ss, w_rs, v_load, v_ss, v_rs, u_ss, u_rs, x_ss, x_rs, z_ss, z_rs, p_ss, p_rs,
    ag_ss, ag_rs, dg_ss, dg_rs, sm_ss, sm_rs, kx_ss, kx_rs, kv_ss, kv_rs, kf_ss, kf_rs, dc_ss, dc_rs,
    t_ss, t_rs, o_ss, o_rs, t3_ss, t3_rs, l_ss, l_rs,
):
    s = lax.axis_index("seq")
    t = lax.axis_index("tensor")
    yl, z = s // 8, s % 8
    yh, x, c = t // 8, (t // 2) % 4, t % 2

    def tid(y_, x_, c_):
        return y_ * 8 + x_ * 2 + c_

    xp_, xm_ = (x + 1) % 4, (x + 3) % 4
    xf_ = (x + 2) % 4
    yo_ = 1 - yh
    sib = (s, tid(yh, x, 1 - c))
    dev_xp = (s, tid(yh, xp_, c))
    dev_xm = (s, tid(yh, xm_, c))
    dev_yo = (s, tid(yo_, x, c))
    dev_zp = (yl * 8 + (z + 1) % 8, t)
    dev_zm = (yl * 8 + (z + 7) % 8, t)
    dev_yl = ((1 - yl) * 8 + z, t)
    turn = jnp.where(c == 0, x, jnp.where(x == 0, 4, 8 - x))
    dev_t3 = (yl * 8 + (z + turn) % 8, yh * 8 + z)
    stays = (z == 0) & (x == 0) & (c == 0)

    started = []

    def copy(src, dst, ss, rs, dev):
        return pltpu.make_async_remote_copy(
            src_ref=src, dst_ref=dst, send_sem=ss, recv_sem=rs, device_id=dev, device_id_type=MESH
        )

    def send(src, dst, ss, rs, dev):
        one = copy(src, dst, ss, rs, dev)
        one.start()
        started.append(one)

    def flush():
        for one in started:
            one.wait_send()
        started.clear()

    def arrive(dst, ss, rs):
        copy(dst, dst, ss, rs, sib).wait_recv()

    def load(src, dst, k):
        one = pltpu.make_async_copy(src, dst, load_sem.at[k])
        one.start()
        return one

    l_th = load(th_h, th_v, 0)
    mine = yh * 4 + x
    l_sh = load(sh_h, hb.at[mine], 1)
    l_small = [load(tgain_h, tgain, 7), load(sgain_h, sgain, 8), load(docs_h, docs, 9)]

    def wkv_part(j, core):
        return wkv_h.at[:, :, pl.ds(pl.multiple_of((j * 2 + core) * COLS, COLS), COLS)]

    def wkv_load(j):
        return pltpu.make_async_copy(wkv_part(j, c), wkv.at[j, c], v_load.at[j])

    def wkv_go(j, carry):
        wkv_load(j).start()
        return carry

    def wo_part(j, core):
        return wo_h.at[:, pl.ds(pl.multiple_of((j * 2 + core) * COLS, COLS), COLS)]

    def wo_load(j):
        return pltpu.make_async_copy(wo_part(j, c), wo.at[j, c], w_load.at[j])

    def wo_send(j):
        return copy(wo_part(j, 1 - c), wo.at[j, c], w_ss.at[j], w_rs.at[j], sib)

    def wo_fetch(j, carry):
        wo_load(j).start()
        return carry

    def wo_go(j, carry):
        wo_send(j).start()
        return carry

    def wo_got(j, carry):
        wo_load(j).wait()
        arrive(wo.at[j, 1 - c], w_ss.at[j], w_rs.at[j])
        return carry

    def wo_end(j, carry):
        wo_send(j).wait_send()
        return carry

    lax.fori_loop(0, 8, wkv_go, 0)
    l_wq = load(wq_h.at[:, c], wq.at[:, c], 3)

    kv_r[...] = jnp.zeros(kv_r.shape, BF16)

    barrier = pltpu.get_barrier_semaphore()
    for dev in (sib, dev_xp, dev_xm, dev_yo, dev_zp, dev_zm, dev_yl):
        pl.semaphore_signal(barrier, inc=1, device_id=dev, device_id_type=MESH)

    class Gather:
        def __init__(self, buf, ss, rs):
            self.buf, self.ss, self.rs = buf, ss, rs
            self.near = [yh * 4 + xm_, yh * 4 + xp_]
            self.opp = yo_ * 4 + x
            self.onear = [yo_ * 4 + xm_, yo_ * 4 + xp_]
            self.far = [yh * 4 + xf_, yo_ * 4 + xf_]
            self.order = [mine] + self.near + [self.opp] + self.onear + self.far

        def part(self, slot, h):
            return self.buf.at[slot, pl.ds(h * 64, 64)]

        def half(self, slot, h, k, dev):
            part = self.part(slot, h)
            send(part, part, self.ss.at[k], self.rs.at[k], dev)

        def got_half(self, slot, h, k):
            arrive(self.part(slot, h), self.ss.at[k], self.rs.at[k])

        def begin(self, h):
            self.half(mine, h, 0 + h, dev_yo)
            self.half(mine, h, 2 + h, dev_xp)
            self.half(mine, h, 4 + h, dev_xm)

        def near_relay(self):
            self.got_half(self.near[0], 0, 2)
            self.half(self.near[0], 0, 6, dev_xp)
            self.got_half(self.near[1], 1, 5)
            self.half(self.near[1], 1, 7, dev_xm)

        def near_rest(self):
            self.got_half(self.near[0], 1, 3)
            self.got_half(self.near[1], 0, 4)

        def opp_half(self, h):
            self.got_half(self.opp, h, 0 + h)
            self.half(self.opp, h, 8 + h, dev_xp)
            self.half(self.opp, h, 10 + h, dev_xm)

        def onear_a(self):
            self.got_half(self.onear[0], 0, 8)
            self.half(self.onear[0], 0, 12, dev_xp)

        def onear_b(self):
            self.got_half(self.onear[1], 1, 11)
            self.half(self.onear[1], 1, 13, dev_xm)

        def onear_rest(self):
            self.got_half(self.onear[0], 1, 9)
            self.got_half(self.onear[1], 0, 10)

        def far_step(self):
            self.got_half(self.far[0], 0, 6)
            self.got_half(self.far[0], 1, 7)

        def ofar_step(self):
            self.got_half(self.far[1], 0, 12)
            self.got_half(self.far[1], 1, 13)

    def pj_send(k):
        rows = pl.ds(k * 256, 256)
        send(pj_h.at[rows], pj.at[yl, rows], p_ss.at[k], p_rs.at[k], dev_yl)

    def wkv_send(j):
        return copy(wkv_part(j, 1 - c), wkv.at[j, c], v_ss.at[j], v_rs.at[j], sib)

    def wq_send(j):
        return copy(wq_h.at[j, 1 - c], wq.at[j, c], u_ss.at[j], u_rs.at[j], sib)

    def w_go(j, carry):
        wkv_send(j).start()
        wq_send(j).start()
        return carry

    def w_end(j, carry):
        wkv_send(j).wait_send()
        wq_send(j).wait_send()
        return carry

    def w_got(slot):
        wkv_load(slot).wait()
        arrive(wkv.at[slot, 1 - c], v_ss.at[slot], v_rs.at[slot])
        arrive(wq.at[slot, 1 - c], u_ss.at[slot], u_rs.at[slot])

    ag = Gather(hb, ag_ss, ag_rs)
    l_sh.wait()

    z_slot = 0
    l_th.wait()
    for one in l_small:
        one.wait()
    docs_z[z] = docs[...]
    part = jnp.zeros((ROWS, 128), F32)
    for i in range(8):
        cols = slice(i * 128, (i + 1) * 128)
        f = th_v[:, cols].astype(F32)
        part = part + f * f
        tg[z_slot, :, cols] = (f * tgain[:, cols]).astype(BF16)
    sg_s[:, COLS:COLS + 128] = jnp.sum(part.T, axis=0, keepdims=True)
    part = jnp.zeros((ROWS, 128), F32)
    for i in range(4):
        f = hb[mine, :, i * 128:(i + 1) * 128].astype(F32)
        part = part + f * f
    sg_s[:, COLS + 128:COLS + 256] = jnp.sum(part.T, axis=0, keepdims=True)
    sg_s[:, 0:COLS] = sgain[...]
    sg_r[mine] = sg_s[...]

    def ring_slot(d):
        return (0, 1, 2, 3, 4, 7, 6, 5)[d % 8]

    def z_ref(d, h):
        return tg.at[ring_slot(d), pl.ds(h * 64, 64)]

    def z_send(k):
        d = k // 2
        send(z_ref(8 - d, k % 2), z_ref(7 - d, k % 2), z_ss.at[k], z_rs.at[k], dev_zp)
        send(z_ref(d, 1 - k % 2), z_ref(d + 1, 1 - k % 2), z_ss.at[8 + k], z_rs.at[8 + k], dev_zm)

    def z_got(k):
        up, down = z_ref(-(k // 2) + 7, k % 2), z_ref(k // 2 + 1, 1 - k % 2)
        arrive(up, z_ss.at[k], z_rs.at[k])
        arrive(down, z_ss.at[8 + k], z_rs.at[8 + k])

    def z_step(k):
        z_got(k)
        if k + 2 < 7:
            z_send(k + 2)

    def small_send(i, k, dev):
        slot = ag.order[i]
        send(sg_r.at[slot], sg_r.at[slot], sm_ss.at[k], sm_rs.at[k], dev)

    def small_got(i, k):
        arrive(sg_r.at[ag.order[i]], sm_ss.at[k], sm_rs.at[k])

    def docs_send(d, k, dev):
        ref = docs_z.at[(z + d) % 8]
        send(ref, ref, dc_ss.at[k], dc_rs.at[k], dev)

    def docs_step(k):
        arrive(docs_z.at[(z + 7 - k) % 8], dc_ss.at[k], dc_rs.at[k])
        if k < 3:
            arrive(docs_z.at[(z + 1 + k) % 8], dc_ss.at[4 + k], dc_rs.at[4 + k])
            docs_send(7 - k, k + 1, dev_zp)
            if k < 2:
                docs_send(1 + k, k + 5, dev_zm)
        else:
            send(docs_z, docs_o, dc_ss.at[8], dc_rs.at[8], dev_yl)

    pl.semaphore_wait(barrier, 7)
    small_send(0, 0, dev_yo)
    small_send(0, 1, dev_xp)
    small_send(0, 2, dev_xm)
    ag.begin(0)
    ag.begin(1)
    docs_send(0, 0, dev_zp)
    docs_send(0, 4, dev_zm)
    pj_send(0)
    z_send(0)
    pj_send(1)
    z_send(1)
    lax.fori_loop(0, 8, w_go, 0)
    l_pj = load(pj_h, pj.at[yl], 4)

    entry = lax.broadcasted_iota(jnp.int32, (64, ROWS), 0).astype(F32)
    position = (s * ROWS + lax.broadcasted_iota(jnp.int32, (64, ROWS), 1)).astype(F32)
    angle = position * jnp.exp(-math.log(500000.0) * (2.0 * entry / HEAD_DIM))
    cos_t[...] = jnp.cos(angle)
    sin_t[...] = jnp.sin(angle)

    def process(slots, first=False):
        blocks, w = [], []
        for slot in slots:
            parts = []
            for i in range(4):
                cols = slice(i * 128, (i + 1) * 128)
                f = hb[slot, :, cols].astype(F32)
                parts.append((f * scale_v[...] * sg_r[slot][:, cols]).astype(BF16))
            blocks.append(jnp.concatenate(parts, axis=1))
        n = jnp.concatenate(blocks, axis=1)
        for slot in slots:
            w_got(slot)
            w.append(wkv[slot].reshape(128, COLS))
        kv = nt_dot(jnp.concatenate(w, axis=1), n)
        for core in range(2):
            w = jnp.concatenate([wq[slot, core] for slot in slots], axis=0)
            q = jnp.dot(n, w, preferred_element_type=F32)
            k = kv[core * 64:core * 64 + 64]
            q_acc[core] = q if first else q_acc[core] + q
            kv_acc[core] = k if first else kv_acc[core] + k

    small_got(1, 1)
    small_send(1, 3, dev_xp)
    small_got(2, 2)
    small_got(3, 0)
    small_send(3, 4, dev_xp)
    small_send(3, 5, dev_xm)
    docs_step(0)
    ag.near_relay()
    small_got(6, 3)
    docs_step(1)
    small_got(4, 4)
    small_send(4, 6, dev_xp)
    small_got(5, 5)
    ag.near_rest()
    pj_send(2)
    ag.opp_half(0)
    z_step(0)
    pj_send(3)
    small_got(7, 6)
    sums = sg_r[0][:, COLS:COLS + 256]
    for i in range(1, 8):
        sums = sums + sg_r[i][:, COLS:COLS + 256]
    sum_s[...] = sums
    send(sum_s, sum_r, x_ss.at[2], x_rs.at[2], sib)
    docs_step(2)
    ag.opp_half(1)
    arrive(sum_r, x_ss.at[2], x_rs.at[2])
    sums = sum_s[...] + sum_r[...]
    ts_v[...] = jnp.broadcast_to(lax.rsqrt(sums[:, 0:128] / DT + 1e-05), (ROWS, 128)).T
    scale_v[...] = jnp.broadcast_to(lax.rsqrt(sums[:, 128:256] / DS + 1e-05), (ROWS, 128)).T
    docs_step(3)
    z_step(1)
    ag.onear_a()
    l_wq.wait()
    process([mine] + ag.near, True)
    ag.onear_b()
    z_step(2)
    ag.far_step()
    process([ag.opp, ag.far[0]])
    ag.onear_rest()
    process(ag.onear)
    z_step(3)
    ag.ofar_step()
    process([ag.far[1]])
    send(kv_acc.at[1 - c], kv_in, x_ss.at[3], x_rs.at[3], sib)
    send(q_acc.at[1 - c], q_in, x_ss.at[4], x_rs.at[4], sib)
    arrive(kv_in, x_ss.at[3], x_rs.at[3])

    row = lax.broadcasted_iota(jnp.int32, (64, 64), 0)
    col = lax.broadcasted_iota(jnp.int32, (64, 64), 1)
    take = ((row >> 3) & 1) * 32 + (row & 7) * 4 + (row >> 4)
    pick = jnp.where(col == take, 1.0, 0.0).astype(BF16)
    kv_mine = (kv_acc[c] + kv_in[...]).astype(BF16)
    kvx_s[...] = jnp.dot(pick, kv_mine, preferred_element_type=F32).astype(BF16).reshape(4, 16, 128)
    kvx_r[t] = kvx_s[t // 4]

    def kvx(k):
        to = (t + k) % 16
        return copy(kvx_s.at[to // 4], kvx_r.at[t], kx_ss.at[k], kx_rs.at[k], (s, to))

    def kvx_go(k, carry):
        kvx(k).start()
        return carry

    def kvx_got(k, carry):
        arrive(kvx_r.at[(t + 16 - k) % 16], kx_ss.at[k], kx_rs.at[k])
        return carry

    def kvx_end(k, carry):
        kvx(k).wait_send()
        return carry

    lax.fori_loop(1, 16, kvx_go, 0)
    lax.fori_loop(0, 8, wo_fetch, 0)
    lax.fori_loop(0, 8, wo_go, 0)
    z_step(4)

    cos2 = jnp.concatenate([cos_t[...], cos_t[...]], axis=0).T
    sin2 = jnp.concatenate([-sin_t[...], sin_t[...]], axis=0).T
    arrive(q_in, x_ss.at[4], x_rs.at[4])
    q_mine = q_acc[c] + q_in[...]
    for h in range(2):
        qh = q_mine[:, h * 128:(h + 1) * 128]
        turned = qh * cos2 + pltpu.roll(qh, 64, 1) * sin2
        q_v[h] = (turned * HEAD_DIM ** (-0.5)).astype(BF16)

    lax.fori_loop(1, 16, kvx_got, 0)
    both = kvx_r[...].astype(F32).reshape(16, 2, 8, ROWS)
    k_raw = both[:, 0].reshape(HEAD_DIM, ROWS)
    v_raw = both[:, 1].reshape(HEAD_DIM, ROWS)
    first, second = k_raw[0:64], k_raw[64:128]
    k_rot = jnp.concatenate(
        [first * cos_t[...] - second * sin_t[...], second * cos_t[...] + first * sin_t[...]], axis=0
    )
    kv_own[0] = k_rot.astype(BF16)
    kv_own[1] = v_raw.T.astype(BF16)
    kv_r[0, 0] = kv_own[0]
    kv_r[1, 0] = kv_own[1]

    def kv_copy(k):
        return copy(kv_own.at[c], kv_r.at[c, k], kv_ss.at[k], kv_rs.at[k], ((s + k) % 16, t))

    def kv_fwd(k):
        return copy(kv_r.at[c, k], kv_r.at[c, k], kf_ss.at[k], kf_rs.at[k], sib)

    def kv_go(k):
        @pl.when(s + k < 16)
        def _():
            kv_copy(k).start()

    def kv_mid(k):
        @pl.when(s >= k)
        def _():
            arrive(kv_r.at[c, k], kv_ss.at[k], kv_rs.at[k])
            kv_fwd(k).start()

    def kv_got(k, carry):
        @pl.when(s >= k)
        def _():
            arrive(kv_r.at[1 - c, k], kf_ss.at[k], kf_rs.at[k])
        return carry

    def kv_end(k, carry):
        @pl.when(s >= k)
        def _():
            kv_fwd(k).wait_send()

        @pl.when(s + k < 16)
        def _():
            kv_copy(k).wait_send()
        return carry

    arrive(docs_o, dc_ss.at[8], dc_rs.at[8])
    for k in range(1, BACK + 1):
        kv_go(k)

    def docs_back(j):
        at = (z + 8 - j) % 8
        return jnp.where(z >= j, docs_z[at], jnp.where(yl == 1, docs_o[at], -1))

    key_doc = jnp.concatenate([docs_back(j) for j in range(BACK + 1)], axis=1)
    row_doc = jnp.broadcast_to(docs[...].astype(F32), (ROWS, ROWS)).T[:, 0:1].astype(jnp.int32)
    wide = (ROWS, (BACK + 1) * ROWS)
    row_at = lax.broadcasted_iota(jnp.int32, wide, 0)
    key_at = lax.broadcasted_iota(jnp.int32, wide, 1)
    allowed = (key_doc == row_doc) & ((key_at >= ROWS) | (key_at <= row_at))
    bias[...] = jnp.where(allowed, 0.0, -1e30)

    class Reduce:
        def __init__(self, y_order, own, sib_s, sib_r, x2, ra, rb, xp, xm, fm, fp, ys, yr, fin, ss, rs):
            self.own, self.sib_s, self.sib_r = own, sib_s, sib_r
            self.x2, self.ra, self.rb, self.xp, self.xm, self.fm, self.fp = x2, ra, rb, xp, xm, fm, fp
            self.ys, self.yr, self.fin, self.ss, self.rs = ys, yr, fin, ss, rs
            self.y_order = y_order
            self.x_order = (xf_, xp_, xm_, x)

        def go(self, src, dst, k, dev):
            send(src, dst, self.ss.at[k], self.rs.at[k], dev)

        def got(self, dst, k):
            arrive(dst, self.ss.at[k], self.rs.at[k])

        def slot(self, k, i):
            return self.y_order[i] * 4 + self.x_order[k]

        def to_sib(self, k, i):
            slot = self.slot(k, i)
            self.go(self.sib_s.at[slot], self.sib_r.at[slot], k * 2 + i, sib)

        def sib_got(self, k, i):
            if self.sib_r is not None:
                self.got(self.sib_r.at[self.slot(k, i)], k * 2 + i)

        def pair(self, k, i, h):
            slot, rows = self.slot(k, i), slice(h * 64, h * 64 + 64)
            value = self.own[slot, rows]
            return value if self.sib_r is None else value + self.sib_r[slot, rows].astype(F32)

        def far(self, i):
            self.sib_got(0, i)
            self.x2[i, 0:64] = self.pair(0, i, 0).astype(BF16)
            self.go(self.x2.at[i, pl.ds(0, 64)], self.ra.at[i], 8 + i, dev_xp)
            self.x2[i, 64:128] = self.pair(0, i, 1).astype(BF16)
            self.go(self.x2.at[i, pl.ds(64, 64)], self.rb.at[i], 10 + i, dev_xm)

        def near(self, i):
            self.sib_got(1, i)
            self.xp[i, 64:128] = self.pair(1, i, 1).astype(BF16)
            self.go(self.xp.at[i, pl.ds(64, 64)], self.fm.at[i, pl.ds(64, 64)], 12 + i, dev_xp)
            self.sib_got(2, i)
            self.xm[i, 0:64] = self.pair(2, i, 0).astype(BF16)
            self.go(self.xm.at[i, pl.ds(0, 64)], self.fp.at[i, pl.ds(0, 64)], 14 + i, dev_xm)

        def relay(self, i):
            self.got(self.ra.at[i], 8 + i)
            self.xp[i, 0:64] = (self.pair(1, i, 0) + self.ra[i].astype(F32)).astype(BF16)
            self.go(self.xp.at[i, pl.ds(0, 64)], self.fm.at[i, pl.ds(0, 64)], 16 + i, dev_xp)
            self.got(self.rb.at[i], 10 + i)
            self.xm[i, 64:128] = (self.pair(2, i, 1) + self.rb[i].astype(F32)).astype(BF16)
            self.go(self.xm.at[i, pl.ds(64, 64)], self.fp.at[i, pl.ds(64, 64)], 18 + i, dev_xm)

        def join(self, i, h):
            rows, at = slice(h * 64, h * 64 + 64), pl.ds(h * 64, 64)
            if h == 0:
                self.sib_got(3, i)
            self.got(self.fm.at[i, at], (16, 12)[h] + i)
            self.got(self.fp.at[i, at], (14, 18)[h] + i)
            return self.pair(3, i, h) + self.fm[i, rows].astype(F32) + self.fp[i, rows].astype(F32)

        def join_one(self, i):
            mine = self.y_order[i] == yh
            for h in range(2):
                rows = slice(h * 64, h * 64 + 64)
                value = self.join(i, h)

                @pl.when(mine)
                def _():
                    self.fin[rows] = value

                @pl.when(jnp.logical_not(mine))
                def _():
                    self.ys[rows] = value.astype(BF16)
                    self.to_opp(h).start()

        def to_opp(self, h):
            at = pl.ds(h * 64, 64)
            return copy(self.ys.at[at], self.yr.at[at], self.ss.at[20 + h], self.rs.at[20 + h], dev_yo)

        def join_other(self):
            for h in range(2):
                self.ys[h * 64:h * 64 + 64] = self.join(0, h).astype(BF16)
                self.to_opp(h).start()

        def join_mine(self):
            for h in range(2):
                self.fin[h * 64:h * 64 + 64] = self.join(1, h)

        def end(self):
            for h in range(2):
                self.to_opp(h).wait_send()

        def last(self, h):
            rows = slice(h * 64, h * 64 + 64)
            self.got(self.yr.at[pl.ds(h * 64, 64)], 20 + h)
            return self.fin[rows] + self.yr[rows].astype(F32)

    rt = Reduce((yl, 1 - yl), t_own, t_sib_s, t_sib_r, t_x2, t_ra, t_rb, t_xp, t_xm, t_fm, t_fp, t_ys, t_yr, t_fin, t_ss, t_rs)

    z_step(5)
    z_step(6)

    def products(core, y_, k, width):
        rows = tg[pl.ds(core * 4, 4), :, k * width:(k + 1) * width].reshape(4 * ROWS, width)
        return jnp.dot(rows, pj[y_, k * width:(k + 1) * width], preferred_element_type=F32).reshape(4, ROWS, COLS)

    l_pj.wait()
    first = pl.ds(yl * 4, 4)
    t_sib_s[first] = products(1 - c, yl, 0, 1024).astype(BF16)
    for k in range(4):
        rt.to_sib(k, 0)
    t_own[first] = products(c, yl, 0, 1024)
    rt.far(0)
    rt.near(0)

    other = pl.ds((1 - yl) * 4, 4)
    for k in range(4):
        arrive(pj.at[1 - yl, pl.ds(k * 256, 256)], p_ss.at[k], p_rs.at[k])
        theirs = products(1 - c, 1 - yl, k, 256)
        if k == 0:
            t_part[...] = theirs
        elif k < 3:
            t_part[...] += theirs
        else:
            t_sib_s[other] = (t_part[...] + theirs).astype(BF16)
            for j in range(4):
                rt.to_sib(j, 1)
        if k == 0:
            t_own[other] = products(c, 1 - yl, k, 256)
        else:
            t_own[other] += products(c, 1 - yl, k, 256)
        if k == 1:
            rt.relay(0)
    rt.far(1)
    rt.near(1)
    rt.join_one(0)
    for k in (1, 2, 3, 4):
        kv_mid(k)
    rt.relay(1)
    for k in (5, 6, 7, 8):
        kv_mid(k)
    rt.join_one(1)

    lax.fori_loop(1, BACK + 1, kv_got, 0)
    keys = jnp.concatenate([kv_r[0, j] for j in range(BACK + 1)], axis=1)
    values = kv_r[1].reshape((BACK + 1) * ROWS, HEAD_DIM)
    for h in range(2):
        scores = jnp.dot(q_v[h], keys, preferred_element_type=F32)
        scores = scores + bias[...]
        probs = jnp.exp(scores - jnp.max(scores, axis=1, keepdims=True))
        total = jnp.sum(probs, axis=1, keepdims=True)
        acc = jnp.dot(probs.astype(BF16), values, preferred_element_type=F32)
        attn_v[c * 2 + h] = (acc / total).astype(BF16)
        send(attn_v.at[c * 2 + h], attn_v.at[c * 2 + h], x_ss.at[5 + h], x_rs.at[5 + h], sib)
    lax.fori_loop(0, 8, wo_got, 0)

    ro = Reduce((yo_, yh), o_own, None, None, o_x2, o_ra, o_rb, o_xp, o_xm, o_fm, o_fp, o_ys, o_yr, o_fin, o_ss, o_rs)

    for h in range(2):
        arrive(attn_v.at[2 - 2 * c + h], x_ss.at[5 + h], x_rs.at[5 + h])
    attn = jnp.concatenate([attn_v[i] for i in range(4)], axis=1)

    def out_block(k, i):
        slot = ro.slot(k, i)
        o_own[slot] = jnp.dot(attn, wo[slot].reshape(COLS, COLS), preferred_element_type=F32)

    def t3(h):
        at = pl.ds(h * 64, 64)
        return copy(t3_s.at[at], t3_r.at[at], t3_ss.at[h], t3_rs.at[h], dev_t3)

    def t3_go(h):
        rows = slice(h * 64, h * 64 + 64)
        t3_s[rows] = rt.last(h).astype(BF16)

        @pl.when(stays)
        def _():
            t3_r[rows] = t3_s[rows]

        @pl.when(jnp.logical_not(stays))
        def _():
            t3(h).start()

    out_block(0, 0)
    ro.far(0)
    out_block(1, 0)
    out_block(2, 0)
    ro.near(0)
    out_block(0, 1)
    ro.relay(0)
    ro.far(1)
    t3_go(0)
    out_block(1, 1)
    out_block(2, 1)
    ro.near(1)
    t3_go(1)
    out_block(3, 0)
    out_block(3, 1)
    ro.relay(1)

    ro.join_other()
    ro.join_mine()

    early = list(started)
    started.clear()

    def before_end():
        for one in early:
            one.wait_send()
        lax.fori_loop(0, 8, w_end, 0)
        lax.fori_loop(0, 8, wo_end, 0)
        lax.fori_loop(1, 16, kvx_end, 0)
        lax.fori_loop(1, BACK + 1, kv_end, 0)
        rt.end()
        ro.end()

        @pl.when(jnp.logical_not(stays))
        def _():
            t3(0).wait_send()
            t3(1).wait_send()

    dg = Gather(db, dg_ss, dg_rs)
    for h in range(2):
        rows = slice(h * 64, h * 64 + 64)
        mixed = hb[mine, rows].astype(F32) + ro.last(h)
        out_s[rows] = mixed.astype(BF16)

        @pl.when(jnp.logical_not(stays))
        def _():
            arrive(t3_r.at[pl.ds(h * 64, 64)], t3_ss.at[h], t3_rs.at[h])

        target = t3_r[rows].astype(F32) * jnp.concatenate([ts_v[rows]] * 4, axis=1)
        difference = mixed - target
        db[mine, rows] = difference.astype(BF16)
        dg.begin(h)
        squares = difference * difference
        l_v[rows] = (
            squares[:, 0:128] + squares[:, 128:256] + squares[:, 256:384] + squares[:, 384:512]
        )
    l_s[...] = jnp.sum(l_v[...].T, axis=0, keepdims=True)
    l_r[t] = l_s[...]

    def loss(k):
        return copy(l_s, l_r.at[t], l_ss.at[k], l_rs.at[k], (s, (t + k) % 16))

    def loss_go(k, carry):
        loss(k).start()
        return carry

    def loss_got(k, carry):
        arrive(l_r.at[(t + 16 - k) % 16], l_ss.at[k], l_rs.at[k])
        return carry

    def loss_end(k, carry):
        loss(k).wait_send()
        return carry

    lax.fori_loop(1, 16, loss_go, 0)

    def add_grad(slots, first=False):
        d = jnp.concatenate([db[slot] for slot in slots], axis=1)
        for core in range(2):
            w = jnp.concatenate([wo[slot, core] for slot in slots], axis=1)
            g = nt_dot(d, w)
            g_acc[core] = g if first else g_acc[core] + g

    dg.near_relay()
    dg.opp_half(0)
    dg.near_rest()
    before_end()
    add_grad([mine] + dg.near, True)
    dg.opp_half(1)
    dg.onear_a()
    dg.far_step()
    add_grad([dg.opp, dg.far[0]])
    dg.onear_b()
    dg.onear_rest()
    add_grad(dg.onear)
    lax.fori_loop(1, 16, loss_got, 0)
    loss_sum = l_r[0]
    for i in range(1, 16):
        loss_sum = loss_sum + l_r[i]
    out_l[...] = loss_sum / DS
    dg.ofar_step()
    add_grad([dg.far[1]])
    send(g_acc.at[1 - c], g_in, x_ss.at[7], x_rs.at[7], sib)
    arrive(g_in, x_ss.at[7], x_rs.at[7])
    out_g[...] = (g_acc[c] + g_in[...]).astype(BF16)

    flush()
    lax.fori_loop(1, 16, loss_end, 0)


def reduce_buffers():
    block = (ROWS, COLS)
    return [
        pltpu.VMEM((2, 64, COLS), BF16),
        pltpu.VMEM((2, 64, COLS), BF16),
        pltpu.VMEM((2,) + block, BF16),
        pltpu.VMEM((2,) + block, BF16),
        pltpu.VMEM((2,) + block, BF16),
        pltpu.VMEM((2,) + block, BF16),
        pltpu.VMEM(block, BF16),
        pltpu.VMEM(block, BF16),
        pltpu.VMEM(block, F32),
    ]


def on_device(
    teacher_hidden, teacher_gain, projector, student_hidden, student_gain,
    query_weight, kv_weight, out_weight, doc_ids,
):
    block = (ROWS, COLS)
    hbm = pl.BlockSpec(memory_space=pltpu.HBM)
    vmem = pl.BlockSpec(memory_space=pltpu.VMEM)
    dma = pltpu.SemaphoreType.DMA
    out_s, out_l, out_g = pl.pallas_call(
        body,
        out_shape=(
            jax.ShapeDtypeStruct(block, BF16),
            jax.ShapeDtypeStruct((1, ROWS), F32),
            jax.ShapeDtypeStruct((ROWS, 256), BF16),
        ),
        in_specs=[hbm] * 9,
        out_specs=(vmem, vmem, vmem),
        scratch_shapes=[
            pltpu.VMEM((1, 1024), F32),
            pltpu.VMEM((1, COLS), F32),
            pltpu.VMEM((1, ROWS), jnp.int32),
            pltpu.VMEM((ROWS, 1024), BF16),
            pltpu.VMEM((8, ROWS, 1024), BF16),
            pltpu.VMEM((2, 1024, COLS), BF16),
            pltpu.VMEM((8, 2, COLS, 256), BF16),
            pltpu.VMEM((8, 2, 2, 32, COLS), BF16),
            pltpu.VMEM((8, 2, 256, COLS), BF16),
            pltpu.VMEM((64, ROWS), F32),
            pltpu.VMEM((64, ROWS), F32),
            pltpu.VMEM((8,) + block, BF16),
            pltpu.VMEM((1, 768), F32),
            pltpu.VMEM((8, 1, 768), F32),
            pltpu.VMEM((1, 256), F32),
            pltpu.VMEM((1, 256), F32),
            pltpu.VMEM((ROWS, 128), F32),
            pltpu.VMEM((2, ROWS, 256), F32),
            pltpu.VMEM((ROWS, 256), F32),
            pltpu.VMEM((2, 64, ROWS), F32),
            pltpu.VMEM((64, ROWS), F32),
            pltpu.VMEM((4, 16, ROWS), BF16),
            pltpu.VMEM((16, 16, ROWS), BF16),
            pltpu.VMEM((2, ROWS, HEAD_DIM), BF16),
            pltpu.VMEM((2, BACK + 1, ROWS, HEAD_DIM), BF16),
            pltpu.VMEM((8, 1, ROWS), jnp.int32),
            pltpu.VMEM((8, 1, ROWS), jnp.int32),
            pltpu.VMEM((2, ROWS, HEAD_DIM), BF16),
            pltpu.VMEM((4, ROWS, HEAD_DIM), BF16),
            pltpu.VMEM((ROWS, (BACK + 1) * ROWS), F32),
            pltpu.VMEM((8,) + block, F32),
            pltpu.VMEM((4,) + block, F32),
            pltpu.VMEM((8,) + block, F32),
            pltpu.VMEM((2,) + block, BF16),
            pltpu.VMEM((8,) + block, BF16),
            pltpu.VMEM((8,) + block, BF16),
            pltpu.VMEM((2,) + block, BF16),
            *reduce_buffers(),
            *reduce_buffers(),
            pltpu.VMEM(block, BF16),
            pltpu.VMEM(block, BF16),
            pltpu.VMEM((ROWS, 128), F32),
            pltpu.VMEM((8,) + block, BF16),
            pltpu.VMEM((2, ROWS, 256), F32),
            pltpu.VMEM((ROWS, 256), F32),
            pltpu.VMEM((ROWS, 128), F32),
            pltpu.VMEM((1, ROWS), F32),
            pltpu.VMEM((16, 1, ROWS), F32),
            dma((10,)),
            *[dma((8,)) for _ in range(10)],
            dma((16,)), dma((16,)), dma((8,)), dma((8,)),
            dma((24,)), dma((24,)), dma((24,)), dma((24,)),
            dma((16,)), dma((16,)), dma((16,)), dma((16,)),
            dma((9,)), dma((9,)), dma((9,)), dma((9,)), dma((9,)), dma((9,)),
            dma((24,)), dma((24,)), dma((24,)), dma((24,)),
            dma((2,)), dma((2,)),
            dma((16,)), dma((16,)),
        ],
        compiler_params=pltpu.CompilerParams(
            collective_id=0, has_side_effects=True, vmem_limit_bytes=40 * 1024 * 1024
        ),
    )(
        *(
            pltpu.with_memory_space_constraint(one, pltpu.HBM)
            for one in (
                teacher_hidden, teacher_gain.reshape(1, -1), projector, student_hidden,
                student_gain.reshape(1, -1), query_weight.reshape(8, 2, COLS, 256), jnp.transpose(kv_weight, (0, 2, 1)),
                out_weight, doc_ids.reshape(1, -1),
            )
        )
    )
    return out_s, out_l.reshape(ROWS), out_g


def solution(mesh):
    in_specs = (
        P("seq", "tensor"),
        P("tensor"),
        P("tensor", "seq"),
        P("seq", "tensor"),
        P("tensor"),
        P(None, "tensor"),
        P(None, None, "tensor"),
        P("tensor", None),
        P("seq"),
    )
    out_specs = (P("seq", "tensor"), P("seq"), P("seq", "tensor"))
    return jax.shard_map(
        on_device, mesh=mesh, in_specs=in_specs, out_specs=out_specs, check_vma=False
    )
```

```python
import math

import jax
import jax.numpy as jnp
from jax import lax
from jax.experimental import pallas as pl
from jax.experimental.pallas import tpu as pltpu
from jax.sharding import PartitionSpec as P

DT = 16384
DS = 8192
HEAD_DIM = 128
HEADS = 32
KV_HEADS = 4
ROWS = 128
COLS = 512
BACK = 8
F32 = jnp.float32
BF16 = jnp.bfloat16
MESH = pl.DeviceIdType.MESH
NT = (((1,), (1,)), ((), ()))


def nt_dot(a, b):
    return lax.dot_general(a, b, NT, preferred_element_type=F32)


def body(
    th_h, tgain_h, pj_h, sh_h, sgain_h, wq_h, wkv_h, wo_h, docs_h,
    out_s, out_l, out_g,
    tgain, sgain, docs, th_v, tg, pj, wq, wkv, wo, cos_t, sin_t,
    hb, sg_s, sg_r, sum_s, sum_r, scale_v, q_acc, q_in, kv_acc, kv_in,
    kvx_s, kvx_r, kv_own, kv_r, docs_z, docs_o, q_v, attn_v, bias,
    t_own, t_part, o_own, o_x2, t_sib_s, t_sib_r, t_x2, t_ra, t_rb, t_xp, t_xm, t_fm, t_fp,
    o_ra, o_rb, o_xp, o_xm, o_fm, o_fp, o_ys, o_yr, o_fin,
    t3_s, t3_r, ts_v, db, g_acc, g_in, l_v, l_s, l_r,
    load_sem, w_load, w_ss, w_rs, v_load, v_ss, v_rs, u_ss, u_rs, x_ss, x_rs, z_ss, z_rs, p_ss, p_rs,
    ag_ss, ag_rs, dg_ss, dg_rs, sm_ss, sm_rs, kx_ss, kx_rs, kv_ss, kv_rs, kf_ss, kf_rs, dc_ss, dc_rs,
    t_ss, t_rs, o_ss, o_rs, t3_ss, t3_rs, l_ss, l_rs,
):
    s = lax.axis_index("seq")
    t = lax.axis_index("tensor")
    yl, z = s // 8, s % 8
    yh, x, c = t // 8, (t // 2) % 4, t % 2

    def tid(y_, x_, c_):
        return y_ * 8 + x_ * 2 + c_

    xp_, xm_ = (x + 1) % 4, (x + 3) % 4
    xf_ = (x + 2) % 4
    yo_ = 1 - yh
    sib = (s, tid(yh, x, 1 - c))
    dev_xp = (s, tid(yh, xp_, c))
    dev_xm = (s, tid(yh, xm_, c))
    dev_yo = (s, tid(yo_, x, c))
    dev_zp = (yl * 8 + (z + 1) % 8, t)
    dev_zm = (yl * 8 + (z + 7) % 8, t)
    dev_yl = ((1 - yl) * 8 + z, t)
    turn = jnp.where(c == 0, x, jnp.where(x == 0, 4, 8 - x))
    stays = (z == 0) & (x == 0) & (c == 0)

    started = []

    def copy(src, dst, ss, rs, dev):
        return pltpu.make_async_remote_copy(
            src_ref=src, dst_ref=dst, send_sem=ss, recv_sem=rs, device_id=dev, device_id_type=MESH
        )

    def send(src, dst, ss, rs, dev):
        one = copy(src, dst, ss, rs, dev)
        one.start()
        started.append(one)

    def flush():
        for one in started:
            one.wait_send()
        started.clear()

    def arrive(dst, ss, rs):
        copy(dst, dst, ss, rs, sib).wait_recv()

    def load(src, dst, k):
        one = pltpu.make_async_copy(src, dst, load_sem.at[k])
        one.start()
        return one

    l_th = load(th_h, th_v, 0)
    mine = yh * 4 + x
    l_sh = load(sh_h, hb.at[mine], 1)
    l_small = [load(tgain_h, tgain, 7), load(sgain_h, sgain, 8), load(docs_h, docs, 9)]

    def wkv_part(j, core):
        return wkv_h.at[:, :, pl.ds(pl.multiple_of((j * 2 + core) * COLS, COLS), COLS)]

    def wkv_load(j):
        return pltpu.make_async_copy(wkv_part(j, c), wkv.at[j, c], v_load.at[j])

    def wkv_go(j, carry):
        wkv_load(j).start()
        return carry

    def wo_part(j, core):
        return wo_h.at[:, pl.ds(pl.multiple_of((j * 2 + core) * COLS, COLS), COLS)]

    def wo_load(j):
        return pltpu.make_async_copy(wo_part(j, c), wo.at[j, c], w_load.at[j])

    def wo_send(j):
        return copy(wo_part(j, 1 - c), wo.at[j, c], w_ss.at[j], w_rs.at[j], sib)

    def wo_fetch(j, carry):
        wo_load(j).start()
        return carry

    def wo_go(j, carry):
        wo_send(j).start()
        return carry

    def wo_got(j, carry):
        wo_load(j).wait()
        arrive(wo.at[j, 1 - c], w_ss.at[j], w_rs.at[j])
        return carry

    def wo_end(j, carry):
        wo_send(j).wait_send()
        return carry

    lax.fori_loop(0, 8, wkv_go, 0)
    l_wq = load(wq_h.at[:, c], wq.at[:, c], 3)

    kv_r[...] = jnp.zeros(kv_r.shape, BF16)

    barrier = pltpu.get_barrier_semaphore()
    for dev in (sib, dev_xp, dev_xm, dev_yo, dev_zp, dev_zm, dev_yl):
        pl.semaphore_signal(barrier, inc=1, device_id=dev, device_id_type=MESH)

    class Gather:
        def __init__(self, buf, ss, rs):
            self.buf, self.ss, self.rs = buf, ss, rs
            self.near = [yh * 4 + xm_, yh * 4 + xp_]
            self.opp = yo_ * 4 + x
            self.onear = [yo_ * 4 + xm_, yo_ * 4 + xp_]
            self.far = [yh * 4 + xf_, yo_ * 4 + xf_]
            self.order = [mine] + self.near + [self.opp] + self.onear + self.far

        def part(self, slot, h):
            return self.buf.at[slot, pl.ds(h * 64, 64)]

        def half(self, slot, h, k, dev):
            part = self.part(slot, h)
            send(part, part, self.ss.at[k], self.rs.at[k], dev)

        def got_half(self, slot, h, k):
            arrive(self.part(slot, h), self.ss.at[k], self.rs.at[k])

        def begin(self, h):
            self.half(mine, h, 0 + h, dev_yo)
            self.half(mine, h, 2 + h, dev_xp)
            self.half(mine, h, 4 + h, dev_xm)

        def near_relay(self):
            self.got_half(self.near[0], 0, 2)
            self.half(self.near[0], 0, 6, dev_xp)
            self.got_half(self.near[1], 1, 5)
            self.half(self.near[1], 1, 7, dev_xm)

        def near_rest(self):
            self.got_half(self.near[0], 1, 3)
            self.got_half(self.near[1], 0, 4)

        def opp_half(self, h):
            self.got_half(self.opp, h, 0 + h)
            self.half(self.opp, h, 8 + h, dev_xp)
            self.half(self.opp, h, 10 + h, dev_xm)

        def onear_a(self):
            self.got_half(self.onear[0], 0, 8)
            self.half(self.onear[0], 0, 12, dev_xp)

        def onear_b(self):
            self.got_half(self.onear[1], 1, 11)
            self.half(self.onear[1], 1, 13, dev_xm)

        def onear_rest(self):
            self.got_half(self.onear[0], 1, 9)
            self.got_half(self.onear[1], 0, 10)

        def far_step(self):
            self.got_half(self.far[0], 0, 6)
            self.got_half(self.far[0], 1, 7)

        def ofar_step(self):
            self.got_half(self.far[1], 0, 12)
            self.got_half(self.far[1], 1, 13)

    def pj_send(k):
        rows = pl.ds(k * 256, 256)
        send(pj_h.at[rows], pj.at[yl, rows], p_ss.at[k], p_rs.at[k], dev_yl)

    def wkv_send(j):
        return copy(wkv_part(j, 1 - c), wkv.at[j, c], v_ss.at[j], v_rs.at[j], sib)

    def wq_send(j):
        return copy(wq_h.at[j, 1 - c], wq.at[j, c], u_ss.at[j], u_rs.at[j], sib)

    def w_go(j, carry):
        wkv_send(j).start()
        wq_send(j).start()
        return carry

    def w_end(j, carry):
        wkv_send(j).wait_send()
        wq_send(j).wait_send()
        return carry

    def w_got(slot):
        wkv_load(slot).wait()
        arrive(wkv.at[slot, 1 - c], v_ss.at[slot], v_rs.at[slot])
        arrive(wq.at[slot, 1 - c], u_ss.at[slot], u_rs.at[slot])

    ag = Gather(hb, ag_ss, ag_rs)
    l_sh.wait()

    z_slot = 0
    l_th.wait()
    for one in l_small:
        one.wait()
    docs_z[z] = docs[...]
    part = jnp.zeros((ROWS, 128), F32)
    for i in range(8):
        cols = slice(i * 128, (i + 1) * 128)
        f = th_v[:, cols].astype(F32)
        part = part + f * f
        tg[z_slot, :, cols] = (f * tgain[:, cols]).astype(BF16)
    sg_s[:, COLS:COLS + 128] = jnp.sum(part.T, axis=0, keepdims=True)
    part = jnp.zeros((ROWS, 128), F32)
    for i in range(4):
        f = hb[mine, :, i * 128:(i + 1) * 128].astype(F32)
        part = part + f * f
    sg_s[:, COLS + 128:COLS + 256] = jnp.sum(part.T, axis=0, keepdims=True)
    sg_s[:, 0:COLS] = sgain[...]
    sg_r[mine] = sg_s[...]

    def ring_slot(d):
        return (0, 1, 2, 3, 4, 7, 6, 5)[d % 8]

    def z_ref(d, h):
        return tg.at[ring_slot(d), pl.ds(h * 64, 64)]

    def z_send(k):
        d = k // 2
        send(z_ref(8 - d, k % 2), z_ref(7 - d, k % 2), z_ss.at[k], z_rs.at[k], dev_zp)
        send(z_ref(d, 1 - k % 2), z_ref(d + 1, 1 - k % 2), z_ss.at[8 + k], z_rs.at[8 + k], dev_zm)

    def z_got(k):
        up, down = z_ref(-(k // 2) + 7, k % 2), z_ref(k // 2 + 1, 1 - k % 2)
        arrive(up, z_ss.at[k], z_rs.at[k])
        arrive(down, z_ss.at[8 + k], z_rs.at[8 + k])

    def z_step(k):
        z_got(k)
        if k + 2 < 7:
            z_send(k + 2)

    def small_send(i, k, dev):
        slot = ag.order[i]
        send(sg_r.at[slot], sg_r.at[slot], sm_ss.at[k], sm_rs.at[k], dev)

    def small_got(i, k):
        arrive(sg_r.at[ag.order[i]], sm_ss.at[k], sm_rs.at[k])

    def docs_send(d, k, dev):
        ref = docs_z.at[(z + d) % 8]
        send(ref, ref, dc_ss.at[k], dc_rs.at[k], dev)

    def docs_step(k):
        arrive(docs_z.at[(z + 7 - k) % 8], dc_ss.at[k], dc_rs.at[k])
        if k < 3:
            arrive(docs_z.at[(z + 1 + k) % 8], dc_ss.at[4 + k], dc_rs.at[4 + k])
            docs_send(7 - k, k + 1, dev_zp)
            if k < 2:
                docs_send(1 + k, k + 5, dev_zm)
        else:
            send(docs_z, docs_o, dc_ss.at[8], dc_rs.at[8], dev_yl)

    pl.semaphore_wait(barrier, 7)
    small_send(0, 0, dev_yo)
    small_send(0, 1, dev_xp)
    small_send(0, 2, dev_xm)
    ag.begin(0)
    ag.begin(1)
    docs_send(0, 0, dev_zp)
    docs_send(0, 4, dev_zm)
    z_send(0)
    pj_send(0)
    lax.fori_loop(0, 8, w_go, 0)
    z_send(1)
    pj_send(1)
    pj_send(2)
    l_pj = load(pj_h, pj.at[yl], 4)

    entry = lax.broadcasted_iota(jnp.int32, (64, ROWS), 0).astype(F32)
    position = (s * ROWS + lax.broadcasted_iota(jnp.int32, (64, ROWS), 1)).astype(F32)
    angle = position * jnp.exp(-math.log(500000.0) * (2.0 * entry / HEAD_DIM))
    cos_t[...] = jnp.cos(angle)
    sin_t[...] = jnp.sin(angle)

    def process(slots, first=False):
        blocks, w = [], []
        for slot in slots:
            parts = []
            for i in range(4):
                cols = slice(i * 128, (i + 1) * 128)
                f = hb[slot, :, cols].astype(F32)
                parts.append((f * scale_v[...] * sg_r[slot][:, cols]).astype(BF16))
            blocks.append(jnp.concatenate(parts, axis=1))
        n = jnp.concatenate(blocks, axis=1)
        for slot in slots:
            w_got(slot)
            w.append(wkv[slot].reshape(128, COLS))
        kv = nt_dot(jnp.concatenate(w, axis=1), n)
        for core in range(2):
            w = jnp.concatenate([wq[slot, core] for slot in slots], axis=0)
            q = jnp.dot(n, w, preferred_element_type=F32)
            k = kv[core * 64:core * 64 + 64]
            q_acc[core] = q if first else q_acc[core] + q
            kv_acc[core] = k if first else kv_acc[core] + k

    small_got(1, 1)
    small_send(1, 3, dev_xp)
    small_got(2, 2)
    small_got(3, 0)
    small_send(3, 4, dev_xp)
    small_send(3, 5, dev_xm)
    docs_step(0)
    ag.near_relay()
    small_got(6, 3)
    docs_step(1)
    small_got(4, 4)
    small_send(4, 6, dev_xp)
    small_got(5, 5)
    ag.near_rest()
    ag.opp_half(0)
    z_step(0)
    pj_send(3)
    small_got(7, 6)
    sums = sg_r[0][:, COLS:COLS + 256]
    for i in range(1, 8):
        sums = sums + sg_r[i][:, COLS:COLS + 256]
    sum_s[...] = sums
    send(sum_s, sum_r, x_ss.at[2], x_rs.at[2], sib)
    docs_step(2)
    ag.opp_half(1)
    arrive(sum_r, x_ss.at[2], x_rs.at[2])
    sums = sum_s[...] + sum_r[...]
    ts_v[...] = jnp.broadcast_to(lax.rsqrt(sums[:, 0:128] / DT + 1e-05), (ROWS, 128)).T
    scale_v[...] = jnp.broadcast_to(lax.rsqrt(sums[:, 128:256] / DS + 1e-05), (ROWS, 128)).T
    docs_step(3)
    z_step(1)
    ag.onear_a()
    l_wq.wait()
    process([mine] + ag.near, True)
    ag.onear_b()
    z_step(2)
    ag.far_step()
    process([ag.opp, ag.far[0]])
    ag.onear_rest()
    process(ag.onear)
    z_step(3)
    ag.ofar_step()
    process([ag.far[1]])
    send(kv_acc.at[1 - c], kv_in, x_ss.at[3], x_rs.at[3], sib)
    send(q_acc.at[1 - c], q_in, x_ss.at[4], x_rs.at[4], sib)
    arrive(kv_in, x_ss.at[3], x_rs.at[3])

    row = lax.broadcasted_iota(jnp.int32, (64, 64), 0)
    col = lax.broadcasted_iota(jnp.int32, (64, 64), 1)
    take = ((row >> 3) & 1) * 32 + (row & 7) * 4 + (row >> 4)
    pick = jnp.where(col == take, 1.0, 0.0).astype(BF16)
    kv_mine = (kv_acc[c] + kv_in[...]).astype(BF16)
    kvx_s[...] = jnp.dot(pick, kv_mine, preferred_element_type=F32).astype(BF16).reshape(4, 16, 128)
    kvx_r[t] = kvx_s[t // 4]

    def kvx(k):
        to = (t + k) % 16
        return copy(kvx_s.at[to // 4], kvx_r.at[t], kx_ss.at[k], kx_rs.at[k], (s, to))

    def kvx_go(k, carry):
        kvx(k).start()
        return carry

    def kvx_got(k, carry):
        arrive(kvx_r.at[(t + 16 - k) % 16], kx_ss.at[k], kx_rs.at[k])
        return carry

    def kvx_end(k, carry):
        kvx(k).wait_send()
        return carry

    lax.fori_loop(1, 16, kvx_go, 0)
    lax.fori_loop(0, 8, wo_fetch, 0)
    lax.fori_loop(0, 8, wo_go, 0)
    z_step(4)

    cos2 = jnp.concatenate([cos_t[...], cos_t[...]], axis=0).T
    sin2 = jnp.concatenate([-sin_t[...], sin_t[...]], axis=0).T
    arrive(q_in, x_ss.at[4], x_rs.at[4])
    q_mine = q_acc[c] + q_in[...]
    for h in range(2):
        qh = q_mine[:, h * 128:(h + 1) * 128]
        turned = qh * cos2 + pltpu.roll(qh, 64, 1) * sin2
        q_v[h] = (turned * HEAD_DIM ** (-0.5)).astype(BF16)

    lax.fori_loop(1, 16, kvx_got, 0)
    both = kvx_r[...].astype(F32).reshape(16, 2, 8, ROWS)
    k_raw = both[:, 0].reshape(HEAD_DIM, ROWS)
    v_raw = both[:, 1].reshape(HEAD_DIM, ROWS)
    first, second = k_raw[0:64], k_raw[64:128]
    k_rot = jnp.concatenate(
        [first * cos_t[...] - second * sin_t[...], second * cos_t[...] + first * sin_t[...]], axis=0
    )
    kv_own[0] = k_rot.astype(BF16)
    kv_own[1] = v_raw.T.astype(BF16)
    kv_r[0, 0] = kv_own[0]
    kv_r[1, 0] = kv_own[1]

    def kv_copy(k):
        return copy(kv_own.at[c], kv_r.at[c, k], kv_ss.at[k], kv_rs.at[k], ((s + k) % 16, t))

    def kv_fwd(k):
        return copy(kv_r.at[c, k], kv_r.at[c, k], kf_ss.at[k], kf_rs.at[k], sib)

    def kv_go(k):
        @pl.when(s + k < 16)
        def _():
            kv_copy(k).start()

    def kv_mid(k):
        @pl.when(s >= k)
        def _():
            arrive(kv_r.at[c, k], kv_ss.at[k], kv_rs.at[k])
            kv_fwd(k).start()

    def kv_got(k, carry):
        @pl.when(s >= k)
        def _():
            arrive(kv_r.at[1 - c, k], kf_ss.at[k], kf_rs.at[k])
        return carry

    def kv_end(k, carry):
        @pl.when(s >= k)
        def _():
            kv_fwd(k).wait_send()

        @pl.when(s + k < 16)
        def _():
            kv_copy(k).wait_send()
        return carry

    arrive(docs_o, dc_ss.at[8], dc_rs.at[8])
    for k in range(1, BACK + 1):
        kv_go(k)

    def docs_back(j):
        at = (z + 8 - j) % 8
        return jnp.where(z >= j, docs_z[at], jnp.where(yl == 1, docs_o[at], -1))

    key_doc = jnp.concatenate([docs_back(j) for j in range(BACK + 1)], axis=1)
    row_doc = jnp.broadcast_to(docs[...].astype(F32), (ROWS, ROWS)).T[:, 0:1].astype(jnp.int32)
    wide = (ROWS, (BACK + 1) * ROWS)
    row_at = lax.broadcasted_iota(jnp.int32, wide, 0)
    key_at = lax.broadcasted_iota(jnp.int32, wide, 1)
    allowed = (key_doc == row_doc) & ((key_at >= ROWS) | (key_at <= row_at))
    bias[...] = jnp.where(allowed, 0.0, -1e30)

    class Reduce:
        def __init__(self, y_order, own, sib_s, sib_r, x2, ra, rb, xp, xm, fm, fp, ys, yr, fin, ss, rs):
            self.own, self.sib_s, self.sib_r = own, sib_s, sib_r
            self.x2, self.ra, self.rb, self.xp, self.xm, self.fm, self.fp = x2, ra, rb, xp, xm, fm, fp
            self.ys, self.yr, self.fin, self.ss, self.rs = ys, yr, fin, ss, rs
            self.y_order = y_order
            self.x_order = (xf_, xp_, xm_, x)

        def go(self, src, dst, k, dev):
            send(src, dst, self.ss.at[k], self.rs.at[k], dev)

        def got(self, dst, k):
            arrive(dst, self.ss.at[k], self.rs.at[k])

        def slot(self, k, i):
            return self.y_order[i] * 4 + self.x_order[k]

        def to_sib(self, k, i):
            slot = self.slot(k, i)
            self.go(self.sib_s.at[slot], self.sib_r.at[slot], k * 2 + i, sib)

        def sib_got(self, k, i):
            if self.sib_r is not None:
                self.got(self.sib_r.at[self.slot(k, i)], k * 2 + i)

        def pair(self, k, i, h):
            slot, rows = self.slot(k, i), slice(h * 64, h * 64 + 64)
            value = self.own[slot, rows]
            return value if self.sib_r is None else value + self.sib_r[slot, rows].astype(F32)

        def far(self, i):
            self.sib_got(0, i)
            self.x2[i, 0:64] = self.pair(0, i, 0).astype(BF16)
            self.go(self.x2.at[i, pl.ds(0, 64)], self.ra.at[i], 8 + i, dev_xp)
            self.x2[i, 64:128] = self.pair(0, i, 1).astype(BF16)
            self.go(self.x2.at[i, pl.ds(64, 64)], self.rb.at[i], 10 + i, dev_xm)

        def near(self, i):
            self.sib_got(1, i)
            self.xp[i, 64:128] = self.pair(1, i, 1).astype(BF16)
            self.go(self.xp.at[i, pl.ds(64, 64)], self.fm.at[i, pl.ds(64, 64)], 12 + i, dev_xp)
            self.sib_got(2, i)
            self.xm[i, 0:64] = self.pair(2, i, 0).astype(BF16)
            self.go(self.xm.at[i, pl.ds(0, 64)], self.fp.at[i, pl.ds(0, 64)], 14 + i, dev_xm)

        def relay(self, i):
            self.got(self.ra.at[i], 8 + i)
            self.xp[i, 0:64] = (self.pair(1, i, 0) + self.ra[i].astype(F32)).astype(BF16)
            self.go(self.xp.at[i, pl.ds(0, 64)], self.fm.at[i, pl.ds(0, 64)], 16 + i, dev_xp)
            self.got(self.rb.at[i], 10 + i)
            self.xm[i, 64:128] = (self.pair(2, i, 1) + self.rb[i].astype(F32)).astype(BF16)
            self.go(self.xm.at[i, pl.ds(64, 64)], self.fp.at[i, pl.ds(64, 64)], 18 + i, dev_xm)

        def join(self, i, h):
            rows, at = slice(h * 64, h * 64 + 64), pl.ds(h * 64, 64)
            if h == 0:
                self.sib_got(3, i)
            self.got(self.fm.at[i, at], (16, 12)[h] + i)
            self.got(self.fp.at[i, at], (14, 18)[h] + i)
            return self.pair(3, i, h) + self.fm[i, rows].astype(F32) + self.fp[i, rows].astype(F32)

        def to_opp(self, h):
            at = pl.ds(h * 64, 64)
            return copy(self.ys.at[at], self.yr.at[at], self.ss.at[20 + h], self.rs.at[20 + h], dev_yo)

        def join_other(self):
            for h in range(2):
                self.ys[h * 64:h * 64 + 64] = self.join(0, h).astype(BF16)
                self.to_opp(h).start()

        def join_mine(self):
            for h in range(2):
                self.fin[h * 64:h * 64 + 64] = self.join(1, h)

        def end(self):
            for h in range(2):
                self.to_opp(h).wait_send()

        def last(self, h):
            rows = slice(h * 64, h * 64 + 64)
            self.got(self.yr.at[pl.ds(h * 64, 64)], 20 + h)
            return self.fin[rows] + self.yr[rows].astype(F32)

    rt = Reduce((yl, 1 - yl), t_own, t_sib_s, t_sib_r, t_x2, t_ra, t_rb, t_xp, t_xm, t_fm, t_fp, None, None, None, t_ss, t_rs)

    def t3(i, h):
        at = pl.ds(h * 64, 64)
        dev = (yl * 8 + (z + turn) % 8, rt.y_order[i] * 8 + z)
        return copy(t3_s.at[i, at], t3_r.at[yh, at], t3_ss.at[i * 2 + h], t3_rs.at[yh * 2 + h], dev)

    def t3_stays(i):
        return stays & (rt.y_order[i] == yh)

    def t_place(i):
        for h in range(2):
            rows = slice(h * 64, h * 64 + 64)
            t3_s[i, rows] = rt.join(i, h).astype(BF16)

            @pl.when(t3_stays(i))
            def _():
                t3_r[yh, rows] = t3_s[i, rows]

            @pl.when(jnp.logical_not(t3_stays(i)))
            def _():
                t3(i, h).start()

    z_step(5)
    z_step(6)

    def products(core, y_, k, width):
        rows = tg[pl.ds(core * 4, 4), :, k * width:(k + 1) * width].reshape(4 * ROWS, width)
        return jnp.dot(rows, pj[y_, k * width:(k + 1) * width], preferred_element_type=F32).reshape(4, ROWS, COLS)

    l_pj.wait()
    first = pl.ds(yl * 4, 4)
    t_sib_s[first] = products(1 - c, yl, 0, 1024).astype(BF16)
    for k in range(4):
        rt.to_sib(k, 0)
    t_own[first] = products(c, yl, 0, 1024)
    rt.far(0)
    rt.near(0)

    other = pl.ds((1 - yl) * 4, 4)
    for k in range(4):
        arrive(pj.at[1 - yl, pl.ds(k * 256, 256)], p_ss.at[k], p_rs.at[k])
        theirs = products(1 - c, 1 - yl, k, 256)
        if k == 0:
            t_part[...] = theirs
        elif k < 3:
            t_part[...] += theirs
        else:
            t_sib_s[other] = (t_part[...] + theirs).astype(BF16)
            for j in range(4):
                rt.to_sib(j, 1)
        if k == 0:
            t_own[other] = products(c, 1 - yl, k, 256)
        else:
            t_own[other] += products(c, 1 - yl, k, 256)
        if k == 1:
            rt.relay(0)
    rt.far(1)
    rt.near(1)
    t_place(0)
    for k in range(1, BACK + 1):
        kv_mid(k)
    rt.relay(1)

    lax.fori_loop(1, BACK + 1, kv_got, 0)
    keys = jnp.concatenate([kv_r[0, j] for j in range(BACK + 1)], axis=1)
    values = kv_r[1].reshape((BACK + 1) * ROWS, HEAD_DIM)
    for h in range(2):
        scores = jnp.dot(q_v[h], keys, preferred_element_type=F32)
        scores = scores + bias[...]
        probs = jnp.exp(scores - jnp.max(scores, axis=1, keepdims=True))
        total = jnp.sum(probs, axis=1, keepdims=True)
        acc = jnp.dot(probs.astype(BF16), values, preferred_element_type=F32)
        attn_v[c * 2 + h] = (acc / total).astype(BF16)
        send(attn_v.at[c * 2 + h], attn_v.at[c * 2 + h], x_ss.at[5 + h], x_rs.at[5 + h], sib)
    lax.fori_loop(0, 8, wo_got, 0)

    ro = Reduce((yo_, yh), o_own, None, None, o_x2, o_ra, o_rb, o_xp, o_xm, o_fm, o_fp, o_ys, o_yr, o_fin, o_ss, o_rs)

    for h in range(2):
        arrive(attn_v.at[2 - 2 * c + h], x_ss.at[5 + h], x_rs.at[5 + h])
    attn = jnp.concatenate([attn_v[i] for i in range(4)], axis=1)

    def out_block(k, i):
        slot = ro.slot(k, i)
        o_own[slot] = jnp.dot(attn, wo[slot].reshape(COLS, COLS), preferred_element_type=F32)

    out_block(0, 0)
    ro.far(0)
    out_block(1, 0)
    out_block(2, 0)
    ro.near(0)
    t_place(1)
    out_block(0, 1)
    ro.relay(0)
    ro.far(1)
    out_block(1, 1)
    out_block(2, 1)
    ro.near(1)
    out_block(3, 0)
    out_block(3, 1)
    ro.relay(1)

    ro.join_other()
    ro.join_mine()

    early = list(started)
    started.clear()

    def before_end():
        for one in early:
            one.wait_send()
        lax.fori_loop(0, 8, w_end, 0)
        lax.fori_loop(0, 8, wo_end, 0)
        lax.fori_loop(1, 16, kvx_end, 0)
        lax.fori_loop(1, BACK + 1, kv_end, 0)
        ro.end()
        for i in range(2):

            @pl.when(jnp.logical_not(t3_stays(i)))
            def _():
                t3(i, 0).wait_send()
                t3(i, 1).wait_send()

    dg = Gather(db, dg_ss, dg_rs)
    for h in range(2):
        rows = slice(h * 64, h * 64 + 64)
        mixed = hb[mine, rows].astype(F32) + ro.last(h)
        out_s[rows] = mixed.astype(BF16)

        for p in range(2):

            @pl.when(jnp.logical_not(stays & (yh == p)))
            def _():
                arrive(t3_r.at[p, pl.ds(h * 64, 64)], t3_ss.at[h], t3_rs.at[p * 2 + h])

        target = t3_r[0, rows].astype(F32) + t3_r[1, rows].astype(F32)
        target = target * jnp.concatenate([ts_v[rows]] * 4, axis=1)
        difference = mixed - target
        db[mine, rows] = difference.astype(BF16)
        dg.begin(h)
        squares = difference * difference
        l_v[rows] = (
            squares[:, 0:128] + squares[:, 128:256] + squares[:, 256:384] + squares[:, 384:512]
        )
    l_s[...] = jnp.sum(l_v[...].T, axis=0, keepdims=True)
    l_r[t] = l_s[...]

    def loss(k):
        return copy(l_s, l_r.at[t], l_ss.at[k], l_rs.at[k], (s, (t + k) % 16))

    def loss_go(k, carry):
        loss(k).start()
        return carry

    def loss_got(k, carry):
        arrive(l_r.at[(t + 16 - k) % 16], l_ss.at[k], l_rs.at[k])
        return carry

    def loss_end(k, carry):
        loss(k).wait_send()
        return carry

    lax.fori_loop(1, 16, loss_go, 0)

    def add_grad(slots, first=False):
        d = jnp.concatenate([db[slot] for slot in slots], axis=1)
        for core in range(2):
            w = jnp.concatenate([wo[slot, core] for slot in slots], axis=1)
            g = nt_dot(d, w)
            g_acc[core] = g if first else g_acc[core] + g

    dg.near_relay()
    dg.opp_half(0)
    dg.near_rest()
    before_end()
    add_grad([mine] + dg.near, True)
    dg.opp_half(1)
    dg.onear_a()
    dg.far_step()
    add_grad([dg.opp, dg.far[0]])
    dg.onear_b()
    dg.onear_rest()
    add_grad(dg.onear)
    lax.fori_loop(1, 16, loss_got, 0)
    loss_sum = l_r[0]
    for i in range(1, 16):
        loss_sum = loss_sum + l_r[i]
    out_l[...] = loss_sum / DS
    dg.ofar_step()
    add_grad([dg.far[1]])
    send(g_acc.at[1 - c], g_in, x_ss.at[7], x_rs.at[7], sib)
    arrive(g_in, x_ss.at[7], x_rs.at[7])
    out_g[...] = (g_acc[c] + g_in[...]).astype(BF16)

    flush()
    lax.fori_loop(1, 16, loss_end, 0)


def reduce_buffers():
    block = (ROWS, COLS)
    return [
        pltpu.VMEM((2, 64, COLS), BF16),
        pltpu.VMEM((2, 64, COLS), BF16),
        pltpu.VMEM((2,) + block, BF16),
        pltpu.VMEM((2,) + block, BF16),
        pltpu.VMEM((2,) + block, BF16),
        pltpu.VMEM((2,) + block, BF16),
        pltpu.VMEM(block, BF16),
        pltpu.VMEM(block, BF16),
        pltpu.VMEM(block, F32),
    ]


def on_device(
    teacher_hidden, teacher_gain, projector, student_hidden, student_gain,
    query_weight, kv_weight, out_weight, doc_ids,
):
    block = (ROWS, COLS)
    hbm = pl.BlockSpec(memory_space=pltpu.HBM)
    vmem = pl.BlockSpec(memory_space=pltpu.VMEM)
    dma = pltpu.SemaphoreType.DMA
    out_s, out_l, out_g = pl.pallas_call(
        body,
        out_shape=(
            jax.ShapeDtypeStruct(block, BF16),
            jax.ShapeDtypeStruct((1, ROWS), F32),
            jax.ShapeDtypeStruct((ROWS, 256), BF16),
        ),
        in_specs=[hbm] * 9,
        out_specs=(vmem, vmem, vmem),
        scratch_shapes=[
            pltpu.VMEM((1, 1024), F32),
            pltpu.VMEM((1, COLS), F32),
            pltpu.VMEM((1, ROWS), jnp.int32),
            pltpu.VMEM((ROWS, 1024), BF16),
            pltpu.VMEM((8, ROWS, 1024), BF16),
            pltpu.VMEM((2, 1024, COLS), BF16),
            pltpu.VMEM((8, 2, COLS, 256), BF16),
            pltpu.VMEM((8, 2, 2, 32, COLS), BF16),
            pltpu.VMEM((8, 2, 256, COLS), BF16),
            pltpu.VMEM((64, ROWS), F32),
            pltpu.VMEM((64, ROWS), F32),
            pltpu.VMEM((8,) + block, BF16),
            pltpu.VMEM((1, 768), F32),
            pltpu.VMEM((8, 1, 768), F32),
            pltpu.VMEM((1, 256), F32),
            pltpu.VMEM((1, 256), F32),
            pltpu.VMEM((ROWS, 128), F32),
            pltpu.VMEM((2, ROWS, 256), F32),
            pltpu.VMEM((ROWS, 256), F32),
            pltpu.VMEM((2, 64, ROWS), F32),
            pltpu.VMEM((64, ROWS), F32),
            pltpu.VMEM((4, 16, ROWS), BF16),
            pltpu.VMEM((16, 16, ROWS), BF16),
            pltpu.VMEM((2, ROWS, HEAD_DIM), BF16),
            pltpu.VMEM((2, BACK + 1, ROWS, HEAD_DIM), BF16),
            pltpu.VMEM((8, 1, ROWS), jnp.int32),
            pltpu.VMEM((8, 1, ROWS), jnp.int32),
            pltpu.VMEM((2, ROWS, HEAD_DIM), BF16),
            pltpu.VMEM((4, ROWS, HEAD_DIM), BF16),
            pltpu.VMEM((ROWS, (BACK + 1) * ROWS), F32),
            pltpu.VMEM((8,) + block, F32),
            pltpu.VMEM((4,) + block, F32),
            pltpu.VMEM((8,) + block, F32),
            pltpu.VMEM((2,) + block, BF16),
            pltpu.VMEM((8,) + block, BF16),
            pltpu.VMEM((8,) + block, BF16),
            pltpu.VMEM((2,) + block, BF16),
            *reduce_buffers()[:6],
            *reduce_buffers(),
            pltpu.VMEM((2,) + block, BF16),
            pltpu.VMEM((2,) + block, BF16),
            pltpu.VMEM((ROWS, 128), F32),
            pltpu.VMEM((8,) + block, BF16),
            pltpu.VMEM((2, ROWS, 256), F32),
            pltpu.VMEM((ROWS, 256), F32),
            pltpu.VMEM((ROWS, 128), F32),
            pltpu.VMEM((1, ROWS), F32),
            pltpu.VMEM((16, 1, ROWS), F32),
            dma((10,)),
            *[dma((8,)) for _ in range(10)],
            dma((16,)), dma((16,)), dma((8,)), dma((8,)),
            dma((24,)), dma((24,)), dma((24,)), dma((24,)),
            dma((16,)), dma((16,)), dma((16,)), dma((16,)),
            dma((9,)), dma((9,)), dma((9,)), dma((9,)), dma((9,)), dma((9,)),
            dma((24,)), dma((24,)), dma((24,)), dma((24,)),
            dma((4,)), dma((4,)),
            dma((16,)), dma((16,)),
        ],
        compiler_params=pltpu.CompilerParams(
            collective_id=0, has_side_effects=True, vmem_limit_bytes=40 * 1024 * 1024
        ),
    )(
        *(
            pltpu.with_memory_space_constraint(one, pltpu.HBM)
            for one in (
                teacher_hidden, teacher_gain.reshape(1, -1), projector, student_hidden,
                student_gain.reshape(1, -1), query_weight.reshape(8, 2, COLS, 256), jnp.transpose(kv_weight, (0, 2, 1)),
                out_weight, doc_ids.reshape(1, -1),
            )
        )
    )
    return out_s, out_l.reshape(ROWS), out_g


def solution(mesh):
    in_specs = (
        P("seq", "tensor"),
        P("tensor"),
        P("tensor", "seq"),
        P("seq", "tensor"),
        P("tensor"),
        P(None, "tensor"),
        P(None, None, "tensor"),
        P("tensor", None),
        P("seq"),
    )
    out_specs = (P("seq", "tensor"), P("seq"), P("seq", "tensor"))
    return jax.shard_map(
        on_device, mesh=mesh, in_specs=in_specs, out_specs=out_specs, check_vma=False
    )
```

```python
import math

import jax
import jax.numpy as jnp
from jax import lax
from jax.experimental import pallas as pl
from jax.experimental.pallas import tpu as pltpu
from jax.sharding import PartitionSpec as P

DT = 16384
DS = 8192
HEAD_DIM = 128
HEADS = 32
KV_HEADS = 4
ROWS = 128
COLS = 512
BACK = 8
F32 = jnp.float32
BF16 = jnp.bfloat16
MESH = pl.DeviceIdType.MESH
NT = (((1,), (1,)), ((), ()))


def nt_dot(a, b):
    return lax.dot_general(a, b, NT, preferred_element_type=F32)


def body(
    th_h, tgain_h, pj_h, sh_h, sgain_h, wq_h, wkv_h, wo_h, docs_h,
    out_s, out_l, out_g,
    tgain, sgain, docs, th_v, tg, pj, wq, wkv, wo, cos_t, sin_t,
    hb, sg_s, sg_r, sum_s, sum_r, scale_v, q_acc, q_in, kv_acc, kv_in,
    kvx_s, kvx_r, kv_own, kv_r, docs_z, docs_o, q_v, attn_v, bias,
    t_own, t_part, o_own, o_x2, t_sib_s, t_sib_r, t_x2, t_ra, t_rb, t_xp, t_xm, t_fm, t_fp,
    o_ra, o_rb, o_xp, o_xm, o_fm, o_fp, o_ys, o_yr, o_fin,
    t3_s, t3_r, ts_v, db, g_acc, g_in, l_v, l_s, l_r,
    load_sem, w_load, w_ss, w_rs, v_load, v_ss, v_rs, u_ss, u_rs, x_ss, x_rs, z_ss, z_rs, p_ss, p_rs,
    ag_ss, ag_rs, dg_ss, dg_rs, sm_ss, sm_rs, kx_ss, kx_rs, kv_ss, kv_rs, kf_ss, kf_rs, dc_ss, dc_rs,
    t_ss, t_rs, o_ss, o_rs, t3_ss, t3_rs, l_ss, l_rs,
):
    s = lax.axis_index("seq")
    t = lax.axis_index("tensor")
    yl, z = s // 8, s % 8
    yh, x, c = t // 8, (t // 2) % 4, t % 2

    def tid(y_, x_, c_):
        return y_ * 8 + x_ * 2 + c_

    xp_, xm_ = (x + 1) % 4, (x + 3) % 4
    xf_ = (x + 2) % 4
    yo_ = 1 - yh
    sib = (s, tid(yh, x, 1 - c))
    dev_xp = (s, tid(yh, xp_, c))
    dev_xm = (s, tid(yh, xm_, c))
    dev_yo = (s, tid(yo_, x, c))
    dev_zp = (yl * 8 + (z + 1) % 8, t)
    dev_zm = (yl * 8 + (z + 7) % 8, t)
    dev_yl = ((1 - yl) * 8 + z, t)
    turn = jnp.where(c == 0, x, jnp.where(x == 0, 4, 8 - x))
    stays = (z == 0) & (x == 0) & (c == 0)

    started = []

    def copy(src, dst, ss, rs, dev):
        return pltpu.make_async_remote_copy(
            src_ref=src, dst_ref=dst, send_sem=ss, recv_sem=rs, device_id=dev, device_id_type=MESH
        )

    def send(src, dst, ss, rs, dev):
        one = copy(src, dst, ss, rs, dev)
        one.start()
        started.append(one)

    def flush():
        for one in started:
            one.wait_send()
        started.clear()

    def arrive(dst, ss, rs):
        copy(dst, dst, ss, rs, sib).wait_recv()

    def load(src, dst, k):
        one = pltpu.make_async_copy(src, dst, load_sem.at[k])
        one.start()
        return one

    l_th = load(th_h, th_v, 0)
    mine = yh * 4 + x
    l_sh = load(sh_h, hb.at[mine], 1)
    l_small = [load(tgain_h, tgain, 7), load(sgain_h, sgain, 8), load(docs_h, docs, 9)]

    def wkv_part(j, core):
        return wkv_h.at[:, :, pl.ds(pl.multiple_of((j * 2 + core) * COLS, COLS), COLS)]

    def wkv_load(j):
        return pltpu.make_async_copy(wkv_part(j, c), wkv.at[j, c], v_load.at[j])

    def wkv_go(j, carry):
        wkv_load(j).start()
        return carry

    def wo_part(j, core):
        return wo_h.at[:, pl.ds(pl.multiple_of((j * 2 + core) * COLS, COLS), COLS)]

    def wo_load(j):
        return pltpu.make_async_copy(wo_part(j, c), wo.at[j, c], w_load.at[j])

    def wo_send(j):
        return copy(wo_part(j, 1 - c), wo.at[j, c], w_ss.at[j], w_rs.at[j], sib)

    def wo_fetch(j, carry):
        wo_load(j).start()
        return carry

    def wo_go(j, carry):
        wo_send(j).start()
        return carry

    def wo_got(j, carry):
        wo_load(j).wait()
        arrive(wo.at[j, 1 - c], w_ss.at[j], w_rs.at[j])
        return carry

    def wo_end(j, carry):
        wo_send(j).wait_send()
        return carry

    lax.fori_loop(0, 8, wkv_go, 0)
    l_wq = load(wq_h.at[:, c], wq.at[:, c], 3)

    kv_r[...] = jnp.zeros(kv_r.shape, BF16)

    barrier = pltpu.get_barrier_semaphore()
    for dev in (sib, dev_xp, dev_xm, dev_yo, dev_zp, dev_zm, dev_yl):
        pl.semaphore_signal(barrier, inc=1, device_id=dev, device_id_type=MESH)

    class Gather:
        def __init__(self, buf, ss, rs):
            self.buf, self.ss, self.rs = buf, ss, rs
            self.near = [yh * 4 + xm_, yh * 4 + xp_]
            self.opp = yo_ * 4 + x
            self.onear = [yo_ * 4 + xm_, yo_ * 4 + xp_]
            self.far = [yh * 4 + xf_, yo_ * 4 + xf_]
            self.order = [mine] + self.near + [self.opp] + self.onear + self.far

        def part(self, slot, h):
            return self.buf.at[slot, pl.ds(h * 64, 64)]

        def half(self, slot, h, k, dev):
            part = self.part(slot, h)
            send(part, part, self.ss.at[k], self.rs.at[k], dev)

        def got_half(self, slot, h, k):
            arrive(self.part(slot, h), self.ss.at[k], self.rs.at[k])

        def begin(self, h):
            self.half(mine, h, 0 + h, dev_yo)
            self.half(mine, h, 2 + h, dev_xp)
            self.half(mine, h, 4 + h, dev_xm)

        def near_relay(self):
            self.got_half(self.near[0], 0, 2)
            self.half(self.near[0], 0, 6, dev_xp)
            self.got_half(self.near[1], 1, 5)
            self.half(self.near[1], 1, 7, dev_xm)

        def near_rest(self):
            self.got_half(self.near[0], 1, 3)
            self.got_half(self.near[1], 0, 4)

        def opp_half(self, h):
            self.got_half(self.opp, h, 0 + h)
            self.half(self.opp, h, 8 + h, dev_xp)
            self.half(self.opp, h, 10 + h, dev_xm)

        def onear_a(self):
            self.got_half(self.onear[0], 0, 8)
            self.half(self.onear[0], 0, 12, dev_xp)

        def onear_b(self):
            self.got_half(self.onear[1], 1, 11)
            self.half(self.onear[1], 1, 13, dev_xm)

        def onear_rest(self):
            self.got_half(self.onear[0], 1, 9)
            self.got_half(self.onear[1], 0, 10)

        def far_step(self):
            self.got_half(self.far[0], 0, 6)
            self.got_half(self.far[0], 1, 7)

        def ofar_step(self):
            self.got_half(self.far[1], 0, 12)
            self.got_half(self.far[1], 1, 13)

    def pj_send(k):
        rows = pl.ds(k * 128, 128)
        send(pj_h.at[rows], pj.at[yl, rows], p_ss.at[k], p_rs.at[k], dev_yl)

    def wkv_send(j):
        return copy(wkv_part(j, 1 - c), wkv.at[j, c], v_ss.at[j], v_rs.at[j], sib)

    def wq_send(j):
        return copy(wq_h.at[j, 1 - c], wq.at[j, c], u_ss.at[j], u_rs.at[j], sib)

    def w_go(j, carry):
        wkv_send(j).start()
        wq_send(j).start()
        return carry

    def w_end(j, carry):
        wkv_send(j).wait_send()
        wq_send(j).wait_send()
        return carry

    def w_got(slot):
        wkv_load(slot).wait()
        arrive(wkv.at[slot, 1 - c], v_ss.at[slot], v_rs.at[slot])
        arrive(wq.at[slot, 1 - c], u_ss.at[slot], u_rs.at[slot])

    ag = Gather(hb, ag_ss, ag_rs)
    l_sh.wait()
    pl.semaphore_wait(barrier, 7)
    ag.begin(0)

    z_slot = 0
    l_th.wait()
    for one in l_small:
        one.wait()
    docs_z[z] = docs[...]
    part = jnp.zeros((ROWS, 128), F32)
    for i in range(8):
        cols = slice(i * 128, (i + 1) * 128)
        f = th_v[:, cols].astype(F32)
        part = part + f * f
        tg[z_slot, :, cols] = (f * tgain[:, cols]).astype(BF16)
    sg_s[:, COLS:COLS + 128] = jnp.sum(part.T, axis=0, keepdims=True)
    part = jnp.zeros((ROWS, 128), F32)
    for i in range(4):
        f = hb[mine, :, i * 128:(i + 1) * 128].astype(F32)
        part = part + f * f
    sg_s[:, COLS + 128:COLS + 256] = jnp.sum(part.T, axis=0, keepdims=True)
    sg_s[:, 0:COLS] = sgain[...]
    sg_r[mine] = sg_s[...]

    def ring_slot(d):
        return (0, 1, 2, 3, 4, 7, 6, 5)[d % 8]

    def z_ref(d, h):
        return tg.at[ring_slot(d), pl.ds(h * 64, 64)]

    def z_send(k):
        d = k // 2
        send(z_ref(8 - d, k % 2), z_ref(7 - d, k % 2), z_ss.at[k], z_rs.at[k], dev_zp)
        send(z_ref(d, 1 - k % 2), z_ref(d + 1, 1 - k % 2), z_ss.at[8 + k], z_rs.at[8 + k], dev_zm)

    def z_got(k):
        up, down = z_ref(-(k // 2) + 7, k % 2), z_ref(k // 2 + 1, 1 - k % 2)
        arrive(up, z_ss.at[k], z_rs.at[k])
        arrive(down, z_ss.at[8 + k], z_rs.at[8 + k])

    def z_step(k):
        z_got(k)
        if k + 2 < 7:
            z_send(k + 2)

    def small_send(i, k, dev):
        slot = ag.order[i]
        send(sg_r.at[slot], sg_r.at[slot], sm_ss.at[k], sm_rs.at[k], dev)

    def small_got(i, k):
        arrive(sg_r.at[ag.order[i]], sm_ss.at[k], sm_rs.at[k])

    def docs_send(d, k, dev):
        ref = docs_z.at[(z + d) % 8]
        send(ref, ref, dc_ss.at[k], dc_rs.at[k], dev)

    def docs_step(k):
        arrive(docs_z.at[(z + 7 - k) % 8], dc_ss.at[k], dc_rs.at[k])
        if k < 3:
            arrive(docs_z.at[(z + 1 + k) % 8], dc_ss.at[4 + k], dc_rs.at[4 + k])
            docs_send(7 - k, k + 1, dev_zp)
            if k < 2:
                docs_send(1 + k, k + 5, dev_zm)
        else:
            send(docs_z, docs_o, dc_ss.at[8], dc_rs.at[8], dev_yl)

    small_send(0, 0, dev_yo)
    small_send(0, 1, dev_xp)
    small_send(0, 2, dev_xm)
    ag.begin(1)
    docs_send(0, 0, dev_zp)
    docs_send(0, 4, dev_zm)
    z_send(0)
    pj_send(0)
    lax.fori_loop(0, 8, w_go, 0)
    z_send(1)
    l_pj = load(pj_h, pj.at[yl], 4)

    entry = lax.broadcasted_iota(jnp.int32, (64, ROWS), 0).astype(F32)
    position = (s * ROWS + lax.broadcasted_iota(jnp.int32, (64, ROWS), 1)).astype(F32)
    angle = position * jnp.exp(-math.log(500000.0) * (2.0 * entry / HEAD_DIM))
    cos_t[...] = jnp.cos(angle)
    sin_t[...] = jnp.sin(angle)

    def process(slots, first=False):
        blocks, w = [], []
        for slot in slots:
            parts = []
            for i in range(4):
                cols = slice(i * 128, (i + 1) * 128)
                f = hb[slot, :, cols].astype(F32)
                parts.append((f * scale_v[...] * sg_r[slot][:, cols]).astype(BF16))
            blocks.append(jnp.concatenate(parts, axis=1))
        n = jnp.concatenate(blocks, axis=1)
        for slot in slots:
            w_got(slot)
            w.append(wkv[slot].reshape(128, COLS))
        kv = nt_dot(jnp.concatenate(w, axis=1), n)
        for core in range(2):
            w = jnp.concatenate([wq[slot, core] for slot in slots], axis=0)
            q = jnp.dot(n, w, preferred_element_type=F32)
            k = kv[core * 64:core * 64 + 64]
            q_acc[core] = q if first else q_acc[core] + q
            kv_acc[core] = k if first else kv_acc[core] + k

    small_got(1, 1)
    small_send(1, 3, dev_xp)
    small_got(2, 2)
    small_got(3, 0)
    small_send(3, 4, dev_xp)
    small_send(3, 5, dev_xm)
    docs_step(0)
    ag.near_relay()
    pj_send(1)
    small_got(6, 3)
    docs_step(1)
    small_got(4, 4)
    small_send(4, 6, dev_xp)
    small_got(5, 5)
    ag.near_rest()
    ag.opp_half(0)
    z_step(0)
    pj_send(2)
    small_got(7, 6)
    sums = sg_r[0][:, COLS:COLS + 256]
    for i in range(1, 8):
        sums = sums + sg_r[i][:, COLS:COLS + 256]
    sum_s[...] = sums
    send(sum_s, sum_r, x_ss.at[2], x_rs.at[2], sib)
    docs_step(2)
    ag.opp_half(1)
    pj_send(3)
    arrive(sum_r, x_ss.at[2], x_rs.at[2])
    sums = sum_s[...] + sum_r[...]
    ts_v[...] = jnp.broadcast_to(lax.rsqrt(sums[:, 0:128] / DT + 1e-05), (ROWS, 128)).T
    scale_v[...] = jnp.broadcast_to(lax.rsqrt(sums[:, 128:256] / DS + 1e-05), (ROWS, 128)).T
    docs_step(3)
    z_step(1)
    ag.onear_a()
    pj_send(4)
    l_wq.wait()
    process([mine] + ag.near, True)
    ag.onear_b()
    pj_send(5)
    z_step(2)
    ag.far_step()
    process([ag.opp, ag.far[0]])
    pj_send(6)
    ag.onear_rest()
    process(ag.onear)
    pj_send(7)
    z_step(3)
    ag.ofar_step()
    process([ag.far[1]])
    send(kv_acc.at[1 - c], kv_in, x_ss.at[3], x_rs.at[3], sib)
    send(q_acc.at[1 - c], q_in, x_ss.at[4], x_rs.at[4], sib)
    arrive(kv_in, x_ss.at[3], x_rs.at[3])

    row = lax.broadcasted_iota(jnp.int32, (64, 64), 0)
    col = lax.broadcasted_iota(jnp.int32, (64, 64), 1)
    take = ((row >> 3) & 1) * 32 + (row & 7) * 4 + (row >> 4)
    pick = jnp.where(col == take, 1.0, 0.0).astype(BF16)
    kv_mine = (kv_acc[c] + kv_in[...]).astype(BF16)
    kvx_s[...] = jnp.dot(pick, kv_mine, preferred_element_type=F32).astype(BF16).reshape(4, 16, 128)
    kvx_r[t] = kvx_s[t // 4]

    def kvx(k):
        to = (t + k) % 16
        return copy(kvx_s.at[to // 4], kvx_r.at[t], kx_ss.at[k], kx_rs.at[k], (s, to))

    def kvx_go(k, carry):
        kvx(k).start()
        return carry

    def kvx_got(k, carry):
        arrive(kvx_r.at[(t + 16 - k) % 16], kx_ss.at[k], kx_rs.at[k])
        return carry

    def kvx_end(k, carry):
        kvx(k).wait_send()
        return carry

    lax.fori_loop(1, 16, kvx_go, 0)
    lax.fori_loop(0, 8, wo_fetch, 0)
    lax.fori_loop(0, 8, wo_go, 0)
    z_step(4)

    cos2 = jnp.concatenate([cos_t[...], cos_t[...]], axis=0).T
    sin2 = jnp.concatenate([-sin_t[...], sin_t[...]], axis=0).T
    arrive(q_in, x_ss.at[4], x_rs.at[4])
    q_mine = q_acc[c] + q_in[...]
    for h in range(2):
        qh = q_mine[:, h * 128:(h + 1) * 128]
        turned = qh * cos2 + pltpu.roll(qh, 64, 1) * sin2
        q_v[h] = (turned * HEAD_DIM ** (-0.5)).astype(BF16)

    lax.fori_loop(1, 16, kvx_got, 0)
    both = kvx_r[...].astype(F32).reshape(16, 2, 8, ROWS)
    k_raw = both[:, 0].reshape(HEAD_DIM, ROWS)
    v_raw = both[:, 1].reshape(HEAD_DIM, ROWS)
    first, second = k_raw[0:64], k_raw[64:128]
    k_rot = jnp.concatenate(
        [first * cos_t[...] - second * sin_t[...], second * cos_t[...] + first * sin_t[...]], axis=0
    )
    kv_own[0] = k_rot.astype(BF16)
    kv_own[1] = v_raw.T.astype(BF16)
    kv_r[0, 0] = kv_own[0]
    kv_r[1, 0] = kv_own[1]

    def kv_copy(k):
        return copy(kv_own.at[c], kv_r.at[c, k], kv_ss.at[k], kv_rs.at[k], ((s + k) % 16, t))

    def kv_fwd(k):
        return copy(kv_r.at[c, k], kv_r.at[c, k], kf_ss.at[k], kf_rs.at[k], sib)

    def kv_go(k):
        @pl.when(s + k < 16)
        def _():
            kv_copy(k).start()

    def kv_mid(k):
        @pl.when(s >= k)
        def _():
            arrive(kv_r.at[c, k], kv_ss.at[k], kv_rs.at[k])
            kv_fwd(k).start()

    def kv_got(k, carry):
        @pl.when(s >= k)
        def _():
            arrive(kv_r.at[1 - c, k], kf_ss.at[k], kf_rs.at[k])
        return carry

    def kv_end(k, carry):
        @pl.when(s >= k)
        def _():
            kv_fwd(k).wait_send()

        @pl.when(s + k < 16)
        def _():
            kv_copy(k).wait_send()
        return carry

    arrive(docs_o, dc_ss.at[8], dc_rs.at[8])
    for k in range(1, BACK + 1):
        kv_go(k)

    def docs_back(j):
        at = (z + 8 - j) % 8
        return jnp.where(z >= j, docs_z[at], jnp.where(yl == 1, docs_o[at], -1))

    key_doc = jnp.concatenate([docs_back(j) for j in range(BACK + 1)], axis=1)
    row_doc = jnp.broadcast_to(docs[...].astype(F32), (ROWS, ROWS)).T[:, 0:1].astype(jnp.int32)
    wide = (ROWS, (BACK + 1) * ROWS)
    row_at = lax.broadcasted_iota(jnp.int32, wide, 0)
    key_at = lax.broadcasted_iota(jnp.int32, wide, 1)
    allowed = (key_doc == row_doc) & ((key_at >= ROWS) | (key_at <= row_at))
    bias[...] = jnp.where(allowed, 0.0, -1e30)

    class Reduce:
        def __init__(self, y_order, own, sib_s, sib_r, x2, ra, rb, xp, xm, fm, fp, ys, yr, fin, ss, rs):
            self.own, self.sib_s, self.sib_r = own, sib_s, sib_r
            self.x2, self.ra, self.rb, self.xp, self.xm, self.fm, self.fp = x2, ra, rb, xp, xm, fm, fp
            self.ys, self.yr, self.fin, self.ss, self.rs = ys, yr, fin, ss, rs
            self.y_order = y_order
            self.x_order = (xf_, xp_, xm_, x)

        def go(self, src, dst, k, dev):
            send(src, dst, self.ss.at[k], self.rs.at[k], dev)

        def got(self, dst, k):
            arrive(dst, self.ss.at[k], self.rs.at[k])

        def slot(self, k, i):
            return self.y_order[i] * 4 + self.x_order[k]

        def to_sib(self, k, i):
            slot = self.slot(k, i)
            self.go(self.sib_s.at[slot], self.sib_r.at[slot], k * 2 + i, sib)

        def sib_got(self, k, i):
            if self.sib_r is not None:
                self.got(self.sib_r.at[self.slot(k, i)], k * 2 + i)

        def pair(self, k, i, h):
            slot, rows = self.slot(k, i), slice(h * 64, h * 64 + 64)
            value = self.own[slot, rows]
            return value if self.sib_r is None else value + self.sib_r[slot, rows].astype(F32)

        def far(self, i):
            self.sib_got(0, i)
            self.x2[i, 0:64] = self.pair(0, i, 0).astype(BF16)
            self.go(self.x2.at[i, pl.ds(0, 64)], self.ra.at[i], 8 + i, dev_xp)
            self.x2[i, 64:128] = self.pair(0, i, 1).astype(BF16)
            self.go(self.x2.at[i, pl.ds(64, 64)], self.rb.at[i], 10 + i, dev_xm)

        def near(self, i):
            self.sib_got(1, i)
            self.xp[i, 64:128] = self.pair(1, i, 1).astype(BF16)
            self.go(self.xp.at[i, pl.ds(64, 64)], self.fm.at[i, pl.ds(64, 64)], 12 + i, dev_xp)
            self.sib_got(2, i)
            self.xm[i, 0:64] = self.pair(2, i, 0).astype(BF16)
            self.go(self.xm.at[i, pl.ds(0, 64)], self.fp.at[i, pl.ds(0, 64)], 14 + i, dev_xm)

        def relay(self, i):
            self.got(self.ra.at[i], 8 + i)
            self.xp[i, 0:64] = (self.pair(1, i, 0) + self.ra[i].astype(F32)).astype(BF16)
            self.go(self.xp.at[i, pl.ds(0, 64)], self.fm.at[i, pl.ds(0, 64)], 16 + i, dev_xp)
            self.got(self.rb.at[i], 10 + i)
            self.xm[i, 64:128] = (self.pair(2, i, 1) + self.rb[i].astype(F32)).astype(BF16)
            self.go(self.xm.at[i, pl.ds(64, 64)], self.fp.at[i, pl.ds(64, 64)], 18 + i, dev_xm)

        def join(self, i, h):
            rows, at = slice(h * 64, h * 64 + 64), pl.ds(h * 64, 64)
            if h == 0:
                self.sib_got(3, i)
            self.got(self.fm.at[i, at], (16, 12)[h] + i)
            self.got(self.fp.at[i, at], (14, 18)[h] + i)
            return self.pair(3, i, h) + self.fm[i, rows].astype(F32) + self.fp[i, rows].astype(F32)

        def to_opp(self, h):
            at = pl.ds(h * 64, 64)
            return copy(self.ys.at[at], self.yr.at[at], self.ss.at[20 + h], self.rs.at[20 + h], dev_yo)

        def join_other(self):
            for h in range(2):
                self.ys[h * 64:h * 64 + 64] = self.join(0, h).astype(BF16)
                self.to_opp(h).start()

        def join_mine(self):
            for h in range(2):
                self.fin[h * 64:h * 64 + 64] = self.join(1, h)

        def end(self):
            for h in range(2):
                self.to_opp(h).wait_send()

        def last(self, h):
            rows = slice(h * 64, h * 64 + 64)
            self.got(self.yr.at[pl.ds(h * 64, 64)], 20 + h)
            return self.fin[rows] + self.yr[rows].astype(F32)

    rt = Reduce((yl, 1 - yl), t_own, t_sib_s, t_sib_r, t_x2, t_ra, t_rb, t_xp, t_xm, t_fm, t_fp, None, None, None, t_ss, t_rs)

    def t3(i, h):
        at = pl.ds(h * 64, 64)
        dev = (yl * 8 + (z + turn) % 8, rt.y_order[i] * 8 + z)
        return copy(t3_s.at[i, at], t3_r.at[yh, at], t3_ss.at[i * 2 + h], t3_rs.at[yh * 2 + h], dev)

    def t3_stays(i):
        return stays & (rt.y_order[i] == yh)

    def t_place(i):
        for h in range(2):
            rows = slice(h * 64, h * 64 + 64)
            t3_s[i, rows] = rt.join(i, h).astype(BF16)

            @pl.when(t3_stays(i))
            def _():
                t3_r[yh, rows] = t3_s[i, rows]

            @pl.when(jnp.logical_not(t3_stays(i)))
            def _():
                t3(i, h).start()

    z_step(5)
    z_step(6)

    def products(core, y_, k, width):
        rows = tg[pl.ds(core * 4, 4), :, k * width:(k + 1) * width].reshape(4 * ROWS, width)
        return jnp.dot(rows, pj[y_, k * width:(k + 1) * width], preferred_element_type=F32).reshape(4, ROWS, COLS)

    l_pj.wait()
    first = pl.ds(yl * 4, 4)
    t_sib_s[first] = products(1 - c, yl, 0, 1024).astype(BF16)
    for k in range(4):
        rt.to_sib(k, 0)
    t_own[first] = products(c, yl, 0, 1024)
    rt.far(0)
    rt.near(0)

    other = pl.ds((1 - yl) * 4, 4)
    for k in range(4):
        for piece in (2 * k, 2 * k + 1):
            arrive(pj.at[1 - yl, pl.ds(piece * 128, 128)], p_ss.at[piece], p_rs.at[piece])
        theirs = products(1 - c, 1 - yl, k, 256)
        if k == 0:
            t_part[...] = theirs
        elif k < 3:
            t_part[...] += theirs
        else:
            t_sib_s[other] = (t_part[...] + theirs).astype(BF16)
            for j in range(4):
                rt.to_sib(j, 1)
        if k == 0:
            t_own[other] = products(c, 1 - yl, k, 256)
        else:
            t_own[other] += products(c, 1 - yl, k, 256)
        if k == 1:
            rt.relay(0)
    rt.far(1)
    rt.near(1)
    t_place(0)
    for k in range(1, BACK + 1):
        kv_mid(k)

    lax.fori_loop(1, BACK + 1, kv_got, 0)
    keys = jnp.concatenate([kv_r[0, j] for j in range(BACK + 1)], axis=1)
    values = kv_r[1].reshape((BACK + 1) * ROWS, HEAD_DIM)
    for h in range(2):
        scores = jnp.dot(q_v[h], keys, preferred_element_type=F32)
        scores = scores + bias[...]
        probs = jnp.exp(scores - jnp.max(scores, axis=1, keepdims=True))
        total = jnp.sum(probs, axis=1, keepdims=True)
        acc = jnp.dot(probs.astype(BF16), values, preferred_element_type=F32)
        attn_v[c * 2 + h] = (acc / total).astype(BF16)
        send(attn_v.at[c * 2 + h], attn_v.at[c * 2 + h], x_ss.at[5 + h], x_rs.at[5 + h], sib)
    lax.fori_loop(0, 8, wo_got, 0)
    rt.relay(1)

    ro = Reduce((yo_, yh), o_own, None, None, o_x2, o_ra, o_rb, o_xp, o_xm, o_fm, o_fp, o_ys, o_yr, o_fin, o_ss, o_rs)

    for h in range(2):
        arrive(attn_v.at[2 - 2 * c + h], x_ss.at[5 + h], x_rs.at[5 + h])
    attn = jnp.concatenate([attn_v[i] for i in range(4)], axis=1)

    def out_block(k, i):
        slot = ro.slot(k, i)
        o_own[slot] = jnp.dot(attn, wo[slot].reshape(COLS, COLS), preferred_element_type=F32)

    out_block(0, 0)
    ro.far(0)
    out_block(1, 0)
    out_block(2, 0)
    ro.near(0)
    out_block(0, 1)
    ro.relay(0)
    ro.far(1)
    out_block(1, 1)
    out_block(2, 1)
    ro.near(1)
    t_place(1)
    out_block(3, 0)
    out_block(3, 1)
    ro.relay(1)

    ro.join_other()
    ro.join_mine()

    early = list(started)
    started.clear()

    def before_end():
        for one in early:
            one.wait_send()
        lax.fori_loop(0, 8, w_end, 0)
        lax.fori_loop(0, 8, wo_end, 0)
        lax.fori_loop(1, 16, kvx_end, 0)
        lax.fori_loop(1, BACK + 1, kv_end, 0)
        ro.end()
        for i in range(2):

            @pl.when(jnp.logical_not(t3_stays(i)))
            def _():
                t3(i, 0).wait_send()
                t3(i, 1).wait_send()

    dg = Gather(db, dg_ss, dg_rs)
    for h in range(2):
        rows = slice(h * 64, h * 64 + 64)
        mixed = hb[mine, rows].astype(F32) + ro.last(h)
        out_s[rows] = mixed.astype(BF16)

        for p in range(2):

            @pl.when(jnp.logical_not(stays & (yh == p)))
            def _():
                arrive(t3_r.at[p, pl.ds(h * 64, 64)], t3_ss.at[h], t3_rs.at[p * 2 + h])

        target = t3_r[0, rows].astype(F32) + t3_r[1, rows].astype(F32)
        target = target * jnp.concatenate([ts_v[rows]] * 4, axis=1)
        difference = mixed - target
        db[mine, rows] = difference.astype(BF16)
        dg.begin(h)
        squares = difference * difference
        l_v[rows] = (
            squares[:, 0:128] + squares[:, 128:256] + squares[:, 256:384] + squares[:, 384:512]
        )
    l_s[...] = jnp.sum(l_v[...].T, axis=0, keepdims=True)
    l_r[t] = l_s[...]

    def loss(k):
        return copy(l_s, l_r.at[t], l_ss.at[k], l_rs.at[k], (s, (t + k) % 16))

    def loss_go(k, carry):
        loss(k).start()
        return carry

    def loss_got(k, carry):
        arrive(l_r.at[(t + 16 - k) % 16], l_ss.at[k], l_rs.at[k])
        return carry

    def loss_end(k, carry):
        loss(k).wait_send()
        return carry

    lax.fori_loop(1, 16, loss_go, 0)

    def add_grad(slots, first=False):
        d = jnp.concatenate([db[slot] for slot in slots], axis=1)
        for core in range(2):
            w = jnp.concatenate([wo[slot, core] for slot in slots], axis=1)
            g = nt_dot(d, w)
            g_acc[core] = g if first else g_acc[core] + g

    dg.near_relay()
    dg.opp_half(0)
    dg.near_rest()
    before_end()
    add_grad([mine] + dg.near, True)
    dg.opp_half(1)
    dg.onear_a()
    dg.far_step()
    add_grad([dg.opp, dg.far[0]])
    dg.onear_b()
    dg.onear_rest()
    add_grad(dg.onear)
    lax.fori_loop(1, 16, loss_got, 0)
    loss_sum = l_r[0]
    for i in range(1, 16):
        loss_sum = loss_sum + l_r[i]
    out_l[...] = loss_sum / DS
    dg.ofar_step()
    add_grad([dg.far[1]])
    send(g_acc.at[1 - c], g_in, x_ss.at[7], x_rs.at[7], sib)
    arrive(g_in, x_ss.at[7], x_rs.at[7])
    out_g[...] = (g_acc[c] + g_in[...]).astype(BF16)

    flush()
    lax.fori_loop(1, 16, loss_end, 0)


def reduce_buffers():
    block = (ROWS, COLS)
    return [
        pltpu.VMEM((2, 64, COLS), BF16),
        pltpu.VMEM((2, 64, COLS), BF16),
        pltpu.VMEM((2,) + block, BF16),
        pltpu.VMEM((2,) + block, BF16),
        pltpu.VMEM((2,) + block, BF16),
        pltpu.VMEM((2,) + block, BF16),
        pltpu.VMEM(block, BF16),
        pltpu.VMEM(block, BF16),
        pltpu.VMEM(block, F32),
    ]


def on_device(
    teacher_hidden, teacher_gain, projector, student_hidden, student_gain,
    query_weight, kv_weight, out_weight, doc_ids,
):
    block = (ROWS, COLS)
    hbm = pl.BlockSpec(memory_space=pltpu.HBM)
    vmem = pl.BlockSpec(memory_space=pltpu.VMEM)
    dma = pltpu.SemaphoreType.DMA
    out_s, out_l, out_g = pl.pallas_call(
        body,
        out_shape=(
            jax.ShapeDtypeStruct(block, BF16),
            jax.ShapeDtypeStruct((1, ROWS), F32),
            jax.ShapeDtypeStruct((ROWS, 256), BF16),
        ),
        in_specs=[hbm] * 9,
        out_specs=(vmem, vmem, vmem),
        scratch_shapes=[
            pltpu.VMEM((1, 1024), F32),
            pltpu.VMEM((1, COLS), F32),
            pltpu.VMEM((1, ROWS), jnp.int32),
            pltpu.VMEM((ROWS, 1024), BF16),
            pltpu.VMEM((8, ROWS, 1024), BF16),
            pltpu.VMEM((2, 1024, COLS), BF16),
            pltpu.VMEM((8, 2, COLS, 256), BF16),
            pltpu.VMEM((8, 2, 2, 32, COLS), BF16),
            pltpu.VMEM((8, 2, 256, COLS), BF16),
            pltpu.VMEM((64, ROWS), F32),
            pltpu.VMEM((64, ROWS), F32),
            pltpu.VMEM((8,) + block, BF16),
            pltpu.VMEM((1, 768), F32),
            pltpu.VMEM((8, 1, 768), F32),
            pltpu.VMEM((1, 256), F32),
            pltpu.VMEM((1, 256), F32),
            pltpu.VMEM((ROWS, 128), F32),
            pltpu.VMEM((2, ROWS, 256), F32),
            pltpu.VMEM((ROWS, 256), F32),
            pltpu.VMEM((2, 64, ROWS), F32),
            pltpu.VMEM((64, ROWS), F32),
            pltpu.VMEM((4, 16, ROWS), BF16),
            pltpu.VMEM((16, 16, ROWS), BF16),
            pltpu.VMEM((2, ROWS, HEAD_DIM), BF16),
            pltpu.VMEM((2, BACK + 1, ROWS, HEAD_DIM), BF16),
            pltpu.VMEM((8, 1, ROWS), jnp.int32),
            pltpu.VMEM((8, 1, ROWS), jnp.int32),
            pltpu.VMEM((2, ROWS, HEAD_DIM), BF16),
            pltpu.VMEM((4, ROWS, HEAD_DIM), BF16),
            pltpu.VMEM((ROWS, (BACK + 1) * ROWS), F32),
            pltpu.VMEM((8,) + block, F32),
            pltpu.VMEM((4,) + block, F32),
            pltpu.VMEM((8,) + block, F32),
            pltpu.VMEM((2,) + block, BF16),
            pltpu.VMEM((8,) + block, BF16),
            pltpu.VMEM((8,) + block, BF16),
            pltpu.VMEM((2,) + block, BF16),
            *reduce_buffers()[:6],
            *reduce_buffers(),
            pltpu.VMEM((2,) + block, BF16),
            pltpu.VMEM((2,) + block, BF16),
            pltpu.VMEM((ROWS, 128), F32),
            pltpu.VMEM((8,) + block, BF16),
            pltpu.VMEM((2, ROWS, 256), F32),
            pltpu.VMEM((ROWS, 256), F32),
            pltpu.VMEM((ROWS, 128), F32),
            pltpu.VMEM((1, ROWS), F32),
            pltpu.VMEM((16, 1, ROWS), F32),
            dma((10,)),
            *[dma((8,)) for _ in range(10)],
            dma((16,)), dma((16,)), dma((8,)), dma((8,)),
            dma((24,)), dma((24,)), dma((24,)), dma((24,)),
            dma((16,)), dma((16,)), dma((16,)), dma((16,)),
            dma((9,)), dma((9,)), dma((9,)), dma((9,)), dma((9,)), dma((9,)),
            dma((24,)), dma((24,)), dma((24,)), dma((24,)),
            dma((4,)), dma((4,)),
            dma((16,)), dma((16,)),
        ],
        compiler_params=pltpu.CompilerParams(
            collective_id=0, has_side_effects=True, vmem_limit_bytes=40 * 1024 * 1024
        ),
    )(
        *(
            pltpu.with_memory_space_constraint(one, pltpu.HBM)
            for one in (
                teacher_hidden, teacher_gain.reshape(1, -1), projector, student_hidden,
                student_gain.reshape(1, -1), query_weight.reshape(8, 2, COLS, 256), jnp.transpose(kv_weight, (0, 2, 1)),
                out_weight, doc_ids.reshape(1, -1),
            )
        )
    )
    return out_s, out_l.reshape(ROWS), out_g


def solution(mesh):
    in_specs = (
        P("seq", "tensor"),
        P("tensor"),
        P("tensor", "seq"),
        P("seq", "tensor"),
        P("tensor"),
        P(None, "tensor"),
        P(None, None, "tensor"),
        P("tensor", None),
        P("seq"),
    )
    out_specs = (P("seq", "tensor"), P("seq"), P("seq", "tensor"))
    return jax.shard_map(
        on_device, mesh=mesh, in_specs=in_specs, out_specs=out_specs, check_vma=False
    )
```

```python
import math

import jax
import jax.numpy as jnp
from jax import lax
from jax.experimental import pallas as pl
from jax.experimental.pallas import tpu as pltpu
from jax.sharding import PartitionSpec as P

DT = 16384
DS = 8192
HEAD_DIM = 128
HEADS = 32
KV_HEADS = 4
ROWS = 128
COLS = 512
BACK = 8
F32 = jnp.float32
BF16 = jnp.bfloat16
MESH = pl.DeviceIdType.MESH
NT = (((1,), (1,)), ((), ()))


def nt_dot(a, b):
    return lax.dot_general(a, b, NT, preferred_element_type=F32)


def body(
    th_h, tgain_h, pj_h, sh_h, sgain_h, wq_h, wkv_h, wo_h, docs_h,
    out_s, out_l, out_g,
    tgain, sgain, docs, th_v, tg, pj, wq, wkv, wo, cos_t, sin_t,
    hb, sg_s, sg_r, sum_s, sum_r, scale_v, q_acc, q_in, kv_acc, kv_in,
    kvx_s, kvx_r, kv_own, kv_r, docs_z, docs_o, q_v, attn_v, bias,
    t_own, t_part, o_own, o_x2, t_sib_s, t_sib_r, t_x2, t_ra, t_rb, t_xp, t_xm, t_fm, t_fp,
    o_ra, o_rb, o_xp, o_xm, o_fm, o_fp, o_ys, o_yr, o_fin,
    t3_s, t3_r, ts_v, db, g_acc, g_in, l_v, l_s, l_r,
    load_sem, w_load, w_ss, w_rs, v_load, v_ss, v_rs, u_ss, u_rs, x_ss, x_rs, z_ss, z_rs, p_ss, p_rs,
    ag_ss, ag_rs, dg_ss, dg_rs, sm_ss, sm_rs, kx_ss, kx_rs, kv_ss, kv_rs, kf_ss, kf_rs, dc_ss, dc_rs,
    t_ss, t_rs, o_ss, o_rs, t3_ss, t3_rs, l_ss, l_rs,
):
    s = lax.axis_index("seq")
    t = lax.axis_index("tensor")
    yl, z = s // 8, s % 8
    yh, x, c = t // 8, (t // 2) % 4, t % 2

    def tid(y_, x_, c_):
        return y_ * 8 + x_ * 2 + c_

    xp_, xm_ = (x + 1) % 4, (x + 3) % 4
    xf_ = (x + 2) % 4
    yo_ = 1 - yh
    sib = (s, tid(yh, x, 1 - c))
    dev_xp = (s, tid(yh, xp_, c))
    dev_xm = (s, tid(yh, xm_, c))
    dev_yo = (s, tid(yo_, x, c))
    dev_zp = (yl * 8 + (z + 1) % 8, t)
    dev_zm = (yl * 8 + (z + 7) % 8, t)
    dev_yl = ((1 - yl) * 8 + z, t)
    turn = jnp.where(c == 0, x, jnp.where(x == 0, 4, 8 - x))
    stays = (z == 0) & (x == 0) & (c == 0)

    started = []

    def copy(src, dst, ss, rs, dev):
        return pltpu.make_async_remote_copy(
            src_ref=src, dst_ref=dst, send_sem=ss, recv_sem=rs, device_id=dev, device_id_type=MESH
        )

    def send(src, dst, ss, rs, dev):
        one = copy(src, dst, ss, rs, dev)
        one.start()
        started.append(one)

    def flush():
        for one in started:
            one.wait_send()
        started.clear()

    def arrive(dst, ss, rs):
        copy(dst, dst, ss, rs, sib).wait_recv()

    def load(src, dst, k):
        one = pltpu.make_async_copy(src, dst, load_sem.at[k])
        one.start()
        return one

    l_th = load(th_h, th_v, 0)
    mine = yh * 4 + x
    l_sh = load(sh_h, hb.at[mine], 1)
    l_small = [load(tgain_h, tgain, 7), load(sgain_h, sgain, 8), load(docs_h, docs, 9)]

    def wkv_part(j, core):
        return wkv_h.at[:, :, pl.ds(pl.multiple_of((j * 2 + core) * COLS, COLS), COLS)]

    def wkv_load(j):
        return pltpu.make_async_copy(wkv_part(j, c), wkv.at[j, c], v_load.at[j])

    def wkv_go(j, carry):
        wkv_load(j).start()
        return carry

    def wo_part(j, core):
        return wo_h.at[:, pl.ds(pl.multiple_of((j * 2 + core) * COLS, COLS), COLS)]

    def wo_load(j):
        return pltpu.make_async_copy(wo_part(j, c), wo.at[j, c], w_load.at[j])

    def wo_send(j):
        return copy(wo_part(j, 1 - c), wo.at[j, c], w_ss.at[j], w_rs.at[j], sib)

    def wo_fetch(j, carry):
        wo_load(j).start()
        return carry

    def wo_go(j, carry):
        wo_send(j).start()
        return carry

    def wo_got(j, carry):
        wo_load(j).wait()
        arrive(wo.at[j, 1 - c], w_ss.at[j], w_rs.at[j])
        return carry

    def wo_end(j, carry):
        wo_send(j).wait_send()
        return carry

    lax.fori_loop(0, 8, wkv_go, 0)
    l_wq = load(wq_h.at[:, c], wq.at[:, c], 3)

    kv_r[...] = jnp.zeros(kv_r.shape, BF16)

    barrier = pltpu.get_barrier_semaphore()
    for dev in (sib, dev_xp, dev_xm, dev_yo, dev_zp, dev_zm, dev_yl):
        pl.semaphore_signal(barrier, inc=1, device_id=dev, device_id_type=MESH)

    class Gather:
        def __init__(self, buf, ss, rs):
            self.buf, self.ss, self.rs = buf, ss, rs
            self.near = [yh * 4 + xm_, yh * 4 + xp_]
            self.opp = yo_ * 4 + x
            self.onear = [yo_ * 4 + xm_, yo_ * 4 + xp_]
            self.far = [yh * 4 + xf_, yo_ * 4 + xf_]
            self.order = [mine] + self.near + [self.opp] + self.onear + self.far

        def part(self, slot, h):
            return self.buf.at[slot, pl.ds(h * 64, 64)]

        def half(self, slot, h, k, dev):
            part = self.part(slot, h)
            send(part, part, self.ss.at[k], self.rs.at[k], dev)

        def got_half(self, slot, h, k):
            arrive(self.part(slot, h), self.ss.at[k], self.rs.at[k])

        def begin(self, h):
            self.half(mine, h, 0 + h, dev_yo)
            self.half(mine, h, 2 + h, dev_xp)
            self.half(mine, h, 4 + h, dev_xm)

        def near_relay(self):
            self.got_half(self.near[0], 0, 2)
            self.half(self.near[0], 0, 6, dev_xp)
            self.got_half(self.near[1], 1, 5)
            self.half(self.near[1], 1, 7, dev_xm)

        def near_rest(self):
            self.got_half(self.near[0], 1, 3)
            self.got_half(self.near[1], 0, 4)

        def opp_half(self, h):
            self.got_half(self.opp, h, 0 + h)
            self.half(self.opp, h, 8 + h, dev_xp)
            self.half(self.opp, h, 10 + h, dev_xm)

        def onear_a(self):
            self.got_half(self.onear[0], 0, 8)
            self.half(self.onear[0], 0, 12, dev_xp)

        def onear_b(self):
            self.got_half(self.onear[1], 1, 11)
            self.half(self.onear[1], 1, 13, dev_xm)

        def onear_rest(self):
            self.got_half(self.onear[0], 1, 9)
            self.got_half(self.onear[1], 0, 10)

        def far_step(self):
            self.got_half(self.far[0], 0, 6)
            self.got_half(self.far[0], 1, 7)

        def ofar_step(self):
            self.got_half(self.far[1], 0, 12)
            self.got_half(self.far[1], 1, 13)

    def pj_send(k):
        rows = pl.ds(k * 256, 256)
        send(pj_h.at[rows], pj.at[yl, rows], p_ss.at[k], p_rs.at[k], dev_yl)

    def wkv_send(j):
        return copy(wkv_part(j, 1 - c), wkv.at[j, c], v_ss.at[j], v_rs.at[j], sib)

    def wq_send(j):
        return copy(wq_h.at[j, 1 - c], wq.at[j, c], u_ss.at[j], u_rs.at[j], sib)

    def w_go(j, carry):
        wkv_send(j).start()
        wq_send(j).start()
        return carry

    def w_end(j, carry):
        wkv_send(j).wait_send()
        wq_send(j).wait_send()
        return carry

    def w_got(slot):
        wkv_load(slot).wait()
        arrive(wkv.at[slot, 1 - c], v_ss.at[slot], v_rs.at[slot])
        arrive(wq.at[slot, 1 - c], u_ss.at[slot], u_rs.at[slot])

    ag = Gather(hb, ag_ss, ag_rs)
    l_sh.wait()

    z_slot = 0
    l_th.wait()
    for one in l_small:
        one.wait()
    docs_z[z] = docs[...]
    part = jnp.zeros((ROWS, 128), F32)
    for i in range(8):
        cols = slice(i * 128, (i + 1) * 128)
        f = th_v[:, cols].astype(F32)
        part = part + f * f
        tg[z_slot, :, cols] = (f * tgain[:, cols]).astype(BF16)
    sg_s[:, COLS:COLS + 128] = jnp.sum(part.T, axis=0, keepdims=True)
    part = jnp.zeros((ROWS, 128), F32)
    for i in range(4):
        f = hb[mine, :, i * 128:(i + 1) * 128].astype(F32)
        part = part + f * f
    sg_s[:, COLS + 128:COLS + 256] = jnp.sum(part.T, axis=0, keepdims=True)
    sg_s[:, 0:COLS] = sgain[...]
    sg_r[mine] = sg_s[...]

    def ring_slot(d):
        return (0, 1, 2, 3, 4, 7, 6, 5)[d % 8]

    def z_ref(d, h):
        return tg.at[ring_slot(d), pl.ds(h * 64, 64)]

    def z_send(k):
        d = k // 2
        send(z_ref(8 - d, k % 2), z_ref(7 - d, k % 2), z_ss.at[k], z_rs.at[k], dev_zp)
        send(z_ref(d, 1 - k % 2), z_ref(d + 1, 1 - k % 2), z_ss.at[8 + k], z_rs.at[8 + k], dev_zm)

    def z_got(k):
        up, down = z_ref(-(k // 2) + 7, k % 2), z_ref(k // 2 + 1, 1 - k % 2)
        arrive(up, z_ss.at[k], z_rs.at[k])
        arrive(down, z_ss.at[8 + k], z_rs.at[8 + k])

    def z_step(k):
        z_got(k)
        if k + 2 < 7:
            z_send(k + 2)

    def small_send(i, k, dev):
        slot = ag.order[i]
        send(sg_r.at[slot], sg_r.at[slot], sm_ss.at[k], sm_rs.at[k], dev)

    def small_got(i, k):
        arrive(sg_r.at[ag.order[i]], sm_ss.at[k], sm_rs.at[k])

    def docs_send(d, k, dev):
        ref = docs_z.at[(z + d) % 8]
        send(ref, ref, dc_ss.at[k], dc_rs.at[k], dev)

    def docs_step(k):
        arrive(docs_z.at[(z + 7 - k) % 8], dc_ss.at[k], dc_rs.at[k])
        if k < 3:
            arrive(docs_z.at[(z + 1 + k) % 8], dc_ss.at[4 + k], dc_rs.at[4 + k])
            docs_send(7 - k, k + 1, dev_zp)
            if k < 2:
                docs_send(1 + k, k + 5, dev_zm)
        else:
            send(docs_z, docs_o, dc_ss.at[8], dc_rs.at[8], dev_yl)

    pl.semaphore_wait(barrier, 7)
    small_send(0, 0, dev_yo)
    small_send(0, 1, dev_xp)
    small_send(0, 2, dev_xm)
    ag.begin(0)
    ag.begin(1)
    docs_send(0, 0, dev_zp)
    docs_send(0, 4, dev_zm)
    z_send(0)
    pj_send(0)
    lax.fori_loop(0, 8, w_go, 0)
    z_send(1)
    pj_send(1)
    pj_send(2)
    l_pj = load(pj_h, pj.at[yl], 4)

    entry = lax.broadcasted_iota(jnp.int32, (64, ROWS), 0).astype(F32)
    position = (s * ROWS + lax.broadcasted_iota(jnp.int32, (64, ROWS), 1)).astype(F32)
    angle = position * jnp.exp(-math.log(500000.0) * (2.0 * entry / HEAD_DIM))
    cos_t[...] = jnp.cos(angle)
    sin_t[...] = jnp.sin(angle)

    def process(slots, first=False):
        blocks, w = [], []
        for slot in slots:
            parts = []
            for i in range(4):
                cols = slice(i * 128, (i + 1) * 128)
                f = hb[slot, :, cols].astype(F32)
                parts.append((f * scale_v[...] * sg_r[slot][:, cols]).astype(BF16))
            blocks.append(jnp.concatenate(parts, axis=1))
        n = jnp.concatenate(blocks, axis=1)
        for slot in slots:
            w_got(slot)
            w.append(wkv[slot].reshape(128, COLS))
        kv = nt_dot(jnp.concatenate(w, axis=1), n)
        for core in range(2):
            w = jnp.concatenate([wq[slot, core] for slot in slots], axis=0)
            q = jnp.dot(n, w, preferred_element_type=F32)
            k = kv[core * 64:core * 64 + 64]
            q_acc[core] = q if first else q_acc[core] + q
            kv_acc[core] = k if first else kv_acc[core] + k

    small_got(1, 1)
    small_send(1, 3, dev_xp)
    small_got(2, 2)
    small_got(3, 0)
    small_send(3, 4, dev_xp)
    small_send(3, 5, dev_xm)
    docs_step(0)
    ag.near_relay()
    small_got(6, 3)
    docs_step(1)
    small_got(4, 4)
    small_send(4, 6, dev_xp)
    small_got(5, 5)
    ag.near_rest()
    ag.opp_half(0)
    z_step(0)
    pj_send(3)
    small_got(7, 6)
    sums = sg_r[0][:, COLS:COLS + 256]
    for i in range(1, 8):
        sums = sums + sg_r[i][:, COLS:COLS + 256]
    sum_s[...] = sums
    send(sum_s, sum_r, x_ss.at[2], x_rs.at[2], sib)
    docs_step(2)
    ag.opp_half(1)
    arrive(sum_r, x_ss.at[2], x_rs.at[2])
    sums = sum_s[...] + sum_r[...]
    ts_v[...] = jnp.broadcast_to(lax.rsqrt(sums[:, 0:128] / DT + 1e-05), (ROWS, 128)).T
    scale_v[...] = jnp.broadcast_to(lax.rsqrt(sums[:, 128:256] / DS + 1e-05), (ROWS, 128)).T
    docs_step(3)
    z_step(1)
    ag.onear_a()
    l_wq.wait()
    process([mine] + ag.near, True)
    ag.onear_b()
    z_step(2)
    ag.far_step()
    process([ag.opp, ag.far[0]])
    ag.onear_rest()
    process(ag.onear)
    z_step(3)
    ag.ofar_step()
    process([ag.far[1]])
    send(kv_acc.at[1 - c], kv_in, x_ss.at[3], x_rs.at[3], sib)
    send(q_acc.at[1 - c], q_in, x_ss.at[4], x_rs.at[4], sib)
    arrive(kv_in, x_ss.at[3], x_rs.at[3])

    row = lax.broadcasted_iota(jnp.int32, (64, 64), 0)
    col = lax.broadcasted_iota(jnp.int32, (64, 64), 1)
    take = ((row >> 3) & 1) * 32 + (row & 7) * 4 + (row >> 4)
    pick = jnp.where(col == take, 1.0, 0.0).astype(BF16)
    kv_mine = (kv_acc[c] + kv_in[...]).astype(BF16)
    kvx_s[...] = jnp.dot(pick, kv_mine, preferred_element_type=F32).astype(BF16).reshape(4, 16, 128)
    kvx_r[t] = kvx_s[t // 4]

    def kvx(k):
        to = (t + k) % 16
        return copy(kvx_s.at[to // 4], kvx_r.at[t], kx_ss.at[k], kx_rs.at[k], (s, to))

    def kvx_go(k, carry):
        kvx(k).start()
        return carry

    def kvx_got(k, carry):
        arrive(kvx_r.at[(t + 16 - k) % 16], kx_ss.at[k], kx_rs.at[k])
        return carry

    def kvx_end(k, carry):
        kvx(k).wait_send()
        return carry

    lax.fori_loop(1, 16, kvx_go, 0)
    lax.fori_loop(0, 8, wo_fetch, 0)
    lax.fori_loop(0, 8, wo_go, 0)
    z_step(4)

    cos2 = jnp.concatenate([cos_t[...], cos_t[...]], axis=0).T
    sin2 = jnp.concatenate([-sin_t[...], sin_t[...]], axis=0).T
    arrive(q_in, x_ss.at[4], x_rs.at[4])
    q_mine = q_acc[c] + q_in[...]
    for h in range(2):
        qh = q_mine[:, h * 128:(h + 1) * 128]
        turned = qh * cos2 + pltpu.roll(qh, 64, 1) * sin2
        q_v[h] = (turned * HEAD_DIM ** (-0.5)).astype(BF16)

    lax.fori_loop(1, 16, kvx_got, 0)
    both = kvx_r[...].astype(F32).reshape(16, 2, 8, ROWS)
    k_raw = both[:, 0].reshape(HEAD_DIM, ROWS)
    v_raw = both[:, 1].reshape(HEAD_DIM, ROWS)
    first, second = k_raw[0:64], k_raw[64:128]
    k_rot = jnp.concatenate(
        [first * cos_t[...] - second * sin_t[...], second * cos_t[...] + first * sin_t[...]], axis=0
    )
    kv_own[0] = k_rot.astype(BF16)
    kv_own[1] = v_raw.T.astype(BF16)
    kv_r[0, 0] = kv_own[0]
    kv_r[1, 0] = kv_own[1]

    def kv_copy(k):
        return copy(kv_own.at[c], kv_r.at[c, k], kv_ss.at[k], kv_rs.at[k], ((s + k) % 16, t))

    def kv_fwd(k):
        return copy(kv_r.at[c, k], kv_r.at[c, k], kf_ss.at[k], kf_rs.at[k], sib)

    def kv_go(k):
        @pl.when(s + k < 16)
        def _():
            kv_copy(k).start()

    def kv_mid(k):
        @pl.when(s >= k)
        def _():
            arrive(kv_r.at[c, k], kv_ss.at[k], kv_rs.at[k])
            kv_fwd(k).start()

    def kv_got(k, carry):
        @pl.when(s >= k)
        def _():
            arrive(kv_r.at[1 - c, k], kf_ss.at[k], kf_rs.at[k])
        return carry

    def kv_end(k, carry):
        @pl.when(s >= k)
        def _():
            kv_fwd(k).wait_send()

        @pl.when(s + k < 16)
        def _():
            kv_copy(k).wait_send()
        return carry

    arrive(docs_o, dc_ss.at[8], dc_rs.at[8])
    for k in range(1, BACK + 1):
        kv_go(k)

    def docs_back(j):
        at = (z + 8 - j) % 8
        return jnp.where(z >= j, docs_z[at], jnp.where(yl == 1, docs_o[at], -1))

    key_doc = jnp.concatenate([docs_back(j) for j in range(BACK + 1)], axis=1)
    row_doc = jnp.broadcast_to(docs[...].astype(F32), (ROWS, ROWS)).T[:, 0:1].astype(jnp.int32)
    wide = (ROWS, (BACK + 1) * ROWS)
    row_at = lax.broadcasted_iota(jnp.int32, wide, 0)
    key_at = lax.broadcasted_iota(jnp.int32, wide, 1)
    allowed = (key_doc == row_doc) & ((key_at >= ROWS) | (key_at <= row_at))
    bias[...] = jnp.where(allowed, 0.0, -1e30)

    class Reduce:
        def __init__(self, y_order, own, sib_s, sib_r, x2, ra, rb, xp, xm, fm, fp, ys, yr, fin, ss, rs):
            self.own, self.sib_s, self.sib_r = own, sib_s, sib_r
            self.x2, self.ra, self.rb, self.xp, self.xm, self.fm, self.fp = x2, ra, rb, xp, xm, fm, fp
            self.ys, self.yr, self.fin, self.ss, self.rs = ys, yr, fin, ss, rs
            self.y_order = y_order
            self.x_order = (xf_, xp_, xm_, x)

        def go(self, src, dst, k, dev):
            send(src, dst, self.ss.at[k], self.rs.at[k], dev)

        def got(self, dst, k):
            arrive(dst, self.ss.at[k], self.rs.at[k])

        def slot(self, k, i):
            return self.y_order[i] * 4 + self.x_order[k]

        def to_sib(self, k, i):
            slot = self.slot(k, i)
            self.go(self.sib_s.at[slot], self.sib_r.at[slot], k * 2 + i, sib)

        def sib_got(self, k, i):
            if self.sib_r is not None:
                self.got(self.sib_r.at[self.slot(k, i)], k * 2 + i)

        def pair(self, k, i, h):
            slot, rows = self.slot(k, i), slice(h * 64, h * 64 + 64)
            value = self.own[slot, rows]
            return value if self.sib_r is None else value + self.sib_r[slot, rows].astype(F32)

        def far(self, i):
            self.sib_got(0, i)
            self.x2[i, 0:64] = self.pair(0, i, 0).astype(BF16)
            self.go(self.x2.at[i, pl.ds(0, 64)], self.ra.at[i], 8 + i, dev_xp)
            self.x2[i, 64:128] = self.pair(0, i, 1).astype(BF16)
            self.go(self.x2.at[i, pl.ds(64, 64)], self.rb.at[i], 10 + i, dev_xm)

        def near(self, i):
            self.sib_got(1, i)
            self.xp[i, 64:128] = self.pair(1, i, 1).astype(BF16)
            self.go(self.xp.at[i, pl.ds(64, 64)], self.fm.at[i, pl.ds(64, 64)], 12 + i, dev_xp)
            self.sib_got(2, i)
            self.xm[i, 0:64] = self.pair(2, i, 0).astype(BF16)
            self.go(self.xm.at[i, pl.ds(0, 64)], self.fp.at[i, pl.ds(0, 64)], 14 + i, dev_xm)

        def relay(self, i):
            self.got(self.ra.at[i], 8 + i)
            self.xp[i, 0:64] = (self.pair(1, i, 0) + self.ra[i].astype(F32)).astype(BF16)
            self.go(self.xp.at[i, pl.ds(0, 64)], self.fm.at[i, pl.ds(0, 64)], 16 + i, dev_xp)
            self.got(self.rb.at[i], 10 + i)
            self.xm[i, 64:128] = (self.pair(2, i, 1) + self.rb[i].astype(F32)).astype(BF16)
            self.go(self.xm.at[i, pl.ds(64, 64)], self.fp.at[i, pl.ds(64, 64)], 18 + i, dev_xm)

        def join(self, i, h):
            rows, at = slice(h * 64, h * 64 + 64), pl.ds(h * 64, 64)
            if h == 0:
                self.sib_got(3, i)
            self.got(self.fm.at[i, at], (16, 12)[h] + i)
            self.got(self.fp.at[i, at], (14, 18)[h] + i)
            return self.pair(3, i, h) + self.fm[i, rows].astype(F32) + self.fp[i, rows].astype(F32)

        def to_opp(self, h):
            at = pl.ds(h * 64, 64)
            return copy(self.ys.at[at], self.yr.at[at], self.ss.at[20 + h], self.rs.at[20 + h], dev_yo)

        def join_other(self):
            for h in range(2):
                self.ys[h * 64:h * 64 + 64] = self.join(0, h).astype(BF16)
                self.to_opp(h).start()

        def join_mine(self):
            for h in range(2):
                self.fin[h * 64:h * 64 + 64] = self.join(1, h)

        def end(self):
            for h in range(2):
                self.to_opp(h).wait_send()

        def last(self, h):
            rows = slice(h * 64, h * 64 + 64)
            self.got(self.yr.at[pl.ds(h * 64, 64)], 20 + h)
            return self.fin[rows] + self.yr[rows].astype(F32)

    rt = Reduce((yl, 1 - yl), t_own, t_sib_s, t_sib_r, t_x2, t_ra, t_rb, t_xp, t_xm, t_fm, t_fp, None, None, None, t_ss, t_rs)

    def t3(i, h):
        at = pl.ds(h * 64, 64)
        dev = (yl * 8 + (z + turn) % 8, rt.y_order[i] * 8 + z)
        return copy(t3_s.at[i, at], t3_r.at[yh, at], t3_ss.at[i * 2 + h], t3_rs.at[yh * 2 + h], dev)

    def t3_stays(i):
        return stays & (rt.y_order[i] == yh)

    def t_place(i):
        for h in range(2):
            rows = slice(h * 64, h * 64 + 64)
            t3_s[i, rows] = rt.join(i, h).astype(BF16)

            @pl.when(t3_stays(i))
            def _():
                t3_r[yh, rows] = t3_s[i, rows]

            @pl.when(jnp.logical_not(t3_stays(i)))
            def _():
                t3(i, h).start()

    z_step(5)
    z_step(6)

    def products(core, y_, k, width):
        rows = tg[pl.ds(core * 4, 4), :, k * width:(k + 1) * width].reshape(4 * ROWS, width)
        return jnp.dot(rows, pj[y_, k * width:(k + 1) * width], preferred_element_type=F32).reshape(4, ROWS, COLS)

    l_pj.wait()
    first = pl.ds(yl * 4, 4)
    t_sib_s[first] = products(1 - c, yl, 0, 1024).astype(BF16)
    for k in range(4):
        rt.to_sib(k, 0)
    t_own[first] = products(c, yl, 0, 1024)
    rt.far(0)
    rt.near(0)

    other = pl.ds((1 - yl) * 4, 4)
    for k in range(4):
        arrive(pj.at[1 - yl, pl.ds(k * 256, 256)], p_ss.at[k], p_rs.at[k])
        theirs = products(1 - c, 1 - yl, k, 256)
        if k == 0:
            t_part[...] = theirs
        elif k < 3:
            t_part[...] += theirs
        else:
            t_sib_s[other] = (t_part[...] + theirs).astype(BF16)
            for j in range(4):
                rt.to_sib(j, 1)
        if k == 0:
            t_own[other] = products(c, 1 - yl, k, 256)
        else:
            t_own[other] += products(c, 1 - yl, k, 256)
        if k == 1:
            rt.relay(0)
    rt.far(1)
    rt.near(1)
    t_place(0)
    for k in (1, 2, 3, 4):
        kv_mid(k)
    rt.relay(1)
    for k in (5, 6, 7, 8):
        kv_mid(k)
    t_place(1)

    lax.fori_loop(1, BACK + 1, kv_got, 0)
    keys = jnp.concatenate([kv_r[0, j] for j in range(BACK + 1)], axis=1)
    values = kv_r[1].reshape((BACK + 1) * ROWS, HEAD_DIM)
    for h in range(2):
        scores = jnp.dot(q_v[h], keys, preferred_element_type=F32)
        scores = scores + bias[...]
        probs = jnp.exp(scores - jnp.max(scores, axis=1, keepdims=True))
        total = jnp.sum(probs, axis=1, keepdims=True)
        acc = jnp.dot(probs.astype(BF16), values, preferred_element_type=F32)
        attn_v[c * 2 + h] = (acc / total).astype(BF16)
        send(attn_v.at[c * 2 + h], attn_v.at[c * 2 + h], x_ss.at[5 + h], x_rs.at[5 + h], sib)
    lax.fori_loop(0, 8, wo_got, 0)

    ro = Reduce((yo_, yh), o_own, None, None, o_x2, o_ra, o_rb, o_xp, o_xm, o_fm, o_fp, o_ys, o_yr, o_fin, o_ss, o_rs)

    for h in range(2):
        arrive(attn_v.at[2 - 2 * c + h], x_ss.at[5 + h], x_rs.at[5 + h])
    attn = jnp.concatenate([attn_v[i] for i in range(4)], axis=1)

    def out_block(k, i):
        slot = ro.slot(k, i)
        o_own[slot] = jnp.dot(attn, wo[slot].reshape(COLS, COLS), preferred_element_type=F32)

    out_block(0, 0)
    ro.far(0)
    out_block(1, 0)
    out_block(2, 0)
    ro.near(0)
    out_block(0, 1)
    ro.relay(0)
    ro.far(1)
    out_block(1, 1)
    out_block(2, 1)
    ro.near(1)
    out_block(3, 0)
    out_block(3, 1)
    ro.relay(1)

    ro.join_other()
    ro.join_mine()

    early = list(started)
    started.clear()

    def before_end():
        for one in early:
            one.wait_send()
        lax.fori_loop(0, 8, w_end, 0)
        lax.fori_loop(0, 8, wo_end, 0)
        lax.fori_loop(1, 16, kvx_end, 0)
        lax.fori_loop(1, BACK + 1, kv_end, 0)
        ro.end()
        for i in range(2):

            @pl.when(jnp.logical_not(t3_stays(i)))
            def _():
                t3(i, 0).wait_send()
                t3(i, 1).wait_send()

    dg = Gather(db, dg_ss, dg_rs)
    for h in range(2):
        rows = slice(h * 64, h * 64 + 64)
        mixed = hb[mine, rows].astype(F32) + ro.last(h)
        out_s[rows] = mixed.astype(BF16)

        for p in range(2):

            @pl.when(jnp.logical_not(stays & (yh == p)))
            def _():
                arrive(t3_r.at[p, pl.ds(h * 64, 64)], t3_ss.at[h], t3_rs.at[p * 2 + h])

        target = t3_r[0, rows].astype(F32) + t3_r[1, rows].astype(F32)
        target = target * jnp.concatenate([ts_v[rows]] * 4, axis=1)
        difference = mixed - target
        db[mine, rows] = difference.astype(BF16)
        dg.begin(h)
        squares = difference * difference
        l_v[rows] = (
            squares[:, 0:128] + squares[:, 128:256] + squares[:, 256:384] + squares[:, 384:512]
        )
    l_s[...] = jnp.sum(l_v[...].T, axis=0, keepdims=True)
    l_r[t] = l_s[...]

    def loss(k):
        return copy(l_s, l_r.at[t], l_ss.at[k], l_rs.at[k], (s, (t + k) % 16))

    def loss_go(k, carry):
        loss(k).start()
        return carry

    def loss_got(k, carry):
        arrive(l_r.at[(t + 16 - k) % 16], l_ss.at[k], l_rs.at[k])
        return carry

    def loss_end(k, carry):
        loss(k).wait_send()
        return carry

    lax.fori_loop(1, 16, loss_go, 0)

    def add_grad(slots, first=False):
        d = jnp.concatenate([db[slot] for slot in slots], axis=1)
        for core in range(2):
            w = jnp.concatenate([wo[slot, core] for slot in slots], axis=1)
            g = nt_dot(d, w)
            g_acc[core] = g if first else g_acc[core] + g

    dg.near_relay()
    dg.opp_half(0)
    dg.near_rest()
    before_end()
    add_grad([mine] + dg.near, True)
    dg.opp_half(1)
    dg.onear_a()
    dg.far_step()
    add_grad([dg.opp, dg.far[0]])
    dg.onear_b()
    dg.onear_rest()
    add_grad(dg.onear)
    lax.fori_loop(1, 16, loss_got, 0)
    loss_sum = l_r[0]
    for i in range(1, 16):
        loss_sum = loss_sum + l_r[i]
    out_l[...] = loss_sum / DS
    dg.ofar_step()
    add_grad([dg.far[1]])
    send(g_acc.at[1 - c], g_in, x_ss.at[7], x_rs.at[7], sib)
    arrive(g_in, x_ss.at[7], x_rs.at[7])
    out_g[...] = (g_acc[c] + g_in[...]).astype(BF16)

    flush()
    lax.fori_loop(1, 16, loss_end, 0)


def reduce_buffers():
    block = (ROWS, COLS)
    return [
        pltpu.VMEM((2, 64, COLS), BF16),
        pltpu.VMEM((2, 64, COLS), BF16),
        pltpu.VMEM((2,) + block, BF16),
        pltpu.VMEM((2,) + block, BF16),
        pltpu.VMEM((2,) + block, BF16),
        pltpu.VMEM((2,) + block, BF16),
        pltpu.VMEM(block, BF16),
        pltpu.VMEM(block, BF16),
        pltpu.VMEM(block, F32),
    ]


def on_device(
    teacher_hidden, teacher_gain, projector, student_hidden, student_gain,
    query_weight, kv_weight, out_weight, doc_ids,
):
    block = (ROWS, COLS)
    hbm = pl.BlockSpec(memory_space=pltpu.HBM)
    vmem = pl.BlockSpec(memory_space=pltpu.VMEM)
    dma = pltpu.SemaphoreType.DMA
    out_s, out_l, out_g = pl.pallas_call(
        body,
        out_shape=(
            jax.ShapeDtypeStruct(block, BF16),
            jax.ShapeDtypeStruct((1, ROWS), F32),
            jax.ShapeDtypeStruct((ROWS, 256), BF16),
        ),
        in_specs=[hbm] * 9,
        out_specs=(vmem, vmem, vmem),
        scratch_shapes=[
            pltpu.VMEM((1, 1024), F32),
            pltpu.VMEM((1, COLS), F32),
            pltpu.VMEM((1, ROWS), jnp.int32),
            pltpu.VMEM((ROWS, 1024), BF16),
            pltpu.VMEM((8, ROWS, 1024), BF16),
            pltpu.VMEM((2, 1024, COLS), BF16),
            pltpu.VMEM((8, 2, COLS, 256), BF16),
            pltpu.VMEM((8, 2, 2, 32, COLS), BF16),
            pltpu.VMEM((8, 2, 256, COLS), BF16),
            pltpu.VMEM((64, ROWS), F32),
            pltpu.VMEM((64, ROWS), F32),
            pltpu.VMEM((8,) + block, BF16),
            pltpu.VMEM((1, 768), F32),
            pltpu.VMEM((8, 1, 768), F32),
            pltpu.VMEM((1, 256), F32),
            pltpu.VMEM((1, 256), F32),
            pltpu.VMEM((ROWS, 128), F32),
            pltpu.VMEM((2, ROWS, 256), F32),
            pltpu.VMEM((ROWS, 256), F32),
            pltpu.VMEM((2, 64, ROWS), F32),
            pltpu.VMEM((64, ROWS), F32),
            pltpu.VMEM((4, 16, ROWS), BF16),
            pltpu.VMEM((16, 16, ROWS), BF16),
            pltpu.VMEM((2, ROWS, HEAD_DIM), BF16),
            pltpu.VMEM((2, BACK + 1, ROWS, HEAD_DIM), BF16),
            pltpu.VMEM((8, 1, ROWS), jnp.int32),
            pltpu.VMEM((8, 1, ROWS), jnp.int32),
            pltpu.VMEM((2, ROWS, HEAD_DIM), BF16),
            pltpu.VMEM((4, ROWS, HEAD_DIM), BF16),
            pltpu.VMEM((ROWS, (BACK + 1) * ROWS), F32),
            pltpu.VMEM((8,) + block, F32),
            pltpu.VMEM((4,) + block, F32),
            pltpu.VMEM((8,) + block, F32),
            pltpu.VMEM((2,) + block, BF16),
            pltpu.VMEM((8,) + block, BF16),
            pltpu.VMEM((8,) + block, BF16),
            pltpu.VMEM((2,) + block, BF16),
            *reduce_buffers()[:6],
            *reduce_buffers(),
            pltpu.VMEM((2,) + block, BF16),
            pltpu.VMEM((2,) + block, BF16),
            pltpu.VMEM((ROWS, 128), F32),
            pltpu.VMEM((8,) + block, BF16),
            pltpu.VMEM((2, ROWS, 256), F32),
            pltpu.VMEM((ROWS, 256), F32),
            pltpu.VMEM((ROWS, 128), F32),
            pltpu.VMEM((1, ROWS), F32),
            pltpu.VMEM((16, 1, ROWS), F32),
            dma((10,)),
            *[dma((8,)) for _ in range(10)],
            dma((16,)), dma((16,)), dma((8,)), dma((8,)),
            dma((24,)), dma((24,)), dma((24,)), dma((24,)),
            dma((16,)), dma((16,)), dma((16,)), dma((16,)),
            dma((9,)), dma((9,)), dma((9,)), dma((9,)), dma((9,)), dma((9,)),
            dma((24,)), dma((24,)), dma((24,)), dma((24,)),
            dma((4,)), dma((4,)),
            dma((16,)), dma((16,)),
        ],
        compiler_params=pltpu.CompilerParams(
            collective_id=0, has_side_effects=True, vmem_limit_bytes=40 * 1024 * 1024
        ),
    )(
        *(
            pltpu.with_memory_space_constraint(one, pltpu.HBM)
            for one in (
                teacher_hidden, teacher_gain.reshape(1, -1), projector, student_hidden,
                student_gain.reshape(1, -1), query_weight.reshape(8, 2, COLS, 256), jnp.transpose(kv_weight, (0, 2, 1)),
                out_weight, doc_ids.reshape(1, -1),
            )
        )
    )
    return out_s, out_l.reshape(ROWS), out_g


def solution(mesh):
    in_specs = (
        P("seq", "tensor"),
        P("tensor"),
        P("tensor", "seq"),
        P("seq", "tensor"),
        P("tensor"),
        P(None, "tensor"),
        P(None, None, "tensor"),
        P("tensor", None),
        P("seq"),
    )
    out_specs = (P("seq", "tensor"), P("seq"), P("seq", "tensor"))
    return jax.shard_map(
        on_device, mesh=mesh, in_specs=in_specs, out_specs=out_specs, check_vma=False
    )
```

```python
import math

import jax
import jax.numpy as jnp
from jax import lax
from jax.experimental import pallas as pl
from jax.experimental.pallas import tpu as pltpu
from jax.sharding import PartitionSpec as P

DT = 16384
DS = 8192
HEAD_DIM = 128
HEADS = 32
KV_HEADS = 4
ROWS = 128
COLS = 512
BACK = 8
F32 = jnp.float32
BF16 = jnp.bfloat16
MESH = pl.DeviceIdType.MESH
NT = (((1,), (1,)), ((), ()))


def nt_dot(a, b):
    return lax.dot_general(a, b, NT, preferred_element_type=F32)


def body(
    th_h, tgain_h, pj_h, sh_h, sgain_h, wq_h, wkv_h, wo_h, docs_h,
    out_s, out_l, out_g,
    tgain, sgain, docs, th_v, tg, pj, wq, wkv, wo, cos_t, sin_t,
    hb, sg_s, sg_r, sum_s, sum_r, scale_v, q_acc, q_in, kv_acc, kv_in,
    kvx_s, kvx_r, kv_own, kv_r, docs_z, docs_o, q_v, attn_v, bias,
    t_own, t_part, o_own, o_x2, t_sib_s, t_sib_r, t_x2, t_ra, t_rb, t_xp, t_xm, t_fm, t_fp,
    o_ra, o_rb, o_xp, o_xm, o_fm, o_fp, o_ys, o_yr, o_fin,
    t3_s, t3_r, ts_v, db, g_acc, g_in, l_v, l_s, l_r,
    load_sem, w_load, w_ss, w_rs, v_load, v_ss, v_rs, u_ss, u_rs, x_ss, x_rs, z_ss, z_rs, p_ss, p_rs,
    ag_ss, ag_rs, dg_ss, dg_rs, sm_ss, sm_rs, kx_ss, kx_rs, kv_ss, kv_rs, kf_ss, kf_rs, dc_ss, dc_rs,
    t_ss, t_rs, o_ss, o_rs, t3_ss, t3_rs, l_ss, l_rs,
):
    s = lax.axis_index("seq")
    t = lax.axis_index("tensor")
    yl, z = s // 8, s % 8
    yh, x, c = t // 8, (t // 2) % 4, t % 2

    def tid(y_, x_, c_):
        return y_ * 8 + x_ * 2 + c_

    xp_, xm_ = (x + 1) % 4, (x + 3) % 4
    xf_ = (x + 2) % 4
    yo_ = 1 - yh
    sib = (s, tid(yh, x, 1 - c))
    dev_xp = (s, tid(yh, xp_, c))
    dev_xm = (s, tid(yh, xm_, c))
    dev_yo = (s, tid(yo_, x, c))
    dev_zp = (yl * 8 + (z + 1) % 8, t)
    dev_zm = (yl * 8 + (z + 7) % 8, t)
    dev_yl = ((1 - yl) * 8 + z, t)
    turn = jnp.where(c == 0, x, jnp.where(x == 0, 4, 8 - x))
    stays = (z == 0) & (x == 0) & (c == 0)

    started = []

    def copy(src, dst, ss, rs, dev):
        return pltpu.make_async_remote_copy(
            src_ref=src, dst_ref=dst, send_sem=ss, recv_sem=rs, device_id=dev, device_id_type=MESH
        )

    def send(src, dst, ss, rs, dev):
        one = copy(src, dst, ss, rs, dev)
        one.start()
        started.append(one)

    def flush():
        for one in started:
            one.wait_send()
        started.clear()

    def arrive(dst, ss, rs):
        copy(dst, dst, ss, rs, sib).wait_recv()

    def load(src, dst, k):
        one = pltpu.make_async_copy(src, dst, load_sem.at[k])
        one.start()
        return one

    l_th = load(th_h, th_v, 0)
    mine = yh * 4 + x
    l_sh = load(sh_h, hb.at[mine], 1)
    l_small = [load(tgain_h, tgain, 7), load(sgain_h, sgain, 8), load(docs_h, docs, 9)]

    def wkv_part(j, core):
        return wkv_h.at[:, :, pl.ds(pl.multiple_of((j * 2 + core) * COLS, COLS), COLS)]

    def wkv_load(j):
        return pltpu.make_async_copy(wkv_part(j, c), wkv.at[j, c], v_load.at[j])

    def wkv_go(j, carry):
        wkv_load(j).start()
        return carry

    def wo_part(j, core):
        return wo_h.at[:, pl.ds(pl.multiple_of((j * 2 + core) * COLS, COLS), COLS)]

    def wo_load(j):
        return pltpu.make_async_copy(wo_part(j, c), wo.at[j, c], w_load.at[j])

    def wo_send(j):
        return copy(wo_part(j, 1 - c), wo.at[j, c], w_ss.at[j], w_rs.at[j], sib)

    def wo_fetch(j, carry):
        wo_load(j).start()
        return carry

    def wo_go(j, carry):
        wo_send(j).start()
        return carry

    def wo_got(j, carry):
        wo_load(j).wait()
        arrive(wo.at[j, 1 - c], w_ss.at[j], w_rs.at[j])
        return carry

    def wo_end(j, carry):
        wo_send(j).wait_send()
        return carry

    lax.fori_loop(0, 8, wkv_go, 0)
    l_wq = load(wq_h.at[:, c], wq.at[:, c], 3)

    kv_r[...] = jnp.zeros(kv_r.shape, BF16)

    barrier = pltpu.get_barrier_semaphore()
    for dev in (sib, dev_xp, dev_xm, dev_yo, dev_zp, dev_zm, dev_yl):
        pl.semaphore_signal(barrier, inc=1, device_id=dev, device_id_type=MESH)

    class Gather:
        def __init__(self, buf, ss, rs):
            self.buf, self.ss, self.rs = buf, ss, rs
            self.near = [yh * 4 + xm_, yh * 4 + xp_]
            self.opp = yo_ * 4 + x
            self.onear = [yo_ * 4 + xm_, yo_ * 4 + xp_]
            self.far = [yh * 4 + xf_, yo_ * 4 + xf_]
            self.order = [mine] + self.near + [self.opp] + self.onear + self.far

        def part(self, slot, h):
            return self.buf.at[slot, pl.ds(h * 64, 64)]

        def half(self, slot, h, k, dev):
            part = self.part(slot, h)
            send(part, part, self.ss.at[k], self.rs.at[k], dev)

        def got_half(self, slot, h, k):
            arrive(self.part(slot, h), self.ss.at[k], self.rs.at[k])

        def begin(self, h):
            self.half(mine, h, 0 + h, dev_yo)
            self.half(mine, h, 2 + h, dev_xp)
            self.half(mine, h, 4 + h, dev_xm)

        def near_relay(self):
            self.got_half(self.near[0], 0, 2)
            self.half(self.near[0], 0, 6, dev_xp)
            self.got_half(self.near[1], 1, 5)
            self.half(self.near[1], 1, 7, dev_xm)

        def near_rest(self):
            self.got_half(self.near[0], 1, 3)
            self.got_half(self.near[1], 0, 4)

        def opp_half(self, h):
            self.got_half(self.opp, h, 0 + h)
            self.half(self.opp, h, 8 + h, dev_xp)
            self.half(self.opp, h, 10 + h, dev_xm)

        def onear_a(self):
            self.got_half(self.onear[0], 0, 8)
            self.half(self.onear[0], 0, 12, dev_xp)

        def onear_b(self):
            self.got_half(self.onear[1], 1, 11)
            self.half(self.onear[1], 1, 13, dev_xm)

        def onear_rest(self):
            self.got_half(self.onear[0], 1, 9)
            self.got_half(self.onear[1], 0, 10)

        def far_step(self):
            self.got_half(self.far[0], 0, 6)
            self.got_half(self.far[0], 1, 7)

        def ofar_step(self):
            self.got_half(self.far[1], 0, 12)
            self.got_half(self.far[1], 1, 13)

    def pj_send(k):
        rows = pl.ds(k * 128, 128)
        send(pj_h.at[rows], pj.at[yl, rows], p_ss.at[k], p_rs.at[k], dev_yl)

    def wkv_send(j):
        return copy(wkv_part(j, 1 - c), wkv.at[j, c], v_ss.at[j], v_rs.at[j], sib)

    def wq_send(j):
        return copy(wq_h.at[j, 1 - c], wq.at[j, c], u_ss.at[j], u_rs.at[j], sib)

    def w_go(j, carry):
        wkv_send(j).start()
        wq_send(j).start()
        return carry

    def w_end(j, carry):
        wkv_send(j).wait_send()
        wq_send(j).wait_send()
        return carry

    def w_got(slot):
        wkv_load(slot).wait()
        arrive(wkv.at[slot, 1 - c], v_ss.at[slot], v_rs.at[slot])
        arrive(wq.at[slot, 1 - c], u_ss.at[slot], u_rs.at[slot])

    ag = Gather(hb, ag_ss, ag_rs)
    l_sh.wait()
    pl.semaphore_wait(barrier, 7)
    ag.begin(0)

    z_slot = 0
    l_th.wait()
    for one in l_small:
        one.wait()
    docs_z[z] = docs[...]
    part = jnp.zeros((ROWS, 128), F32)
    for i in range(8):
        cols = slice(i * 128, (i + 1) * 128)
        f = th_v[:, cols].astype(F32)
        part = part + f * f
        tg[z_slot, :, cols] = (f * tgain[:, cols]).astype(BF16)
    sg_s[:, COLS:COLS + 128] = jnp.sum(part.T, axis=0, keepdims=True)
    part = jnp.zeros((ROWS, 128), F32)
    for i in range(4):
        f = hb[mine, :, i * 128:(i + 1) * 128].astype(F32)
        part = part + f * f
    sg_s[:, COLS + 128:COLS + 256] = jnp.sum(part.T, axis=0, keepdims=True)
    sg_s[:, 0:COLS] = sgain[...]
    sg_r[mine] = sg_s[...]

    def ring_slot(d):
        return (0, 1, 2, 3, 4, 7, 6, 5)[d % 8]

    def z_ref(d, h):
        return tg.at[ring_slot(d), pl.ds(h * 64, 64)]

    def z_send(k):
        d = k // 2
        send(z_ref(8 - d, k % 2), z_ref(7 - d, k % 2), z_ss.at[k], z_rs.at[k], dev_zp)
        send(z_ref(d, 1 - k % 2), z_ref(d + 1, 1 - k % 2), z_ss.at[8 + k], z_rs.at[8 + k], dev_zm)

    def z_got(k):
        up, down = z_ref(-(k // 2) + 7, k % 2), z_ref(k // 2 + 1, 1 - k % 2)
        arrive(up, z_ss.at[k], z_rs.at[k])
        arrive(down, z_ss.at[8 + k], z_rs.at[8 + k])

    def z_step(k):
        z_got(k)
        if k + 2 < 7:
            z_send(k + 2)

    def small_send(i, k, dev):
        slot = ag.order[i]
        send(sg_r.at[slot], sg_r.at[slot], sm_ss.at[k], sm_rs.at[k], dev)

    def small_got(i, k):
        arrive(sg_r.at[ag.order[i]], sm_ss.at[k], sm_rs.at[k])

    def docs_send(d, k, dev):
        ref = docs_z.at[(z + d) % 8]
        send(ref, ref, dc_ss.at[k], dc_rs.at[k], dev)

    def docs_step(k):
        arrive(docs_z.at[(z + 7 - k) % 8], dc_ss.at[k], dc_rs.at[k])
        if k < 3:
            arrive(docs_z.at[(z + 1 + k) % 8], dc_ss.at[4 + k], dc_rs.at[4 + k])
            docs_send(7 - k, k + 1, dev_zp)
            if k < 2:
                docs_send(1 + k, k + 5, dev_zm)
        else:
            send(docs_z, docs_o, dc_ss.at[8], dc_rs.at[8], dev_yl)

    small_send(0, 0, dev_yo)
    small_send(0, 1, dev_xp)
    small_send(0, 2, dev_xm)
    ag.begin(1)
    docs_send(0, 0, dev_zp)
    docs_send(0, 4, dev_zm)
    lax.fori_loop(0, 8, w_go, 0)
    z_send(0)
    pj_send(0)
    z_send(1)
    l_pj = load(pj_h, pj.at[yl], 4)

    entry = lax.broadcasted_iota(jnp.int32, (64, ROWS), 0).astype(F32)
    position = (s * ROWS + lax.broadcasted_iota(jnp.int32, (64, ROWS), 1)).astype(F32)
    angle = position * jnp.exp(-math.log(500000.0) * (2.0 * entry / HEAD_DIM))
    cos_t[...] = jnp.cos(angle)
    sin_t[...] = jnp.sin(angle)

    def process(slots, first=False):
        blocks, w = [], []
        for slot in slots:
            parts = []
            for i in range(4):
                cols = slice(i * 128, (i + 1) * 128)
                f = hb[slot, :, cols].astype(F32)
                parts.append((f * scale_v[...] * sg_r[slot][:, cols]).astype(BF16))
            blocks.append(jnp.concatenate(parts, axis=1))
        n = jnp.concatenate(blocks, axis=1)
        for slot in slots:
            w_got(slot)
            w.append(wkv[slot].reshape(128, COLS))
        kv = nt_dot(jnp.concatenate(w, axis=1), n)
        for core in range(2):
            w = jnp.concatenate([wq[slot, core] for slot in slots], axis=0)
            q = jnp.dot(n, w, preferred_element_type=F32)
            k = kv[core * 64:core * 64 + 64]
            q_acc[core] = q if first else q_acc[core] + q
            kv_acc[core] = k if first else kv_acc[core] + k

    small_got(1, 1)
    small_send(1, 3, dev_xp)
    small_got(2, 2)
    small_got(3, 0)
    small_send(3, 4, dev_xp)
    small_send(3, 5, dev_xm)
    docs_step(0)
    ag.near_relay()
    pj_send(1)
    small_got(6, 3)
    docs_step(1)
    small_got(4, 4)
    small_send(4, 6, dev_xp)
    small_got(5, 5)
    ag.near_rest()
    ag.opp_half(0)
    z_step(0)
    pj_send(2)
    small_got(7, 6)
    sums = sg_r[0][:, COLS:COLS + 256]
    for i in range(1, 8):
        sums = sums + sg_r[i][:, COLS:COLS + 256]
    sum_s[...] = sums
    send(sum_s, sum_r, x_ss.at[2], x_rs.at[2], sib)
    docs_step(2)
    ag.opp_half(1)
    pj_send(3)
    arrive(sum_r, x_ss.at[2], x_rs.at[2])
    sums = sum_s[...] + sum_r[...]
    ts_v[...] = jnp.broadcast_to(lax.rsqrt(sums[:, 0:128] / DT + 1e-05), (ROWS, 128)).T
    scale_v[...] = jnp.broadcast_to(lax.rsqrt(sums[:, 128:256] / DS + 1e-05), (ROWS, 128)).T
    docs_step(3)
    z_step(1)
    ag.onear_a()
    pj_send(4)
    l_wq.wait()
    process([mine] + ag.near, True)
    ag.onear_b()
    pj_send(5)
    ag.far_step()
    process([ag.opp, ag.far[0]])
    pj_send(6)
    ag.onear_rest()
    process(ag.onear)
    pj_send(7)
    ag.ofar_step()
    process([ag.far[1]])
    send(kv_acc.at[1 - c], kv_in, x_ss.at[3], x_rs.at[3], sib)
    send(q_acc.at[1 - c], q_in, x_ss.at[4], x_rs.at[4], sib)
    z_step(2)
    arrive(kv_in, x_ss.at[3], x_rs.at[3])

    row = lax.broadcasted_iota(jnp.int32, (64, 64), 0)
    col = lax.broadcasted_iota(jnp.int32, (64, 64), 1)
    take = ((row >> 3) & 1) * 32 + (row & 7) * 4 + (row >> 4)
    pick = jnp.where(col == take, 1.0, 0.0).astype(BF16)
    kv_mine = (kv_acc[c] + kv_in[...]).astype(BF16)
    kvx_s[...] = jnp.dot(pick, kv_mine, preferred_element_type=F32).astype(BF16).reshape(4, 16, 128)
    kvx_r[t] = kvx_s[t // 4]

    def kvx(k):
        to = (t + k) % 16
        return copy(kvx_s.at[to // 4], kvx_r.at[t], kx_ss.at[k], kx_rs.at[k], (s, to))

    def kvx_go(k, carry):
        kvx(k).start()
        return carry

    def kvx_got(k, carry):
        arrive(kvx_r.at[(t + 16 - k) % 16], kx_ss.at[k], kx_rs.at[k])
        return carry

    def kvx_end(k, carry):
        kvx(k).wait_send()
        return carry

    lax.fori_loop(1, 16, kvx_go, 0)
    lax.fori_loop(0, 8, wo_fetch, 0)
    lax.fori_loop(0, 8, wo_go, 0)
    z_step(3)

    cos2 = jnp.concatenate([cos_t[...], cos_t[...]], axis=0).T
    sin2 = jnp.concatenate([-sin_t[...], sin_t[...]], axis=0).T
    arrive(q_in, x_ss.at[4], x_rs.at[4])
    q_mine = q_acc[c] + q_in[...]
    for h in range(2):
        qh = q_mine[:, h * 128:(h + 1) * 128]
        turned = qh * cos2 + pltpu.roll(qh, 64, 1) * sin2
        q_v[h] = (turned * HEAD_DIM ** (-0.5)).astype(BF16)

    lax.fori_loop(1, 16, kvx_got, 0)
    both = kvx_r[...].astype(F32).reshape(16, 2, 8, ROWS)
    k_raw = both[:, 0].reshape(HEAD_DIM, ROWS)
    v_raw = both[:, 1].reshape(HEAD_DIM, ROWS)
    first, second = k_raw[0:64], k_raw[64:128]
    k_rot = jnp.concatenate(
        [first * cos_t[...] - second * sin_t[...], second * cos_t[...] + first * sin_t[...]], axis=0
    )
    kv_own[0] = k_rot.astype(BF16)
    kv_own[1] = v_raw.T.astype(BF16)
    kv_r[0, 0] = kv_own[0]
    kv_r[1, 0] = kv_own[1]

    def kv_copy(k):
        return copy(kv_own.at[c], kv_r.at[c, k], kv_ss.at[k], kv_rs.at[k], ((s + k) % 16, t))

    def kv_fwd(k):
        return copy(kv_r.at[c, k], kv_r.at[c, k], kf_ss.at[k], kf_rs.at[k], sib)

    def kv_go(k):
        @pl.when(s + k < 16)
        def _():
            kv_copy(k).start()

    def kv_mid(k):
        @pl.when(s >= k)
        def _():
            arrive(kv_r.at[c, k], kv_ss.at[k], kv_rs.at[k])
            kv_fwd(k).start()

    def kv_got(k, carry):
        @pl.when(s >= k)
        def _():
            arrive(kv_r.at[1 - c, k], kf_ss.at[k], kf_rs.at[k])
        return carry

    def kv_end(k, carry):
        @pl.when(s >= k)
        def _():
            kv_fwd(k).wait_send()

        @pl.when(s + k < 16)
        def _():
            kv_copy(k).wait_send()
        return carry

    arrive(docs_o, dc_ss.at[8], dc_rs.at[8])
    for k in range(1, BACK + 1):
        kv_go(k)

    def docs_back(j):
        at = (z + 8 - j) % 8
        return jnp.where(z >= j, docs_z[at], jnp.where(yl == 1, docs_o[at], -1))

    key_doc = jnp.concatenate([docs_back(j) for j in range(BACK + 1)], axis=1)
    row_doc = jnp.broadcast_to(docs[...].astype(F32), (ROWS, ROWS)).T[:, 0:1].astype(jnp.int32)
    wide = (ROWS, (BACK + 1) * ROWS)
    row_at = lax.broadcasted_iota(jnp.int32, wide, 0)
    key_at = lax.broadcasted_iota(jnp.int32, wide, 1)
    allowed = (key_doc == row_doc) & ((key_at >= ROWS) | (key_at <= row_at))
    bias[...] = jnp.where(allowed, 0.0, -1e30)

    class Reduce:
        def __init__(self, y_order, own, sib_s, sib_r, x2, ra, rb, xp, xm, fm, fp, ys, yr, fin, ss, rs):
            self.own, self.sib_s, self.sib_r = own, sib_s, sib_r
            self.x2, self.ra, self.rb, self.xp, self.xm, self.fm, self.fp = x2, ra, rb, xp, xm, fm, fp
            self.ys, self.yr, self.fin, self.ss, self.rs = ys, yr, fin, ss, rs
            self.y_order = y_order
            self.x_order = (xf_, xp_, xm_, x)

        def go(self, src, dst, k, dev):
            send(src, dst, self.ss.at[k], self.rs.at[k], dev)

        def got(self, dst, k):
            arrive(dst, self.ss.at[k], self.rs.at[k])

        def slot(self, k, i):
            return self.y_order[i] * 4 + self.x_order[k]

        def to_sib(self, k, i):
            slot = self.slot(k, i)
            self.go(self.sib_s.at[slot], self.sib_r.at[slot], k * 2 + i, sib)

        def sib_got(self, k, i):
            if self.sib_r is not None:
                self.got(self.sib_r.at[self.slot(k, i)], k * 2 + i)

        def pair(self, k, i, h):
            slot, rows = self.slot(k, i), slice(h * 64, h * 64 + 64)
            value = self.own[slot, rows]
            return value if self.sib_r is None else value + self.sib_r[slot, rows].astype(F32)

        def far(self, i):
            self.sib_got(0, i)
            self.x2[i, 0:64] = self.pair(0, i, 0).astype(BF16)
            self.go(self.x2.at[i, pl.ds(0, 64)], self.ra.at[i], 8 + i, dev_xp)
            self.x2[i, 64:128] = self.pair(0, i, 1).astype(BF16)
            self.go(self.x2.at[i, pl.ds(64, 64)], self.rb.at[i], 10 + i, dev_xm)

        def near(self, i):
            self.sib_got(1, i)
            self.xp[i, 64:128] = self.pair(1, i, 1).astype(BF16)
            self.go(self.xp.at[i, pl.ds(64, 64)], self.fm.at[i, pl.ds(64, 64)], 12 + i, dev_xp)
            self.sib_got(2, i)
            self.xm[i, 0:64] = self.pair(2, i, 0).astype(BF16)
            self.go(self.xm.at[i, pl.ds(0, 64)], self.fp.at[i, pl.ds(0, 64)], 14 + i, dev_xm)

        def relay(self, i):
            self.got(self.ra.at[i], 8 + i)
            self.xp[i, 0:64] = (self.pair(1, i, 0) + self.ra[i].astype(F32)).astype(BF16)
            self.go(self.xp.at[i, pl.ds(0, 64)], self.fm.at[i, pl.ds(0, 64)], 16 + i, dev_xp)
            self.got(self.rb.at[i], 10 + i)
            self.xm[i, 64:128] = (self.pair(2, i, 1) + self.rb[i].astype(F32)).astype(BF16)
            self.go(self.xm.at[i, pl.ds(64, 64)], self.fp.at[i, pl.ds(64, 64)], 18 + i, dev_xm)

        def join(self, i, h):
            rows, at = slice(h * 64, h * 64 + 64), pl.ds(h * 64, 64)
            if h == 0:
                self.sib_got(3, i)
            self.got(self.fm.at[i, at], (16, 12)[h] + i)
            self.got(self.fp.at[i, at], (14, 18)[h] + i)
            return self.pair(3, i, h) + self.fm[i, rows].astype(F32) + self.fp[i, rows].astype(F32)

        def to_opp(self, h):
            at = pl.ds(h * 64, 64)
            return copy(self.ys.at[at], self.yr.at[at], self.ss.at[20 + h], self.rs.at[20 + h], dev_yo)

        def join_other(self):
            for h in range(2):
                self.ys[h * 64:h * 64 + 64] = self.join(0, h).astype(BF16)
                self.to_opp(h).start()

        def join_mine(self):
            for h in range(2):
                self.fin[h * 64:h * 64 + 64] = self.join(1, h)

        def end(self):
            for h in range(2):
                self.to_opp(h).wait_send()

        def last(self, h):
            rows = slice(h * 64, h * 64 + 64)
            self.got(self.yr.at[pl.ds(h * 64, 64)], 20 + h)
            return self.fin[rows] + self.yr[rows].astype(F32)

    rt = Reduce((yl, 1 - yl), t_own, t_sib_s, t_sib_r, t_x2, t_ra, t_rb, t_xp, t_xm, t_fm, t_fp, None, None, None, t_ss, t_rs)

    def t3(i, h):
        at = pl.ds(h * 64, 64)
        dev = (yl * 8 + (z + turn) % 8, rt.y_order[i] * 8 + z)
        return copy(t3_s.at[i, at], t3_r.at[yh, at], t3_ss.at[i * 2 + h], t3_rs.at[yh * 2 + h], dev)

    def t3_stays(i):
        return stays & (rt.y_order[i] == yh)

    def t_place(i):
        for h in range(2):
            rows = slice(h * 64, h * 64 + 64)
            t3_s[i, rows] = rt.join(i, h).astype(BF16)

            @pl.when(t3_stays(i))
            def _():
                t3_r[yh, rows] = t3_s[i, rows]

            @pl.when(jnp.logical_not(t3_stays(i)))
            def _():
                t3(i, h).start()

    z_step(4)
    z_step(5)
    z_step(6)

    def products(core, y_, k, width):
        rows = tg[pl.ds(core * 4, 4), :, k * width:(k + 1) * width].reshape(4 * ROWS, width)
        return jnp.dot(rows, pj[y_, k * width:(k + 1) * width], preferred_element_type=F32).reshape(4, ROWS, COLS)

    l_pj.wait()
    first = pl.ds(yl * 4, 4)
    t_sib_s[first] = products(1 - c, yl, 0, 1024).astype(BF16)
    for k in range(4):
        rt.to_sib(k, 0)
    t_own[first] = products(c, yl, 0, 1024)
    rt.far(0)
    rt.near(0)

    other = pl.ds((1 - yl) * 4, 4)
    for k in range(4):
        for piece in (2 * k, 2 * k + 1):
            arrive(pj.at[1 - yl, pl.ds(piece * 128, 128)], p_ss.at[piece], p_rs.at[piece])
        theirs = products(1 - c, 1 - yl, k, 256)
        if k == 0:
            t_part[...] = theirs
        elif k < 3:
            t_part[...] += theirs
        else:
            t_sib_s[other] = (t_part[...] + theirs).astype(BF16)
            for j in range(4):
                rt.to_sib(j, 1)
        if k == 0:
            t_own[other] = products(c, 1 - yl, k, 256)
        else:
            t_own[other] += products(c, 1 - yl, k, 256)
        if k == 1:
            rt.relay(0)
    rt.far(1)
    rt.near(1)
    t_place(0)
    for k in range(1, BACK + 1):
        kv_mid(k)

    lax.fori_loop(1, BACK + 1, kv_got, 0)
    keys = jnp.concatenate([kv_r[0, j] for j in range(BACK + 1)], axis=1)
    values = kv_r[1].reshape((BACK + 1) * ROWS, HEAD_DIM)
    for h in range(2):
        scores = jnp.dot(q_v[h], keys, preferred_element_type=F32)
        scores = scores + bias[...]
        probs = jnp.exp(scores - jnp.max(scores, axis=1, keepdims=True))
        total = jnp.sum(probs, axis=1, keepdims=True)
        acc = jnp.dot(probs.astype(BF16), values, preferred_element_type=F32)
        attn_v[c * 2 + h] = (acc / total).astype(BF16)
        send(attn_v.at[c * 2 + h], attn_v.at[c * 2 + h], x_ss.at[5 + h], x_rs.at[5 + h], sib)
    lax.fori_loop(0, 8, wo_got, 0)
    rt.relay(1)

    ro = Reduce((yo_, yh), o_own, None, None, o_x2, o_ra, o_rb, o_xp, o_xm, o_fm, o_fp, o_ys, o_yr, o_fin, o_ss, o_rs)

    for h in range(2):
        arrive(attn_v.at[2 - 2 * c + h], x_ss.at[5 + h], x_rs.at[5 + h])
    attn = jnp.concatenate([attn_v[i] for i in range(4)], axis=1)

    def out_block(k, i):
        slot = ro.slot(k, i)
        o_own[slot] = jnp.dot(attn, wo[slot].reshape(COLS, COLS), preferred_element_type=F32)

    out_block(0, 0)
    ro.far(0)
    out_block(1, 0)
    out_block(2, 0)
    ro.near(0)
    out_block(0, 1)
    ro.relay(0)
    ro.far(1)
    out_block(1, 1)
    out_block(2, 1)
    ro.near(1)
    t_place(1)
    out_block(3, 0)
    out_block(3, 1)
    ro.relay(1)

    ro.join_other()
    ro.join_mine()

    early = list(started)
    started.clear()

    def before_end():
        for one in early:
            one.wait_send()
        lax.fori_loop(0, 8, w_end, 0)
        lax.fori_loop(0, 8, wo_end, 0)
        lax.fori_loop(1, 16, kvx_end, 0)
        lax.fori_loop(1, BACK + 1, kv_end, 0)
        ro.end()
        for i in range(2):

            @pl.when(jnp.logical_not(t3_stays(i)))
            def _():
                t3(i, 0).wait_send()
                t3(i, 1).wait_send()

    dg = Gather(db, dg_ss, dg_rs)
    for h in range(2):
        rows = slice(h * 64, h * 64 + 64)
        mixed = hb[mine, rows].astype(F32) + ro.last(h)
        out_s[rows] = mixed.astype(BF16)

        for p in range(2):

            @pl.when(jnp.logical_not(stays & (yh == p)))
            def _():
                arrive(t3_r.at[p, pl.ds(h * 64, 64)], t3_ss.at[h], t3_rs.at[p * 2 + h])

        target = t3_r[0, rows].astype(F32) + t3_r[1, rows].astype(F32)
        target = target * jnp.concatenate([ts_v[rows]] * 4, axis=1)
        difference = mixed - target
        db[mine, rows] = difference.astype(BF16)
        dg.begin(h)
        squares = difference * difference
        l_v[rows] = (
            squares[:, 0:128] + squares[:, 128:256] + squares[:, 256:384] + squares[:, 384:512]
        )
    l_s[...] = jnp.sum(l_v[...].T, axis=0, keepdims=True)
    l_r[t] = l_s[...]

    def loss(k):
        return copy(l_s, l_r.at[t], l_ss.at[k], l_rs.at[k], (s, (t + k) % 16))

    def loss_go(k, carry):
        loss(k).start()
        return carry

    def loss_got(k, carry):
        arrive(l_r.at[(t + 16 - k) % 16], l_ss.at[k], l_rs.at[k])
        return carry

    def loss_end(k, carry):
        loss(k).wait_send()
        return carry

    lax.fori_loop(1, 16, loss_go, 0)

    def add_grad(slots, first=False):
        d = jnp.concatenate([db[slot] for slot in slots], axis=1)
        for core in range(2):
            w = jnp.concatenate([wo[slot, core] for slot in slots], axis=1)
            g = nt_dot(d, w)
            g_acc[core] = g if first else g_acc[core] + g

    dg.near_relay()
    dg.opp_half(0)
    dg.near_rest()
    before_end()
    add_grad([mine] + dg.near, True)
    dg.opp_half(1)
    dg.onear_a()
    dg.far_step()
    add_grad([dg.opp, dg.far[0]])
    dg.onear_b()
    dg.onear_rest()
    add_grad(dg.onear)
    lax.fori_loop(1, 16, loss_got, 0)
    loss_sum = l_r[0]
    for i in range(1, 16):
        loss_sum = loss_sum + l_r[i]
    out_l[...] = loss_sum / DS
    dg.ofar_step()
    add_grad([dg.far[1]])
    send(g_acc.at[1 - c], g_in, x_ss.at[7], x_rs.at[7], sib)
    arrive(g_in, x_ss.at[7], x_rs.at[7])
    out_g[...] = (g_acc[c] + g_in[...]).astype(BF16)

    flush()
    lax.fori_loop(1, 16, loss_end, 0)


def reduce_buffers():
    block = (ROWS, COLS)
    return [
        pltpu.VMEM((2, 64, COLS), BF16),
        pltpu.VMEM((2, 64, COLS), BF16),
        pltpu.VMEM((2,) + block, BF16),
        pltpu.VMEM((2,) + block, BF16),
        pltpu.VMEM((2,) + block, BF16),
        pltpu.VMEM((2,) + block, BF16),
        pltpu.VMEM(block, BF16),
        pltpu.VMEM(block, BF16),
        pltpu.VMEM(block, F32),
    ]


def on_device(
    teacher_hidden, teacher_gain, projector, student_hidden, student_gain,
    query_weight, kv_weight, out_weight, doc_ids,
):
    block = (ROWS, COLS)
    hbm = pl.BlockSpec(memory_space=pltpu.HBM)
    vmem = pl.BlockSpec(memory_space=pltpu.VMEM)
    dma = pltpu.SemaphoreType.DMA
    out_s, out_l, out_g = pl.pallas_call(
        body,
        out_shape=(
            jax.ShapeDtypeStruct(block, BF16),
            jax.ShapeDtypeStruct((1, ROWS), F32),
            jax.ShapeDtypeStruct((ROWS, 256), BF16),
        ),
        in_specs=[hbm] * 9,
        out_specs=(vmem, vmem, vmem),
        scratch_shapes=[
            pltpu.VMEM((1, 1024), F32),
            pltpu.VMEM((1, COLS), F32),
            pltpu.VMEM((1, ROWS), jnp.int32),
            pltpu.VMEM((ROWS, 1024), BF16),
            pltpu.VMEM((8, ROWS, 1024), BF16),
            pltpu.VMEM((2, 1024, COLS), BF16),
            pltpu.VMEM((8, 2, COLS, 256), BF16),
            pltpu.VMEM((8, 2, 2, 32, COLS), BF16),
            pltpu.VMEM((8, 2, 256, COLS), BF16),
            pltpu.VMEM((64, ROWS), F32),
            pltpu.VMEM((64, ROWS), F32),
            pltpu.VMEM((8,) + block, BF16),
            pltpu.VMEM((1, 768), F32),
            pltpu.VMEM((8, 1, 768), F32),
            pltpu.VMEM((1, 256), F32),
            pltpu.VMEM((1, 256), F32),
            pltpu.VMEM((ROWS, 128), F32),
            pltpu.VMEM((2, ROWS, 256), F32),
            pltpu.VMEM((ROWS, 256), F32),
            pltpu.VMEM((2, 64, ROWS), F32),
            pltpu.VMEM((64, ROWS), F32),
            pltpu.VMEM((4, 16, ROWS), BF16),
            pltpu.VMEM((16, 16, ROWS), BF16),
            pltpu.VMEM((2, ROWS, HEAD_DIM), BF16),
            pltpu.VMEM((2, BACK + 1, ROWS, HEAD_DIM), BF16),
            pltpu.VMEM((8, 1, ROWS), jnp.int32),
            pltpu.VMEM((8, 1, ROWS), jnp.int32),
            pltpu.VMEM((2, ROWS, HEAD_DIM), BF16),
            pltpu.VMEM((4, ROWS, HEAD_DIM), BF16),
            pltpu.VMEM((ROWS, (BACK + 1) * ROWS), F32),
            pltpu.VMEM((8,) + block, F32),
            pltpu.VMEM((4,) + block, F32),
            pltpu.VMEM((8,) + block, F32),
            pltpu.VMEM((2,) + block, BF16),
            pltpu.VMEM((8,) + block, BF16),
            pltpu.VMEM((8,) + block, BF16),
            pltpu.VMEM((2,) + block, BF16),
            *reduce_buffers()[:6],
            *reduce_buffers(),
            pltpu.VMEM((2,) + block, BF16),
            pltpu.VMEM((2,) + block, BF16),
            pltpu.VMEM((ROWS, 128), F32),
            pltpu.VMEM((8,) + block, BF16),
            pltpu.VMEM((2, ROWS, 256), F32),
            pltpu.VMEM((ROWS, 256), F32),
            pltpu.VMEM((ROWS, 128), F32),
            pltpu.VMEM((1, ROWS), F32),
            pltpu.VMEM((16, 1, ROWS), F32),
            dma((10,)),
            *[dma((8,)) for _ in range(10)],
            dma((16,)), dma((16,)), dma((8,)), dma((8,)),
            dma((24,)), dma((24,)), dma((24,)), dma((24,)),
            dma((16,)), dma((16,)), dma((16,)), dma((16,)),
            dma((9,)), dma((9,)), dma((9,)), dma((9,)), dma((9,)), dma((9,)),
            dma((24,)), dma((24,)), dma((24,)), dma((24,)),
            dma((4,)), dma((4,)),
            dma((16,)), dma((16,)),
        ],
        compiler_params=pltpu.CompilerParams(
            collective_id=0, has_side_effects=True, vmem_limit_bytes=40 * 1024 * 1024
        ),
    )(
        *(
            pltpu.with_memory_space_constraint(one, pltpu.HBM)
            for one in (
                teacher_hidden, teacher_gain.reshape(1, -1), projector, student_hidden,
                student_gain.reshape(1, -1), query_weight.reshape(8, 2, COLS, 256), jnp.transpose(kv_weight, (0, 2, 1)),
                out_weight, doc_ids.reshape(1, -1),
            )
        )
    )
    return out_s, out_l.reshape(ROWS), out_g


def solution(mesh):
    in_specs = (
        P("seq", "tensor"),
        P("tensor"),
        P("tensor", "seq"),
        P("seq", "tensor"),
        P("tensor"),
        P(None, "tensor"),
        P(None, None, "tensor"),
        P("tensor", None),
        P("seq"),
    )
    out_specs = (P("seq", "tensor"), P("seq"), P("seq", "tensor"))
    return jax.shard_map(
        on_device, mesh=mesh, in_specs=in_specs, out_specs=out_specs, check_vma=False
    )
```

```python
import math

import jax
import jax.numpy as jnp
from jax import lax
from jax.experimental import pallas as pl
from jax.experimental.pallas import tpu as pltpu
from jax.sharding import PartitionSpec as P

DT = 16384
DS = 8192
HEAD_DIM = 128
HEADS = 32
KV_HEADS = 4
ROWS = 128
COLS = 512
BACK = 8
F32 = jnp.float32
BF16 = jnp.bfloat16
MESH = pl.DeviceIdType.MESH
NT = (((1,), (1,)), ((), ()))


def nt_dot(a, b):
    return lax.dot_general(a, b, NT, preferred_element_type=F32)


def body(
    th_h, tgain_h, pj_h, sh_h, sgain_h, wq_h, wkv_h, wo_h, docs_h,
    out_s, out_l, out_g,
    tgain, sgain, docs, th_v, tg, pj, wq, wkv, wo, cos_t, sin_t,
    hb, sg_s, sg_r, sum_s, sum_r, scale_v, q_acc, q_in, kv_acc, kv_in,
    kvx_s, kvx_r, kv_own, kv_r, docs_z, docs_o, q_v, attn_v, bias,
    t_own, t_part, o_own, o_x2, t_sib_s, t_sib_r, t_x2, t_ra, t_rb, t_xp, t_xm, t_fm, t_fp,
    o_ra, o_rb, o_xp, o_xm, o_fm, o_fp, o_ys, o_yr, o_fin,
    t3_s, t3_r, ts_v, db, g_acc, g_in, l_v, l_s, l_r,
    load_sem, w_load, w_ss, w_rs, v_load, v_ss, v_rs, u_ss, u_rs, x_ss, x_rs, z_ss, z_rs, p_ss, p_rs,
    ag_ss, ag_rs, dg_ss, dg_rs, sm_ss, sm_rs, kx_ss, kx_rs, kv_ss, kv_rs, kf_ss, kf_rs, dc_ss, dc_rs,
    t_ss, t_rs, o_ss, o_rs, t3_ss, t3_rs, l_ss, l_rs,
):
    s = lax.axis_index("seq")
    t = lax.axis_index("tensor")
    yl, z = s // 8, s % 8
    yh, x, c = t // 8, (t // 2) % 4, t % 2

    def tid(y_, x_, c_):
        return y_ * 8 + x_ * 2 + c_

    xp_, xm_ = (x + 1) % 4, (x + 3) % 4
    xf_ = (x + 2) % 4
    yo_ = 1 - yh
    sib = (s, tid(yh, x, 1 - c))
    dev_xp = (s, tid(yh, xp_, c))
    dev_xm = (s, tid(yh, xm_, c))
    dev_yo = (s, tid(yo_, x, c))
    dev_zp = (yl * 8 + (z + 1) % 8, t)
    dev_zm = (yl * 8 + (z + 7) % 8, t)
    dev_yl = ((1 - yl) * 8 + z, t)
    turn = jnp.where(c == 0, x, jnp.where(x == 0, 4, 8 - x))
    stays = (z == 0) & (x == 0) & (c == 0)

    started = []

    def copy(src, dst, ss, rs, dev):
        return pltpu.make_async_remote_copy(
            src_ref=src, dst_ref=dst, send_sem=ss, recv_sem=rs, device_id=dev, device_id_type=MESH
        )

    def send(src, dst, ss, rs, dev):
        one = copy(src, dst, ss, rs, dev)
        one.start()
        started.append(one)

    def flush():
        for one in started:
            one.wait_send()
        started.clear()

    def arrive(dst, ss, rs):
        copy(dst, dst, ss, rs, sib).wait_recv()

    def load(src, dst, k):
        one = pltpu.make_async_copy(src, dst, load_sem.at[k])
        one.start()
        return one

    l_th = load(th_h, th_v, 0)
    mine = yh * 4 + x
    l_sh = load(sh_h, hb.at[mine], 1)
    l_small = [load(tgain_h, tgain, 7), load(sgain_h, sgain, 8), load(docs_h, docs, 9)]

    def wkv_part(j, core):
        return wkv_h.at[:, :, pl.ds(pl.multiple_of((j * 2 + core) * COLS, COLS), COLS)]

    def wkv_load(j):
        return pltpu.make_async_copy(wkv_part(j, c), wkv.at[j, c], v_load.at[j])

    def wkv_go(j, carry):
        wkv_load(j).start()
        return carry

    def wo_part(j, core):
        return wo_h.at[:, pl.ds(pl.multiple_of((j * 2 + core) * COLS, COLS), COLS)]

    def wo_load(j):
        return pltpu.make_async_copy(wo_part(j, c), wo.at[j, c], w_load.at[j])

    def wo_send(j):
        return copy(wo_part(j, 1 - c), wo.at[j, c], w_ss.at[j], w_rs.at[j], sib)

    def wo_fetch(j, carry):
        wo_load(j).start()
        return carry

    def wo_go(j, carry):
        wo_send(j).start()
        return carry

    def wo_got(j, carry):
        wo_load(j).wait()
        arrive(wo.at[j, 1 - c], w_ss.at[j], w_rs.at[j])
        return carry

    def wo_end(j, carry):
        wo_send(j).wait_send()
        return carry

    lax.fori_loop(0, 8, wkv_go, 0)
    l_wq = load(wq_h.at[:, c], wq.at[:, c], 3)

    kv_r[...] = jnp.zeros(kv_r.shape, BF16)

    barrier = pltpu.get_barrier_semaphore()
    for dev in (sib, dev_xp, dev_xm, dev_yo, dev_zp, dev_zm, dev_yl):
        pl.semaphore_signal(barrier, inc=1, device_id=dev, device_id_type=MESH)

    class Gather:
        def __init__(self, buf, ss, rs):
            self.buf, self.ss, self.rs = buf, ss, rs
            self.near = [yh * 4 + xm_, yh * 4 + xp_]
            self.opp = yo_ * 4 + x
            self.onear = [yo_ * 4 + xm_, yo_ * 4 + xp_]
            self.far = [yh * 4 + xf_, yo_ * 4 + xf_]
            self.order = [mine] + self.near + [self.opp] + self.onear + self.far

        def part(self, slot, h):
            return self.buf.at[slot, pl.ds(h * 64, 64)]

        def half(self, slot, h, k, dev):
            part = self.part(slot, h)
            send(part, part, self.ss.at[k], self.rs.at[k], dev)

        def got_half(self, slot, h, k):
            arrive(self.part(slot, h), self.ss.at[k], self.rs.at[k])

        def begin(self, h):
            self.half(mine, h, 0 + h, dev_yo)
            self.half(mine, h, 2 + h, dev_xp)
            self.half(mine, h, 4 + h, dev_xm)

        def near_relay(self):
            self.got_half(self.near[0], 0, 2)
            self.half(self.near[0], 0, 6, dev_xp)
            self.got_half(self.near[1], 1, 5)
            self.half(self.near[1], 1, 7, dev_xm)

        def near_rest(self):
            self.got_half(self.near[0], 1, 3)
            self.got_half(self.near[1], 0, 4)

        def opp_half(self, h):
            self.got_half(self.opp, h, 0 + h)
            self.half(self.opp, h, 8 + h, dev_xp)
            self.half(self.opp, h, 10 + h, dev_xm)

        def onear_a(self):
            self.got_half(self.onear[0], 0, 8)
            self.half(self.onear[0], 0, 12, dev_xp)

        def onear_b(self):
            self.got_half(self.onear[1], 1, 11)
            self.half(self.onear[1], 1, 13, dev_xm)

        def onear_rest(self):
            self.got_half(self.onear[0], 1, 9)
            self.got_half(self.onear[1], 0, 10)

        def far_step(self):
            self.got_half(self.far[0], 0, 6)
            self.got_half(self.far[0], 1, 7)

        def ofar_step(self):
            self.got_half(self.far[1], 0, 12)
            self.got_half(self.far[1], 1, 13)

    def pj_send(k):
        rows = pl.ds(k * 256, 256)
        send(pj_h.at[rows], pj.at[yl, rows], p_ss.at[k], p_rs.at[k], dev_yl)

    def wkv_send(j):
        return copy(wkv_part(j, 1 - c), wkv.at[j, c], v_ss.at[j], v_rs.at[j], sib)

    def wq_send(j):
        return copy(wq_h.at[j, 1 - c], wq.at[j, c], u_ss.at[j], u_rs.at[j], sib)

    def w_go(j, carry):
        wkv_send(j).start()
        wq_send(j).start()
        return carry

    def w_end(j, carry):
        wkv_send(j).wait_send()
        wq_send(j).wait_send()
        return carry

    def w_got(slot):
        wkv_load(slot).wait()
        arrive(wkv.at[slot, 1 - c], v_ss.at[slot], v_rs.at[slot])
        arrive(wq.at[slot, 1 - c], u_ss.at[slot], u_rs.at[slot])

    ag = Gather(hb, ag_ss, ag_rs)
    l_sh.wait()

    z_slot = 0
    l_th.wait()
    for one in l_small:
        one.wait()
    docs_z[z] = docs[...]
    part = jnp.zeros((ROWS, 128), F32)
    for i in range(8):
        cols = slice(i * 128, (i + 1) * 128)
        f = th_v[:, cols].astype(F32)
        part = part + f * f
        tg[z_slot, :, cols] = (f * tgain[:, cols]).astype(BF16)
    sg_s[:, COLS:COLS + 128] = jnp.sum(part.T, axis=0, keepdims=True)
    part = jnp.zeros((ROWS, 128), F32)
    for i in range(4):
        f = hb[mine, :, i * 128:(i + 1) * 128].astype(F32)
        part = part + f * f
    sg_s[:, COLS + 128:COLS + 256] = jnp.sum(part.T, axis=0, keepdims=True)
    sg_s[:, 0:COLS] = sgain[...]
    sg_r[mine] = sg_s[...]

    def ring_slot(d):
        return (0, 1, 2, 3, 4, 7, 6, 5)[d % 8]

    def z_ref(d, h):
        return tg.at[ring_slot(d), pl.ds(h * 64, 64)]

    def z_send(k):
        d = k // 2
        send(z_ref(8 - d, k % 2), z_ref(7 - d, k % 2), z_ss.at[k], z_rs.at[k], dev_zp)
        send(z_ref(d, 1 - k % 2), z_ref(d + 1, 1 - k % 2), z_ss.at[8 + k], z_rs.at[8 + k], dev_zm)

    def z_got(k):
        up, down = z_ref(-(k // 2) + 7, k % 2), z_ref(k // 2 + 1, 1 - k % 2)
        arrive(up, z_ss.at[k], z_rs.at[k])
        arrive(down, z_ss.at[8 + k], z_rs.at[8 + k])

    def z_step(k):
        z_got(k)
        if k + 2 < 7:
            z_send(k + 2)

    def small_send(i, k, dev):
        slot = ag.order[i]
        send(sg_r.at[slot], sg_r.at[slot], sm_ss.at[k], sm_rs.at[k], dev)

    def small_got(i, k):
        arrive(sg_r.at[ag.order[i]], sm_ss.at[k], sm_rs.at[k])

    def docs_send(d, k, dev):
        ref = docs_z.at[(z + d) % 8]
        send(ref, ref, dc_ss.at[k], dc_rs.at[k], dev)

    def docs_step(k):
        arrive(docs_z.at[(z + 7 - k) % 8], dc_ss.at[k], dc_rs.at[k])
        if k < 3:
            arrive(docs_z.at[(z + 1 + k) % 8], dc_ss.at[4 + k], dc_rs.at[4 + k])
            docs_send(7 - k, k + 1, dev_zp)
            if k < 2:
                docs_send(1 + k, k + 5, dev_zm)
        else:
            send(docs_z, docs_o, dc_ss.at[8], dc_rs.at[8], dev_yl)

    pl.semaphore_wait(barrier, 7)
    small_send(0, 0, dev_yo)
    small_send(0, 1, dev_xp)
    small_send(0, 2, dev_xm)
    ag.begin(0)
    ag.begin(1)
    docs_send(0, 0, dev_zp)
    docs_send(0, 4, dev_zm)
    z_send(0)
    z_send(1)
    pj_send(0)
    lax.fori_loop(0, 8, w_go, 0)
    pj_send(1)
    pj_send(2)
    l_pj = load(pj_h, pj.at[yl], 4)

    entry = lax.broadcasted_iota(jnp.int32, (64, ROWS), 0).astype(F32)
    position = (s * ROWS + lax.broadcasted_iota(jnp.int32, (64, ROWS), 1)).astype(F32)
    angle = position * jnp.exp(-math.log(500000.0) * (2.0 * entry / HEAD_DIM))
    cos_t[...] = jnp.cos(angle)
    sin_t[...] = jnp.sin(angle)

    def process(slots, first=False):
        blocks, w = [], []
        for slot in slots:
            parts = []
            for i in range(4):
                cols = slice(i * 128, (i + 1) * 128)
                f = hb[slot, :, cols].astype(F32)
                parts.append((f * scale_v[...] * sg_r[slot][:, cols]).astype(BF16))
            blocks.append(jnp.concatenate(parts, axis=1))
        n = jnp.concatenate(blocks, axis=1)
        for slot in slots:
            w_got(slot)
            w.append(wkv[slot].reshape(128, COLS))
        kv = nt_dot(jnp.concatenate(w, axis=1), n)
        for core in range(2):
            w = jnp.concatenate([wq[slot, core] for slot in slots], axis=0)
            q = jnp.dot(n, w, preferred_element_type=F32)
            k = kv[core * 64:core * 64 + 64]
            q_acc[core] = q if first else q_acc[core] + q
            kv_acc[core] = k if first else kv_acc[core] + k

    small_got(1, 1)
    small_send(1, 3, dev_xp)
    small_got(2, 2)
    small_got(3, 0)
    small_send(3, 4, dev_xp)
    small_send(3, 5, dev_xm)
    docs_step(0)
    ag.near_relay()
    z_step(0)
    small_got(6, 3)
    docs_step(1)
    small_got(4, 4)
    small_send(4, 6, dev_xp)
    small_got(5, 5)
    ag.near_rest()
    ag.opp_half(0)
    z_step(1)
    pj_send(3)
    small_got(7, 6)
    sums = sg_r[0][:, COLS:COLS + 256]
    for i in range(1, 8):
        sums = sums + sg_r[i][:, COLS:COLS + 256]
    sum_s[...] = sums
    send(sum_s, sum_r, x_ss.at[2], x_rs.at[2], sib)
    docs_step(2)
    ag.opp_half(1)
    z_step(2)
    arrive(sum_r, x_ss.at[2], x_rs.at[2])
    sums = sum_s[...] + sum_r[...]
    ts_v[...] = jnp.broadcast_to(lax.rsqrt(sums[:, 0:128] / DT + 1e-05), (ROWS, 128)).T
    scale_v[...] = jnp.broadcast_to(lax.rsqrt(sums[:, 128:256] / DS + 1e-05), (ROWS, 128)).T
    docs_step(3)
    ag.onear_a()
    z_step(3)
    l_wq.wait()
    process([mine] + ag.near, True)
    ag.onear_b()
    ag.far_step()
    z_step(4)
    process([ag.opp, ag.far[0]])
    ag.onear_rest()
    process(ag.onear)
    ag.ofar_step()
    process([ag.far[1]])
    send(kv_acc.at[1 - c], kv_in, x_ss.at[3], x_rs.at[3], sib)
    send(q_acc.at[1 - c], q_in, x_ss.at[4], x_rs.at[4], sib)
    arrive(kv_in, x_ss.at[3], x_rs.at[3])

    row = lax.broadcasted_iota(jnp.int32, (64, 64), 0)
    col = lax.broadcasted_iota(jnp.int32, (64, 64), 1)
    take = ((row >> 3) & 1) * 32 + (row & 7) * 4 + (row >> 4)
    pick = jnp.where(col == take, 1.0, 0.0).astype(BF16)
    kv_mine = (kv_acc[c] + kv_in[...]).astype(BF16)
    kvx_s[...] = jnp.dot(pick, kv_mine, preferred_element_type=F32).astype(BF16).reshape(4, 16, 128)
    kvx_r[t] = kvx_s[t // 4]

    def kvx(k):
        to = (t + k) % 16
        return copy(kvx_s.at[to // 4], kvx_r.at[t], kx_ss.at[k], kx_rs.at[k], (s, to))

    def kvx_go(k, carry):
        kvx(k).start()
        return carry

    def kvx_got(k, carry):
        arrive(kvx_r.at[(t + 16 - k) % 16], kx_ss.at[k], kx_rs.at[k])
        return carry

    def kvx_end(k, carry):
        kvx(k).wait_send()
        return carry

    lax.fori_loop(1, 16, kvx_go, 0)
    lax.fori_loop(0, 8, wo_fetch, 0)
    lax.fori_loop(0, 8, wo_go, 0)

    cos2 = jnp.concatenate([cos_t[...], cos_t[...]], axis=0).T
    sin2 = jnp.concatenate([-sin_t[...], sin_t[...]], axis=0).T
    arrive(q_in, x_ss.at[4], x_rs.at[4])
    q_mine = q_acc[c] + q_in[...]
    for h in range(2):
        qh = q_mine[:, h * 128:(h + 1) * 128]
        turned = qh * cos2 + pltpu.roll(qh, 64, 1) * sin2
        q_v[h] = (turned * HEAD_DIM ** (-0.5)).astype(BF16)

    lax.fori_loop(1, 16, kvx_got, 0)
    both = kvx_r[...].astype(F32).reshape(16, 2, 8, ROWS)
    k_raw = both[:, 0].reshape(HEAD_DIM, ROWS)
    v_raw = both[:, 1].reshape(HEAD_DIM, ROWS)
    first, second = k_raw[0:64], k_raw[64:128]
    k_rot = jnp.concatenate(
        [first * cos_t[...] - second * sin_t[...], second * cos_t[...] + first * sin_t[...]], axis=0
    )
    kv_own[0] = k_rot.astype(BF16)
    kv_own[1] = v_raw.T.astype(BF16)
    kv_r[0, 0] = kv_own[0]
    kv_r[1, 0] = kv_own[1]

    def kv_copy(k):
        return copy(kv_own.at[c], kv_r.at[c, k], kv_ss.at[k], kv_rs.at[k], ((s + k) % 16, t))

    def kv_fwd(k):
        return copy(kv_r.at[c, k], kv_r.at[c, k], kf_ss.at[k], kf_rs.at[k], sib)

    def kv_go(k):
        @pl.when(s + k < 16)
        def _():
            kv_copy(k).start()

    def kv_mid(k):
        @pl.when(s >= k)
        def _():
            arrive(kv_r.at[c, k], kv_ss.at[k], kv_rs.at[k])
            kv_fwd(k).start()

    def kv_got(k, carry):
        @pl.when(s >= k)
        def _():
            arrive(kv_r.at[1 - c, k], kf_ss.at[k], kf_rs.at[k])
        return carry

    def kv_end(k, carry):
        @pl.when(s >= k)
        def _():
            kv_fwd(k).wait_send()

        @pl.when(s + k < 16)
        def _():
            kv_copy(k).wait_send()
        return carry

    arrive(docs_o, dc_ss.at[8], dc_rs.at[8])
    for k in range(1, BACK + 1):
        kv_go(k)

    def docs_back(j):
        at = (z + 8 - j) % 8
        return jnp.where(z >= j, docs_z[at], jnp.where(yl == 1, docs_o[at], -1))

    key_doc = jnp.concatenate([docs_back(j) for j in range(BACK + 1)], axis=1)
    row_doc = jnp.broadcast_to(docs[...].astype(F32), (ROWS, ROWS)).T[:, 0:1].astype(jnp.int32)
    wide = (ROWS, (BACK + 1) * ROWS)
    row_at = lax.broadcasted_iota(jnp.int32, wide, 0)
    key_at = lax.broadcasted_iota(jnp.int32, wide, 1)
    allowed = (key_doc == row_doc) & ((key_at >= ROWS) | (key_at <= row_at))
    bias[...] = jnp.where(allowed, 0.0, -1e30)

    class Reduce:
        def __init__(self, y_order, own, sib_s, sib_r, x2, ra, rb, xp, xm, fm, fp, ys, yr, fin, ss, rs):
            self.own, self.sib_s, self.sib_r = own, sib_s, sib_r
            self.x2, self.ra, self.rb, self.xp, self.xm, self.fm, self.fp = x2, ra, rb, xp, xm, fm, fp
            self.ys, self.yr, self.fin, self.ss, self.rs = ys, yr, fin, ss, rs
            self.y_order = y_order
            self.x_order = (xf_, xp_, xm_, x)

        def go(self, src, dst, k, dev):
            send(src, dst, self.ss.at[k], self.rs.at[k], dev)

        def got(self, dst, k):
            arrive(dst, self.ss.at[k], self.rs.at[k])

        def slot(self, k, i):
            return self.y_order[i] * 4 + self.x_order[k]

        def to_sib(self, k, i):
            slot = self.slot(k, i)
            self.go(self.sib_s.at[slot], self.sib_r.at[slot], k * 2 + i, sib)

        def sib_got(self, k, i):
            if self.sib_r is not None:
                self.got(self.sib_r.at[self.slot(k, i)], k * 2 + i)

        def pair(self, k, i, h):
            slot, rows = self.slot(k, i), slice(h * 64, h * 64 + 64)
            value = self.own[slot, rows]
            return value if self.sib_r is None else value + self.sib_r[slot, rows].astype(F32)

        def far(self, i):
            self.sib_got(0, i)
            self.x2[i, 0:64] = self.pair(0, i, 0).astype(BF16)
            self.go(self.x2.at[i, pl.ds(0, 64)], self.ra.at[i], 8 + i, dev_xp)
            self.x2[i, 64:128] = self.pair(0, i, 1).astype(BF16)
            self.go(self.x2.at[i, pl.ds(64, 64)], self.rb.at[i], 10 + i, dev_xm)

        def near(self, i):
            self.sib_got(1, i)
            self.xp[i, 64:128] = self.pair(1, i, 1).astype(BF16)
            self.go(self.xp.at[i, pl.ds(64, 64)], self.fm.at[i, pl.ds(64, 64)], 12 + i, dev_xp)
            self.sib_got(2, i)
            self.xm[i, 0:64] = self.pair(2, i, 0).astype(BF16)
            self.go(self.xm.at[i, pl.ds(0, 64)], self.fp.at[i, pl.ds(0, 64)], 14 + i, dev_xm)

        def relay(self, i):
            self.got(self.ra.at[i], 8 + i)
            self.xp[i, 0:64] = (self.pair(1, i, 0) + self.ra[i].astype(F32)).astype(BF16)
            self.go(self.xp.at[i, pl.ds(0, 64)], self.fm.at[i, pl.ds(0, 64)], 16 + i, dev_xp)
            self.got(self.rb.at[i], 10 + i)
            self.xm[i, 64:128] = (self.pair(2, i, 1) + self.rb[i].astype(F32)).astype(BF16)
            self.go(self.xm.at[i, pl.ds(64, 64)], self.fp.at[i, pl.ds(64, 64)], 18 + i, dev_xm)

        def join(self, i, h):
            rows, at = slice(h * 64, h * 64 + 64), pl.ds(h * 64, 64)
            if h == 0:
                self.sib_got(3, i)
            self.got(self.fm.at[i, at], (16, 12)[h] + i)
            self.got(self.fp.at[i, at], (14, 18)[h] + i)
            return self.pair(3, i, h) + self.fm[i, rows].astype(F32) + self.fp[i, rows].astype(F32)

        def to_opp(self, h):
            at = pl.ds(h * 64, 64)
            return copy(self.ys.at[at], self.yr.at[at], self.ss.at[20 + h], self.rs.at[20 + h], dev_yo)

        def join_other(self):
            for h in range(2):
                self.ys[h * 64:h * 64 + 64] = self.join(0, h).astype(BF16)
                self.to_opp(h).start()

        def join_mine(self):
            for h in range(2):
                self.fin[h * 64:h * 64 + 64] = self.join(1, h)

        def end(self):
            for h in range(2):
                self.to_opp(h).wait_send()

        def last(self, h):
            rows = slice(h * 64, h * 64 + 64)
            self.got(self.yr.at[pl.ds(h * 64, 64)], 20 + h)
            return self.fin[rows] + self.yr[rows].astype(F32)

    rt = Reduce((yl, 1 - yl), t_own, t_sib_s, t_sib_r, t_x2, t_ra, t_rb, t_xp, t_xm, t_fm, t_fp, None, None, None, t_ss, t_rs)

    def t3(i, h):
        at = pl.ds(h * 64, 64)
        dev = (yl * 8 + (z + turn) % 8, rt.y_order[i] * 8 + z)
        return copy(t3_s.at[i, at], t3_r.at[yh, at], t3_ss.at[i * 2 + h], t3_rs.at[yh * 2 + h], dev)

    def t3_stays(i):
        return stays & (rt.y_order[i] == yh)

    def t_place(i):
        for h in range(2):
            rows = slice(h * 64, h * 64 + 64)
            t3_s[i, rows] = rt.join(i, h).astype(BF16)

            @pl.when(t3_stays(i))
            def _():
                t3_r[yh, rows] = t3_s[i, rows]

            @pl.when(jnp.logical_not(t3_stays(i)))
            def _():
                t3(i, h).start()

    z_step(5)
    z_step(6)

    def products(core, y_, k, width):
        rows = tg[pl.ds(core * 4, 4), :, k * width:(k + 1) * width].reshape(4 * ROWS, width)
        return jnp.dot(rows, pj[y_, k * width:(k + 1) * width], preferred_element_type=F32).reshape(4, ROWS, COLS)

    l_pj.wait()
    first = pl.ds(yl * 4, 4)
    t_sib_s[first] = products(1 - c, yl, 0, 1024).astype(BF16)
    for k in range(4):
        rt.to_sib(k, 0)
    t_own[first] = products(c, yl, 0, 1024)
    rt.far(0)
    rt.near(0)

    other = pl.ds((1 - yl) * 4, 4)
    for k in range(4):
        arrive(pj.at[1 - yl, pl.ds(k * 256, 256)], p_ss.at[k], p_rs.at[k])
        theirs = products(1 - c, 1 - yl, k, 256)
        if k == 0:
            t_part[...] = theirs
        elif k < 3:
            t_part[...] += theirs
        else:
            t_sib_s[other] = (t_part[...] + theirs).astype(BF16)
            for j in range(4):
                rt.to_sib(j, 1)
        if k == 0:
            t_own[other] = products(c, 1 - yl, k, 256)
        else:
            t_own[other] += products(c, 1 - yl, k, 256)
        if k == 1:
            rt.relay(0)
    rt.far(1)
    rt.near(1)
    t_place(0)
    for k in range(1, BACK + 1):
        kv_mid(k)
    rt.relay(1)

    lax.fori_loop(1, BACK + 1, kv_got, 0)
    keys = jnp.concatenate([kv_r[0, j] for j in range(BACK + 1)], axis=1)
    values = kv_r[1].reshape((BACK + 1) * ROWS, HEAD_DIM)
    for h in range(2):
        scores = jnp.dot(q_v[h], keys, preferred_element_type=F32)
        scores = scores + bias[...]
        probs = jnp.exp(scores - jnp.max(scores, axis=1, keepdims=True))
        total = jnp.sum(probs, axis=1, keepdims=True)
        acc = jnp.dot(probs.astype(BF16), values, preferred_element_type=F32)
        attn_v[c * 2 + h] = (acc / total).astype(BF16)
        send(attn_v.at[c * 2 + h], attn_v.at[c * 2 + h], x_ss.at[5 + h], x_rs.at[5 + h], sib)
    lax.fori_loop(0, 8, wo_got, 0)

    ro = Reduce((yo_, yh), o_own, None, None, o_x2, o_ra, o_rb, o_xp, o_xm, o_fm, o_fp, o_ys, o_yr, o_fin, o_ss, o_rs)

    for h in range(2):
        arrive(attn_v.at[2 - 2 * c + h], x_ss.at[5 + h], x_rs.at[5 + h])
    attn = jnp.concatenate([attn_v[i] for i in range(4)], axis=1)

    def out_block(k, i):
        slot = ro.slot(k, i)
        o_own[slot] = jnp.dot(attn, wo[slot].reshape(COLS, COLS), preferred_element_type=F32)

    out_block(0, 0)
    ro.far(0)
    out_block(1, 0)
    out_block(2, 0)
    ro.near(0)
    t_place(1)
    out_block(0, 1)
    ro.relay(0)
    ro.far(1)
    out_block(1, 1)
    out_block(2, 1)
    ro.near(1)
    out_block(3, 0)
    out_block(3, 1)
    ro.relay(1)

    ro.join_other()
    ro.join_mine()

    early = list(started)
    started.clear()

    def before_end():
        for one in early:
            one.wait_send()
        lax.fori_loop(0, 8, w_end, 0)
        lax.fori_loop(0, 8, wo_end, 0)
        lax.fori_loop(1, 16, kvx_end, 0)
        lax.fori_loop(1, BACK + 1, kv_end, 0)
        ro.end()
        for i in range(2):

            @pl.when(jnp.logical_not(t3_stays(i)))
            def _():
                t3(i, 0).wait_send()
                t3(i, 1).wait_send()

    dg = Gather(db, dg_ss, dg_rs)
    for h in range(2):
        rows = slice(h * 64, h * 64 + 64)
        mixed = hb[mine, rows].astype(F32) + ro.last(h)
        out_s[rows] = mixed.astype(BF16)

        for p in range(2):

            @pl.when(jnp.logical_not(stays & (yh == p)))
            def _():
                arrive(t3_r.at[p, pl.ds(h * 64, 64)], t3_ss.at[h], t3_rs.at[p * 2 + h])

        target = t3_r[0, rows].astype(F32) + t3_r[1, rows].astype(F32)
        target = target * jnp.concatenate([ts_v[rows]] * 4, axis=1)
        difference = mixed - target
        db[mine, rows] = difference.astype(BF16)
        dg.begin(h)
        squares = difference * difference
        l_v[rows] = (
            squares[:, 0:128] + squares[:, 128:256] + squares[:, 256:384] + squares[:, 384:512]
        )
    l_s[...] = jnp.sum(l_v[...].T, axis=0, keepdims=True)
    l_r[t] = l_s[...]

    def loss(k):
        return copy(l_s, l_r.at[t], l_ss.at[k], l_rs.at[k], (s, (t + k) % 16))

    def loss_go(k, carry):
        loss(k).start()
        return carry

    def loss_got(k, carry):
        arrive(l_r.at[(t + 16 - k) % 16], l_ss.at[k], l_rs.at[k])
        return carry

    def loss_end(k, carry):
        loss(k).wait_send()
        return carry

    lax.fori_loop(1, 16, loss_go, 0)

    def add_grad(slots, first=False):
        d = jnp.concatenate([db[slot] for slot in slots], axis=1)
        for core in range(2):
            w = jnp.concatenate([wo[slot, core] for slot in slots], axis=1)
            g = nt_dot(d, w)
            g_acc[core] = g if first else g_acc[core] + g

    dg.near_relay()
    dg.opp_half(0)
    dg.near_rest()
    before_end()
    add_grad([mine] + dg.near, True)
    dg.opp_half(1)
    dg.onear_a()
    dg.far_step()
    add_grad([dg.opp, dg.far[0]])
    dg.onear_b()
    dg.onear_rest()
    add_grad(dg.onear)
    lax.fori_loop(1, 16, loss_got, 0)
    loss_sum = l_r[0]
    for i in range(1, 16):
        loss_sum = loss_sum + l_r[i]
    out_l[...] = loss_sum / DS
    dg.ofar_step()
    add_grad([dg.far[1]])
    send(g_acc.at[1 - c], g_in, x_ss.at[7], x_rs.at[7], sib)
    arrive(g_in, x_ss.at[7], x_rs.at[7])
    out_g[...] = (g_acc[c] + g_in[...]).astype(BF16)

    flush()
    lax.fori_loop(1, 16, loss_end, 0)


def reduce_buffers():
    block = (ROWS, COLS)
    return [
        pltpu.VMEM((2, 64, COLS), BF16),
        pltpu.VMEM((2, 64, COLS), BF16),
        pltpu.VMEM((2,) + block, BF16),
        pltpu.VMEM((2,) + block, BF16),
        pltpu.VMEM((2,) + block, BF16),
        pltpu.VMEM((2,) + block, BF16),
        pltpu.VMEM(block, BF16),
        pltpu.VMEM(block, BF16),
        pltpu.VMEM(block, F32),
    ]


def on_device(
    teacher_hidden, teacher_gain, projector, student_hidden, student_gain,
    query_weight, kv_weight, out_weight, doc_ids,
):
    block = (ROWS, COLS)
    hbm = pl.BlockSpec(memory_space=pltpu.HBM)
    vmem = pl.BlockSpec(memory_space=pltpu.VMEM)
    dma = pltpu.SemaphoreType.DMA
    out_s, out_l, out_g = pl.pallas_call(
        body,
        out_shape=(
            jax.ShapeDtypeStruct(block, BF16),
            jax.ShapeDtypeStruct((1, ROWS), F32),
            jax.ShapeDtypeStruct((ROWS, 256), BF16),
        ),
        in_specs=[hbm] * 9,
        out_specs=(vmem, vmem, vmem),
        scratch_shapes=[
            pltpu.VMEM((1, 1024), F32),
            pltpu.VMEM((1, COLS), F32),
            pltpu.VMEM((1, ROWS), jnp.int32),
            pltpu.VMEM((ROWS, 1024), BF16),
            pltpu.VMEM((8, ROWS, 1024), BF16),
            pltpu.VMEM((2, 1024, COLS), BF16),
            pltpu.VMEM((8, 2, COLS, 256), BF16),
            pltpu.VMEM((8, 2, 2, 32, COLS), BF16),
            pltpu.VMEM((8, 2, 256, COLS), BF16),
            pltpu.VMEM((64, ROWS), F32),
            pltpu.VMEM((64, ROWS), F32),
            pltpu.VMEM((8,) + block, BF16),
            pltpu.VMEM((1, 768), F32),
            pltpu.VMEM((8, 1, 768), F32),
            pltpu.VMEM((1, 256), F32),
            pltpu.VMEM((1, 256), F32),
            pltpu.VMEM((ROWS, 128), F32),
            pltpu.VMEM((2, ROWS, 256), F32),
            pltpu.VMEM((ROWS, 256), F32),
            pltpu.VMEM((2, 64, ROWS), F32),
            pltpu.VMEM((64, ROWS), F32),
            pltpu.VMEM((4, 16, ROWS), BF16),
            pltpu.VMEM((16, 16, ROWS), BF16),
            pltpu.VMEM((2, ROWS, HEAD_DIM), BF16),
            pltpu.VMEM((2, BACK + 1, ROWS, HEAD_DIM), BF16),
            pltpu.VMEM((8, 1, ROWS), jnp.int32),
            pltpu.VMEM((8, 1, ROWS), jnp.int32),
            pltpu.VMEM((2, ROWS, HEAD_DIM), BF16),
            pltpu.VMEM((4, ROWS, HEAD_DIM), BF16),
            pltpu.VMEM((ROWS, (BACK + 1) * ROWS), F32),
            pltpu.VMEM((8,) + block, F32),
            pltpu.VMEM((4,) + block, F32),
            pltpu.VMEM((8,) + block, F32),
            pltpu.VMEM((2,) + block, BF16),
            pltpu.VMEM((8,) + block, BF16),
            pltpu.VMEM((8,) + block, BF16),
            pltpu.VMEM((2,) + block, BF16),
            *reduce_buffers()[:6],
            *reduce_buffers(),
            pltpu.VMEM((2,) + block, BF16),
            pltpu.VMEM((2,) + block, BF16),
            pltpu.VMEM((ROWS, 128), F32),
            pltpu.VMEM((8,) + block, BF16),
            pltpu.VMEM((2, ROWS, 256), F32),
            pltpu.VMEM((ROWS, 256), F32),
            pltpu.VMEM((ROWS, 128), F32),
            pltpu.VMEM((1, ROWS), F32),
            pltpu.VMEM((16, 1, ROWS), F32),
            dma((10,)),
            *[dma((8,)) for _ in range(10)],
            dma((16,)), dma((16,)), dma((8,)), dma((8,)),
            dma((24,)), dma((24,)), dma((24,)), dma((24,)),
            dma((16,)), dma((16,)), dma((16,)), dma((16,)),
            dma((9,)), dma((9,)), dma((9,)), dma((9,)), dma((9,)), dma((9,)),
            dma((24,)), dma((24,)), dma((24,)), dma((24,)),
            dma((4,)), dma((4,)),
            dma((16,)), dma((16,)),
        ],
        compiler_params=pltpu.CompilerParams(
            collective_id=0, has_side_effects=True, vmem_limit_bytes=40 * 1024 * 1024
        ),
    )(
        *(
            pltpu.with_memory_space_constraint(one, pltpu.HBM)
            for one in (
                teacher_hidden, teacher_gain.reshape(1, -1), projector, student_hidden,
                student_gain.reshape(1, -1), query_weight.reshape(8, 2, COLS, 256), jnp.transpose(kv_weight, (0, 2, 1)),
                out_weight, doc_ids.reshape(1, -1),
            )
        )
    )
    return out_s, out_l.reshape(ROWS), out_g


def solution(mesh):
    in_specs = (
        P("seq", "tensor"),
        P("tensor"),
        P("tensor", "seq"),
        P("seq", "tensor"),
        P("tensor"),
        P(None, "tensor"),
        P(None, None, "tensor"),
        P("tensor", None),
        P("seq"),
    )
    out_specs = (P("seq", "tensor"), P("seq"), P("seq", "tensor"))
    return jax.shard_map(
        on_device, mesh=mesh, in_specs=in_specs, out_specs=out_specs, check_vma=False
    )
```

```python
import math

import jax
import jax.numpy as jnp
from jax import lax
from jax.experimental import pallas as pl
from jax.experimental.pallas import tpu as pltpu
from jax.sharding import PartitionSpec as P

DT = 16384
DS = 8192
HEAD_DIM = 128
HEADS = 32
KV_HEADS = 4
ROWS = 128
COLS = 512
BACK = 8
F32 = jnp.float32
BF16 = jnp.bfloat16
MESH = pl.DeviceIdType.MESH
NT = (((1,), (1,)), ((), ()))


def nt_dot(a, b):
    return lax.dot_general(a, b, NT, preferred_element_type=F32)


def body(
    th_h, tgain_h, pj_h, sh_h, sgain_h, wq_h, wkv_h, wo_h, docs_h,
    out_s, out_l, out_g,
    tgain, sgain, docs, th_v, tg, pj, wq, wkv, wo, cos_t, sin_t,
    hb, sg_s, sg_r, sum_s, sum_r, scale_v, hn, q_acc, kv_acc, kv_in,
    kvx_s, kvx_r, kv_own, kv_r, docs_z, docs_o, q_v, attn_v, bias,
    t_own, t_part, o_own, o_x2, t_sib_s, t_sib_r, t_x2, t_ra, t_rb, t_xp, t_xm, t_fm, t_fp,
    o_ra, o_rb, o_xp, o_xm, o_fm, o_fp, o_ys, o_yr, o_fin,
    t3_s, t3_r, ts_v, db, g_acc, g_in, l_v, l_s, l_r,
    load_sem, w_load, w_ss, w_rs, v_load, v_ss, v_rs, x_ss, x_rs, z_ss, z_rs, p_ss, p_rs,
    ag_ss, ag_rs, dg_ss, dg_rs, sm_ss, sm_rs, kx_ss, kx_rs, kv_ss, kv_rs, kf_ss, kf_rs, dc_ss, dc_rs,
    t_ss, t_rs, o_ss, o_rs, t3_ss, t3_rs, l_ss, l_rs,
):
    s = lax.axis_index("seq")
    t = lax.axis_index("tensor")
    yl, z = s // 8, s % 8
    yh, x, c = t // 8, (t // 2) % 4, t % 2

    def tid(y_, x_, c_):
        return y_ * 8 + x_ * 2 + c_

    xp_, xm_ = (x + 1) % 4, (x + 3) % 4
    xf_ = (x + 2) % 4
    yo_ = 1 - yh
    sib = (s, tid(yh, x, 1 - c))
    dev_xp = (s, tid(yh, xp_, c))
    dev_xm = (s, tid(yh, xm_, c))
    dev_yo = (s, tid(yo_, x, c))
    dev_zp = (yl * 8 + (z + 1) % 8, t)
    dev_zm = (yl * 8 + (z + 7) % 8, t)
    dev_yl = ((1 - yl) * 8 + z, t)
    turn = jnp.where(c == 0, x, jnp.where(x == 0, 4, 8 - x))
    stays = (z == 0) & (x == 0) & (c == 0)

    started = []

    def copy(src, dst, ss, rs, dev):
        return pltpu.make_async_remote_copy(
            src_ref=src, dst_ref=dst, send_sem=ss, recv_sem=rs, device_id=dev, device_id_type=MESH
        )

    def send(src, dst, ss, rs, dev):
        one = copy(src, dst, ss, rs, dev)
        one.start()
        started.append(one)

    def flush():
        for one in started:
            one.wait_send()
        started.clear()

    def arrive(dst, ss, rs):
        copy(dst, dst, ss, rs, sib).wait_recv()

    def load(src, dst, k):
        one = pltpu.make_async_copy(src, dst, load_sem.at[k])
        one.start()
        return one

    l_th = load(th_h, th_v, 0)
    mine = yh * 4 + x
    l_sh = load(sh_h, hb.at[mine], 1)
    l_small = [load(tgain_h, tgain, 7), load(sgain_h, sgain, 8), load(docs_h, docs, 9)]

    def wkv_part(j, core):
        return wkv_h.at[:, :, pl.ds(pl.multiple_of((j * 2 + core) * COLS, COLS), COLS)]

    def wkv_load(j):
        return pltpu.make_async_copy(wkv_part(j, c), wkv.at[j, c], v_load.at[j])

    def wkv_go(j, carry):
        wkv_load(j).start()
        return carry

    def wo_part(j, core):
        return wo_h.at[:, pl.ds(pl.multiple_of((j * 2 + core) * COLS, COLS), COLS)]

    def wo_load(j):
        return pltpu.make_async_copy(wo_part(j, c), wo.at[j, c], w_load.at[j])

    def wo_send(j):
        return copy(wo_part(j, 1 - c), wo.at[j, c], w_ss.at[j], w_rs.at[j], sib)

    def wo_fetch(j, carry):
        wo_load(j).start()
        return carry

    def wo_go(j, carry):
        wo_send(j).start()
        return carry

    def wo_got(j, carry):
        wo_load(j).wait()
        arrive(wo.at[j, 1 - c], w_ss.at[j], w_rs.at[j])
        return carry

    def wo_end(j, carry):
        wo_send(j).wait_send()
        return carry

    lax.fori_loop(0, 8, wkv_go, 0)

    kv_r[...] = jnp.zeros(kv_r.shape, BF16)

    barrier = pltpu.get_barrier_semaphore()
    for dev in (sib, dev_xp, dev_xm, dev_yo, dev_zp, dev_zm, dev_yl):
        pl.semaphore_signal(barrier, inc=1, device_id=dev, device_id_type=MESH)

    class Gather:
        def __init__(self, buf, ss, rs):
            self.buf, self.ss, self.rs = buf, ss, rs
            self.near = [yh * 4 + xm_, yh * 4 + xp_]
            self.opp = yo_ * 4 + x
            self.onear = [yo_ * 4 + xm_, yo_ * 4 + xp_]
            self.far = [yh * 4 + xf_, yo_ * 4 + xf_]
            self.order = [mine] + self.near + [self.opp] + self.onear + self.far

        def part(self, slot, h):
            return self.buf.at[slot, pl.ds(h * 64, 64)]

        def half(self, slot, h, k, dev):
            part = self.part(slot, h)
            send(part, part, self.ss.at[k], self.rs.at[k], dev)

        def got_half(self, slot, h, k):
            arrive(self.part(slot, h), self.ss.at[k], self.rs.at[k])

        def begin(self, h):
            self.half(mine, h, 0 + h, dev_yo)
            self.half(mine, h, 2 + h, dev_xp)
            self.half(mine, h, 4 + h, dev_xm)

        def near_relay(self):
            self.got_half(self.near[0], 0, 2)
            self.half(self.near[0], 0, 6, dev_xp)
            self.got_half(self.near[1], 1, 5)
            self.half(self.near[1], 1, 7, dev_xm)

        def near_rest(self):
            self.got_half(self.near[0], 1, 3)
            self.got_half(self.near[1], 0, 4)

        def opp_half(self, h):
            self.got_half(self.opp, h, 0 + h)
            self.half(self.opp, h, 8 + h, dev_xp)
            self.half(self.opp, h, 10 + h, dev_xm)

        def onear_a(self):
            self.got_half(self.onear[0], 0, 8)
            self.half(self.onear[0], 0, 12, dev_xp)

        def onear_b(self):
            self.got_half(self.onear[1], 1, 11)
            self.half(self.onear[1], 1, 13, dev_xm)

        def onear_rest(self):
            self.got_half(self.onear[0], 1, 9)
            self.got_half(self.onear[1], 0, 10)

        def far_step(self):
            self.got_half(self.far[0], 0, 6)
            self.got_half(self.far[0], 1, 7)

        def ofar_step(self):
            self.got_half(self.far[1], 0, 12)
            self.got_half(self.far[1], 1, 13)

    def pj_send(k):
        rows = pl.ds(k * 256, 256)
        send(pj_h.at[rows], pj.at[yl, rows], p_ss.at[k], p_rs.at[k], dev_yl)

    def wkv_send(j):
        return copy(wkv_part(j, 1 - c), wkv.at[j, c], v_ss.at[j], v_rs.at[j], sib)

    def w_go(j, carry):
        wkv_send(j).start()
        return carry

    def w_end(j, carry):
        wkv_send(j).wait_send()
        return carry

    def w_got(slot):
        wkv_load(slot).wait()
        arrive(wkv.at[slot, 1 - c], v_ss.at[slot], v_rs.at[slot])

    ag = Gather(hb, ag_ss, ag_rs)
    l_sh.wait()

    z_slot = 0
    l_th.wait()
    for one in l_small:
        one.wait()
    docs_z[z] = docs[...]
    part = jnp.zeros((ROWS, 128), F32)
    for i in range(8):
        cols = slice(i * 128, (i + 1) * 128)
        f = th_v[:, cols].astype(F32)
        part = part + f * f
        tg[z_slot, :, cols] = (f * tgain[:, cols]).astype(BF16)
    sg_s[:, COLS:COLS + 128] = jnp.sum(part.T, axis=0, keepdims=True)
    part = jnp.zeros((ROWS, 128), F32)
    for i in range(4):
        f = hb[mine, :, i * 128:(i + 1) * 128].astype(F32)
        part = part + f * f
    sg_s[:, COLS + 128:COLS + 256] = jnp.sum(part.T, axis=0, keepdims=True)
    sg_s[:, 0:COLS] = sgain[...]
    sg_r[mine] = sg_s[...]

    def ring_slot(d):
        return (0, 1, 2, 3, 4, 7, 6, 5)[d % 8]

    def z_ref(d, h):
        return tg.at[ring_slot(d), pl.ds(h * 64, 64)]

    def z_send(k):
        d = k // 2
        send(z_ref(8 - d, k % 2), z_ref(7 - d, k % 2), z_ss.at[k], z_rs.at[k], dev_zp)
        send(z_ref(d, 1 - k % 2), z_ref(d + 1, 1 - k % 2), z_ss.at[8 + k], z_rs.at[8 + k], dev_zm)

    def z_got(k):
        up, down = z_ref(-(k // 2) + 7, k % 2), z_ref(k // 2 + 1, 1 - k % 2)
        arrive(up, z_ss.at[k], z_rs.at[k])
        arrive(down, z_ss.at[8 + k], z_rs.at[8 + k])

    def z_step(k):
        z_got(k)
        if k + 2 < 7:
            z_send(k + 2)

    def small_send(i, k, dev):
        slot = ag.order[i]
        send(sg_r.at[slot], sg_r.at[slot], sm_ss.at[k], sm_rs.at[k], dev)

    def small_got(i, k):
        arrive(sg_r.at[ag.order[i]], sm_ss.at[k], sm_rs.at[k])

    def docs_send(d, k, dev):
        ref = docs_z.at[(z + d) % 8]
        send(ref, ref, dc_ss.at[k], dc_rs.at[k], dev)

    def docs_step(k):
        arrive(docs_z.at[(z + 7 - k) % 8], dc_ss.at[k], dc_rs.at[k])
        if k < 3:
            arrive(docs_z.at[(z + 1 + k) % 8], dc_ss.at[4 + k], dc_rs.at[4 + k])
            docs_send(7 - k, k + 1, dev_zp)
            if k < 2:
                docs_send(1 + k, k + 5, dev_zm)
        else:
            send(docs_z, docs_o, dc_ss.at[8], dc_rs.at[8], dev_yl)

    pl.semaphore_wait(barrier, 7)
    small_send(0, 0, dev_yo)
    small_send(0, 1, dev_xp)
    small_send(0, 2, dev_xm)
    ag.begin(0)
    ag.begin(1)
    docs_send(0, 0, dev_zp)
    docs_send(0, 4, dev_zm)
    z_send(0)
    pj_send(0)
    z_send(1)
    lax.fori_loop(0, 8, w_go, 0)
    pj_send(1)
    pj_send(2)
    l_pj = load(pj_h, pj.at[yl], 4)
    l_wq = load(wq_h, wq, 3)

    entry = lax.broadcasted_iota(jnp.int32, (64, ROWS), 0).astype(F32)
    position = (s * ROWS + lax.broadcasted_iota(jnp.int32, (64, ROWS), 1)).astype(F32)
    angle = position * jnp.exp(-math.log(500000.0) * (2.0 * entry / HEAD_DIM))
    cos_t[...] = jnp.cos(angle)
    sin_t[...] = jnp.sin(angle)

    def process(slots, first=False):
        blocks, w = [], []
        for slot in slots:
            parts = []
            for i in range(4):
                cols = slice(i * 128, (i + 1) * 128)
                f = hb[slot, :, cols].astype(F32)
                parts.append((f * scale_v[...] * sg_r[slot][:, cols]).astype(BF16))
            blocks.append(jnp.concatenate(parts, axis=1))
        n = jnp.concatenate(blocks, axis=1)
        for slot in slots:
            w_got(slot)
            w.append(wkv[slot].reshape(128, COLS))
        for slot, block in zip(slots, blocks):
            hn[c, slot] = block
        kv = nt_dot(jnp.concatenate(w, axis=1), n)
        for core in range(2):
            k = kv[core * 64:core * 64 + 64]
            kv_acc[core] = k if first else kv_acc[core] + k

    def queries(core):
        n = jnp.concatenate([hn[core, j] for j in range(8)], axis=1)
        w = jnp.concatenate([wq[j, core] for j in range(8)], axis=0)
        return jnp.dot(n, w, preferred_element_type=F32)

    small_got(1, 1)
    small_send(1, 3, dev_xp)
    small_got(2, 2)
    small_got(3, 0)
    small_send(3, 4, dev_xp)
    small_send(3, 5, dev_xm)
    docs_step(0)
    ag.near_relay()
    small_got(6, 3)
    docs_step(1)
    small_got(4, 4)
    small_send(4, 6, dev_xp)
    small_got(5, 5)
    ag.near_rest()
    ag.opp_half(0)
    z_step(0)
    pj_send(3)
    small_got(7, 6)
    sums = sg_r[0][:, COLS:COLS + 256]
    for i in range(1, 8):
        sums = sums + sg_r[i][:, COLS:COLS + 256]
    sum_s[...] = sums
    send(sum_s, sum_r, x_ss.at[2], x_rs.at[2], sib)
    docs_step(2)
    ag.opp_half(1)
    arrive(sum_r, x_ss.at[2], x_rs.at[2])
    sums = sum_s[...] + sum_r[...]
    ts_v[...] = jnp.broadcast_to(lax.rsqrt(sums[:, 0:128] / DT + 1e-05), (ROWS, 128)).T
    scale_v[...] = jnp.broadcast_to(lax.rsqrt(sums[:, 128:256] / DS + 1e-05), (ROWS, 128)).T
    docs_step(3)
    z_step(1)
    ag.onear_a()
    process([mine] + ag.near, True)
    ag.onear_b()
    z_step(2)
    ag.far_step()
    process([ag.opp, ag.far[0]])
    ag.onear_rest()
    process(ag.onear)
    z_step(3)
    ag.ofar_step()
    process([ag.far[1]])
    send(kv_acc.at[1 - c], kv_in, x_ss.at[3], x_rs.at[3], sib)
    arrive(kv_in, x_ss.at[3], x_rs.at[3])

    row = lax.broadcasted_iota(jnp.int32, (64, 64), 0)
    col = lax.broadcasted_iota(jnp.int32, (64, 64), 1)
    take = ((row >> 3) & 1) * 32 + (row & 7) * 4 + (row >> 4)
    pick = jnp.where(col == take, 1.0, 0.0).astype(BF16)
    kv_mine = (kv_acc[c] + kv_in[...]).astype(BF16)
    kvx_s[...] = jnp.dot(pick, kv_mine, preferred_element_type=F32).astype(BF16).reshape(4, 16, 128)
    kvx_r[t] = kvx_s[t // 4]

    def kvx(k):
        to = (t + k) % 16
        return copy(kvx_s.at[to // 4], kvx_r.at[t], kx_ss.at[k], kx_rs.at[k], (s, to))

    def kvx_go(k, carry):
        kvx(k).start()
        return carry

    def kvx_got(k, carry):
        arrive(kvx_r.at[(t + 16 - k) % 16], kx_ss.at[k], kx_rs.at[k])
        return carry

    def kvx_end(k, carry):
        kvx(k).wait_send()
        return carry

    lax.fori_loop(1, 16, kvx_go, 0)
    send(hn.at[c], hn.at[c], x_ss.at[4], x_rs.at[4], sib)
    lax.fori_loop(0, 8, wo_fetch, 0)
    lax.fori_loop(0, 8, wo_go, 0)
    z_step(4)

    l_wq.wait()
    q_acc[...] = queries(c)
    lax.fori_loop(1, 16, kvx_got, 0)
    both = kvx_r[...].astype(F32).reshape(16, 2, 8, ROWS)
    k_raw = both[:, 0].reshape(HEAD_DIM, ROWS)
    v_raw = both[:, 1].reshape(HEAD_DIM, ROWS)
    first, second = k_raw[0:64], k_raw[64:128]
    k_rot = jnp.concatenate(
        [first * cos_t[...] - second * sin_t[...], second * cos_t[...] + first * sin_t[...]], axis=0
    )
    kv_own[0] = k_rot.astype(BF16)
    kv_own[1] = v_raw.T.astype(BF16)
    kv_r[0, 0] = kv_own[0]
    kv_r[1, 0] = kv_own[1]

    def kv_copy(k):
        return copy(kv_own.at[c], kv_r.at[c, k], kv_ss.at[k], kv_rs.at[k], ((s + k) % 16, t))

    def kv_fwd(k):
        return copy(kv_r.at[c, k], kv_r.at[c, k], kf_ss.at[k], kf_rs.at[k], sib)

    def kv_go(k):
        @pl.when(s + k < 16)
        def _():
            kv_copy(k).start()

    def kv_mid(k):
        @pl.when(s >= k)
        def _():
            arrive(kv_r.at[c, k], kv_ss.at[k], kv_rs.at[k])
            kv_fwd(k).start()

    def kv_got(k, carry):
        @pl.when(s >= k)
        def _():
            arrive(kv_r.at[1 - c, k], kf_ss.at[k], kf_rs.at[k])
        return carry

    def kv_end(k, carry):
        @pl.when(s >= k)
        def _():
            kv_fwd(k).wait_send()

        @pl.when(s + k < 16)
        def _():
            kv_copy(k).wait_send()
        return carry

    arrive(docs_o, dc_ss.at[8], dc_rs.at[8])
    for k in range(1, BACK + 1):
        kv_go(k)

    cos2 = jnp.concatenate([cos_t[...], cos_t[...]], axis=0).T
    sin2 = jnp.concatenate([-sin_t[...], sin_t[...]], axis=0).T
    arrive(hn.at[1 - c], x_ss.at[4], x_rs.at[4])
    q_mine = q_acc[...] + queries(1 - c)
    for h in range(2):
        qh = q_mine[:, h * 128:(h + 1) * 128]
        turned = qh * cos2 + pltpu.roll(qh, 64, 1) * sin2
        q_v[h] = (turned * HEAD_DIM ** (-0.5)).astype(BF16)

    def docs_back(j):
        at = (z + 8 - j) % 8
        return jnp.where(z >= j, docs_z[at], jnp.where(yl == 1, docs_o[at], -1))

    key_doc = jnp.concatenate([docs_back(j) for j in range(BACK + 1)], axis=1)
    row_doc = jnp.broadcast_to(docs[...].astype(F32), (ROWS, ROWS)).T[:, 0:1].astype(jnp.int32)
    wide = (ROWS, (BACK + 1) * ROWS)
    row_at = lax.broadcasted_iota(jnp.int32, wide, 0)
    key_at = lax.broadcasted_iota(jnp.int32, wide, 1)
    allowed = (key_doc == row_doc) & ((key_at >= ROWS) | (key_at <= row_at))
    bias[...] = jnp.where(allowed, 0.0, -1e30)

    class Reduce:
        def __init__(self, y_order, own, sib_s, sib_r, x2, ra, rb, xp, xm, fm, fp, ys, yr, fin, ss, rs):
            self.own, self.sib_s, self.sib_r = own, sib_s, sib_r
            self.x2, self.ra, self.rb, self.xp, self.xm, self.fm, self.fp = x2, ra, rb, xp, xm, fm, fp
            self.ys, self.yr, self.fin, self.ss, self.rs = ys, yr, fin, ss, rs
            self.y_order = y_order
            self.x_order = (xf_, xp_, xm_, x)

        def go(self, src, dst, k, dev):
            send(src, dst, self.ss.at[k], self.rs.at[k], dev)

        def got(self, dst, k):
            arrive(dst, self.ss.at[k], self.rs.at[k])

        def slot(self, k, i):
            return self.y_order[i] * 4 + self.x_order[k]

        def to_sib(self, k, i):
            slot = self.slot(k, i)
            self.go(self.sib_s.at[slot], self.sib_r.at[slot], k * 2 + i, sib)

        def sib_got(self, k, i):
            if self.sib_r is not None:
                self.got(self.sib_r.at[self.slot(k, i)], k * 2 + i)

        def pair(self, k, i, h):
            slot, rows = self.slot(k, i), slice(h * 64, h * 64 + 64)
            value = self.own[slot, rows]
            return value if self.sib_r is None else value + self.sib_r[slot, rows].astype(F32)

        def far(self, i):
            self.sib_got(0, i)
            self.x2[i, 0:64] = self.pair(0, i, 0).astype(BF16)
            self.go(self.x2.at[i, pl.ds(0, 64)], self.ra.at[i], 8 + i, dev_xp)
            self.x2[i, 64:128] = self.pair(0, i, 1).astype(BF16)
            self.go(self.x2.at[i, pl.ds(64, 64)], self.rb.at[i], 10 + i, dev_xm)

        def near(self, i):
            self.sib_got(1, i)
            self.xp[i, 64:128] = self.pair(1, i, 1).astype(BF16)
            self.go(self.xp.at[i, pl.ds(64, 64)], self.fm.at[i, pl.ds(64, 64)], 12 + i, dev_xp)
            self.sib_got(2, i)
            self.xm[i, 0:64] = self.pair(2, i, 0).astype(BF16)
            self.go(self.xm.at[i, pl.ds(0, 64)], self.fp.at[i, pl.ds(0, 64)], 14 + i, dev_xm)

        def relay(self, i):
            self.got(self.ra.at[i], 8 + i)
            self.xp[i, 0:64] = (self.pair(1, i, 0) + self.ra[i].astype(F32)).astype(BF16)
            self.go(self.xp.at[i, pl.ds(0, 64)], self.fm.at[i, pl.ds(0, 64)], 16 + i, dev_xp)
            self.got(self.rb.at[i], 10 + i)
            self.xm[i, 64:128] = (self.pair(2, i, 1) + self.rb[i].astype(F32)).astype(BF16)
            self.go(self.xm.at[i, pl.ds(64, 64)], self.fp.at[i, pl.ds(64, 64)], 18 + i, dev_xm)

        def join(self, i, h):
            rows, at = slice(h * 64, h * 64 + 64), pl.ds(h * 64, 64)
            if h == 0:
                self.sib_got(3, i)
            self.got(self.fm.at[i, at], (16, 12)[h] + i)
            self.got(self.fp.at[i, at], (14, 18)[h] + i)
            return self.pair(3, i, h) + self.fm[i, rows].astype(F32) + self.fp[i, rows].astype(F32)

        def to_opp(self, h):
            at = pl.ds(h * 64, 64)
            return copy(self.ys.at[at], self.yr.at[at], self.ss.at[20 + h], self.rs.at[20 + h], dev_yo)

        def join_other(self):
            for h in range(2):
                self.ys[h * 64:h * 64 + 64] = self.join(0, h).astype(BF16)
                self.to_opp(h).start()

        def join_mine(self):
            for h in range(2):
                self.fin[h * 64:h * 64 + 64] = self.join(1, h)

        def end(self):
            for h in range(2):
                self.to_opp(h).wait_send()

        def last(self, h):
            rows = slice(h * 64, h * 64 + 64)
            self.got(self.yr.at[pl.ds(h * 64, 64)], 20 + h)
            return self.fin[rows] + self.yr[rows].astype(F32)

    rt = Reduce((yl, 1 - yl), t_own, t_sib_s, t_sib_r, t_x2, t_ra, t_rb, t_xp, t_xm, t_fm, t_fp, None, None, None, t_ss, t_rs)

    def t3(i, h):
        at = pl.ds(h * 64, 64)
        dev = (yl * 8 + (z + turn) % 8, rt.y_order[i] * 8 + z)
        return copy(t3_s.at[i, at], t3_r.at[yh, at], t3_ss.at[i * 2 + h], t3_rs.at[yh * 2 + h], dev)

    def t3_stays(i):
        return stays & (rt.y_order[i] == yh)

    def t_place(i):
        for h in range(2):
            rows = slice(h * 64, h * 64 + 64)
            t3_s[i, rows] = rt.join(i, h).astype(BF16)

            @pl.when(t3_stays(i))
            def _():
                t3_r[yh, rows] = t3_s[i, rows]

            @pl.when(jnp.logical_not(t3_stays(i)))
            def _():
                t3(i, h).start()

    z_step(5)
    z_step(6)

    def products(core, y_, k, width):
        rows = tg[pl.ds(core * 4, 4), :, k * width:(k + 1) * width].reshape(4 * ROWS, width)
        return jnp.dot(rows, pj[y_, k * width:(k + 1) * width], preferred_element_type=F32).reshape(4, ROWS, COLS)

    l_pj.wait()
    first = pl.ds(yl * 4, 4)
    t_sib_s[first] = products(1 - c, yl, 0, 1024).astype(BF16)
    for k in range(4):
        rt.to_sib(k, 0)
    t_own[first] = products(c, yl, 0, 1024)
    rt.far(0)
    rt.near(0)

    other = pl.ds((1 - yl) * 4, 4)
    for k in range(4):
        arrive(pj.at[1 - yl, pl.ds(k * 256, 256)], p_ss.at[k], p_rs.at[k])
        theirs = products(1 - c, 1 - yl, k, 256)
        if k == 0:
            t_part[...] = theirs
        elif k < 3:
            t_part[...] += theirs
        else:
            t_sib_s[other] = (t_part[...] + theirs).astype(BF16)
            for j in range(4):
                rt.to_sib(j, 1)
        if k == 0:
            t_own[other] = products(c, 1 - yl, k, 256)
        else:
            t_own[other] += products(c, 1 - yl, k, 256)
        if k == 1:
            rt.relay(0)
    rt.far(1)
    rt.near(1)
    t_place(0)
    for k in range(1, BACK + 1):
        kv_mid(k)
    rt.relay(1)

    lax.fori_loop(1, BACK + 1, kv_got, 0)
    keys = jnp.concatenate([kv_r[0, j] for j in range(BACK + 1)], axis=1)
    values = kv_r[1].reshape((BACK + 1) * ROWS, HEAD_DIM)
    for h in range(2):
        scores = jnp.dot(q_v[h], keys, preferred_element_type=F32)
        scores = scores + bias[...]
        probs = jnp.exp(scores - jnp.max(scores, axis=1, keepdims=True))
        total = jnp.sum(probs, axis=1, keepdims=True)
        acc = jnp.dot(probs.astype(BF16), values, preferred_element_type=F32)
        attn_v[c * 2 + h] = (acc / total).astype(BF16)
        send(attn_v.at[c * 2 + h], attn_v.at[c * 2 + h], x_ss.at[5 + h], x_rs.at[5 + h], sib)
    lax.fori_loop(0, 8, wo_got, 0)

    ro = Reduce((yo_, yh), o_own, None, None, o_x2, o_ra, o_rb, o_xp, o_xm, o_fm, o_fp, o_ys, o_yr, o_fin, o_ss, o_rs)

    for h in range(2):
        arrive(attn_v.at[2 - 2 * c + h], x_ss.at[5 + h], x_rs.at[5 + h])
    attn = jnp.concatenate([attn_v[i] for i in range(4)], axis=1)

    def out_block(k, i):
        slot = ro.slot(k, i)
        o_own[slot] = jnp.dot(attn, wo[slot].reshape(COLS, COLS), preferred_element_type=F32)

    out_block(0, 0)
    ro.far(0)
    out_block(1, 0)
    out_block(2, 0)
    ro.near(0)
    t_place(1)
    out_block(0, 1)
    ro.relay(0)
    ro.far(1)
    out_block(1, 1)
    out_block(2, 1)
    ro.near(1)
    out_block(3, 0)
    out_block(3, 1)
    ro.relay(1)

    ro.join_other()
    ro.join_mine()

    early = list(started)
    started.clear()

    def before_end():
        for one in early:
            one.wait_send()
        lax.fori_loop(0, 8, w_end, 0)
        lax.fori_loop(0, 8, wo_end, 0)
        lax.fori_loop(1, 16, kvx_end, 0)
        lax.fori_loop(1, BACK + 1, kv_end, 0)
        ro.end()
        for i in range(2):

            @pl.when(jnp.logical_not(t3_stays(i)))
            def _():
                t3(i, 0).wait_send()
                t3(i, 1).wait_send()

    dg = Gather(db, dg_ss, dg_rs)
    for h in range(2):
        rows = slice(h * 64, h * 64 + 64)
        mixed = hb[mine, rows].astype(F32) + ro.last(h)
        out_s[rows] = mixed.astype(BF16)

        for p in range(2):

            @pl.when(jnp.logical_not(stays & (yh == p)))
            def _():
                arrive(t3_r.at[p, pl.ds(h * 64, 64)], t3_ss.at[h], t3_rs.at[p * 2 + h])

        target = t3_r[0, rows].astype(F32) + t3_r[1, rows].astype(F32)
        target = target * jnp.concatenate([ts_v[rows]] * 4, axis=1)
        difference = mixed - target
        db[mine, rows] = difference.astype(BF16)
        dg.begin(h)
        squares = difference * difference
        l_v[rows] = (
            squares[:, 0:128] + squares[:, 128:256] + squares[:, 256:384] + squares[:, 384:512]
        )
    l_s[...] = jnp.sum(l_v[...].T, axis=0, keepdims=True)
    l_r[t] = l_s[...]

    def loss(k):
        return copy(l_s, l_r.at[t], l_ss.at[k], l_rs.at[k], (s, (t + k) % 16))

    def loss_go(k, carry):
        loss(k).start()
        return carry

    def loss_got(k, carry):
        arrive(l_r.at[(t + 16 - k) % 16], l_ss.at[k], l_rs.at[k])
        return carry

    def loss_end(k, carry):
        loss(k).wait_send()
        return carry

    lax.fori_loop(1, 16, loss_go, 0)

    def add_grad(slots, first=False):
        d = jnp.concatenate([db[slot] for slot in slots], axis=1)
        for core in range(2):
            w = jnp.concatenate([wo[slot, core] for slot in slots], axis=1)
            g = nt_dot(d, w)
            g_acc[core] = g if first else g_acc[core] + g

    dg.near_relay()
    dg.opp_half(0)
    dg.near_rest()
    before_end()
    add_grad([mine] + dg.near, True)
    dg.opp_half(1)
    dg.onear_a()
    dg.far_step()
    add_grad([dg.opp, dg.far[0]])
    dg.onear_b()
    dg.onear_rest()
    add_grad(dg.onear)
    lax.fori_loop(1, 16, loss_got, 0)
    loss_sum = l_r[0]
    for i in range(1, 16):
        loss_sum = loss_sum + l_r[i]
    out_l[...] = loss_sum / DS
    dg.ofar_step()
    add_grad([dg.far[1]])
    send(g_acc.at[1 - c], g_in, x_ss.at[7], x_rs.at[7], sib)
    arrive(g_in, x_ss.at[7], x_rs.at[7])
    out_g[...] = (g_acc[c] + g_in[...]).astype(BF16)

    flush()
    lax.fori_loop(1, 16, loss_end, 0)


def reduce_buffers():
    block = (ROWS, COLS)
    return [
        pltpu.VMEM((2, 64, COLS), BF16),
        pltpu.VMEM((2, 64, COLS), BF16),
        pltpu.VMEM((2,) + block, BF16),
        pltpu.VMEM((2,) + block, BF16),
        pltpu.VMEM((2,) + block, BF16),
        pltpu.VMEM((2,) + block, BF16),
        pltpu.VMEM(block, BF16),
        pltpu.VMEM(block, BF16),
        pltpu.VMEM(block, F32),
    ]


def on_device(
    teacher_hidden, teacher_gain, projector, student_hidden, student_gain,
    query_weight, kv_weight, out_weight, doc_ids,
):
    block = (ROWS, COLS)
    hbm = pl.BlockSpec(memory_space=pltpu.HBM)
    vmem = pl.BlockSpec(memory_space=pltpu.VMEM)
    dma = pltpu.SemaphoreType.DMA
    out_s, out_l, out_g = pl.pallas_call(
        body,
        out_shape=(
            jax.ShapeDtypeStruct(block, BF16),
            jax.ShapeDtypeStruct((1, ROWS), F32),
            jax.ShapeDtypeStruct((ROWS, 256), BF16),
        ),
        in_specs=[hbm] * 9,
        out_specs=(vmem, vmem, vmem),
        scratch_shapes=[
            pltpu.VMEM((1, 1024), F32),
            pltpu.VMEM((1, COLS), F32),
            pltpu.VMEM((1, ROWS), jnp.int32),
            pltpu.VMEM((ROWS, 1024), BF16),
            pltpu.VMEM((8, ROWS, 1024), BF16),
            pltpu.VMEM((2, 1024, COLS), BF16),
            pltpu.VMEM((8, 2, COLS, 256), BF16),
            pltpu.VMEM((8, 2, 2, 32, COLS), BF16),
            pltpu.VMEM((8, 2, 256, COLS), BF16),
            pltpu.VMEM((64, ROWS), F32),
            pltpu.VMEM((64, ROWS), F32),
            pltpu.VMEM((8,) + block, BF16),
            pltpu.VMEM((1, 768), F32),
            pltpu.VMEM((8, 1, 768), F32),
            pltpu.VMEM((1, 256), F32),
            pltpu.VMEM((1, 256), F32),
            pltpu.VMEM((ROWS, 128), F32),
            pltpu.VMEM((2, 8) + block, BF16),
            pltpu.VMEM((ROWS, 256), F32),
            pltpu.VMEM((2, 64, ROWS), F32),
            pltpu.VMEM((64, ROWS), F32),
            pltpu.VMEM((4, 16, ROWS), BF16),
            pltpu.VMEM((16, 16, ROWS), BF16),
            pltpu.VMEM((2, ROWS, HEAD_DIM), BF16),
            pltpu.VMEM((2, BACK + 1, ROWS, HEAD_DIM), BF16),
            pltpu.VMEM((8, 1, ROWS), jnp.int32),
            pltpu.VMEM((8, 1, ROWS), jnp.int32),
            pltpu.VMEM((2, ROWS, HEAD_DIM), BF16),
            pltpu.VMEM((4, ROWS, HEAD_DIM), BF16),
            pltpu.VMEM((ROWS, (BACK + 1) * ROWS), F32),
            pltpu.VMEM((8,) + block, F32),
            pltpu.VMEM((4,) + block, F32),
            pltpu.VMEM((8,) + block, F32),
            pltpu.VMEM((2,) + block, BF16),
            pltpu.VMEM((8,) + block, BF16),
            pltpu.VMEM((8,) + block, BF16),
            pltpu.VMEM((2,) + block, BF16),
            *reduce_buffers()[:6],
            *reduce_buffers(),
            pltpu.VMEM((2,) + block, BF16),
            pltpu.VMEM((2,) + block, BF16),
            pltpu.VMEM((ROWS, 128), F32),
            pltpu.VMEM((8,) + block, BF16),
            pltpu.VMEM((2, ROWS, 256), F32),
            pltpu.VMEM((ROWS, 256), F32),
            pltpu.VMEM((ROWS, 128), F32),
            pltpu.VMEM((1, ROWS), F32),
            pltpu.VMEM((16, 1, ROWS), F32),
            dma((10,)),
            *[dma((8,)) for _ in range(8)],
            dma((16,)), dma((16,)), dma((8,)), dma((8,)),
            dma((24,)), dma((24,)), dma((24,)), dma((24,)),
            dma((16,)), dma((16,)), dma((16,)), dma((16,)),
            dma((9,)), dma((9,)), dma((9,)), dma((9,)), dma((9,)), dma((9,)),
            dma((24,)), dma((24,)), dma((24,)), dma((24,)),
            dma((4,)), dma((4,)),
            dma((16,)), dma((16,)),
        ],
        compiler_params=pltpu.CompilerParams(
            collective_id=0, has_side_effects=True, vmem_limit_bytes=40 * 1024 * 1024
        ),
    )(
        *(
            pltpu.with_memory_space_constraint(one, pltpu.HBM)
            for one in (
                teacher_hidden, teacher_gain.reshape(1, -1), projector, student_hidden,
                student_gain.reshape(1, -1), query_weight.reshape(8, 2, COLS, 256), jnp.transpose(kv_weight, (0, 2, 1)),
                out_weight, doc_ids.reshape(1, -1),
            )
        )
    )
    return out_s, out_l.reshape(ROWS), out_g


def solution(mesh):
    in_specs = (
        P("seq", "tensor"),
        P("tensor"),
        P("tensor", "seq"),
        P("seq", "tensor"),
        P("tensor"),
        P(None, "tensor"),
        P(None, None, "tensor"),
        P("tensor", None),
        P("seq"),
    )
    out_specs = (P("seq", "tensor"), P("seq"), P("seq", "tensor"))
    return jax.shard_map(
        on_device, mesh=mesh, in_specs=in_specs, out_specs=out_specs, check_vma=False
    )
```

```python
import math

import jax
import jax.numpy as jnp
from jax import lax
from jax.experimental import pallas as pl
from jax.experimental.pallas import tpu as pltpu
from jax.sharding import PartitionSpec as P

DT = 16384
DS = 8192
HEAD_DIM = 128
HEADS = 32
KV_HEADS = 4
ROWS = 128
COLS = 512
BACK = 8
F32 = jnp.float32
BF16 = jnp.bfloat16
MESH = pl.DeviceIdType.MESH
NT = (((1,), (1,)), ((), ()))


def nt_dot(a, b):
    return lax.dot_general(a, b, NT, preferred_element_type=F32)


def body(
    th_h, tgain_h, pj_h, sh_h, sgain_h, wq_h, wkv_h, wo_h, docs_h,
    out_s, out_l, out_g,
    tgain, sgain, docs, th_v, tg, pj, wq, wkv, wo, cos_t, sin_t,
    hb, sg_s, sg_r, sum_s, sum_r, scale_v, q_acc, q_in, kv_acc, kv_in,
    kvx_s, kvx_r, kv_own, kv_r, docs_z, docs_o, q_v, attn_v, bias,
    t_own, t_part, o_own, o_x2, t_sib_s, t_sib_r, t_x2, t_ra, t_rb, t_xp, t_xm, t_fm, t_fp,
    o_ra, o_rb, o_xp, o_xm, o_fm, o_fp, o_ys, o_yr, o_fin,
    t3_s, t3_r, ts_v, db, g_acc, g_in, l_v, l_s, l_r,
    load_sem, w_load, w_ss, w_rs, v_load, v_ss, v_rs, u_ss, u_rs, x_ss, x_rs, z_ss, z_rs, p_ss, p_rs,
    ag_ss, ag_rs, dg_ss, dg_rs, sm_ss, sm_rs, kx_ss, kx_rs, kv_ss, kv_rs, kf_ss, kf_rs, dc_ss, dc_rs,
    t_ss, t_rs, o_ss, o_rs, t3_ss, t3_rs, l_ss, l_rs,
):
    s = lax.axis_index("seq")
    t = lax.axis_index("tensor")
    yl, z = s // 8, s % 8
    yh, x, c = t // 8, (t // 2) % 4, t % 2

    def tid(y_, x_, c_):
        return y_ * 8 + x_ * 2 + c_

    xp_, xm_ = (x + 1) % 4, (x + 3) % 4
    xf_ = (x + 2) % 4
    yo_ = 1 - yh
    sib = (s, tid(yh, x, 1 - c))
    dev_xp = (s, tid(yh, xp_, c))
    dev_xm = (s, tid(yh, xm_, c))
    dev_yo = (s, tid(yo_, x, c))
    dev_zp = (yl * 8 + (z + 1) % 8, t)
    dev_zm = (yl * 8 + (z + 7) % 8, t)
    dev_yl = ((1 - yl) * 8 + z, t)
    turn = jnp.where(c == 0, x, jnp.where(x == 0, 4, 8 - x))
    stays = (z == 0) & (x == 0) & (c == 0)

    started = []

    def copy(src, dst, ss, rs, dev):
        return pltpu.make_async_remote_copy(
            src_ref=src, dst_ref=dst, send_sem=ss, recv_sem=rs, device_id=dev, device_id_type=MESH
        )

    def send(src, dst, ss, rs, dev):
        one = copy(src, dst, ss, rs, dev)
        one.start()
        started.append(one)

    def flush():
        for one in started:
            one.wait_send()
        started.clear()

    def arrive(dst, ss, rs):
        copy(dst, dst, ss, rs, sib).wait_recv()

    def load(src, dst, k):
        one = pltpu.make_async_copy(src, dst, load_sem.at[k])
        one.start()
        return one

    l_th = load(th_h, th_v, 0)
    mine = yh * 4 + x
    l_sh = load(sh_h, hb.at[mine], 1)
    l_small = [load(tgain_h, tgain, 7), load(sgain_h, sgain, 8), load(docs_h, docs, 9)]

    def wkv_part(j, core):
        return wkv_h.at[:, :, pl.ds(pl.multiple_of((j * 2 + core) * COLS, COLS), COLS)]

    def wkv_load(j):
        return pltpu.make_async_copy(wkv_part(j, c), wkv.at[j, c], v_load.at[j])

    def wkv_go(j, carry):
        wkv_load(j).start()
        return carry

    def wo_part(j, core):
        return wo_h.at[:, pl.ds(pl.multiple_of((j * 2 + core) * COLS, COLS), COLS)]

    def wo_load(j):
        return pltpu.make_async_copy(wo_part(j, c), wo.at[j, c], w_load.at[j])

    def wo_send(j):
        return copy(wo_part(j, 1 - c), wo.at[j, c], w_ss.at[j], w_rs.at[j], sib)

    def wo_fetch(j, carry):
        wo_load(j).start()
        return carry

    def wo_go(j, carry):
        wo_send(j).start()
        return carry

    def wo_got(j, carry):
        wo_load(j).wait()
        arrive(wo.at[j, 1 - c], w_ss.at[j], w_rs.at[j])
        return carry

    def wo_end(j, carry):
        wo_send(j).wait_send()
        return carry

    lax.fori_loop(0, 8, wkv_go, 0)
    l_wq = load(wq_h.at[:, c], wq.at[:, c], 3)

    kv_r[...] = jnp.zeros(kv_r.shape, BF16)

    barrier = pltpu.get_barrier_semaphore()
    for dev in (sib, dev_xp, dev_xm, dev_yo, dev_zp, dev_zm, dev_yl):
        pl.semaphore_signal(barrier, inc=1, device_id=dev, device_id_type=MESH)

    class Gather:
        def __init__(self, buf, ss, rs):
            self.buf, self.ss, self.rs = buf, ss, rs
            self.near = [yh * 4 + xm_, yh * 4 + xp_]
            self.opp = yo_ * 4 + x
            self.onear = [yo_ * 4 + xm_, yo_ * 4 + xp_]
            self.far = [yh * 4 + xf_, yo_ * 4 + xf_]
            self.order = [mine] + self.near + [self.opp] + self.onear + self.far

        def part(self, slot, h):
            return self.buf.at[slot, pl.ds(h * 64, 64)]

        def half(self, slot, h, k, dev):
            part = self.part(slot, h)
            send(part, part, self.ss.at[k], self.rs.at[k], dev)

        def got_half(self, slot, h, k):
            arrive(self.part(slot, h), self.ss.at[k], self.rs.at[k])

        def begin(self, h):
            self.half(mine, h, 0 + h, dev_yo)
            self.half(mine, h, 2 + h, dev_xp)
            self.half(mine, h, 4 + h, dev_xm)

        def near_relay(self):
            self.got_half(self.near[0], 0, 2)
            self.half(self.near[0], 0, 6, dev_xp)
            self.got_half(self.near[1], 1, 5)
            self.half(self.near[1], 1, 7, dev_xm)

        def near_rest(self):
            self.got_half(self.near[0], 1, 3)
            self.got_half(self.near[1], 0, 4)

        def opp_half(self, h):
            self.got_half(self.opp, h, 0 + h)
            self.half(self.opp, h, 8 + h, dev_xp)
            self.half(self.opp, h, 10 + h, dev_xm)

        def onear_a(self):
            self.got_half(self.onear[0], 0, 8)
            self.half(self.onear[0], 0, 12, dev_xp)

        def onear_b(self):
            self.got_half(self.onear[1], 1, 11)
            self.half(self.onear[1], 1, 13, dev_xm)

        def onear_rest(self):
            self.got_half(self.onear[0], 1, 9)
            self.got_half(self.onear[1], 0, 10)

        def far_step(self):
            self.got_half(self.far[0], 0, 6)
            self.got_half(self.far[0], 1, 7)

        def ofar_step(self):
            self.got_half(self.far[1], 0, 12)
            self.got_half(self.far[1], 1, 13)

    def pj_send(k):
        rows = pl.ds(k * 256, 256)
        return copy(pj_h.at[rows], pj.at[yl, rows], p_ss.at[k], p_rs.at[k], dev_yl)

    def pj_start(k, half):
        @pl.when(yl == half)
        def _():
            pj_send(k).start()

    def wkv_send(j):
        return copy(wkv_part(j, 1 - c), wkv.at[j, c], v_ss.at[j], v_rs.at[j], sib)

    def wq_send(j):
        return copy(wq_h.at[j, 1 - c], wq.at[j, c], u_ss.at[j], u_rs.at[j], sib)

    def w_go(j, carry):
        wkv_send(j).start()
        wq_send(j).start()
        return carry

    def w_end(j, carry):
        wkv_send(j).wait_send()
        wq_send(j).wait_send()
        return carry

    def w_got(slot):
        wkv_load(slot).wait()
        arrive(wkv.at[slot, 1 - c], v_ss.at[slot], v_rs.at[slot])
        arrive(wq.at[slot, 1 - c], u_ss.at[slot], u_rs.at[slot])

    ag = Gather(hb, ag_ss, ag_rs)
    l_sh.wait()
    pl.semaphore_wait(barrier, 7)
    ag.begin(0)

    z_slot = 0
    l_th.wait()
    for one in l_small:
        one.wait()
    docs_z[z] = docs[...]
    part = jnp.zeros((ROWS, 128), F32)
    for i in range(8):
        cols = slice(i * 128, (i + 1) * 128)
        f = th_v[:, cols].astype(F32)
        part = part + f * f
        tg[z_slot, :, cols] = (f * tgain[:, cols]).astype(BF16)
    sg_s[:, COLS:COLS + 128] = jnp.sum(part.T, axis=0, keepdims=True)
    part = jnp.zeros((ROWS, 128), F32)
    for i in range(4):
        f = hb[mine, :, i * 128:(i + 1) * 128].astype(F32)
        part = part + f * f
    sg_s[:, COLS + 128:COLS + 256] = jnp.sum(part.T, axis=0, keepdims=True)
    sg_s[:, 0:COLS] = sgain[...]
    sg_r[mine] = sg_s[...]

    def ring_slot(d):
        return (0, 1, 2, 3, 4, 7, 6, 5)[d % 8]

    def z_ref(d, h):
        return tg.at[ring_slot(d), pl.ds(h * 64, 64)]

    def z_send(k):
        d = k // 2
        send(z_ref(8 - d, k % 2), z_ref(7 - d, k % 2), z_ss.at[k], z_rs.at[k], dev_zp)
        send(z_ref(d, 1 - k % 2), z_ref(d + 1, 1 - k % 2), z_ss.at[8 + k], z_rs.at[8 + k], dev_zm)

    def z_got(k):
        up, down = z_ref(-(k // 2) + 7, k % 2), z_ref(k // 2 + 1, 1 - k % 2)
        arrive(up, z_ss.at[k], z_rs.at[k])
        arrive(down, z_ss.at[8 + k], z_rs.at[8 + k])

    def z_step(k):
        z_got(k)
        if k + 2 < 7:
            z_send(k + 2)

    def small_send(i, k, dev):
        slot = ag.order[i]
        send(sg_r.at[slot], sg_r.at[slot], sm_ss.at[k], sm_rs.at[k], dev)

    def small_got(i, k):
        arrive(sg_r.at[ag.order[i]], sm_ss.at[k], sm_rs.at[k])

    def docs_send(d, k, dev):
        ref = docs_z.at[(z + d) % 8]
        send(ref, ref, dc_ss.at[k], dc_rs.at[k], dev)

    def docs_step(k):
        arrive(docs_z.at[(z + 7 - k) % 8], dc_ss.at[k], dc_rs.at[k])
        if k < 3:
            arrive(docs_z.at[(z + 1 + k) % 8], dc_ss.at[4 + k], dc_rs.at[4 + k])
            docs_send(7 - k, k + 1, dev_zp)
            if k < 2:
                docs_send(1 + k, k + 5, dev_zm)
        else:
            send(docs_z, docs_o, dc_ss.at[8], dc_rs.at[8], dev_yl)

    small_send(0, 0, dev_yo)
    small_send(0, 1, dev_xp)
    small_send(0, 2, dev_xm)
    ag.begin(1)
    docs_send(0, 0, dev_zp)
    docs_send(0, 4, dev_zm)
    z_send(0)
    pj_start(0, 1)
    z_send(1)
    pj_start(1, 1)
    lax.fori_loop(0, 8, w_go, 0)
    pj_start(2, 1)
    pj_start(3, 1)
    pj_start(0, 0)
    l_pj = load(pj_h, pj.at[yl], 4)

    entry = lax.broadcasted_iota(jnp.int32, (64, ROWS), 0).astype(F32)
    position = (s * ROWS + lax.broadcasted_iota(jnp.int32, (64, ROWS), 1)).astype(F32)
    angle = position * jnp.exp(-math.log(500000.0) * (2.0 * entry / HEAD_DIM))
    cos_t[...] = jnp.cos(angle)
    sin_t[...] = jnp.sin(angle)

    def process(slots, first=False):
        blocks, w = [], []
        for slot in slots:
            parts = []
            for i in range(4):
                cols = slice(i * 128, (i + 1) * 128)
                f = hb[slot, :, cols].astype(F32)
                parts.append((f * scale_v[...] * sg_r[slot][:, cols]).astype(BF16))
            blocks.append(jnp.concatenate(parts, axis=1))
        n = jnp.concatenate(blocks, axis=1)
        for slot in slots:
            w_got(slot)
            w.append(wkv[slot].reshape(128, COLS))
        kv = nt_dot(jnp.concatenate(w, axis=1), n)
        for core in range(2):
            w = jnp.concatenate([wq[slot, core] for slot in slots], axis=0)
            q = jnp.dot(n, w, preferred_element_type=F32)
            k = kv[core * 64:core * 64 + 64]
            q_acc[core] = q if first else q_acc[core] + q
            kv_acc[core] = k if first else kv_acc[core] + k

    small_got(1, 1)
    small_send(1, 3, dev_xp)
    small_got(2, 2)
    small_got(3, 0)
    small_send(3, 4, dev_xp)
    small_send(3, 5, dev_xm)
    docs_step(0)
    ag.near_relay()
    small_got(6, 3)
    docs_step(1)
    small_got(4, 4)
    small_send(4, 6, dev_xp)
    small_got(5, 5)
    ag.near_rest()
    pj_start(1, 0)
    ag.opp_half(0)
    z_step(0)
    pj_start(2, 0)
    small_got(7, 6)
    sums = sg_r[0][:, COLS:COLS + 256]
    for i in range(1, 8):
        sums = sums + sg_r[i][:, COLS:COLS + 256]
    sum_s[...] = sums
    send(sum_s, sum_r, x_ss.at[2], x_rs.at[2], sib)
    docs_step(2)
    ag.opp_half(1)
    pj_start(3, 0)
    arrive(sum_r, x_ss.at[2], x_rs.at[2])
    sums = sum_s[...] + sum_r[...]
    ts_v[...] = jnp.broadcast_to(lax.rsqrt(sums[:, 0:128] / DT + 1e-05), (ROWS, 128)).T
    scale_v[...] = jnp.broadcast_to(lax.rsqrt(sums[:, 128:256] / DS + 1e-05), (ROWS, 128)).T
    docs_step(3)
    z_step(1)
    ag.onear_a()
    l_wq.wait()
    process([mine] + ag.near, True)
    ag.onear_b()
    z_step(2)
    ag.far_step()
    process([ag.opp, ag.far[0]])
    ag.onear_rest()
    process(ag.onear)
    z_step(3)
    ag.ofar_step()
    process([ag.far[1]])
    send(kv_acc.at[1 - c], kv_in, x_ss.at[3], x_rs.at[3], sib)
    send(q_acc.at[1 - c], q_in, x_ss.at[4], x_rs.at[4], sib)
    arrive(kv_in, x_ss.at[3], x_rs.at[3])

    row = lax.broadcasted_iota(jnp.int32, (64, 64), 0)
    col = lax.broadcasted_iota(jnp.int32, (64, 64), 1)
    take = ((row >> 3) & 1) * 32 + (row & 7) * 4 + (row >> 4)
    pick = jnp.where(col == take, 1.0, 0.0).astype(BF16)
    kv_mine = (kv_acc[c] + kv_in[...]).astype(BF16)
    kvx_s[...] = jnp.dot(pick, kv_mine, preferred_element_type=F32).astype(BF16).reshape(4, 16, 128)
    kvx_r[t] = kvx_s[t // 4]

    def kvx(k):
        to = (t + k) % 16
        return copy(kvx_s.at[to // 4], kvx_r.at[t], kx_ss.at[k], kx_rs.at[k], (s, to))

    def kvx_go(k, carry):
        kvx(k).start()
        return carry

    def kvx_got(k, carry):
        arrive(kvx_r.at[(t + 16 - k) % 16], kx_ss.at[k], kx_rs.at[k])
        return carry

    def kvx_end(k, carry):
        kvx(k).wait_send()
        return carry

    lax.fori_loop(1, 16, kvx_go, 0)
    lax.fori_loop(0, 8, wo_fetch, 0)
    lax.fori_loop(0, 8, wo_go, 0)
    z_step(4)

    cos2 = jnp.concatenate([cos_t[...], cos_t[...]], axis=0).T
    sin2 = jnp.concatenate([-sin_t[...], sin_t[...]], axis=0).T
    arrive(q_in, x_ss.at[4], x_rs.at[4])
    q_mine = q_acc[c] + q_in[...]
    for h in range(2):
        qh = q_mine[:, h * 128:(h + 1) * 128]
        turned = qh * cos2 + pltpu.roll(qh, 64, 1) * sin2
        q_v[h] = (turned * HEAD_DIM ** (-0.5)).astype(BF16)

    lax.fori_loop(1, 16, kvx_got, 0)
    both = kvx_r[...].astype(F32).reshape(16, 2, 8, ROWS)
    k_raw = both[:, 0].reshape(HEAD_DIM, ROWS)
    v_raw = both[:, 1].reshape(HEAD_DIM, ROWS)
    first, second = k_raw[0:64], k_raw[64:128]
    k_rot = jnp.concatenate(
        [first * cos_t[...] - second * sin_t[...], second * cos_t[...] + first * sin_t[...]], axis=0
    )
    kv_own[0] = k_rot.astype(BF16)
    kv_own[1] = v_raw.T.astype(BF16)
    kv_r[0, 0] = kv_own[0]
    kv_r[1, 0] = kv_own[1]

    def kv_copy(k):
        return copy(kv_own.at[c], kv_r.at[c, k], kv_ss.at[k], kv_rs.at[k], ((s + k) % 16, t))

    def kv_fwd(k):
        return copy(kv_r.at[c, k], kv_r.at[c, k], kf_ss.at[k], kf_rs.at[k], sib)

    def kv_go(k):
        @pl.when(s + k < 16)
        def _():
            kv_copy(k).start()

    def kv_mid(k):
        @pl.when(s >= k)
        def _():
            arrive(kv_r.at[c, k], kv_ss.at[k], kv_rs.at[k])
            kv_fwd(k).start()

    def kv_got(k, carry):
        @pl.when(s >= k)
        def _():
            arrive(kv_r.at[1 - c, k], kf_ss.at[k], kf_rs.at[k])
        return carry

    def kv_end(k, carry):
        @pl.when(s >= k)
        def _():
            kv_fwd(k).wait_send()

        @pl.when(s + k < 16)
        def _():
            kv_copy(k).wait_send()
        return carry

    arrive(docs_o, dc_ss.at[8], dc_rs.at[8])
    for k in range(1, BACK + 1):
        kv_go(k)

    def docs_back(j):
        at = (z + 8 - j) % 8
        return jnp.where(z >= j, docs_z[at], jnp.where(yl == 1, docs_o[at], -1))

    key_doc = jnp.concatenate([docs_back(j) for j in range(BACK + 1)], axis=1)
    row_doc = jnp.broadcast_to(docs[...].astype(F32), (ROWS, ROWS)).T[:, 0:1].astype(jnp.int32)
    wide = (ROWS, (BACK + 1) * ROWS)
    row_at = lax.broadcasted_iota(jnp.int32, wide, 0)
    key_at = lax.broadcasted_iota(jnp.int32, wide, 1)
    allowed = (key_doc == row_doc) & ((key_at >= ROWS) | (key_at <= row_at))
    bias[...] = jnp.where(allowed, 0.0, -1e30)

    class Reduce:
        def __init__(self, y_order, own, sib_s, sib_r, x2, ra, rb, xp, xm, fm, fp, ys, yr, fin, ss, rs):
            self.own, self.sib_s, self.sib_r = own, sib_s, sib_r
            self.x2, self.ra, self.rb, self.xp, self.xm, self.fm, self.fp = x2, ra, rb, xp, xm, fm, fp
            self.ys, self.yr, self.fin, self.ss, self.rs = ys, yr, fin, ss, rs
            self.y_order = y_order
            self.x_order = (xf_, xp_, xm_, x)

        def go(self, src, dst, k, dev):
            send(src, dst, self.ss.at[k], self.rs.at[k], dev)

        def got(self, dst, k):
            arrive(dst, self.ss.at[k], self.rs.at[k])

        def slot(self, k, i):
            return self.y_order[i] * 4 + self.x_order[k]

        def to_sib(self, k, i):
            slot = self.slot(k, i)
            self.go(self.sib_s.at[slot], self.sib_r.at[slot], k * 2 + i, sib)

        def sib_got(self, k, i):
            if self.sib_r is not None:
                self.got(self.sib_r.at[self.slot(k, i)], k * 2 + i)

        def pair(self, k, i, h):
            slot, rows = self.slot(k, i), slice(h * 64, h * 64 + 64)
            value = self.own[slot, rows]
            return value if self.sib_r is None else value + self.sib_r[slot, rows].astype(F32)

        def far(self, i):
            self.sib_got(0, i)
            self.x2[i, 0:64] = self.pair(0, i, 0).astype(BF16)
            self.go(self.x2.at[i, pl.ds(0, 64)], self.ra.at[i], 8 + i, dev_xp)
            self.x2[i, 64:128] = self.pair(0, i, 1).astype(BF16)
            self.go(self.x2.at[i, pl.ds(64, 64)], self.rb.at[i], 10 + i, dev_xm)

        def near(self, i):
            self.sib_got(1, i)
            self.xp[i, 64:128] = self.pair(1, i, 1).astype(BF16)
            self.go(self.xp.at[i, pl.ds(64, 64)], self.fm.at[i, pl.ds(64, 64)], 12 + i, dev_xp)
            self.sib_got(2, i)
            self.xm[i, 0:64] = self.pair(2, i, 0).astype(BF16)
            self.go(self.xm.at[i, pl.ds(0, 64)], self.fp.at[i, pl.ds(0, 64)], 14 + i, dev_xm)

        def relay(self, i):
            self.got(self.ra.at[i], 8 + i)
            self.xp[i, 0:64] = (self.pair(1, i, 0) + self.ra[i].astype(F32)).astype(BF16)
            self.go(self.xp.at[i, pl.ds(0, 64)], self.fm.at[i, pl.ds(0, 64)], 16 + i, dev_xp)
            self.got(self.rb.at[i], 10 + i)
            self.xm[i, 64:128] = (self.pair(2, i, 1) + self.rb[i].astype(F32)).astype(BF16)
            self.go(self.xm.at[i, pl.ds(64, 64)], self.fp.at[i, pl.ds(64, 64)], 18 + i, dev_xm)

        def join(self, i, h):
            rows, at = slice(h * 64, h * 64 + 64), pl.ds(h * 64, 64)
            if h == 0:
                self.sib_got(3, i)
            self.got(self.fm.at[i, at], (16, 12)[h] + i)
            self.got(self.fp.at[i, at], (14, 18)[h] + i)
            return self.pair(3, i, h) + self.fm[i, rows].astype(F32) + self.fp[i, rows].astype(F32)

        def to_opp(self, h):
            at = pl.ds(h * 64, 64)
            return copy(self.ys.at[at], self.yr.at[at], self.ss.at[20 + h], self.rs.at[20 + h], dev_yo)

        def join_other(self):
            for h in range(2):
                self.ys[h * 64:h * 64 + 64] = self.join(0, h).astype(BF16)
                self.to_opp(h).start()

        def join_mine(self):
            for h in range(2):
                self.fin[h * 64:h * 64 + 64] = self.join(1, h)

        def end(self):
            for h in range(2):
                self.to_opp(h).wait_send()

        def last(self, h):
            rows = slice(h * 64, h * 64 + 64)
            self.got(self.yr.at[pl.ds(h * 64, 64)], 20 + h)
            return self.fin[rows] + self.yr[rows].astype(F32)

    rt = Reduce((yl, 1 - yl), t_own, t_sib_s, t_sib_r, t_x2, t_ra, t_rb, t_xp, t_xm, t_fm, t_fp, None, None, None, t_ss, t_rs)

    def t3(i, h):
        at = pl.ds(h * 64, 64)
        dev = (yl * 8 + (z + turn) % 8, rt.y_order[i] * 8 + z)
        return copy(t3_s.at[i, at], t3_r.at[yh, at], t3_ss.at[i * 2 + h], t3_rs.at[yh * 2 + h], dev)

    def t3_stays(i):
        return stays & (rt.y_order[i] == yh)

    def t_place(i):
        for h in range(2):
            rows = slice(h * 64, h * 64 + 64)
            t3_s[i, rows] = rt.join(i, h).astype(BF16)

            @pl.when(t3_stays(i))
            def _():
                t3_r[yh, rows] = t3_s[i, rows]

            @pl.when(jnp.logical_not(t3_stays(i)))
            def _():
                t3(i, h).start()

    z_step(5)
    z_step(6)

    def products(core, y_, k, width):
        rows = tg[pl.ds(core * 4, 4), :, k * width:(k + 1) * width].reshape(4 * ROWS, width)
        return jnp.dot(rows, pj[y_, k * width:(k + 1) * width], preferred_element_type=F32).reshape(4, ROWS, COLS)

    l_pj.wait()
    first = pl.ds(yl * 4, 4)
    t_sib_s[first] = products(1 - c, yl, 0, 1024).astype(BF16)
    for k in range(4):
        rt.to_sib(k, 0)
    t_own[first] = products(c, yl, 0, 1024)
    rt.far(0)
    rt.near(0)

    other = pl.ds((1 - yl) * 4, 4)
    for k in range(4):
        arrive(pj.at[1 - yl, pl.ds(k * 256, 256)], p_ss.at[k], p_rs.at[k])
        theirs = products(1 - c, 1 - yl, k, 256)
        if k == 0:
            t_part[...] = theirs
        elif k < 3:
            t_part[...] += theirs
        else:
            t_sib_s[other] = (t_part[...] + theirs).astype(BF16)
            for j in range(4):
                rt.to_sib(j, 1)
        if k == 0:
            t_own[other] = products(c, 1 - yl, k, 256)
        else:
            t_own[other] += products(c, 1 - yl, k, 256)
        if k == 1:
            rt.relay(0)
    rt.far(1)
    rt.near(1)
    t_place(0)
    for k in range(1, BACK + 1):
        kv_mid(k)

    lax.fori_loop(1, BACK + 1, kv_got, 0)
    keys = jnp.concatenate([kv_r[0, j] for j in range(BACK + 1)], axis=1)
    values = kv_r[1].reshape((BACK + 1) * ROWS, HEAD_DIM)
    for h in range(2):
        scores = jnp.dot(q_v[h], keys, preferred_element_type=F32)
        scores = scores + bias[...]
        probs = jnp.exp(scores - jnp.max(scores, axis=1, keepdims=True))
        total = jnp.sum(probs, axis=1, keepdims=True)
        acc = jnp.dot(probs.astype(BF16), values, preferred_element_type=F32)
        attn_v[c * 2 + h] = (acc / total).astype(BF16)
        send(attn_v.at[c * 2 + h], attn_v.at[c * 2 + h], x_ss.at[5 + h], x_rs.at[5 + h], sib)
    lax.fori_loop(0, 8, wo_got, 0)
    rt.relay(1)

    ro = Reduce((yo_, yh), o_own, None, None, o_x2, o_ra, o_rb, o_xp, o_xm, o_fm, o_fp, o_ys, o_yr, o_fin, o_ss, o_rs)

    for h in range(2):
        arrive(attn_v.at[2 - 2 * c + h], x_ss.at[5 + h], x_rs.at[5 + h])
    attn = jnp.concatenate([attn_v[i] for i in range(4)], axis=1)

    def out_block(k, i):
        slot = ro.slot(k, i)
        o_own[slot] = jnp.dot(attn, wo[slot].reshape(COLS, COLS), preferred_element_type=F32)

    out_block(0, 0)
    ro.far(0)
    out_block(1, 0)
    out_block(2, 0)
    ro.near(0)
    t_place(1)
    out_block(0, 1)
    ro.relay(0)
    ro.far(1)
    out_block(1, 1)
    out_block(2, 1)
    ro.near(1)
    out_block(3, 0)
    out_block(3, 1)
    ro.relay(1)

    ro.join_other()
    ro.join_mine()

    early = list(started)
    started.clear()

    def before_end():
        for one in early:
            one.wait_send()
        for k in range(4):
            pj_send(k).wait_send()
        lax.fori_loop(0, 8, w_end, 0)
        lax.fori_loop(0, 8, wo_end, 0)
        lax.fori_loop(1, 16, kvx_end, 0)
        lax.fori_loop(1, BACK + 1, kv_end, 0)
        ro.end()
        for i in range(2):

            @pl.when(jnp.logical_not(t3_stays(i)))
            def _():
                t3(i, 0).wait_send()
                t3(i, 1).wait_send()

    dg = Gather(db, dg_ss, dg_rs)
    for h in range(2):
        rows = slice(h * 64, h * 64 + 64)
        mixed = hb[mine, rows].astype(F32) + ro.last(h)
        out_s[rows] = mixed.astype(BF16)

        for p in range(2):

            @pl.when(jnp.logical_not(stays & (yh == p)))
            def _():
                arrive(t3_r.at[p, pl.ds(h * 64, 64)], t3_ss.at[h], t3_rs.at[p * 2 + h])

        target = t3_r[0, rows].astype(F32) + t3_r[1, rows].astype(F32)
        target = target * jnp.concatenate([ts_v[rows]] * 4, axis=1)
        difference = mixed - target
        db[mine, rows] = difference.astype(BF16)
        dg.begin(h)
        squares = difference * difference
        l_v[rows] = (
            squares[:, 0:128] + squares[:, 128:256] + squares[:, 256:384] + squares[:, 384:512]
        )
    l_s[...] = jnp.sum(l_v[...].T, axis=0, keepdims=True)
    l_r[t] = l_s[...]

    def loss(k):
        return copy(l_s, l_r.at[t], l_ss.at[k], l_rs.at[k], (s, (t + k) % 16))

    def loss_go(k, carry):
        loss(k).start()
        return carry

    def loss_got(k, carry):
        arrive(l_r.at[(t + 16 - k) % 16], l_ss.at[k], l_rs.at[k])
        return carry

    def loss_end(k, carry):
        loss(k).wait_send()
        return carry

    lax.fori_loop(1, 16, loss_go, 0)

    def add_grad(slots, first=False):
        d = jnp.concatenate([db[slot] for slot in slots], axis=1)
        for core in range(2):
            w = jnp.concatenate([wo[slot, core] for slot in slots], axis=1)
            g = nt_dot(d, w)
            g_acc[core] = g if first else g_acc[core] + g

    dg.near_relay()
    dg.opp_half(0)
    dg.near_rest()
    before_end()
    add_grad([mine] + dg.near, True)
    dg.opp_half(1)
    dg.onear_a()
    dg.far_step()
    add_grad([dg.opp, dg.far[0]])
    dg.onear_b()
    dg.onear_rest()
    add_grad(dg.onear)
    lax.fori_loop(1, 16, loss_got, 0)
    loss_sum = l_r[0]
    for i in range(1, 16):
        loss_sum = loss_sum + l_r[i]
    out_l[...] = loss_sum / DS
    dg.ofar_step()
    add_grad([dg.far[1]])
    send(g_acc.at[1 - c], g_in, x_ss.at[7], x_rs.at[7], sib)
    arrive(g_in, x_ss.at[7], x_rs.at[7])
    out_g[...] = (g_acc[c] + g_in[...]).astype(BF16)

    flush()
    lax.fori_loop(1, 16, loss_end, 0)


def reduce_buffers():
    block = (ROWS, COLS)
    return [
        pltpu.VMEM((2, 64, COLS), BF16),
        pltpu.VMEM((2, 64, COLS), BF16),
        pltpu.VMEM((2,) + block, BF16),
        pltpu.VMEM((2,) + block, BF16),
        pltpu.VMEM((2,) + block, BF16),
        pltpu.VMEM((2,) + block, BF16),
        pltpu.VMEM(block, BF16),
        pltpu.VMEM(block, BF16),
        pltpu.VMEM(block, F32),
    ]


def on_device(
    teacher_hidden, teacher_gain, projector, student_hidden, student_gain,
    query_weight, kv_weight, out_weight, doc_ids,
):
    block = (ROWS, COLS)
    hbm = pl.BlockSpec(memory_space=pltpu.HBM)
    vmem = pl.BlockSpec(memory_space=pltpu.VMEM)
    dma = pltpu.SemaphoreType.DMA
    out_s, out_l, out_g = pl.pallas_call(
        body,
        out_shape=(
            jax.ShapeDtypeStruct(block, BF16),
            jax.ShapeDtypeStruct((1, ROWS), F32),
            jax.ShapeDtypeStruct((ROWS, 256), BF16),
        ),
        in_specs=[hbm] * 9,
        out_specs=(vmem, vmem, vmem),
        scratch_shapes=[
            pltpu.VMEM((1, 1024), F32),
            pltpu.VMEM((1, COLS), F32),
            pltpu.VMEM((1, ROWS), jnp.int32),
            pltpu.VMEM((ROWS, 1024), BF16),
            pltpu.VMEM((8, ROWS, 1024), BF16),
            pltpu.VMEM((2, 1024, COLS), BF16),
            pltpu.VMEM((8, 2, COLS, 256), BF16),
            pltpu.VMEM((8, 2, 2, 32, COLS), BF16),
            pltpu.VMEM((8, 2, 256, COLS), BF16),
            pltpu.VMEM((64, ROWS), F32),
            pltpu.VMEM((64, ROWS), F32),
            pltpu.VMEM((8,) + block, BF16),
            pltpu.VMEM((1, 768), F32),
            pltpu.VMEM((8, 1, 768), F32),
            pltpu.VMEM((1, 256), F32),
            pltpu.VMEM((1, 256), F32),
            pltpu.VMEM((ROWS, 128), F32),
            pltpu.VMEM((2, ROWS, 256), F32),
            pltpu.VMEM((ROWS, 256), F32),
            pltpu.VMEM((2, 64, ROWS), F32),
            pltpu.VMEM((64, ROWS), F32),
            pltpu.VMEM((4, 16, ROWS), BF16),
            pltpu.VMEM((16, 16, ROWS), BF16),
            pltpu.VMEM((2, ROWS, HEAD_DIM), BF16),
            pltpu.VMEM((2, BACK + 1, ROWS, HEAD_DIM), BF16),
            pltpu.VMEM((8, 1, ROWS), jnp.int32),
            pltpu.VMEM((8, 1, ROWS), jnp.int32),
            pltpu.VMEM((2, ROWS, HEAD_DIM), BF16),
            pltpu.VMEM((4, ROWS, HEAD_DIM), BF16),
            pltpu.VMEM((ROWS, (BACK + 1) * ROWS), F32),
            pltpu.VMEM((8,) + block, F32),
            pltpu.VMEM((4,) + block, F32),
            pltpu.VMEM((8,) + block, F32),
            pltpu.VMEM((2,) + block, BF16),
            pltpu.VMEM((8,) + block, BF16),
            pltpu.VMEM((8,) + block, BF16),
            pltpu.VMEM((2,) + block, BF16),
            *reduce_buffers()[:6],
            *reduce_buffers(),
            pltpu.VMEM((2,) + block, BF16),
            pltpu.VMEM((2,) + block, BF16),
            pltpu.VMEM((ROWS, 128), F32),
            pltpu.VMEM((8,) + block, BF16),
            pltpu.VMEM((2, ROWS, 256), F32),
            pltpu.VMEM((ROWS, 256), F32),
            pltpu.VMEM((ROWS, 128), F32),
            pltpu.VMEM((1, ROWS), F32),
            pltpu.VMEM((16, 1, ROWS), F32),
            dma((10,)),
            *[dma((8,)) for _ in range(10)],
            dma((16,)), dma((16,)), dma((8,)), dma((8,)),
            dma((24,)), dma((24,)), dma((24,)), dma((24,)),
            dma((16,)), dma((16,)), dma((16,)), dma((16,)),
            dma((9,)), dma((9,)), dma((9,)), dma((9,)), dma((9,)), dma((9,)),
            dma((24,)), dma((24,)), dma((24,)), dma((24,)),
            dma((4,)), dma((4,)),
            dma((16,)), dma((16,)),
        ],
        compiler_params=pltpu.CompilerParams(
            collective_id=0, has_side_effects=True, vmem_limit_bytes=40 * 1024 * 1024
        ),
    )(
        *(
            pltpu.with_memory_space_constraint(one, pltpu.HBM)
            for one in (
                teacher_hidden, teacher_gain.reshape(1, -1), projector, student_hidden,
                student_gain.reshape(1, -1), query_weight.reshape(8, 2, COLS, 256), jnp.transpose(kv_weight, (0, 2, 1)),
                out_weight, doc_ids.reshape(1, -1),
            )
        )
    )
    return out_s, out_l.reshape(ROWS), out_g


def solution(mesh):
    in_specs = (
        P("seq", "tensor"),
        P("tensor"),
        P("tensor", "seq"),
        P("seq", "tensor"),
        P("tensor"),
        P(None, "tensor"),
        P(None, None, "tensor"),
        P("tensor", None),
        P("seq"),
    )
    out_specs = (P("seq", "tensor"), P("seq"), P("seq", "tensor"))
    return jax.shard_map(
        on_device, mesh=mesh, in_specs=in_specs, out_specs=out_specs, check_vma=False
    )
```

```python
import math

import jax
import jax.numpy as jnp
from jax import lax
from jax.experimental import pallas as pl
from jax.experimental.pallas import tpu as pltpu
from jax.sharding import PartitionSpec as P

DT = 16384
DS = 8192
HEAD_DIM = 128
HEADS = 32
KV_HEADS = 4
ROWS = 128
COLS = 512
BACK = 8
F32 = jnp.float32
BF16 = jnp.bfloat16
MESH = pl.DeviceIdType.MESH
NT = (((1,), (1,)), ((), ()))


def nt_dot(a, b):
    return lax.dot_general(a, b, NT, preferred_element_type=F32)


def body(
    th_h, tgain_h, pj_h, sh_h, sgain_h, wq_h, wkv_h, wo_h, docs_h,
    out_s, out_l, out_g,
    tgain, sgain, docs, th_v, tg, pj, wq, wkv, wo, cos_t, sin_t,
    hb, sg_s, sg_r, sum_s, sum_r, scale_v, q_acc, q_in, kv_acc, kv_in,
    kvx_s, kvx_r, kv_own, kv_r, docs_z, docs_o, q_v, attn_v, bias,
    t_own, t_part, o_own, o_x2, t_sib_s, t_sib_r, t_x2, t_ra, t_rb, t_xp, t_xm, t_fm, t_fp,
    o_ra, o_rb, o_xp, o_xm, o_fm, o_fp, o_ys, o_yr, o_fin,
    t3_s, t3_r, ts_v, db, g_acc, g_in, l_v, l_s, l_r,
    load_sem, w_load, w_ss, w_rs, v_load, v_ss, v_rs, u_ss, u_rs, x_ss, x_rs, z_ss, z_rs, p_ss, p_rs,
    ag_ss, ag_rs, dg_ss, dg_rs, sm_ss, sm_rs, kx_ss, kx_rs, kv_ss, kv_rs, kf_ss, kf_rs, dc_ss, dc_rs,
    t_ss, t_rs, o_ss, o_rs, t3_ss, t3_rs, l_ss, l_rs,
):
    s = lax.axis_index("seq")
    t = lax.axis_index("tensor")
    yl, z = s // 8, s % 8
    yh, x, c = t // 8, (t // 2) % 4, t % 2

    def tid(y_, x_, c_):
        return y_ * 8 + x_ * 2 + c_

    xp_, xm_ = (x + 1) % 4, (x + 3) % 4
    xf_ = (x + 2) % 4
    yo_ = 1 - yh
    sib = (s, tid(yh, x, 1 - c))
    dev_xp = (s, tid(yh, xp_, c))
    dev_xm = (s, tid(yh, xm_, c))
    dev_yo = (s, tid(yo_, x, c))
    dev_zp = (yl * 8 + (z + 1) % 8, t)
    dev_zm = (yl * 8 + (z + 7) % 8, t)
    dev_yl = ((1 - yl) * 8 + z, t)
    turn = jnp.where(c == 0, x, jnp.where(x == 0, 4, 8 - x))
    stays = (z == 0) & (x == 0) & (c == 0)

    started = []

    def copy(src, dst, ss, rs, dev):
        return pltpu.make_async_remote_copy(
            src_ref=src, dst_ref=dst, send_sem=ss, recv_sem=rs, device_id=dev, device_id_type=MESH
        )

    def send(src, dst, ss, rs, dev):
        one = copy(src, dst, ss, rs, dev)
        one.start()
        started.append(one)

    def flush():
        for one in started:
            one.wait_send()
        started.clear()

    def arrive(dst, ss, rs):
        copy(dst, dst, ss, rs, sib).wait_recv()

    def load(src, dst, k):
        one = pltpu.make_async_copy(src, dst, load_sem.at[k])
        one.start()
        return one

    l_th = load(th_h, th_v, 0)
    mine = yh * 4 + x
    l_sh = load(sh_h, hb.at[mine], 1)
    l_small = [load(tgain_h, tgain, 7), load(sgain_h, sgain, 8), load(docs_h, docs, 9)]

    def wkv_part(j, core):
        return wkv_h.at[:, :, pl.ds(pl.multiple_of((j * 2 + core) * COLS, COLS), COLS)]

    def wkv_load(j):
        return pltpu.make_async_copy(wkv_part(j, c), wkv.at[j, c], v_load.at[j])

    def wkv_go(j, carry):
        wkv_load(j).start()
        return carry

    def wo_part(j, core):
        return wo_h.at[:, pl.ds(pl.multiple_of((j * 2 + core) * COLS, COLS), COLS)]

    def wo_load(j):
        return pltpu.make_async_copy(wo_part(j, c), wo.at[j, c], w_load.at[j])

    def wo_send(j):
        return copy(wo_part(j, 1 - c), wo.at[j, c], w_ss.at[j], w_rs.at[j], sib)

    def wo_fetch(j, carry):
        wo_load(j).start()
        return carry

    def wo_go(j, carry):
        wo_send(j).start()
        return carry

    def wo_got(j, carry):
        wo_load(j).wait()
        arrive(wo.at[j, 1 - c], w_ss.at[j], w_rs.at[j])
        return carry

    def wo_end(j, carry):
        wo_send(j).wait_send()
        return carry

    lax.fori_loop(0, 8, wkv_go, 0)
    l_wq = load(wq_h.at[:, c], wq.at[:, c], 3)

    kv_r[...] = jnp.zeros(kv_r.shape, BF16)

    barrier = pltpu.get_barrier_semaphore()
    for dev in (sib, dev_xp, dev_xm, dev_yo, dev_zp, dev_zm, dev_yl):
        pl.semaphore_signal(barrier, inc=1, device_id=dev, device_id_type=MESH)

    class Gather:
        def __init__(self, buf, ss, rs):
            self.buf, self.ss, self.rs = buf, ss, rs
            self.near = [yh * 4 + xm_, yh * 4 + xp_]
            self.opp = yo_ * 4 + x
            self.onear = [yo_ * 4 + xm_, yo_ * 4 + xp_]
            self.far = [yh * 4 + xf_, yo_ * 4 + xf_]
            self.order = [mine] + self.near + [self.opp] + self.onear + self.far

        def part(self, slot, h):
            return self.buf.at[slot, pl.ds(h * 64, 64)]

        def half(self, slot, h, k, dev):
            part = self.part(slot, h)
            send(part, part, self.ss.at[k], self.rs.at[k], dev)

        def got_half(self, slot, h, k):
            arrive(self.part(slot, h), self.ss.at[k], self.rs.at[k])

        def begin(self, h):
            self.half(mine, h, 0 + h, dev_yo)
            self.half(mine, h, 2 + h, dev_xp)
            self.half(mine, h, 4 + h, dev_xm)

        def near_relay(self):
            self.got_half(self.near[0], 0, 2)
            self.half(self.near[0], 0, 6, dev_xp)
            self.got_half(self.near[1], 1, 5)
            self.half(self.near[1], 1, 7, dev_xm)

        def near_rest(self):
            self.got_half(self.near[0], 1, 3)
            self.got_half(self.near[1], 0, 4)

        def opp_half(self, h):
            self.got_half(self.opp, h, 0 + h)
            self.half(self.opp, h, 8 + h, dev_xp)
            self.half(self.opp, h, 10 + h, dev_xm)

        def onear_a(self):
            self.got_half(self.onear[0], 0, 8)
            self.half(self.onear[0], 0, 12, dev_xp)

        def onear_b(self):
            self.got_half(self.onear[1], 1, 11)
            self.half(self.onear[1], 1, 13, dev_xm)

        def onear_rest(self):
            self.got_half(self.onear[0], 1, 9)
            self.got_half(self.onear[1], 0, 10)

        def far_step(self):
            self.got_half(self.far[0], 0, 6)
            self.got_half(self.far[0], 1, 7)

        def ofar_step(self):
            self.got_half(self.far[1], 0, 12)
            self.got_half(self.far[1], 1, 13)

    def pj_send(k):
        rows = pl.ds(k * 256, 256)
        send(pj_h.at[rows], pj.at[yl, rows], p_ss.at[k], p_rs.at[k], dev_yl)

    def wkv_send(j):
        return copy(wkv_part(j, 1 - c), wkv.at[j, c], v_ss.at[j], v_rs.at[j], sib)

    def wq_send(j):
        return copy(wq_h.at[j, 1 - c], wq.at[j, c], u_ss.at[j], u_rs.at[j], sib)

    def w_go(j, carry):
        wkv_send(j).start()
        wq_send(j).start()
        return carry

    def w_end(j, carry):
        wkv_send(j).wait_send()
        wq_send(j).wait_send()
        return carry

    def w_got(slot):
        wkv_load(slot).wait()
        arrive(wkv.at[slot, 1 - c], v_ss.at[slot], v_rs.at[slot])
        arrive(wq.at[slot, 1 - c], u_ss.at[slot], u_rs.at[slot])

    ag = Gather(hb, ag_ss, ag_rs)
    l_sh.wait()

    z_slot = 0
    l_th.wait()
    for one in l_small:
        one.wait()
    docs_z[z] = docs[...]
    part = jnp.zeros((ROWS, 128), F32)
    for i in range(8):
        cols = slice(i * 128, (i + 1) * 128)
        f = th_v[:, cols].astype(F32)
        part = part + f * f
        tg[z_slot, :, cols] = (f * tgain[:, cols]).astype(BF16)
    sg_s[:, COLS:COLS + 128] = jnp.sum(part.T, axis=0, keepdims=True)
    part = jnp.zeros((ROWS, 128), F32)
    for i in range(4):
        f = hb[mine, :, i * 128:(i + 1) * 128].astype(F32)
        part = part + f * f
    sg_s[:, COLS + 128:COLS + 256] = jnp.sum(part.T, axis=0, keepdims=True)
    sg_s[:, 0:COLS] = sgain[...]
    sg_r[mine] = sg_s[...]

    def ring_slot(d):
        return (0, 1, 2, 3, 4, 7, 6, 5)[d % 8]

    def z_ref(d, h):
        return tg.at[ring_slot(d), pl.ds(h * 64, 64)]

    def z_send(k):
        d = k // 2
        send(z_ref(8 - d, k % 2), z_ref(7 - d, k % 2), z_ss.at[k], z_rs.at[k], dev_zp)
        send(z_ref(d, 1 - k % 2), z_ref(d + 1, 1 - k % 2), z_ss.at[8 + k], z_rs.at[8 + k], dev_zm)

    def z_got(k):
        up, down = z_ref(-(k // 2) + 7, k % 2), z_ref(k // 2 + 1, 1 - k % 2)
        arrive(up, z_ss.at[k], z_rs.at[k])
        arrive(down, z_ss.at[8 + k], z_rs.at[8 + k])

    def z_step(k):
        z_got(k)
        if k + 2 < 7:
            z_send(k + 2)

    def small_send(i, k, dev):
        slot = ag.order[i]
        send(sg_r.at[slot], sg_r.at[slot], sm_ss.at[k], sm_rs.at[k], dev)

    def small_got(i, k):
        arrive(sg_r.at[ag.order[i]], sm_ss.at[k], sm_rs.at[k])

    def docs_send(d, k, dev):
        ref = docs_z.at[(z + d) % 8]
        send(ref, ref, dc_ss.at[k], dc_rs.at[k], dev)

    def docs_step(k):
        arrive(docs_z.at[(z + 7 - k) % 8], dc_ss.at[k], dc_rs.at[k])
        if k < 3:
            arrive(docs_z.at[(z + 1 + k) % 8], dc_ss.at[4 + k], dc_rs.at[4 + k])
            docs_send(7 - k, k + 1, dev_zp)
            if k < 2:
                docs_send(1 + k, k + 5, dev_zm)
        else:
            send(docs_z, docs_o, dc_ss.at[8], dc_rs.at[8], dev_yl)

    pl.semaphore_wait(barrier, 7)
    small_send(0, 0, dev_yo)
    small_send(0, 1, dev_xp)
    small_send(0, 2, dev_xm)
    ag.begin(0)
    ag.begin(1)
    docs_send(0, 0, dev_zp)
    docs_send(0, 4, dev_zm)
    z_send(0)
    pj_send(0)
    lax.fori_loop(0, 8, w_go, 0)
    z_send(1)
    pj_send(1)
    pj_send(2)
    l_pj = load(pj_h, pj.at[yl], 4)

    entry = lax.broadcasted_iota(jnp.int32, (64, ROWS), 0).astype(F32)
    position = (s * ROWS + lax.broadcasted_iota(jnp.int32, (64, ROWS), 1)).astype(F32)
    angle = position * jnp.exp(-math.log(500000.0) * (2.0 * entry / HEAD_DIM))
    cos_t[...] = jnp.cos(angle)
    sin_t[...] = jnp.sin(angle)

    def process(slots, first=False):
        blocks, w = [], []
        for slot in slots:
            parts = []
            for i in range(4):
                cols = slice(i * 128, (i + 1) * 128)
                f = hb[slot, :, cols].astype(F32)
                parts.append((f * scale_v[...] * sg_r[slot][:, cols]).astype(BF16))
            blocks.append(jnp.concatenate(parts, axis=1))
        n = jnp.concatenate(blocks, axis=1)
        for slot in slots:
            w_got(slot)
            w.append(wkv[slot].reshape(128, COLS))
        kv = nt_dot(jnp.concatenate(w, axis=1), n)
        for core in range(2):
            w = jnp.concatenate([wq[slot, core] for slot in slots], axis=0)
            q = jnp.dot(n, w, preferred_element_type=F32)
            k = kv[core * 64:core * 64 + 64]
            q_acc[core] = q if first else q_acc[core] + q
            kv_acc[core] = k if first else kv_acc[core] + k

    small_got(1, 1)
    small_send(1, 3, dev_xp)
    small_got(2, 2)
    small_got(3, 0)
    small_send(3, 4, dev_xp)
    small_send(3, 5, dev_xm)
    docs_step(0)
    ag.near_relay()
    small_got(6, 3)
    docs_step(1)
    small_got(4, 4)
    small_send(4, 6, dev_xp)
    small_got(5, 5)
    ag.near_rest()
    ag.opp_half(0)
    z_step(0)
    pj_send(3)
    small_got(7, 6)
    sums = sg_r[0][:, COLS:COLS + 256]
    for i in range(1, 8):
        sums = sums + sg_r[i][:, COLS:COLS + 256]
    sum_s[...] = sums
    send(sum_s, sum_r, x_ss.at[2], x_rs.at[2], sib)
    docs_step(2)
    ag.opp_half(1)
    arrive(sum_r, x_ss.at[2], x_rs.at[2])
    sums = sum_s[...] + sum_r[...]
    ts_v[...] = jnp.broadcast_to(lax.rsqrt(sums[:, 0:128] / DT + 1e-05), (ROWS, 128)).T
    scale_v[...] = jnp.broadcast_to(lax.rsqrt(sums[:, 128:256] / DS + 1e-05), (ROWS, 128)).T
    docs_step(3)
    z_step(1)
    ag.onear_a()
    l_wq.wait()
    process([mine] + ag.near, True)
    ag.onear_b()
    z_step(2)
    ag.far_step()
    process([ag.opp, ag.far[0]])
    ag.onear_rest()
    process(ag.onear)
    z_step(3)
    ag.ofar_step()
    process([ag.far[1]])
    send(kv_acc.at[1 - c], kv_in, x_ss.at[3], x_rs.at[3], sib)
    send(q_acc.at[1 - c], q_in, x_ss.at[4], x_rs.at[4], sib)
    arrive(kv_in, x_ss.at[3], x_rs.at[3])

    row = lax.broadcasted_iota(jnp.int32, (64, 64), 0)
    col = lax.broadcasted_iota(jnp.int32, (64, 64), 1)
    take = ((row >> 3) & 1) * 32 + (row & 7) * 4 + (row >> 4)
    pick = jnp.where(col == take, 1.0, 0.0).astype(BF16)
    kv_mine = (kv_acc[c] + kv_in[...]).astype(BF16)
    kvx_s[...] = jnp.dot(pick, kv_mine, preferred_element_type=F32).astype(BF16).reshape(4, 16, 128)
    kvx_r[t] = kvx_s[t // 4]

    def kvx(k):
        to = (t + k) % 16
        return copy(kvx_s.at[to // 4], kvx_r.at[t], kx_ss.at[k], kx_rs.at[k], (s, to))

    def kvx_go(k, carry):
        kvx(k).start()
        return carry

    def kvx_got(k, carry):
        arrive(kvx_r.at[(t + 16 - k) % 16], kx_ss.at[k], kx_rs.at[k])
        return carry

    def kvx_end(k, carry):
        kvx(k).wait_send()
        return carry

    lax.fori_loop(1, 16, kvx_go, 0)
    lax.fori_loop(0, 8, wo_fetch, 0)
    lax.fori_loop(0, 8, wo_go, 0)
    z_step(4)

    cos2 = jnp.concatenate([cos_t[...], cos_t[...]], axis=0).T
    sin2 = jnp.concatenate([-sin_t[...], sin_t[...]], axis=0).T
    arrive(q_in, x_ss.at[4], x_rs.at[4])
    q_mine = q_acc[c] + q_in[...]
    for h in range(2):
        qh = q_mine[:, h * 128:(h + 1) * 128]
        turned = qh * cos2 + pltpu.roll(qh, 64, 1) * sin2
        q_v[h] = (turned * HEAD_DIM ** (-0.5)).astype(BF16)

    lax.fori_loop(1, 16, kvx_got, 0)
    both = kvx_r[...].astype(F32).reshape(16, 2, 8, ROWS)
    k_raw = both[:, 0].reshape(HEAD_DIM, ROWS)
    v_raw = both[:, 1].reshape(HEAD_DIM, ROWS)
    first, second = k_raw[0:64], k_raw[64:128]
    k_rot = jnp.concatenate(
        [first * cos_t[...] - second * sin_t[...], second * cos_t[...] + first * sin_t[...]], axis=0
    )
    kv_own[0] = k_rot.astype(BF16)
    kv_own[1] = v_raw.T.astype(BF16)
    kv_r[0, 0] = kv_own[0]
    kv_r[1, 0] = kv_own[1]

    def kv_copy(k):
        return copy(kv_own.at[c], kv_r.at[c, k], kv_ss.at[k], kv_rs.at[k], ((s + k) % 16, t))

    def kv_fwd(k):
        return copy(kv_r.at[c, k], kv_r.at[c, k], kf_ss.at[k], kf_rs.at[k], sib)

    def kv_go(k):
        @pl.when(s + k < 16)
        def _():
            kv_copy(k).start()

    def kv_mid(k):
        @pl.when(s >= k)
        def _():
            arrive(kv_r.at[c, k], kv_ss.at[k], kv_rs.at[k])
            kv_fwd(k).start()

    def kv_got(k, carry):
        @pl.when(s >= k)
        def _():
            arrive(kv_r.at[1 - c, k], kf_ss.at[k], kf_rs.at[k])
        return carry

    def kv_end(k, carry):
        @pl.when(s >= k)
        def _():
            kv_fwd(k).wait_send()

        @pl.when(s + k < 16)
        def _():
            kv_copy(k).wait_send()
        return carry

    arrive(docs_o, dc_ss.at[8], dc_rs.at[8])
    for k in (4, 5, 3, 6, 8, 7, 2, 1):
        kv_go(k)

    def docs_back(j):
        at = (z + 8 - j) % 8
        return jnp.where(z >= j, docs_z[at], jnp.where(yl == 1, docs_o[at], -1))

    key_doc = jnp.concatenate([docs_back(j) for j in range(BACK + 1)], axis=1)
    row_doc = jnp.broadcast_to(docs[...].astype(F32), (ROWS, ROWS)).T[:, 0:1].astype(jnp.int32)
    wide = (ROWS, (BACK + 1) * ROWS)
    row_at = lax.broadcasted_iota(jnp.int32, wide, 0)
    key_at = lax.broadcasted_iota(jnp.int32, wide, 1)
    allowed = (key_doc == row_doc) & ((key_at >= ROWS) | (key_at <= row_at))
    bias[...] = jnp.where(allowed, 0.0, -1e30)

    class Reduce:
        def __init__(self, y_order, own, sib_s, sib_r, x2, ra, rb, xp, xm, fm, fp, ys, yr, fin, ss, rs):
            self.own, self.sib_s, self.sib_r = own, sib_s, sib_r
            self.x2, self.ra, self.rb, self.xp, self.xm, self.fm, self.fp = x2, ra, rb, xp, xm, fm, fp
            self.ys, self.yr, self.fin, self.ss, self.rs = ys, yr, fin, ss, rs
            self.y_order = y_order
            self.x_order = (xf_, xp_, xm_, x)

        def go(self, src, dst, k, dev):
            send(src, dst, self.ss.at[k], self.rs.at[k], dev)

        def got(self, dst, k):
            arrive(dst, self.ss.at[k], self.rs.at[k])

        def slot(self, k, i):
            return self.y_order[i] * 4 + self.x_order[k]

        def to_sib(self, k, i):
            slot = self.slot(k, i)
            self.go(self.sib_s.at[slot], self.sib_r.at[slot], k * 2 + i, sib)

        def sib_got(self, k, i):
            if self.sib_r is not None:
                self.got(self.sib_r.at[self.slot(k, i)], k * 2 + i)

        def pair(self, k, i, h):
            slot, rows = self.slot(k, i), slice(h * 64, h * 64 + 64)
            value = self.own[slot, rows]
            return value if self.sib_r is None else value + self.sib_r[slot, rows].astype(F32)

        def far(self, i):
            self.sib_got(0, i)
            self.x2[i, 0:64] = self.pair(0, i, 0).astype(BF16)
            self.go(self.x2.at[i, pl.ds(0, 64)], self.ra.at[i], 8 + i, dev_xp)
            self.x2[i, 64:128] = self.pair(0, i, 1).astype(BF16)
            self.go(self.x2.at[i, pl.ds(64, 64)], self.rb.at[i], 10 + i, dev_xm)

        def near(self, i):
            self.sib_got(1, i)
            self.xp[i, 64:128] = self.pair(1, i, 1).astype(BF16)
            self.go(self.xp.at[i, pl.ds(64, 64)], self.fm.at[i, pl.ds(64, 64)], 12 + i, dev_xp)
            self.sib_got(2, i)
            self.xm[i, 0:64] = self.pair(2, i, 0).astype(BF16)
            self.go(self.xm.at[i, pl.ds(0, 64)], self.fp.at[i, pl.ds(0, 64)], 14 + i, dev_xm)

        def relay(self, i):
            self.got(self.ra.at[i], 8 + i)
            self.xp[i, 0:64] = (self.pair(1, i, 0) + self.ra[i].astype(F32)).astype(BF16)
            self.go(self.xp.at[i, pl.ds(0, 64)], self.fm.at[i, pl.ds(0, 64)], 16 + i, dev_xp)
            self.got(self.rb.at[i], 10 + i)
            self.xm[i, 64:128] = (self.pair(2, i, 1) + self.rb[i].astype(F32)).astype(BF16)
            self.go(self.xm.at[i, pl.ds(64, 64)], self.fp.at[i, pl.ds(64, 64)], 18 + i, dev_xm)

        def join(self, i, h):
            rows, at = slice(h * 64, h * 64 + 64), pl.ds(h * 64, 64)
            if h == 0:
                self.sib_got(3, i)
            self.got(self.fm.at[i, at], (16, 12)[h] + i)
            self.got(self.fp.at[i, at], (14, 18)[h] + i)
            return self.pair(3, i, h) + self.fm[i, rows].astype(F32) + self.fp[i, rows].astype(F32)

        def to_opp(self, h):
            at = pl.ds(h * 64, 64)
            return copy(self.ys.at[at], self.yr.at[at], self.ss.at[20 + h], self.rs.at[20 + h], dev_yo)

        def join_other(self):
            for h in range(2):
                self.ys[h * 64:h * 64 + 64] = self.join(0, h).astype(BF16)
                self.to_opp(h).start()

        def join_mine(self):
            for h in range(2):
                self.fin[h * 64:h * 64 + 64] = self.join(1, h)

        def end(self):
            for h in range(2):
                self.to_opp(h).wait_send()

        def last(self, h):
            rows = slice(h * 64, h * 64 + 64)
            self.got(self.yr.at[pl.ds(h * 64, 64)], 20 + h)
            return self.fin[rows] + self.yr[rows].astype(F32)

    rt = Reduce((yl, 1 - yl), t_own, t_sib_s, t_sib_r, t_x2, t_ra, t_rb, t_xp, t_xm, t_fm, t_fp, None, None, None, t_ss, t_rs)

    def t3(i, h):
        at = pl.ds(h * 64, 64)
        dev = (yl * 8 + (z + turn) % 8, rt.y_order[i] * 8 + z)
        return copy(t3_s.at[i, at], t3_r.at[yh, at], t3_ss.at[i * 2 + h], t3_rs.at[yh * 2 + h], dev)

    def t3_stays(i):
        return stays & (rt.y_order[i] == yh)

    def t_place(i):
        for h in range(2):
            rows = slice(h * 64, h * 64 + 64)
            t3_s[i, rows] = rt.join(i, h).astype(BF16)

            @pl.when(t3_stays(i))
            def _():
                t3_r[yh, rows] = t3_s[i, rows]

            @pl.when(jnp.logical_not(t3_stays(i)))
            def _():
                t3(i, h).start()

    z_step(5)
    z_step(6)

    def products(core, y_, k, width):
        rows = tg[pl.ds(core * 4, 4), :, k * width:(k + 1) * width].reshape(4 * ROWS, width)
        return jnp.dot(rows, pj[y_, k * width:(k + 1) * width], preferred_element_type=F32).reshape(4, ROWS, COLS)

    l_pj.wait()
    first = pl.ds(yl * 4, 4)
    t_sib_s[first] = products(1 - c, yl, 0, 1024).astype(BF16)
    for k in range(4):
        rt.to_sib(k, 0)
    t_own[first] = products(c, yl, 0, 1024)
    rt.far(0)
    rt.near(0)

    other = pl.ds((1 - yl) * 4, 4)
    for k in range(4):
        arrive(pj.at[1 - yl, pl.ds(k * 256, 256)], p_ss.at[k], p_rs.at[k])
        theirs = products(1 - c, 1 - yl, k, 256)
        if k == 0:
            t_part[...] = theirs
        elif k < 3:
            t_part[...] += theirs
        else:
            t_sib_s[other] = (t_part[...] + theirs).astype(BF16)
            for j in range(4):
                rt.to_sib(j, 1)
        if k == 0:
            t_own[other] = products(c, 1 - yl, k, 256)
        else:
            t_own[other] += products(c, 1 - yl, k, 256)
        if k == 1:
            rt.relay(0)
    rt.far(1)
    rt.near(1)
    t_place(0)
    for k in range(1, BACK + 1):
        kv_mid(k)
    rt.relay(1)

    lax.fori_loop(1, BACK + 1, kv_got, 0)
    keys = jnp.concatenate([kv_r[0, j] for j in range(BACK + 1)], axis=1)
    values = kv_r[1].reshape((BACK + 1) * ROWS, HEAD_DIM)
    for h in range(2):
        scores = jnp.dot(q_v[h], keys, preferred_element_type=F32)
        scores = scores + bias[...]
        probs = jnp.exp(scores - jnp.max(scores, axis=1, keepdims=True))
        total = jnp.sum(probs, axis=1, keepdims=True)
        acc = jnp.dot(probs.astype(BF16), values, preferred_element_type=F32)
        attn_v[c * 2 + h] = (acc / total).astype(BF16)
        send(attn_v.at[c * 2 + h], attn_v.at[c * 2 + h], x_ss.at[5 + h], x_rs.at[5 + h], sib)
    lax.fori_loop(0, 8, wo_got, 0)

    ro = Reduce((yo_, yh), o_own, None, None, o_x2, o_ra, o_rb, o_xp, o_xm, o_fm, o_fp, o_ys, o_yr, o_fin, o_ss, o_rs)

    for h in range(2):
        arrive(attn_v.at[2 - 2 * c + h], x_ss.at[5 + h], x_rs.at[5 + h])
    attn = jnp.concatenate([attn_v[i] for i in range(4)], axis=1)

    def out_block(k, i):
        slot = ro.slot(k, i)
        o_own[slot] = jnp.dot(attn, wo[slot].reshape(COLS, COLS), preferred_element_type=F32)

    out_block(0, 0)
    ro.far(0)
    out_block(1, 0)
    out_block(2, 0)
    ro.near(0)
    t_place(1)
    out_block(0, 1)
    ro.relay(0)
    ro.far(1)
    out_block(1, 1)
    out_block(2, 1)
    ro.near(1)
    out_block(3, 0)
    out_block(3, 1)
    ro.relay(1)

    ro.join_other()
    ro.join_mine()

    early = list(started)
    started.clear()

    def before_end():
        for one in early:
            one.wait_send()
        lax.fori_loop(0, 8, w_end, 0)
        lax.fori_loop(0, 8, wo_end, 0)
        lax.fori_loop(1, 16, kvx_end, 0)
        lax.fori_loop(1, BACK + 1, kv_end, 0)
        ro.end()
        for i in range(2):

            @pl.when(jnp.logical_not(t3_stays(i)))
            def _():
                t3(i, 0).wait_send()
                t3(i, 1).wait_send()

    dg = Gather(db, dg_ss, dg_rs)
    for h in range(2):
        rows = slice(h * 64, h * 64 + 64)
        mixed = hb[mine, rows].astype(F32) + ro.last(h)
        out_s[rows] = mixed.astype(BF16)

        for p in range(2):

            @pl.when(jnp.logical_not(stays & (yh == p)))
            def _():
                arrive(t3_r.at[p, pl.ds(h * 64, 64)], t3_ss.at[h], t3_rs.at[p * 2 + h])

        target = t3_r[0, rows].astype(F32) + t3_r[1, rows].astype(F32)
        target = target * jnp.concatenate([ts_v[rows]] * 4, axis=1)
        difference = mixed - target
        db[mine, rows] = difference.astype(BF16)
        dg.begin(h)
        squares = difference * difference
        l_v[rows] = (
            squares[:, 0:128] + squares[:, 128:256] + squares[:, 256:384] + squares[:, 384:512]
        )
    l_s[...] = jnp.sum(l_v[...].T, axis=0, keepdims=True)
    l_r[t] = l_s[...]

    def loss(k):
        return copy(l_s, l_r.at[t], l_ss.at[k], l_rs.at[k], (s, (t + k) % 16))

    def loss_go(k, carry):
        loss(k).start()
        return carry

    def loss_got(k, carry):
        arrive(l_r.at[(t + 16 - k) % 16], l_ss.at[k], l_rs.at[k])
        return carry

    def loss_end(k, carry):
        loss(k).wait_send()
        return carry

    lax.fori_loop(1, 16, loss_go, 0)

    def add_grad(slots, first=False):
        d = jnp.concatenate([db[slot] for slot in slots], axis=1)
        for core in range(2):
            w = jnp.concatenate([wo[slot, core] for slot in slots], axis=1)
            g = nt_dot(d, w)
            g_acc[core] = g if first else g_acc[core] + g

    dg.near_relay()
    dg.opp_half(0)
    dg.near_rest()
    add_grad([mine] + dg.near, True)
    dg.opp_half(1)
    dg.onear_a()
    dg.onear_b()
    dg.far_step()
    add_grad([dg.opp, dg.far[0]])
    before_end()
    dg.onear_rest()
    add_grad(dg.onear)
    lax.fori_loop(1, 16, loss_got, 0)
    loss_sum = l_r[0]
    for i in range(1, 16):
        loss_sum = loss_sum + l_r[i]
    out_l[...] = loss_sum / DS
    dg.ofar_step()
    add_grad([dg.far[1]])
    send(g_acc.at[1 - c], g_in, x_ss.at[7], x_rs.at[7], sib)
    arrive(g_in, x_ss.at[7], x_rs.at[7])
    out_g[...] = (g_acc[c] + g_in[...]).astype(BF16)

    flush()
    lax.fori_loop(1, 16, loss_end, 0)


def reduce_buffers():
    block = (ROWS, COLS)
    return [
        pltpu.VMEM((2, 64, COLS), BF16),
        pltpu.VMEM((2, 64, COLS), BF16),
        pltpu.VMEM((2,) + block, BF16),
        pltpu.VMEM((2,) + block, BF16),
        pltpu.VMEM((2,) + block, BF16),
        pltpu.VMEM((2,) + block, BF16),
        pltpu.VMEM(block, BF16),
        pltpu.VMEM(block, BF16),
        pltpu.VMEM(block, F32),
    ]


def on_device(
    teacher_hidden, teacher_gain, projector, student_hidden, student_gain,
    query_weight, kv_weight, out_weight, doc_ids,
):
    block = (ROWS, COLS)
    hbm = pl.BlockSpec(memory_space=pltpu.HBM)
    vmem = pl.BlockSpec(memory_space=pltpu.VMEM)
    dma = pltpu.SemaphoreType.DMA
    out_s, out_l, out_g = pl.pallas_call(
        body,
        out_shape=(
            jax.ShapeDtypeStruct(block, BF16),
            jax.ShapeDtypeStruct((1, ROWS), F32),
            jax.ShapeDtypeStruct((ROWS, 256), BF16),
        ),
        in_specs=[hbm] * 9,
        out_specs=(vmem, vmem, vmem),
        scratch_shapes=[
            pltpu.VMEM((1, 1024), F32),
            pltpu.VMEM((1, COLS), F32),
            pltpu.VMEM((1, ROWS), jnp.int32),
            pltpu.VMEM((ROWS, 1024), BF16),
            pltpu.VMEM((8, ROWS, 1024), BF16),
            pltpu.VMEM((2, 1024, COLS), BF16),
            pltpu.VMEM((8, 2, COLS, 256), BF16),
            pltpu.VMEM((8, 2, 2, 32, COLS), BF16),
            pltpu.VMEM((8, 2, 256, COLS), BF16),
            pltpu.VMEM((64, ROWS), F32),
            pltpu.VMEM((64, ROWS), F32),
            pltpu.VMEM((8,) + block, BF16),
            pltpu.VMEM((1, 768), F32),
            pltpu.VMEM((8, 1, 768), F32),
            pltpu.VMEM((1, 256), F32),
            pltpu.VMEM((1, 256), F32),
            pltpu.VMEM((ROWS, 128), F32),
            pltpu.VMEM((2, ROWS, 256), F32),
            pltpu.VMEM((ROWS, 256), F32),
            pltpu.VMEM((2, 64, ROWS), F32),
            pltpu.VMEM((64, ROWS), F32),
            pltpu.VMEM((4, 16, ROWS), BF16),
            pltpu.VMEM((16, 16, ROWS), BF16),
            pltpu.VMEM((2, ROWS, HEAD_DIM), BF16),
            pltpu.VMEM((2, BACK + 1, ROWS, HEAD_DIM), BF16),
            pltpu.VMEM((8, 1, ROWS), jnp.int32),
            pltpu.VMEM((8, 1, ROWS), jnp.int32),
            pltpu.VMEM((2, ROWS, HEAD_DIM), BF16),
            pltpu.VMEM((4, ROWS, HEAD_DIM), BF16),
            pltpu.VMEM((ROWS, (BACK + 1) * ROWS), F32),
            pltpu.VMEM((8,) + block, F32),
            pltpu.VMEM((4,) + block, F32),
            pltpu.VMEM((8,) + block, F32),
            pltpu.VMEM((2,) + block, BF16),
            pltpu.VMEM((8,) + block, BF16),
            pltpu.VMEM((8,) + block, BF16),
            pltpu.VMEM((2,) + block, BF16),
            *reduce_buffers()[:6],
            *reduce_buffers(),
            pltpu.VMEM((2,) + block, BF16),
            pltpu.VMEM((2,) + block, BF16),
            pltpu.VMEM((ROWS, 128), F32),
            pltpu.VMEM((8,) + block, BF16),
            pltpu.VMEM((2, ROWS, 256), F32),
            pltpu.VMEM((ROWS, 256), F32),
            pltpu.VMEM((ROWS, 128), F32),
            pltpu.VMEM((1, ROWS), F32),
            pltpu.VMEM((16, 1, ROWS), F32),
            dma((10,)),
            *[dma((8,)) for _ in range(10)],
            dma((16,)), dma((16,)), dma((8,)), dma((8,)),
            dma((24,)), dma((24,)), dma((24,)), dma((24,)),
            dma((16,)), dma((16,)), dma((16,)), dma((16,)),
            dma((9,)), dma((9,)), dma((9,)), dma((9,)), dma((9,)), dma((9,)),
            dma((24,)), dma((24,)), dma((24,)), dma((24,)),
            dma((4,)), dma((4,)),
            dma((16,)), dma((16,)),
        ],
        compiler_params=pltpu.CompilerParams(
            collective_id=0, has_side_effects=True, vmem_limit_bytes=40 * 1024 * 1024
        ),
    )(
        *(
            pltpu.with_memory_space_constraint(one, pltpu.HBM)
            for one in (
                teacher_hidden, teacher_gain.reshape(1, -1), projector, student_hidden,
                student_gain.reshape(1, -1), query_weight.reshape(8, 2, COLS, 256), jnp.transpose(kv_weight, (0, 2, 1)),
                out_weight, doc_ids.reshape(1, -1),
            )
        )
    )
    return out_s, out_l.reshape(ROWS), out_g


def solution(mesh):
    in_specs = (
        P("seq", "tensor"),
        P("tensor"),
        P("tensor", "seq"),
        P("seq", "tensor"),
        P("tensor"),
        P(None, "tensor"),
        P(None, None, "tensor"),
        P("tensor", None),
        P("seq"),
    )
    out_specs = (P("seq", "tensor"), P("seq"), P("seq", "tensor"))
    return jax.shard_map(
        on_device, mesh=mesh, in_specs=in_specs, out_specs=out_specs, check_vma=False
    )
```

```python
import math

import jax
import jax.numpy as jnp
from jax import lax
from jax.experimental import pallas as pl
from jax.experimental.pallas import tpu as pltpu
from jax.sharding import PartitionSpec as P

DT = 16384
DS = 8192
HEAD_DIM = 128
HEADS = 32
KV_HEADS = 4
ROWS = 128
COLS = 512
BACK = 8
F32 = jnp.float32
BF16 = jnp.bfloat16
MESH = pl.DeviceIdType.MESH
NT = (((1,), (1,)), ((), ()))


def nt_dot(a, b):
    return lax.dot_general(a, b, NT, preferred_element_type=F32)


def body(
    th_h, tgain_h, pj_h, sh_h, sgain_h, wq_h, wkv_h, wo_h, docs_h,
    out_s, out_l, out_g,
    tgain, sgain, docs, th_v, tg, pj, wq, wkv, wo, cos_t, sin_t,
    hb, sg_s, sg_r, sum_s, sum_r, scale_v, q_acc, q_in, kv_acc, kv_in,
    kvx_s, kvx_r, kv_own, kv_r, docs_z, docs_o, q_v, attn_v, bias,
    t_own, t_part, o_own, o_x2, t_sib_s, t_sib_r, t_x2, t_ra, t_rb, t_xp, t_xm, t_fm, t_fp,
    o_ra, o_rb, o_xp, o_xm, o_fm, o_fp, o_ys, o_yr, o_fin,
    t3_s, t3_r, ts_v, db, g_acc, g_in, l_v, l_s, l_r,
    load_sem, w_load, w_ss, w_rs, v_load, v_ss, v_rs, u_ss, u_rs, x_ss, x_rs, z_ss, z_rs, p_ss, p_rs,
    ag_ss, ag_rs, dg_ss, dg_rs, sm_ss, sm_rs, kx_ss, kx_rs, kv_ss, kv_rs, kf_ss, kf_rs, dc_ss, dc_rs,
    t_ss, t_rs, o_ss, o_rs, t3_ss, t3_rs, l_ss, l_rs,
):
    s = lax.axis_index("seq")
    t = lax.axis_index("tensor")
    yl, z = s // 8, s % 8
    yh, x, c = t // 8, (t // 2) % 4, t % 2

    def tid(y_, x_, c_):
        return y_ * 8 + x_ * 2 + c_

    xp_, xm_ = (x + 1) % 4, (x + 3) % 4
    xf_ = (x + 2) % 4
    yo_ = 1 - yh
    sib = (s, tid(yh, x, 1 - c))
    dev_xp = (s, tid(yh, xp_, c))
    dev_xm = (s, tid(yh, xm_, c))
    dev_yo = (s, tid(yo_, x, c))
    dev_zp = (yl * 8 + (z + 1) % 8, t)
    dev_zm = (yl * 8 + (z + 7) % 8, t)
    dev_yl = ((1 - yl) * 8 + z, t)
    turn = jnp.where(c == 0, x, jnp.where(x == 0, 4, 8 - x))
    stays = (z == 0) & (x == 0) & (c == 0)

    started = []

    def copy(src, dst, ss, rs, dev):
        return pltpu.make_async_remote_copy(
            src_ref=src, dst_ref=dst, send_sem=ss, recv_sem=rs, device_id=dev, device_id_type=MESH
        )

    def send(src, dst, ss, rs, dev):
        one = copy(src, dst, ss, rs, dev)
        one.start()
        started.append(one)

    def flush():
        for one in started:
            one.wait_send()
        started.clear()

    def arrive(dst, ss, rs):
        copy(dst, dst, ss, rs, sib).wait_recv()

    def load(src, dst, k):
        one = pltpu.make_async_copy(src, dst, load_sem.at[k])
        one.start()
        return one

    l_th = load(th_h, th_v, 0)
    mine = yh * 4 + x
    l_sh = load(sh_h, hb.at[mine], 1)
    l_small = [load(tgain_h, tgain, 7), load(sgain_h, sgain, 8), load(docs_h, docs, 9)]

    def wkv_part(j, core):
        return wkv_h.at[:, :, pl.ds(pl.multiple_of((j * 2 + core) * COLS, COLS), COLS)]

    def wkv_load(j):
        return pltpu.make_async_copy(wkv_part(j, c), wkv.at[j, c], v_load.at[j])

    def wkv_go(j, carry):
        wkv_load(j).start()
        return carry

    def wo_part(j, core):
        return wo_h.at[:, pl.ds(pl.multiple_of((j * 2 + core) * COLS, COLS), COLS)]

    def wo_load(j):
        return pltpu.make_async_copy(wo_part(j, c), wo.at[j, c], w_load.at[j])

    def wo_send(j):
        return copy(wo_part(j, 1 - c), wo.at[j, c], w_ss.at[j], w_rs.at[j], sib)

    def wo_fetch(j, carry):
        wo_load(j).start()
        return carry

    def wo_go(j, carry):
        wo_send(j).start()
        return carry

    def wo_got(j, carry):
        wo_load(j).wait()
        arrive(wo.at[j, 1 - c], w_ss.at[j], w_rs.at[j])
        return carry

    def wo_end(j, carry):
        wo_send(j).wait_send()
        return carry

    lax.fori_loop(0, 8, wkv_go, 0)
    l_wq = load(wq_h.at[:, c], wq.at[:, c], 3)

    kv_r[...] = jnp.zeros(kv_r.shape, BF16)

    barrier = pltpu.get_barrier_semaphore()
    for dev in (sib, dev_xp, dev_xm, dev_yo, dev_zp, dev_zm, dev_yl):
        pl.semaphore_signal(barrier, inc=1, device_id=dev, device_id_type=MESH)

    class Gather:
        def __init__(self, buf, ss, rs):
            self.buf, self.ss, self.rs = buf, ss, rs
            self.near = [yh * 4 + xm_, yh * 4 + xp_]
            self.opp = yo_ * 4 + x
            self.onear = [yo_ * 4 + xm_, yo_ * 4 + xp_]
            self.far = [yh * 4 + xf_, yo_ * 4 + xf_]
            self.order = [mine] + self.near + [self.opp] + self.onear + self.far

        def part(self, slot, h):
            return self.buf.at[slot, pl.ds(h * 64, 64)]

        def half(self, slot, h, k, dev):
            part = self.part(slot, h)
            send(part, part, self.ss.at[k], self.rs.at[k], dev)

        def got_half(self, slot, h, k):
            arrive(self.part(slot, h), self.ss.at[k], self.rs.at[k])

        def begin(self, h):
            self.half(mine, h, 0 + h, dev_yo)
            self.half(mine, h, 2 + h, dev_xp)
            self.half(mine, h, 4 + h, dev_xm)

        def near_relay(self):
            self.got_half(self.near[0], 0, 2)
            self.half(self.near[0], 0, 6, dev_xp)
            self.got_half(self.near[1], 1, 5)
            self.half(self.near[1], 1, 7, dev_xm)

        def near_rest(self):
            self.got_half(self.near[0], 1, 3)
            self.got_half(self.near[1], 0, 4)

        def opp_half(self, h):
            self.got_half(self.opp, h, 0 + h)
            self.half(self.opp, h, 8 + h, dev_xp)
            self.half(self.opp, h, 10 + h, dev_xm)

        def onear_a(self):
            self.got_half(self.onear[0], 0, 8)
            self.half(self.onear[0], 0, 12, dev_xp)

        def onear_b(self):
            self.got_half(self.onear[1], 1, 11)
            self.half(self.onear[1], 1, 13, dev_xm)

        def onear_rest(self):
            self.got_half(self.onear[0], 1, 9)
            self.got_half(self.onear[1], 0, 10)

        def far_step(self):
            self.got_half(self.far[0], 0, 6)
            self.got_half(self.far[0], 1, 7)

        def ofar_step(self):
            self.got_half(self.far[1], 0, 12)
            self.got_half(self.far[1], 1, 13)

    def pj_send(k):
        rows = pl.ds(k * 256, 256)
        send(pj_h.at[rows], pj.at[yl, rows], p_ss.at[k], p_rs.at[k], dev_yl)

    def wkv_send(j):
        return copy(wkv_part(j, 1 - c), wkv.at[j, c], v_ss.at[j], v_rs.at[j], sib)

    def wq_send(j):
        return copy(wq_h.at[j, 1 - c], wq.at[j, c], u_ss.at[j], u_rs.at[j], sib)

    def w_go(j, carry):
        wkv_send(j).start()
        wq_send(j).start()
        return carry

    def w_end(j, carry):
        wkv_send(j).wait_send()
        wq_send(j).wait_send()
        return carry

    def w_got(slot):
        wkv_load(slot).wait()
        arrive(wkv.at[slot, 1 - c], v_ss.at[slot], v_rs.at[slot])
        arrive(wq.at[slot, 1 - c], u_ss.at[slot], u_rs.at[slot])

    ag = Gather(hb, ag_ss, ag_rs)
    l_sh.wait()

    z_slot = 0
    l_th.wait()
    for one in l_small:
        one.wait()
    docs_z[z] = docs[...]
    part = jnp.zeros((ROWS, 128), F32)
    for i in range(8):
        cols = slice(i * 128, (i + 1) * 128)
        f = th_v[:, cols].astype(F32)
        part = part + f * f
        tg[z_slot, :, cols] = (f * tgain[:, cols]).astype(BF16)
    sg_s[:, COLS:COLS + 128] = jnp.sum(part.T, axis=0, keepdims=True)
    part = jnp.zeros((ROWS, 128), F32)
    for i in range(4):
        f = hb[mine, :, i * 128:(i + 1) * 128].astype(F32)
        part = part + f * f
    sg_s[:, COLS + 128:COLS + 256] = jnp.sum(part.T, axis=0, keepdims=True)
    sg_s[:, 0:COLS] = sgain[...]
    sg_r[mine] = sg_s[...]

    def ring_slot(d):
        return (0, 1, 2, 3, 4, 7, 6, 5)[d % 8]

    def z_ref(d, h):
        return tg.at[ring_slot(d), pl.ds(h * 64, 64)]

    def z_send(k):
        d = k // 2
        send(z_ref(8 - d, k % 2), z_ref(7 - d, k % 2), z_ss.at[k], z_rs.at[k], dev_zp)
        send(z_ref(d, 1 - k % 2), z_ref(d + 1, 1 - k % 2), z_ss.at[8 + k], z_rs.at[8 + k], dev_zm)

    def z_got(k):
        up, down = z_ref(-(k // 2) + 7, k % 2), z_ref(k // 2 + 1, 1 - k % 2)
        arrive(up, z_ss.at[k], z_rs.at[k])
        arrive(down, z_ss.at[8 + k], z_rs.at[8 + k])

    def z_step(k):
        z_got(k)
        if k + 2 < 7:
            z_send(k + 2)

    def small_send(i, k, dev):
        slot = ag.order[i]
        send(sg_r.at[slot], sg_r.at[slot], sm_ss.at[k], sm_rs.at[k], dev)

    def small_got(i, k):
        arrive(sg_r.at[ag.order[i]], sm_ss.at[k], sm_rs.at[k])

    def docs_send(d, k, dev):
        ref = docs_z.at[(z + d) % 8]
        send(ref, ref, dc_ss.at[k], dc_rs.at[k], dev)

    def docs_step(k):
        arrive(docs_z.at[(z + 7 - k) % 8], dc_ss.at[k], dc_rs.at[k])
        if k < 3:
            arrive(docs_z.at[(z + 1 + k) % 8], dc_ss.at[4 + k], dc_rs.at[4 + k])
            docs_send(7 - k, k + 1, dev_zp)
            if k < 2:
                docs_send(1 + k, k + 5, dev_zm)
        else:
            send(docs_z, docs_o, dc_ss.at[8], dc_rs.at[8], dev_yl)

    pl.semaphore_wait(barrier, 7)
    small_send(0, 0, dev_yo)
    small_send(0, 1, dev_xp)
    small_send(0, 2, dev_xm)
    ag.begin(0)
    ag.begin(1)
    docs_send(0, 0, dev_zp)
    docs_send(0, 4, dev_zm)
    z_send(0)
    pj_send(0)
    lax.fori_loop(0, 8, w_go, 0)
    z_send(1)
    pj_send(1)
    pj_send(2)
    l_pj = load(pj_h, pj.at[yl], 4)

    entry = lax.broadcasted_iota(jnp.int32, (64, ROWS), 0).astype(F32)
    position = (s * ROWS + lax.broadcasted_iota(jnp.int32, (64, ROWS), 1)).astype(F32)
    angle = position * jnp.exp(-math.log(500000.0) * (2.0 * entry / HEAD_DIM))
    cos_t[...] = jnp.cos(angle)
    sin_t[...] = jnp.sin(angle)

    def process(slots, first=False):
        blocks, w = [], []
        for slot in slots:
            parts = []
            for i in range(4):
                cols = slice(i * 128, (i + 1) * 128)
                f = hb[slot, :, cols].astype(F32)
                parts.append((f * scale_v[...] * sg_r[slot][:, cols]).astype(BF16))
            blocks.append(jnp.concatenate(parts, axis=1))
        n = jnp.concatenate(blocks, axis=1)
        for slot in slots:
            w_got(slot)
            w.append(wkv[slot].reshape(128, COLS))
        kv = nt_dot(jnp.concatenate(w, axis=1), n)
        for core in range(2):
            w = jnp.concatenate([wq[slot, core] for slot in slots], axis=0)
            q = jnp.dot(n, w, preferred_element_type=F32)
            k = kv[core * 64:core * 64 + 64]
            q_acc[core] = q if first else q_acc[core] + q
            kv_acc[core] = k if first else kv_acc[core] + k

    small_got(1, 1)
    small_send(1, 3, dev_xp)
    small_got(2, 2)
    small_got(3, 0)
    small_send(3, 4, dev_xp)
    small_send(3, 5, dev_xm)
    docs_step(0)
    ag.near_relay()
    small_got(6, 3)
    docs_step(1)
    small_got(4, 4)
    small_send(4, 6, dev_xp)
    small_got(5, 5)
    ag.near_rest()
    ag.opp_half(0)
    z_step(0)
    pj_send(3)
    small_got(7, 6)
    sums = sg_r[0][:, COLS:COLS + 256]
    for i in range(1, 8):
        sums = sums + sg_r[i][:, COLS:COLS + 256]
    sum_s[...] = sums
    send(sum_s, sum_r, x_ss.at[2], x_rs.at[2], sib)
    docs_step(2)
    ag.opp_half(1)
    arrive(sum_r, x_ss.at[2], x_rs.at[2])
    sums = sum_s[...] + sum_r[...]
    ts_v[...] = jnp.broadcast_to(lax.rsqrt(sums[:, 0:128] / DT + 1e-05), (ROWS, 128)).T
    scale_v[...] = jnp.broadcast_to(lax.rsqrt(sums[:, 128:256] / DS + 1e-05), (ROWS, 128)).T
    docs_step(3)
    z_step(1)
    ag.onear_a()
    l_wq.wait()
    process([mine] + ag.near, True)
    ag.onear_b()
    z_step(2)
    ag.far_step()
    process([ag.opp, ag.far[0]])
    ag.onear_rest()
    process(ag.onear)
    z_step(3)
    ag.ofar_step()
    process([ag.far[1]])
    send(kv_acc.at[1 - c], kv_in, x_ss.at[3], x_rs.at[3], sib)
    send(q_acc.at[1 - c], q_in, x_ss.at[4], x_rs.at[4], sib)
    arrive(kv_in, x_ss.at[3], x_rs.at[3])

    row = lax.broadcasted_iota(jnp.int32, (64, 64), 0)
    col = lax.broadcasted_iota(jnp.int32, (64, 64), 1)
    take = ((row >> 3) & 1) * 32 + (row & 7) * 4 + (row >> 4)
    pick = jnp.where(col == take, 1.0, 0.0).astype(BF16)
    kv_mine = (kv_acc[c] + kv_in[...]).astype(BF16)
    kvx_s[...] = jnp.dot(pick, kv_mine, preferred_element_type=F32).astype(BF16).reshape(4, 16, 128)
    kvx_r[t] = kvx_s[t // 4]

    def kvx(k):
        to = (t + k) % 16
        return copy(kvx_s.at[to // 4], kvx_r.at[t], kx_ss.at[k], kx_rs.at[k], (s, to))

    def kvx_go(k, carry):
        kvx(k).start()
        return carry

    def kvx_got(k, carry):
        arrive(kvx_r.at[(t + 16 - k) % 16], kx_ss.at[k], kx_rs.at[k])
        return carry

    def kvx_end(k, carry):
        kvx(k).wait_send()
        return carry

    lax.fori_loop(1, 16, kvx_go, 0)
    lax.fori_loop(0, 8, wo_fetch, 0)
    lax.fori_loop(0, 8, wo_go, 0)
    z_step(4)

    cos2 = jnp.concatenate([cos_t[...], cos_t[...]], axis=0).T
    sin2 = jnp.concatenate([-sin_t[...], sin_t[...]], axis=0).T
    arrive(q_in, x_ss.at[4], x_rs.at[4])
    q_mine = q_acc[c] + q_in[...]
    for h in range(2):
        qh = q_mine[:, h * 128:(h + 1) * 128]
        turned = qh * cos2 + pltpu.roll(qh, 64, 1) * sin2
        q_v[h] = (turned * HEAD_DIM ** (-0.5)).astype(BF16)

    lax.fori_loop(1, 16, kvx_got, 0)
    both = kvx_r[...].astype(F32).reshape(16, 2, 8, ROWS)
    k_raw = both[:, 0].reshape(HEAD_DIM, ROWS)
    v_raw = both[:, 1].reshape(HEAD_DIM, ROWS)
    first, second = k_raw[0:64], k_raw[64:128]
    k_rot = jnp.concatenate(
        [first * cos_t[...] - second * sin_t[...], second * cos_t[...] + first * sin_t[...]], axis=0
    )
    kv_own[0] = k_rot.astype(BF16)
    kv_own[1] = v_raw.T.astype(BF16)
    kv_r[0, 0] = kv_own[0]
    kv_r[1, 0] = kv_own[1]

    def kv_copy(k):
        return copy(kv_own.at[c], kv_r.at[c, k], kv_ss.at[k], kv_rs.at[k], ((s + k) % 16, t))

    def kv_fwd(k):
        return copy(kv_r.at[c, k], kv_r.at[c, k], kf_ss.at[k], kf_rs.at[k], sib)

    def kv_go(k):
        @pl.when(s + k < 16)
        def _():
            kv_copy(k).start()

    def kv_mid(k):
        @pl.when(s >= k)
        def _():
            arrive(kv_r.at[c, k], kv_ss.at[k], kv_rs.at[k])
            kv_fwd(k).start()

    def kv_got(k, carry):
        @pl.when(s >= k)
        def _():
            arrive(kv_r.at[1 - c, k], kf_ss.at[k], kf_rs.at[k])
        return carry

    def kv_end(k, carry):
        @pl.when(s >= k)
        def _():
            kv_fwd(k).wait_send()

        @pl.when(s + k < 16)
        def _():
            kv_copy(k).wait_send()
        return carry

    arrive(docs_o, dc_ss.at[8], dc_rs.at[8])
    for k in (4, 5, 3, 6, 8, 7, 2, 1):
        kv_go(k)

    def docs_back(j):
        at = (z + 8 - j) % 8
        return jnp.where(z >= j, docs_z[at], jnp.where(yl == 1, docs_o[at], -1))

    key_doc = jnp.concatenate([docs_back(j) for j in range(BACK + 1)], axis=1)
    row_doc = jnp.broadcast_to(docs[...].astype(F32), (ROWS, ROWS)).T[:, 0:1].astype(jnp.int32)
    wide = (ROWS, (BACK + 1) * ROWS)
    row_at = lax.broadcasted_iota(jnp.int32, wide, 0)
    key_at = lax.broadcasted_iota(jnp.int32, wide, 1)
    allowed = (key_doc == row_doc) & ((key_at >= ROWS) | (key_at <= row_at))
    bias[...] = jnp.where(allowed, 0.0, -1e30)

    class Reduce:
        def __init__(self, y_order, own, sib_s, sib_r, x2, ra, rb, xp, xm, fm, fp, ys, yr, fin, ss, rs):
            self.own, self.sib_s, self.sib_r = own, sib_s, sib_r
            self.x2, self.ra, self.rb, self.xp, self.xm, self.fm, self.fp = x2, ra, rb, xp, xm, fm, fp
            self.ys, self.yr, self.fin, self.ss, self.rs = ys, yr, fin, ss, rs
            self.y_order = y_order
            self.x_order = (xf_, xp_, xm_, x)

        def go(self, src, dst, k, dev):
            send(src, dst, self.ss.at[k], self.rs.at[k], dev)

        def got(self, dst, k):
            arrive(dst, self.ss.at[k], self.rs.at[k])

        def slot(self, k, i):
            return self.y_order[i] * 4 + self.x_order[k]

        def to_sib(self, k, i):
            slot = self.slot(k, i)
            self.go(self.sib_s.at[slot], self.sib_r.at[slot], k * 2 + i, sib)

        def sib_got(self, k, i):
            if self.sib_r is not None:
                self.got(self.sib_r.at[self.slot(k, i)], k * 2 + i)

        def pair(self, k, i, h):
            slot, rows = self.slot(k, i), slice(h * 64, h * 64 + 64)
            value = self.own[slot, rows]
            return value if self.sib_r is None else value + self.sib_r[slot, rows].astype(F32)

        def far(self, i):
            self.sib_got(0, i)
            self.x2[i, 0:64] = self.pair(0, i, 0).astype(BF16)
            self.go(self.x2.at[i, pl.ds(0, 64)], self.ra.at[i], 8 + i, dev_xp)
            self.x2[i, 64:128] = self.pair(0, i, 1).astype(BF16)
            self.go(self.x2.at[i, pl.ds(64, 64)], self.rb.at[i], 10 + i, dev_xm)

        def near(self, i):
            self.sib_got(1, i)
            self.xp[i, 64:128] = self.pair(1, i, 1).astype(BF16)
            self.go(self.xp.at[i, pl.ds(64, 64)], self.fm.at[i, pl.ds(64, 64)], 12 + i, dev_xp)
            self.sib_got(2, i)
            self.xm[i, 0:64] = self.pair(2, i, 0).astype(BF16)
            self.go(self.xm.at[i, pl.ds(0, 64)], self.fp.at[i, pl.ds(0, 64)], 14 + i, dev_xm)

        def relay(self, i):
            self.got(self.ra.at[i], 8 + i)
            self.xp[i, 0:64] = (self.pair(1, i, 0) + self.ra[i].astype(F32)).astype(BF16)
            self.go(self.xp.at[i, pl.ds(0, 64)], self.fm.at[i, pl.ds(0, 64)], 16 + i, dev_xp)
            self.got(self.rb.at[i], 10 + i)
            self.xm[i, 64:128] = (self.pair(2, i, 1) + self.rb[i].astype(F32)).astype(BF16)
            self.go(self.xm.at[i, pl.ds(64, 64)], self.fp.at[i, pl.ds(64, 64)], 18 + i, dev_xm)

        def join(self, i, h):
            rows, at = slice(h * 64, h * 64 + 64), pl.ds(h * 64, 64)
            if h == 0:
                self.sib_got(3, i)
            self.got(self.fm.at[i, at], (16, 12)[h] + i)
            self.got(self.fp.at[i, at], (14, 18)[h] + i)
            return self.pair(3, i, h) + self.fm[i, rows].astype(F32) + self.fp[i, rows].astype(F32)

        def to_opp(self, h):
            at = pl.ds(h * 64, 64)
            return copy(self.ys.at[at], self.yr.at[at], self.ss.at[20 + h], self.rs.at[20 + h], dev_yo)

        def join_other(self):
            for h in range(2):
                self.ys[h * 64:h * 64 + 64] = self.join(0, h).astype(BF16)
                self.to_opp(h).start()

        def join_mine(self):
            for h in range(2):
                self.fin[h * 64:h * 64 + 64] = self.join(1, h)

        def end(self):
            for h in range(2):
                self.to_opp(h).wait_send()

        def last(self, h):
            rows = slice(h * 64, h * 64 + 64)
            self.got(self.yr.at[pl.ds(h * 64, 64)], 20 + h)
            return self.fin[rows] + self.yr[rows].astype(F32)

    rt = Reduce((yl, 1 - yl), t_own, t_sib_s, t_sib_r, t_x2, t_ra, t_rb, t_xp, t_xm, t_fm, t_fp, None, None, None, t_ss, t_rs)

    def t3(i, h):
        at = pl.ds(h * 64, 64)
        dev = (yl * 8 + (z + turn) % 8, rt.y_order[i] * 8 + z)
        return copy(t3_s.at[i, at], t3_r.at[yh, at], t3_ss.at[i * 2 + h], t3_rs.at[yh * 2 + h], dev)

    def t3_stays(i):
        return stays & (rt.y_order[i] == yh)

    def t_place(i):
        for h in range(2):
            rows = slice(h * 64, h * 64 + 64)
            t3_s[i, rows] = rt.join(i, h).astype(BF16)

            @pl.when(t3_stays(i))
            def _():
                t3_r[yh, rows] = t3_s[i, rows]

            @pl.when(jnp.logical_not(t3_stays(i)))
            def _():
                t3(i, h).start()

    z_step(5)
    z_step(6)

    def products(core, y_, k, width):
        rows = tg[pl.ds(core * 4, 4), :, k * width:(k + 1) * width].reshape(4 * ROWS, width)
        return jnp.dot(rows, pj[y_, k * width:(k + 1) * width], preferred_element_type=F32).reshape(4, ROWS, COLS)

    l_pj.wait()
    first = pl.ds(yl * 4, 4)
    t_sib_s[first] = products(1 - c, yl, 0, 1024).astype(BF16)
    for k in range(4):
        rt.to_sib(k, 0)
    t_own[first] = products(c, yl, 0, 1024)
    rt.far(0)
    rt.near(0)

    other = pl.ds((1 - yl) * 4, 4)
    for k in range(4):
        arrive(pj.at[1 - yl, pl.ds(k * 256, 256)], p_ss.at[k], p_rs.at[k])
        theirs = products(1 - c, 1 - yl, k, 256)
        if k == 0:
            t_part[...] = theirs
        elif k < 3:
            t_part[...] += theirs
        else:
            t_sib_s[other] = (t_part[...] + theirs).astype(BF16)
            for j in range(4):
                rt.to_sib(j, 1)
        if k == 0:
            t_own[other] = products(c, 1 - yl, k, 256)
        else:
            t_own[other] += products(c, 1 - yl, k, 256)
        if k == 1:
            rt.relay(0)
    rt.far(1)
    rt.near(1)
    t_place(0)
    for k in range(1, BACK + 1):
        kv_mid(k)

    lax.fori_loop(1, BACK + 1, kv_got, 0)
    keys = jnp.concatenate([kv_r[0, j] for j in range(BACK + 1)], axis=1)
    values = kv_r[1].reshape((BACK + 1) * ROWS, HEAD_DIM)
    for h in range(2):
        scores = jnp.dot(q_v[h], keys, preferred_element_type=F32)
        scores = scores + bias[...]
        probs = jnp.exp(scores - jnp.max(scores, axis=1, keepdims=True))
        total = jnp.sum(probs, axis=1, keepdims=True)
        acc = jnp.dot(probs.astype(BF16), values, preferred_element_type=F32)
        attn_v[c * 2 + h] = (acc / total).astype(BF16)
        send(attn_v.at[c * 2 + h], attn_v.at[c * 2 + h], x_ss.at[5 + h], x_rs.at[5 + h], sib)
    lax.fori_loop(0, 8, wo_got, 0)
    rt.relay(1)

    ro = Reduce((yo_, yh), o_own, None, None, o_x2, o_ra, o_rb, o_xp, o_xm, o_fm, o_fp, o_ys, o_yr, o_fin, o_ss, o_rs)

    for h in range(2):
        arrive(attn_v.at[2 - 2 * c + h], x_ss.at[5 + h], x_rs.at[5 + h])
    attn = jnp.concatenate([attn_v[i] for i in range(4)], axis=1)

    def out_block(k, i):
        slot = ro.slot(k, i)
        o_own[slot] = jnp.dot(attn, wo[slot].reshape(COLS, COLS), preferred_element_type=F32)

    out_block(0, 0)
    ro.far(0)
    out_block(1, 0)
    out_block(2, 0)
    ro.near(0)
    t_place(1)
    out_block(0, 1)
    ro.relay(0)
    ro.far(1)
    out_block(1, 1)
    out_block(2, 1)
    ro.near(1)
    out_block(3, 0)
    out_block(3, 1)
    ro.relay(1)

    ro.join_other()
    ro.join_mine()

    early = list(started)
    started.clear()

    def before_end():
        for one in early:
            one.wait_send()
        lax.fori_loop(0, 8, w_end, 0)
        lax.fori_loop(0, 8, wo_end, 0)
        lax.fori_loop(1, 16, kvx_end, 0)
        lax.fori_loop(1, BACK + 1, kv_end, 0)
        ro.end()
        for i in range(2):

            @pl.when(jnp.logical_not(t3_stays(i)))
            def _():
                t3(i, 0).wait_send()
                t3(i, 1).wait_send()

    dg = Gather(db, dg_ss, dg_rs)
    for h in range(2):
        rows = slice(h * 64, h * 64 + 64)
        mixed = hb[mine, rows].astype(F32) + ro.last(h)
        out_s[rows] = mixed.astype(BF16)

        for p in range(2):

            @pl.when(jnp.logical_not(stays & (yh == p)))
            def _():
                arrive(t3_r.at[p, pl.ds(h * 64, 64)], t3_ss.at[h], t3_rs.at[p * 2 + h])

        target = t3_r[0, rows].astype(F32) + t3_r[1, rows].astype(F32)
        target = target * jnp.concatenate([ts_v[rows]] * 4, axis=1)
        difference = mixed - target
        db[mine, rows] = difference.astype(BF16)
        dg.begin(h)
        squares = difference * difference
        l_v[rows] = (
            squares[:, 0:128] + squares[:, 128:256] + squares[:, 256:384] + squares[:, 384:512]
        )
    l_s[...] = jnp.sum(l_v[...].T, axis=0, keepdims=True)
    l_r[t] = l_s[...]

    def loss(k):
        return copy(l_s, l_r.at[t], l_ss.at[k], l_rs.at[k], (s, (t + k) % 16))

    def loss_go(k, carry):
        loss(k).start()
        return carry

    def loss_got(k, carry):
        arrive(l_r.at[(t + 16 - k) % 16], l_ss.at[k], l_rs.at[k])
        return carry

    def loss_end(k, carry):
        loss(k).wait_send()
        return carry

    lax.fori_loop(1, 16, loss_go, 0)

    def add_grad(slots, first=False):
        d = jnp.concatenate([db[slot] for slot in slots], axis=1)
        for core in range(2):
            w = jnp.concatenate([wo[slot, core] for slot in slots], axis=1)
            g = nt_dot(d, w)
            g_acc[core] = g if first else g_acc[core] + g

    dg.near_relay()
    dg.opp_half(0)
    dg.near_rest()
    add_grad([mine] + dg.near, True)
    dg.opp_half(1)
    dg.onear_a()
    dg.onear_b()
    dg.far_step()
    add_grad([dg.opp, dg.far[0]])
    before_end()
    dg.onear_rest()
    add_grad(dg.onear)
    lax.fori_loop(1, 16, loss_got, 0)
    loss_sum = l_r[0]
    for i in range(1, 16):
        loss_sum = loss_sum + l_r[i]
    out_l[...] = loss_sum / DS
    dg.ofar_step()
    add_grad([dg.far[1]])
    send(g_acc.at[1 - c], g_in, x_ss.at[7], x_rs.at[7], sib)
    arrive(g_in, x_ss.at[7], x_rs.at[7])
    out_g[...] = (g_acc[c] + g_in[...]).astype(BF16)

    flush()
    lax.fori_loop(1, 16, loss_end, 0)


def reduce_buffers():
    block = (ROWS, COLS)
    return [
        pltpu.VMEM((2, 64, COLS), BF16),
        pltpu.VMEM((2, 64, COLS), BF16),
        pltpu.VMEM((2,) + block, BF16),
        pltpu.VMEM((2,) + block, BF16),
        pltpu.VMEM((2,) + block, BF16),
        pltpu.VMEM((2,) + block, BF16),
        pltpu.VMEM(block, BF16),
        pltpu.VMEM(block, BF16),
        pltpu.VMEM(block, F32),
    ]


def on_device(
    teacher_hidden, teacher_gain, projector, student_hidden, student_gain,
    query_weight, kv_weight, out_weight, doc_ids,
):
    block = (ROWS, COLS)
    hbm = pl.BlockSpec(memory_space=pltpu.HBM)
    vmem = pl.BlockSpec(memory_space=pltpu.VMEM)
    dma = pltpu.SemaphoreType.DMA
    out_s, out_l, out_g = pl.pallas_call(
        body,
        out_shape=(
            jax.ShapeDtypeStruct(block, BF16),
            jax.ShapeDtypeStruct((1, ROWS), F32),
            jax.ShapeDtypeStruct((ROWS, 256), BF16),
        ),
        in_specs=[hbm] * 9,
        out_specs=(vmem, vmem, vmem),
        scratch_shapes=[
            pltpu.VMEM((1, 1024), F32),
            pltpu.VMEM((1, COLS), F32),
            pltpu.VMEM((1, ROWS), jnp.int32),
            pltpu.VMEM((ROWS, 1024), BF16),
            pltpu.VMEM((8, ROWS, 1024), BF16),
            pltpu.VMEM((2, 1024, COLS), BF16),
            pltpu.VMEM((8, 2, COLS, 256), BF16),
            pltpu.VMEM((8, 2, 2, 32, COLS), BF16),
            pltpu.VMEM((8, 2, 256, COLS), BF16),
            pltpu.VMEM((64, ROWS), F32),
            pltpu.VMEM((64, ROWS), F32),
            pltpu.VMEM((8,) + block, BF16),
            pltpu.VMEM((1, 768), F32),
            pltpu.VMEM((8, 1, 768), F32),
            pltpu.VMEM((1, 256), F32),
            pltpu.VMEM((1, 256), F32),
            pltpu.VMEM((ROWS, 128), F32),
            pltpu.VMEM((2, ROWS, 256), F32),
            pltpu.VMEM((ROWS, 256), F32),
            pltpu.VMEM((2, 64, ROWS), F32),
            pltpu.VMEM((64, ROWS), F32),
            pltpu.VMEM((4, 16, ROWS), BF16),
            pltpu.VMEM((16, 16, ROWS), BF16),
            pltpu.VMEM((2, ROWS, HEAD_DIM), BF16),
            pltpu.VMEM((2, BACK + 1, ROWS, HEAD_DIM), BF16),
            pltpu.VMEM((8, 1, ROWS), jnp.int32),
            pltpu.VMEM((8, 1, ROWS), jnp.int32),
            pltpu.VMEM((2, ROWS, HEAD_DIM), BF16),
            pltpu.VMEM((4, ROWS, HEAD_DIM), BF16),
            pltpu.VMEM((ROWS, (BACK + 1) * ROWS), F32),
            pltpu.VMEM((8,) + block, F32),
            pltpu.VMEM((4,) + block, F32),
            pltpu.VMEM((8,) + block, F32),
            pltpu.VMEM((2,) + block, BF16),
            pltpu.VMEM((8,) + block, BF16),
            pltpu.VMEM((8,) + block, BF16),
            pltpu.VMEM((2,) + block, BF16),
            *reduce_buffers()[:6],
            *reduce_buffers(),
            pltpu.VMEM((2,) + block, BF16),
            pltpu.VMEM((2,) + block, BF16),
            pltpu.VMEM((ROWS, 128), F32),
            pltpu.VMEM((8,) + block, BF16),
            pltpu.VMEM((2, ROWS, 256), F32),
            pltpu.VMEM((ROWS, 256), F32),
            pltpu.VMEM((ROWS, 128), F32),
            pltpu.VMEM((1, ROWS), F32),
            pltpu.VMEM((16, 1, ROWS), F32),
            dma((10,)),
            *[dma((8,)) for _ in range(10)],
            dma((16,)), dma((16,)), dma((8,)), dma((8,)),
            dma((24,)), dma((24,)), dma((24,)), dma((24,)),
            dma((16,)), dma((16,)), dma((16,)), dma((16,)),
            dma((9,)), dma((9,)), dma((9,)), dma((9,)), dma((9,)), dma((9,)),
            dma((24,)), dma((24,)), dma((24,)), dma((24,)),
            dma((4,)), dma((4,)),
            dma((16,)), dma((16,)),
        ],
        compiler_params=pltpu.CompilerParams(
            collective_id=0, has_side_effects=True, vmem_limit_bytes=40 * 1024 * 1024
        ),
    )(
        *(
            pltpu.with_memory_space_constraint(one, pltpu.HBM)
            for one in (
                teacher_hidden, teacher_gain.reshape(1, -1), projector, student_hidden,
                student_gain.reshape(1, -1), query_weight.reshape(8, 2, COLS, 256), jnp.transpose(kv_weight, (0, 2, 1)),
                out_weight, doc_ids.reshape(1, -1),
            )
        )
    )
    return out_s, out_l.reshape(ROWS), out_g


def solution(mesh):
    in_specs = (
        P("seq", "tensor"),
        P("tensor"),
        P("tensor", "seq"),
        P("seq", "tensor"),
        P("tensor"),
        P(None, "tensor"),
        P(None, None, "tensor"),
        P("tensor", None),
        P("seq"),
    )
    out_specs = (P("seq", "tensor"), P("seq"), P("seq", "tensor"))
    return jax.shard_map(
        on_device, mesh=mesh, in_specs=in_specs, out_specs=out_specs, check_vma=False
    )
```
